32 devices in a mesh: seq: 8 (over z, y), fsdp: 4 (over x, core).
Axes of the slice: x: 2, y: 2, z: 4, core: 2. Of those that a mesh axis runs over, the one named last changes fastest.
Arguments:
- tokens: bfloat16 [4, 4096, 2048], P('fsdp', 'seq'), may hold values from -9 to 9
- qkv_weight: bfloat16 [2048, 1536], P('fsdp'), may hold values from -0.26516504 to 0.26516504
- near_offset: int32 [4], replicated, may hold values from 0 to 3
- far_offset: int32 [4], replicated, may hold values from 0 to 31
Outputs:
- mixed: bfloat16 [4, 4096, 512], P('fsdp', 'seq')
The draws below stay inside these ranges and needn't reach their ends.
All inputs are finite; a program needn't handle non-finite values.
Results may differ from the reference program's by a relative error of at most 0.0074.
Values may be sent and summed in bfloat16 or wider, within the bound.
No kernel may reach another device: no remote copies, remote signals or barrier semaphores. Data moves between devices by JAX's collectives and lax.ppermute only.
A program may use at most 64 MiB of HBM per device.

```python
import jax
import jax.numpy as jnp
from jax import lax

D = 2048
HEADS = 4
HEAD_DIM = 128
BLOCK = 128
STRIDE = 8
TOK_DEV = 512
SEQS = 4
LEN = 4096
NEAR_RATE = 4
FAR_RATE = 32
N_SEQ = 8


def draw_tokens(key, part):
    random_part = jnp.clip(jax.random.normal(jax.random.fold_in(key, 1), (SEQS, LEN, D), jnp.float32), -6.0, 6.0)
    return random_part.astype(jnp.bfloat16)


def draw_qkv_weight(key, part):
    qkv_width = HEADS * HEAD_DIM
    column_scale = jnp.concatenate([jnp.full((qkv_width,), 1.6, jnp.float32), jnp.ones((2 * qkv_width,), jnp.float32)])
    drawn_part = jnp.clip(jax.random.normal(jax.random.fold_in(key, 5), (D, 3 * qkv_width), jnp.float32), -6.0, 6.0) * D ** (-0.5)
    drawn_part = drawn_part * column_scale[None, :]
    return drawn_part.astype(jnp.bfloat16)


def set_ends(values, own_key, least, high):
    longest = values.shape.index(max(values.shape))
    spots = []
    for shift in (0, 1):
        where = [jax.random.randint(jax.random.fold_in(own_key, axis), (), 0, length) for axis, length in enumerate(values.shape)]
        where[longest] = (where[longest] + shift) % values.shape[longest]
        spots.append(tuple(where))
    return values.at[spots[0]].set(least).at[spots[1]].set(high)


def setup_inputs(seed: int = 0) -> dict:
    key_of = jax.random.split(jax.random.key(seed), 5)
    return {
        "tokens": draw_tokens(jax.random.fold_in(key_of[4], 71), 0),
        "qkv_weight": draw_qkv_weight(jax.random.fold_in(key_of[4], 71), 0),
        "near_offset": set_ends(jax.random.randint(key_of[2], (HEADS,), 0, NEAR_RATE), jax.random.fold_in(key_of[2], 1), 0, NEAR_RATE - 1).astype(jnp.int32),
        "far_offset": set_ends(jax.random.randint(key_of[3], (HEADS,), 0, FAR_RATE), jax.random.fold_in(key_of[3], 1), 0, FAR_RATE - 1).astype(jnp.int32),
    }


NEG = -1e30


def causal_stats(packed):
    query, key_block, value_block = packed
    length_rows = query.shape[0]
    scores = jnp.einsum('qd,kd->qk', query.astype(jnp.float32), key_block.astype(jnp.float32)) * (HEAD_DIM ** -0.5)
    positions = jnp.arange(length_rows)
    scores = jnp.where(positions[None, :] <= positions[:, None], scores, NEG)
    best_score = jnp.max(scores, axis=1)
    weights = jnp.exp(scores - best_score[:, None])
    weight_sum = jnp.sum(weights, axis=1)
    rounded = lax.optimization_barrier(weights.astype(jnp.bfloat16))
    weighted = jnp.einsum('qk,kd->qd', rounded.astype(jnp.float32), value_block.astype(jnp.float32))
    return best_score, weight_sum, weighted


def reference(tokens, qkv_weight, near_offset, far_offset):
    def one_sequence(sequence):
        qkv_width = HEADS * HEAD_DIM
        device_count = N_SEQ
        block_rate = TOK_DEV // BLOCK
        near_size = min(16, N_SEQ)
        half_size = near_size // 2
        far_size = min(16, N_SEQ // STRIDE)
        far_groups = device_count // (STRIDE * far_size)
        head_index = jnp.arange(HEADS)
        projected = jnp.dot(sequence, qkv_weight, preferred_element_type=jnp.float32).astype(jnp.bfloat16)
        query = projected[:, :qkv_width].reshape(LEN, HEADS, HEAD_DIM)
        key_all = projected[:, qkv_width:2 * qkv_width].reshape(LEN, HEADS, HEAD_DIM)
        value_all = projected[:, 2 * qkv_width:].reshape(LEN, HEADS, HEAD_DIM)

        def local_view(field):
            arranged = field.reshape(device_count, TOK_DEV, HEADS, HEAD_DIM).transpose(0, 2, 1, 3)
            return arranged.reshape(device_count * HEADS, TOK_DEV, HEAD_DIM)

        local_top, local_sum, local_out = lax.map(causal_stats, (local_view(query), local_view(key_all), local_view(value_all)))
        local_top = local_top.reshape(device_count, HEADS, block_rate, BLOCK)
        local_sum = local_sum.reshape(device_count, HEADS, block_rate, BLOCK)
        local_out = local_out.reshape(device_count, HEADS, block_rate, BLOCK, HEAD_DIM)

        def near_view(field):
            blocks = field.reshape(device_count, block_rate, BLOCK, HEADS, HEAD_DIM)
            picked = blocks[:, near_offset, :, head_index, :]
            padding = jnp.zeros((HEADS, half_size, BLOCK, HEAD_DIM), picked.dtype)
            assembled = jnp.concatenate([picked[:, :half_size], padding, picked[:, half_size:], padding], axis=1)
            return assembled.reshape(HEADS * (device_count // near_size + 1), near_size * BLOCK, HEAD_DIM)

        def near_back(field):
            shaped = field.reshape((HEADS, device_count + near_size) + field.shape[1:][:0] + (BLOCK,) + field.shape[2:])
            return jnp.concatenate([shaped[:, :half_size], shaped[:, near_size:device_count + half_size]], axis=1)

        near_top, near_sum, near_out = lax.map(causal_stats, (near_view(query), near_view(key_all), near_view(value_all)))
        near_top = near_back(near_top.reshape(HEADS, (device_count + near_size) * BLOCK)).transpose(1, 0, 2)[:, :, None, :]
        near_sum = near_back(near_sum.reshape(HEADS, (device_count + near_size) * BLOCK)).transpose(1, 0, 2)[:, :, None, :]
        near_out = near_back(near_out.reshape(HEADS, (device_count + near_size) * BLOCK, HEAD_DIM)).transpose(1, 0, 2, 3)[:, :, None, :, :]
        near_mask = (jnp.arange(block_rate)[None, :] == near_offset[:, None])[None, :, :, None]
        near_top = jnp.where(near_mask, near_top, NEG)

        far_class = far_offset // block_rate
        far_block = far_offset % block_rate

        def far_view(field):
            blocks = field.reshape(far_groups, far_size, STRIDE, block_rate, BLOCK, HEADS, HEAD_DIM)
            picked = blocks[:, :, far_class, far_block, :, head_index, :]
            return picked.reshape(HEADS * far_groups, far_size * BLOCK, HEAD_DIM)

        far_top, far_sum, far_out = lax.map(causal_stats, (far_view(query), far_view(key_all), far_view(value_all)))
        full_shape = (far_groups, far_size, STRIDE, HEADS, block_rate, BLOCK)

        def spread(field):
            arranged = field.reshape(HEADS, far_groups, far_size, BLOCK).transpose(1, 2, 0, 3)[:, :, None, :, None, :]
            return jnp.broadcast_to(arranged, full_shape).reshape(device_count, HEADS, block_rate, BLOCK)

        far_top_full = spread(far_top)
        far_sum_full = spread(far_sum)
        arranged_out = far_out.reshape(HEADS, far_groups, far_size, BLOCK, HEAD_DIM).transpose(1, 2, 0, 3, 4)[:, :, None, :, None, :, :]
        far_out_full = jnp.broadcast_to(arranged_out, full_shape + (HEAD_DIM,)).reshape(device_count, HEADS, block_rate, BLOCK, HEAD_DIM)
        class_match = jnp.arange(STRIDE)[:, None, None] == far_class[None, :, None]
        block_match = jnp.arange(block_rate)[None, None, :] == far_block[None, :, None]
        far_mask = jnp.broadcast_to((class_match & block_match)[None, None, :, :, :, None], full_shape).reshape(device_count, HEADS, block_rate, BLOCK)
        far_top_full = jnp.where(far_mask, far_top_full, NEG)

        best_score = jnp.maximum(jnp.maximum(local_top, near_top), far_top_full)
        local_weight = jnp.exp(local_top - best_score)
        near_weight = jnp.where(near_mask, jnp.exp(near_top - best_score), 0.0)
        far_weight = jnp.where(far_mask, jnp.exp(far_top_full - best_score), 0.0)
        numerator = local_weight[..., None] * local_out + near_weight[..., None] * near_out + far_weight[..., None] * far_out_full
        denominator = local_weight * local_sum + near_weight * near_sum + far_weight * far_sum_full
        mixed = numerator / denominator[..., None]
        return mixed.transpose(0, 2, 3, 1, 4).reshape(LEN, qkv_width).astype(jnp.bfloat16)

    return lax.map(one_sequence, tokens)
```

```python
import functools
import math

import jax
import jax.numpy as jnp
from jax import lax
from jax.experimental import pallas as pl
from jax.experimental.pallas import tpu as pltpu
from jax.sharding import PartitionSpec as P

HEADS = 4
HEAD_DIM = 128
BLOCK = 128
STRIDE = 8
WIDTH = HEADS * HEAD_DIM
PAIR = 2 * HEAD_DIM
NEG = -1e30
SCALE2 = HEAD_DIM ** (-0.5) * math.log2(math.e)
VMEM_LIMIT = 48 * 1024 * 1024
F32 = jnp.float32
BF16 = jnp.bfloat16


def near_place(index, half, size):
    if index < half:
        return 0, index
    return 1 + (index - half) // size, (index - half) % size


def shift_pairs(count, place, step):
    pairs = []
    for source in range(count - step):
        if place(source)[0] == place(source + step)[0]:
            pairs.append((source, source + step))
    return pairs


def swap(value, axis, bit):
    count = lax.axis_size(axis)
    return lax.ppermute(value, axis, [(i, i ^ bit) for i in range(count)])


def rows_of(block):
    return pl.ds(pl.multiple_of(block * BLOCK, BLOCK), BLOCK)


def qk(query, key):
    return lax.dot_general(query, key, (((1,), (1,)), ((), ())), preferred_element_type=F32)


def pv(weights, value):
    return jnp.dot(weights.astype(BF16), value, preferred_element_type=F32)


def kv_kernel(pieces, slots, slot_at, meta, *refs):
    tokens, weights = refs[:pieces], refs[pieces : 2 * pieces]
    kv = refs[2 * pieces]
    packs = refs[2 * pieces + 1 :]
    total = jnp.dot(tokens[0][...], weights[0][...], preferred_element_type=F32)
    for piece in range(1, pieces):
        total += jnp.dot(tokens[piece][...], weights[piece][...], preferred_element_type=F32)
    kv[...] = total.astype(BF16)
    step = pl.program_id(0)
    for i in range(2):
        head = (2 * step + i) % HEADS
        lanes = slice(i * HEAD_DIM, (i + 1) * HEAD_DIM)
        for slot in range(slots):
            block = meta[slot_at + HEADS * slot + head]
            packs[slot][:, lanes] = kv[rows_of(block), lanes]


def attend_kernel(pieces, slots, slot_at, match_at, meta, *refs):
    tokens, weights = refs[:pieces], refs[pieces : 2 * pieces]
    key, value = refs[2 * pieces : 2 * pieces + 2]
    out = refs[2 * pieces + 2]
    state = refs[2 * pieces + 3 : 2 * pieces + 3 + 4 * slots]
    query, acc_all, top_all, sum_all = refs[2 * pieces + 3 + 4 * slots :]
    total = jnp.dot(tokens[0][...], weights[0][...], preferred_element_type=F32)
    for piece in range(1, pieces):
        total += jnp.dot(tokens[piece][...], weights[piece][...], preferred_element_type=F32)
    query[...] = total.astype(BF16)
    step = pl.program_id(0)
    blocks = query.shape[0] // BLOCK
    row = lax.broadcasted_iota(jnp.int32, (BLOCK, BLOCK), 0)
    column = lax.broadcasted_iota(jnp.int32, (BLOCK, BLOCK), 1)
    causal = column <= row
    for i in range(2):
        head = 2 * step + i
        lanes = slice(i * HEAD_DIM, (i + 1) * HEAD_DIM)
        near_block = meta[slot_at + head]
        far_block = meta[slot_at + HEADS + head]
        far_match = meta[match_at + head]
        for b in range(blocks):
            rows = slice(b * BLOCK, (b + 1) * BLOCK)
            times = (
                1 + jnp.where(near_block == b, 1, 0) + jnp.where(far_block == b, far_match, 0)
            ).astype(F32)
            mine = query[rows, lanes]
            diagonal = jnp.where(causal, qk(mine, key[rows, lanes]), NEG)
            top = jnp.max(diagonal, axis=1, keepdims=True)
            if b:
                before = qk(mine, key[: b * BLOCK, lanes])
                top = jnp.maximum(top, jnp.max(before, axis=1, keepdims=True))
            weight = jnp.exp2((diagonal - top) * SCALE2) * times
            summed = jnp.sum(weight, axis=1, keepdims=True)
            acc = pv(weight, value[rows, lanes])
            if b:
                weight = jnp.exp2((before - top) * SCALE2)
                summed += jnp.sum(weight, axis=1, keepdims=True)
                acc += pv(weight, value[: b * BLOCK, lanes])
            out[rows, lanes] = (acc / summed).astype(BF16)
            acc_all[rows, lanes] = acc
            top_all[rows, lanes] = jnp.broadcast_to(top, (BLOCK, HEAD_DIM))
            sum_all[rows, lanes] = jnp.broadcast_to(summed, (BLOCK, HEAD_DIM))
        for slot in range(slots):
            rows = rows_of((near_block, far_block)[slot])
            for target, source in zip(state[4 * slot :], (query, acc_all, top_all, sum_all)):
                target[:, lanes] = source[rows, lanes]


def merge_kernel(shifts, slot_at, match_at, place_at, meta, *refs):
    slots = len(shifts)
    state = refs[: 4 * slots]
    packs = refs[4 * slots : 4 * slots + sum(shifts)]
    before, out = refs[4 * slots + sum(shifts) :]
    out[...] = before[...]
    for head in range(HEADS):
        lanes = slice(head * HEAD_DIM, (head + 1) * HEAD_DIM)
        value_lanes = slice(WIDTH + head * HEAD_DIM, WIDTH + (head + 1) * HEAD_DIM)
        near_block = meta[slot_at + head]
        far_block = meta[slot_at + HEADS + head]
        far_match = meta[match_at + head]
        earlier = None
        for slot in range(slots):
            query, acc, top, summed = (ref[:, lanes] for ref in state[4 * slot : 4 * slot + 4])
            if slot:
                same = near_block == far_block
                acc, top, summed = (
                    jnp.where(same, new, old) for new, old in zip(earlier, (acc, top, summed))
                )
            place = meta[place_at + slot]
            first = sum(shifts[:slot])
            scores = []
            for step in range(1, shifts[slot] + 1):
                seen = place >= step
                if slot:
                    seen = seen & (far_match == 1)
                score = qk(query, packs[first + step - 1][:, lanes])
                scores.append(jnp.where(seen, score, NEG))
            best = top
            for score in scores:
                best = jnp.maximum(best, jnp.max(score, axis=1, keepdims=True))
            decay = jnp.exp2((top - best) * SCALE2)
            acc = acc * decay
            summed = summed * decay
            for step, score in enumerate(scores):
                weight = jnp.exp2((score - best) * SCALE2)
                summed = summed + jnp.sum(weight, axis=1, keepdims=True)
                acc = acc + pv(weight, packs[first + step][:, value_lanes])
            out[rows_of((near_block, far_block)[slot]), lanes] = (acc / summed).astype(BF16)
            earlier = (acc, best, summed)


def body(tokens, qkv_weight, near_offset, far_offset):
    sequence = tokens[0]
    row_count, depth = sequence.shape
    share = qkv_weight.shape[0]
    block_rate = row_count // BLOCK
    seq_size = lax.axis_size("seq")
    seq_index = lax.axis_index("seq")
    pieces = lax.axis_size("fsdp")
    mine = lax.axis_index("fsdp")
    near_size = min(16, seq_size)
    half = near_size // 2
    far_size = max(1, min(16, seq_size // STRIDE))
    near_at = lambda i: near_place(i, half, near_size)
    far_at = lambda i: (i // (STRIDE * far_size) * STRIDE + i % STRIDE, i // STRIDE % far_size)
    near_shifts = max(near_at(i)[1] for i in range(seq_size))
    far_shifts = far_size - 1
    slots = 2 if far_shifts else 1

    slot_at, match_at, place_at = pieces, pieces + 2 * HEADS, pieces + 3 * HEADS
    near_position = jnp.where(seq_index < half, seq_index, (seq_index - half) % near_size)
    far_position = seq_index // STRIDE % far_size
    far_match = (seq_index % STRIDE == far_offset // block_rate).astype(jnp.int32)
    meta = jnp.concatenate(
        [
            mine ^ jnp.arange(pieces, dtype=jnp.int32),
            near_offset,
            far_offset % block_rate,
            far_match,
            jnp.stack([near_position, far_position]).astype(jnp.int32),
        ]
    )

    own_kv = qkv_weight[:, WIDTH:]
    own_q = qkv_weight[:, :WIDTH]
    kv_pieces = [(qkv_weight, 2)]
    q_pieces = [(qkv_weight, 0)]
    if pieces > 1:
        other = swap(qkv_weight, "fsdp", 1)
        kv_pieces.append((other, 2))
        q_pieces.append((other, 0))
    for bit in range(2, pieces, 2):
        arrived = swap(own_kv, "fsdp", bit)
        kv_pieces += [(arrived, 0), (swap(arrived, "fsdp", 1), 0)]
        own_q, _ = lax.optimization_barrier((own_q, arrived))
    for bit in range(2, pieces, 2):
        arrived = swap(own_q, "fsdp", bit)
        q_pieces += [(arrived, 0), (swap(arrived, "fsdp", 1), 0)]

    def token_spec(piece):
        return pl.BlockSpec((row_count, share), lambda j, meta: (0, meta[piece]))

    def weight_spec(offset):
        return pl.BlockSpec((share, PAIR), lambda j, meta: (0, j + offset))

    token_specs = [token_spec(piece) for piece in range(pieces)]
    params = pltpu.CompilerParams(vmem_limit_bytes=VMEM_LIMIT)
    slot_block = pl.BlockSpec((BLOCK, PAIR), lambda j, meta: (0, j))

    kv, *packs = pl.pallas_call(
        functools.partial(kv_kernel, pieces, slots, slot_at),
        grid_spec=pltpu.PrefetchScalarGridSpec(
            num_scalar_prefetch=1,
            grid=(2 * WIDTH // PAIR,),
            in_specs=token_specs + [weight_spec(offset) for _, offset in kv_pieces],
            out_specs=[pl.BlockSpec((row_count, PAIR), lambda j, meta: (0, j))] + [slot_block] * slots,
        ),
        out_shape=[jax.ShapeDtypeStruct((row_count, 2 * WIDTH), BF16)]
        + [jax.ShapeDtypeStruct((BLOCK, 2 * WIDTH), BF16)] * slots,
        compiler_params=params,
        cost_estimate=pl.CostEstimate(
            flops=4 * row_count * depth * WIDTH, bytes_accessed=8 * depth * WIDTH, transcendentals=0
        ),
        name="project_kv",
    )(meta, *[sequence] * pieces, *[array for array, _ in kv_pieces])

    near_packs = [
        lax.ppermute(packs[0], "seq", shift_pairs(seq_size, near_at, step))
        for step in range(1, near_shifts + 1)
    ]
    far_packs = [
        lax.ppermute(packs[1], "seq", shift_pairs(seq_size, far_at, step * STRIDE))
        for step in range(1, far_shifts + 1)
    ]

    state_types = [BF16, F32, F32, F32]
    partial_out, *state = pl.pallas_call(
        functools.partial(attend_kernel, pieces, slots, slot_at, match_at),
        grid_spec=pltpu.PrefetchScalarGridSpec(
            num_scalar_prefetch=1,
            grid=(WIDTH // PAIR,),
            in_specs=token_specs
            + [weight_spec(offset) for _, offset in q_pieces]
            + [
                pl.BlockSpec((row_count, PAIR), lambda j, meta: (0, j)),
                pl.BlockSpec((row_count, PAIR), lambda j, meta: (0, j + WIDTH // PAIR)),
            ],
            out_specs=[pl.BlockSpec((row_count, PAIR), lambda j, meta: (0, j))]
            + [slot_block] * (4 * slots),
            scratch_shapes=[pltpu.VMEM((row_count, PAIR), kind) for kind in state_types],
        ),
        out_shape=[jax.ShapeDtypeStruct((row_count, WIDTH), BF16)]
        + [jax.ShapeDtypeStruct((BLOCK, WIDTH), kind) for kind in state_types] * slots,
        compiler_params=params,
        cost_estimate=pl.CostEstimate(
            flops=2 * row_count * depth * WIDTH + 4 * row_count * row_count * WIDTH,
            bytes_accessed=4 * depth * WIDTH,
            transcendentals=HEADS * row_count * row_count,
        ),
        name="attend_local",
    )(meta, *[sequence] * pieces, *[array for array, _ in q_pieces], kv, kv)

    whole = pl.BlockSpec(memory_space=pltpu.VMEM)
    shifts = (near_shifts, far_shifts)[:slots]
    merged = pl.pallas_call(
        functools.partial(merge_kernel, shifts, slot_at, match_at, place_at),
        in_specs=[pl.BlockSpec(memory_space=pltpu.SMEM)] + [whole] * (4 * slots + sum(shifts) + 1),
        out_specs=whole,
        out_shape=jax.ShapeDtypeStruct((row_count, WIDTH), BF16),
        compiler_params=params,
        cost_estimate=pl.CostEstimate(
            flops=4 * BLOCK * BLOCK * WIDTH * sum(shifts),
            bytes_accessed=4 * BLOCK * WIDTH * sum(shifts),
            transcendentals=BLOCK * BLOCK * HEADS * sum(shifts),
        ),
        name="merge_near",
    )(meta, *state, *near_packs, *far_packs, partial_out)
    return merged[None]


def solution(mesh):
    in_specs = (P("fsdp", "seq", None), P("fsdp", None), P(), P())
    out_specs = P("fsdp", "seq", None)
    return jax.shard_map(body, mesh=mesh, in_specs=in_specs, out_specs=out_specs, check_vma=False)
```

```python
import functools
import math

import jax
import jax.numpy as jnp
from jax import lax
from jax.experimental import pallas as pl
from jax.experimental.pallas import tpu as pltpu
from jax.sharding import PartitionSpec as P

HEADS = 4
HEAD_DIM = 128
BLOCK = 128
STRIDE = 8
WIDTH = HEADS * HEAD_DIM
PAIR = 2 * HEAD_DIM
NEG = -1e30
SCALE2 = HEAD_DIM ** (-0.5) * math.log2(math.e)
VMEM_LIMIT = 24 * 1024 * 1024
F32 = jnp.float32
BF16 = jnp.bfloat16


def near_place(index, half, size):
    if index < half:
        return 0, index
    return 1 + (index - half) // size, (index - half) % size


def shift_pairs(count, place, step):
    pairs = []
    for source in range(count - step):
        if place(source)[0] == place(source + step)[0]:
            pairs.append((source, source + step))
    return pairs


def swap(value, axis, bit):
    count = lax.axis_size(axis)
    return lax.ppermute(value, axis, [(i, i ^ bit) for i in range(count)])


def after(value, *others):
    return lax.optimization_barrier((value,) + others)[0]


def rows_of(block):
    return pl.ds(pl.multiple_of(block * BLOCK, BLOCK), BLOCK)


def qk(query, key):
    return lax.dot_general(query, key, (((1,), (1,)), ((), ())), preferred_element_type=F32)


def pv(weights, value):
    return jnp.dot(weights.astype(BF16), value, preferred_element_type=F32)


def add_up(tokens, places, weights):
    total = None
    for place, weight in zip(places, weights):
        depth = weight.shape[0]
        columns = pl.ds(pl.multiple_of(place, depth), depth)
        term = jnp.dot(tokens[:, columns], weight[...], preferred_element_type=F32)
        total = term if total is None else total + term
    return total


def start_kernel(places_at, meta, tokens, *refs):
    weights, out = refs[:-1], refs[-1]
    places = [meta[at] for at in places_at]
    for j in range(out.shape[1] // PAIR):
        lanes = slice(j * PAIR, (j + 1) * PAIR)
        out[:, lanes] = add_up(tokens, places, [weight.at[:, lanes] for weight in weights])


def kv_kernel(pair, places_at, slots, slot_at, meta, tokens, partial, *refs):
    weights, kv, packs = refs[: len(places_at)], refs[len(places_at)], refs[len(places_at) + 1 :]
    places = [meta[at] for at in places_at]
    for field in range(2):
        lanes = slice(field * PAIR, (field + 1) * PAIR)
        first = (field + 1) * WIDTH + pair * PAIR
        total = partial[:, first : first + PAIR]
        if weights:
            total = total + add_up(tokens, places, [weight.at[:, lanes] for weight in weights])
        kv[:, lanes] = total.astype(BF16)
    for slot in range(slots):
        for i in range(2):
            rows = rows_of(meta[slot_at + HEADS * slot + 2 * pair + i])
            for field in range(2):
                lanes = slice(field * PAIR + i * HEAD_DIM, field * PAIR + (i + 1) * HEAD_DIM)
                packs[slot][:, lanes] = kv[rows, lanes]


def attend_kernel(places_at, slots, slot_at, match_at, meta, tokens, partial, *refs):
    weights, refs = refs[: len(places_at)], refs[len(places_at) :]
    kv, out, refs = refs[:2], refs[2], refs[3:]
    state, scratch = refs[: 4 * slots], refs[4 * slots :]
    query, acc_all, top_all, sum_all = scratch
    places = [meta[at] for at in places_at]
    blocks = query.shape[0] // BLOCK
    row = lax.broadcasted_iota(jnp.int32, (BLOCK, BLOCK), 0)
    column = lax.broadcasted_iota(jnp.int32, (BLOCK, BLOCK), 1)
    causal = column <= row
    for pair in range(HEADS // 2):
        lanes = slice(pair * PAIR, (pair + 1) * PAIR)
        total = partial[:, lanes]
        if weights:
            total = total + add_up(tokens, places, [weight.at[:, lanes] for weight in weights])
        query[:, lanes] = total.astype(BF16)
    for head in range(HEADS):
        lanes = slice(head * HEAD_DIM, (head + 1) * HEAD_DIM)
        key_lanes = slice(head % 2 * HEAD_DIM, (head % 2 + 1) * HEAD_DIM)
        value_lanes = slice(PAIR + head % 2 * HEAD_DIM, PAIR + (head % 2 + 1) * HEAD_DIM)
        field = kv[head // 2]
        near_block = meta[slot_at + head]
        far_block = meta[slot_at + HEADS + head]
        far_match = meta[match_at + head]
        for b in range(blocks):
            rows = slice(b * BLOCK, (b + 1) * BLOCK)
            times = (
                1 + jnp.where(near_block == b, 1, 0) + jnp.where(far_block == b, far_match, 0)
            ).astype(F32)
            mine = query[rows, lanes]
            diagonal = jnp.where(causal, qk(mine, field[rows, key_lanes]), NEG)
            top = jnp.max(diagonal, axis=1, keepdims=True)
            if b:
                before = qk(mine, field[: b * BLOCK, key_lanes])
                top = jnp.maximum(top, jnp.max(before, axis=1, keepdims=True))
            weight = jnp.exp2((diagonal - top) * SCALE2) * times
            summed = jnp.sum(weight, axis=1, keepdims=True)
            acc = pv(weight, field[rows, value_lanes])
            if b:
                weight = jnp.exp2((before - top) * SCALE2)
                summed += jnp.sum(weight, axis=1, keepdims=True)
                acc += pv(weight, field[: b * BLOCK, value_lanes])
            out[rows, lanes] = (acc / summed).astype(BF16)
            acc_all[rows, lanes] = acc
            top_all[rows, lanes] = jnp.broadcast_to(top, (BLOCK, HEAD_DIM))
            sum_all[rows, lanes] = jnp.broadcast_to(summed, (BLOCK, HEAD_DIM))
        for slot in range(slots):
            rows = rows_of((near_block, far_block)[slot])
            for target, source in zip(state[4 * slot :], scratch):
                target[:, lanes] = source[rows, lanes]


def merge_kernel(shifts, slot_at, match_at, place_at, meta, *refs):
    slots = len(shifts)
    state = refs[: 4 * slots]
    packs = refs[4 * slots : 4 * slots + 2 * sum(shifts)]
    before, out = refs[4 * slots + 2 * sum(shifts) :]
    out[...] = before[...]
    for head in range(HEADS):
        lanes = slice(head * HEAD_DIM, (head + 1) * HEAD_DIM)
        key_lanes = slice(head % 2 * HEAD_DIM, (head % 2 + 1) * HEAD_DIM)
        value_lanes = slice(PAIR + head % 2 * HEAD_DIM, PAIR + (head % 2 + 1) * HEAD_DIM)
        near_block = meta[slot_at + head]
        far_block = meta[slot_at + HEADS + head]
        far_match = meta[match_at + head]
        earlier = None
        for slot in range(slots):
            query, acc, top, summed = (ref[:, lanes] for ref in state[4 * slot : 4 * slot + 4])
            if slot:
                same = near_block == far_block
                acc, top, summed = (
                    jnp.where(same, new, old) for new, old in zip(earlier, (acc, top, summed))
                )
            place = meta[place_at + slot]
            first = 2 * sum(shifts[:slot]) + head // 2 * shifts[slot]
            fields = packs[first : first + shifts[slot]]
            scores = []
            for step, field in enumerate(fields):
                seen = place > step
                if slot:
                    seen = seen & (far_match == 1)
                scores.append(jnp.where(seen, qk(query, field[:, key_lanes]), NEG))
            best = top
            for score in scores:
                best = jnp.maximum(best, jnp.max(score, axis=1, keepdims=True))
            decay = jnp.exp2((top - best) * SCALE2)
            acc = acc * decay
            summed = summed * decay
            for score, field in zip(scores, fields):
                weight = jnp.exp2((score - best) * SCALE2)
                summed = summed + jnp.sum(weight, axis=1, keepdims=True)
                acc = acc + pv(weight, field[:, value_lanes])
            out[rows_of((near_block, far_block)[slot]), lanes] = (acc / summed).astype(BF16)
            earlier = (acc, best, summed)


def body(tokens, qkv_weight, near_offset, far_offset):
    sequence = tokens[0]
    row_count, depth = sequence.shape
    share = qkv_weight.shape[0]
    half_share = share // 2
    block_rate = row_count // BLOCK
    seq_size = lax.axis_size("seq")
    seq_index = lax.axis_index("seq")
    pieces = lax.axis_size("fsdp")
    mine = lax.axis_index("fsdp")
    near_size = min(16, seq_size)
    half = near_size // 2
    far_size = max(1, min(16, seq_size // STRIDE))
    near_at = lambda i: near_place(i, half, near_size)
    far_at = lambda i: (i // (STRIDE * far_size) * STRIDE + i % STRIDE, i // STRIDE % far_size)
    near_shifts = max(near_at(i)[1] for i in range(seq_size))
    far_shifts = far_size - 1
    slots = 2 if far_shifts else 1
    shifts = (near_shifts, far_shifts)[:slots]

    near_position = jnp.where(seq_index < half, seq_index, (seq_index - half) % near_size)
    far_position = seq_index // STRIDE % far_size
    far_match = (seq_index % STRIDE == far_offset // block_rate).astype(jnp.int32)
    side = seq_index % 2
    full_places = [(mine ^ j) * share for j in range(pieces)]
    half_places = [[place + side * half_share, place + (1 - side) * half_share] for place in full_places]
    scalars = full_places + sum(half_places, []) + [near_position, far_position]
    meta = jnp.concatenate(
        [jnp.stack([jnp.asarray(scalar, jnp.int32) for scalar in scalars])]
        + [near_offset, far_offset % block_rate, far_match]
    )
    place_at = 3 * pieces
    slot_at = place_at + 2
    match_at = slot_at + 2 * HEADS

    own_half = lax.dynamic_slice_in_dim(qkv_weight, side * half_share, half_share, 0)
    local, sent = [qkv_weight], []
    if pieces > 2:
        for pair in range(HEADS // 2):
            sent.append(
                jnp.concatenate(
                    [own_half[:, field * WIDTH + pair * PAIR :][:, :PAIR] for field in (1, 2)], axis=1
                )
            )
    first_hop = [[swap(value, "fsdp", bit) for bit in range(2, pieces, 2)] for value in sent[:1]]
    if pieces > 1:
        local.append(swap(qkv_weight, "fsdp", 1))
    first_hop += [
        [swap(after(value, sent[0]), "fsdp", bit) for bit in range(2, pieces, 2)] for value in sent[1:]
    ]

    params = pltpu.CompilerParams(vmem_limit_bytes=VMEM_LIMIT)
    scalar_spec = pl.BlockSpec(memory_space=pltpu.SMEM)
    whole = pl.BlockSpec(memory_space=pltpu.VMEM)

    def call(kernel, args, results, flops, exps, name, scratch=()):
        size = lambda value: math.prod(value.shape) * value.dtype.itemsize
        return pl.pallas_call(
            kernel,
            in_specs=[scalar_spec] + [whole] * len(args),
            out_specs=[whole] * len(results),
            out_shape=results,
            scratch_shapes=list(scratch),
            compiler_params=params,
            cost_estimate=pl.CostEstimate(
                flops=flops, bytes_accessed=sum(map(size, [*args, *results])), transcendentals=exps
            ),
            name=name,
        )(meta, *args)

    shape = jax.ShapeDtypeStruct
    (partial,) = call(
        functools.partial(start_kernel, list(range(len(local)))),
        [sequence, *local],
        [shape((row_count, 3 * WIDTH), F32)],
        2 * row_count * share * len(local) * 3 * WIDTH,
        0,
        "project_own",
    )

    kvs, near_packs, far_packs = [], [], []
    before = partial
    for pair in range(HEADS // 2):
        crossed, kv_places = [], []
        for direct, bit in zip(first_hop[pair] if first_hop else [], range(2, pieces, 2)):
            passed = after(swap(direct, "seq", 1), before)
            crossed += [direct, swap(direct, "fsdp", 1), passed, swap(passed, "fsdp", 1)]
            for half_number in range(2):
                for piece in (bit, bit ^ 1):
                    kv_places.append(pieces + 2 * piece + half_number)
        kv, *packs = call(
            functools.partial(kv_kernel, pair, kv_places, slots, slot_at),
            [sequence, partial, *crossed],
            [shape((row_count, 2 * PAIR), BF16)] + [shape((BLOCK, 2 * PAIR), BF16)] * slots,
            2 * row_count * share * (pieces - len(local)) * 2 * PAIR,
            0,
            f"project_kv{pair}",
        )
        kvs.append(kv)
        before = kv
        near_packs += [
            lax.ppermute(packs[0], "seq", shift_pairs(seq_size, near_at, step))
            for step in range(1, near_shifts + 1)
        ]
        far_packs += [
            lax.ppermute(packs[1], "seq", shift_pairs(seq_size, far_at, step * STRIDE))
            for step in range(1, far_shifts + 1)
        ]

    crossed_q, q_places = [], []
    for bit in range(2, pieces, 2):
        own_q = after(qkv_weight, first_hop[0][0])[:, :WIDTH]
        arrived = after(swap(own_q, "fsdp", bit), kvs[-1])
        crossed_q += [arrived, swap(arrived, "fsdp", 1)]
        q_places += [bit, bit ^ 1]

    state_types = [BF16, F32, F32, F32]
    partial_out, *state = call(
        functools.partial(attend_kernel, q_places, slots, slot_at, match_at),
        [sequence, partial, *crossed_q, *kvs],
        [shape((row_count, WIDTH), BF16)] + [shape((BLOCK, WIDTH), kind) for kind in state_types] * slots,
        2 * row_count * share * (pieces - len(local)) * WIDTH + 4 * row_count * row_count * WIDTH,
        HEADS * row_count * row_count,
        "attend_local",
        [pltpu.VMEM((row_count, WIDTH), kind) for kind in state_types],
    )

    (merged,) = call(
        functools.partial(merge_kernel, shifts, slot_at, match_at, place_at),
        [*state, *near_packs, *far_packs, partial_out],
        [shape((row_count, WIDTH), BF16)],
        4 * BLOCK * BLOCK * WIDTH * sum(shifts),
        BLOCK * BLOCK * HEADS * sum(shifts),
        "merge_near",
    )
    return merged[None]


def solution(mesh):
    in_specs = (P("fsdp", "seq", None), P("fsdp", None), P(), P())
    out_specs = P("fsdp", "seq", None)
    return jax.shard_map(body, mesh=mesh, in_specs=in_specs, out_specs=out_specs, check_vma=False)
```

```python
import functools
import math

import jax
import jax.numpy as jnp
from jax import lax
from jax.experimental import pallas as pl
from jax.experimental.pallas import tpu as pltpu
from jax.sharding import PartitionSpec as P

HEADS = 4
HEAD_DIM = 128
BLOCK = 128
STRIDE = 8
WIDTH = HEADS * HEAD_DIM
PAIR = 2 * HEAD_DIM
NEG = -1e30
SCALE2 = HEAD_DIM ** (-0.5) * math.log2(math.e)
VMEM_LIMIT = 24 * 1024 * 1024

MODEL_FLOPS = {"cut": 6900000000, "pro": 1840000, "att": 3680000, "mer": 1610000}
F32 = jnp.float32
BF16 = jnp.bfloat16


def near_place(index, half, size):
    if index < half:
        return 0, index
    return 1 + (index - half) // size, (index - half) % size


def shift_pairs(count, place, step):
    pairs = []
    for source in range(count - step):
        if place(source)[0] == place(source + step)[0]:
            pairs.append((source, source + step))
    return pairs


def swap(value, axis, bit):
    count = lax.axis_size(axis)
    return lax.ppermute(value, axis, [(i, i ^ bit) for i in range(count)])


def after(value, *others):
    return lax.optimization_barrier((value,) + others)[0]


def rows_of(block):
    return pl.ds(pl.multiple_of(block * BLOCK, BLOCK), BLOCK)


def qk(query, key):
    return lax.dot_general(query, key, (((1,), (1,)), ((), ())), preferred_element_type=F32)


def pv(weights, value):
    return jnp.dot(weights.astype(BF16), value, preferred_element_type=F32)


def add_up(tokens, places, weights):
    total = None
    for place, weight in zip(places, weights):
        depth = weight.shape[0]
        columns = pl.ds(pl.multiple_of(place, depth), depth)
        term = jnp.dot(tokens[:, columns], weight[...], preferred_element_type=F32)
        total = term if total is None else total + term
    return total


def kv_kernel(pair, own_at, places_at, slots, slot_at, meta, tokens, *refs):
    local, refs = refs[: len(own_at)], refs[len(own_at) :]
    weights, kv, packs = refs[: len(places_at)], refs[len(places_at)], refs[len(places_at) + 1 :]
    places = [meta[at] for at in [*own_at, *places_at]]
    for field in range(2):
        lanes = slice(field * PAIR, (field + 1) * PAIR)
        first = (field + 1) * WIDTH + pair * PAIR
        parts = [weight.at[:, first : first + PAIR] for weight in local]
        parts += [weight.at[:, lanes] for weight in weights]
        kv[:, lanes] = add_up(tokens, places, parts).astype(BF16)
    for slot in range(slots):
        for i in range(2):
            rows = rows_of(meta[slot_at + HEADS * slot + 2 * pair + i])
            for field in range(2):
                lanes = slice(field * PAIR + i * HEAD_DIM, field * PAIR + (i + 1) * HEAD_DIM)
                packs[slot][:, lanes] = kv[rows, lanes]


def attend_kernel(pair, own_at, places_at, slots, slot_at, match_at, meta, tokens, *refs):
    local, refs = refs[: len(own_at)], refs[len(own_at) :]
    weights, refs = refs[: len(places_at)], refs[len(places_at) :]
    field, out, refs = refs[0], refs[1], refs[2:]
    state, scratch = refs[: 4 * slots], refs[4 * slots :]
    query, acc_all, top_all, sum_all = scratch
    places = [meta[at] for at in [*own_at, *places_at]]
    blocks = query.shape[0] // BLOCK
    row = lax.broadcasted_iota(jnp.int32, (BLOCK, BLOCK), 0)
    column = lax.broadcasted_iota(jnp.int32, (BLOCK, BLOCK), 1)
    causal = column <= row
    columns = slice(pair * PAIR, (pair + 1) * PAIR)
    total = add_up(tokens, places, [weight.at[:, columns] for weight in [*local, *weights]])
    query[...] = total.astype(BF16)
    for i in range(2):
        head = 2 * pair + i
        lanes = slice(i * HEAD_DIM, (i + 1) * HEAD_DIM)
        value_lanes = slice(PAIR + i * HEAD_DIM, PAIR + (i + 1) * HEAD_DIM)
        near_block = meta[slot_at + head]
        far_block = meta[slot_at + HEADS + head]
        far_match = meta[match_at + head]
        for b in range(blocks):
            rows = slice(b * BLOCK, (b + 1) * BLOCK)
            times = (
                1 + jnp.where(near_block == b, 1, 0) + jnp.where(far_block == b, far_match, 0)
            ).astype(F32)
            mine = query[rows, lanes]
            diagonal = jnp.where(causal, qk(mine, field[rows, lanes]), NEG)
            top = jnp.max(diagonal, axis=1, keepdims=True)
            if b:
                before = qk(mine, field[: b * BLOCK, lanes])
                top = jnp.maximum(top, jnp.max(before, axis=1, keepdims=True))
            weight = jnp.exp2((diagonal - top) * SCALE2) * times
            summed = jnp.sum(weight, axis=1, keepdims=True)
            acc = pv(weight, field[rows, value_lanes])
            if b:
                weight = jnp.exp2((before - top) * SCALE2)
                summed += jnp.sum(weight, axis=1, keepdims=True)
                acc += pv(weight, field[: b * BLOCK, value_lanes])
            out[rows, lanes] = (acc / summed).astype(BF16)
            acc_all[rows, lanes] = acc
            top_all[rows, lanes] = jnp.broadcast_to(top, (BLOCK, HEAD_DIM))
            sum_all[rows, lanes] = jnp.broadcast_to(summed, (BLOCK, HEAD_DIM))
        for slot in range(slots):
            rows = rows_of((near_block, far_block)[slot])
            for target, source in zip(state[4 * slot :], scratch):
                target[:, lanes] = source[rows, lanes]


def merge_kernel(pair, shifts, slot_at, match_at, place_at, meta, *refs):
    slots = len(shifts)
    state = refs[: 4 * slots]
    packs = refs[4 * slots : 4 * slots + sum(shifts)]
    before, out = refs[4 * slots + sum(shifts) : -1], refs[-1]
    for done, part in enumerate(before):
        out[:, done * PAIR : (done + 1) * PAIR] = part[...]
    for i in range(2):
        head = 2 * pair + i
        lanes = slice(i * HEAD_DIM, (i + 1) * HEAD_DIM)
        value_lanes = slice(PAIR + i * HEAD_DIM, PAIR + (i + 1) * HEAD_DIM)
        first_lane = (len(before) - 1) * PAIR + i * HEAD_DIM
        near_block = meta[slot_at + head]
        far_block = meta[slot_at + HEADS + head]
        far_match = meta[match_at + head]
        earlier = None
        for slot in range(slots):
            query, acc, top, summed = (ref[:, lanes] for ref in state[4 * slot : 4 * slot + 4])
            if slot:
                same = near_block == far_block
                acc, top, summed = (
                    jnp.where(same, new, old) for new, old in zip(earlier, (acc, top, summed))
                )
            place = meta[place_at + slot]
            first = sum(shifts[:slot])
            fields = packs[first : first + shifts[slot]]
            scores = []
            for step, field in enumerate(fields):
                seen = place > step
                if slot:
                    seen = seen & (far_match == 1)
                scores.append(jnp.where(seen, qk(query, field[:, lanes]), NEG))
            best = top
            for score in scores:
                best = jnp.maximum(best, jnp.max(score, axis=1, keepdims=True))
            decay = jnp.exp2((top - best) * SCALE2)
            acc = acc * decay
            summed = summed * decay
            for score, field in zip(scores, fields):
                weight = jnp.exp2((score - best) * SCALE2)
                summed = summed + jnp.sum(weight, axis=1, keepdims=True)
                acc = acc + pv(weight, field[:, value_lanes])
            out[rows_of((near_block, far_block)[slot]), first_lane : first_lane + HEAD_DIM] = (
                acc / summed
            ).astype(BF16)
            earlier = (acc, best, summed)


def cut_kernel(side_ref, weight, *refs):
    halves, query, sems = refs[:-2], refs[-2], refs[-1]
    rows = halves[0].shape[0]
    mine = pl.ds(pl.multiple_of(side_ref[0] * rows, rows), rows)
    copies = []
    for pair, half in enumerate(halves):
        for field in range(2):
            source = weight.at[mine, pl.ds((field + 1) * WIDTH + pair * PAIR, PAIR)]
            target = half.at[:, pl.ds(field * PAIR, PAIR)]
            copies.append(pltpu.make_async_copy(source, target, sems.at[len(copies)]))
    copies.append(pltpu.make_async_copy(weight.at[:, pl.ds(0, WIDTH)], query, sems.at[len(copies)]))
    for copy in copies:
        copy.start()
    for copy in copies:
        copy.wait()


def body(tokens, qkv_weight, near_offset, far_offset):
    sequence = tokens[0]
    row_count, depth = sequence.shape
    share = qkv_weight.shape[0]
    half_share = share // 2
    block_rate = row_count // BLOCK
    seq_size = lax.axis_size("seq")
    seq_index = lax.axis_index("seq")
    pieces = lax.axis_size("fsdp")
    mine = lax.axis_index("fsdp")
    near_size = min(16, seq_size)
    half = near_size // 2
    far_size = max(1, min(16, seq_size // STRIDE))
    near_at = lambda i: near_place(i, half, near_size)
    far_at = lambda i: (i // (STRIDE * far_size) * STRIDE + i % STRIDE, i // STRIDE % far_size)
    near_shifts = max(near_at(i)[1] for i in range(seq_size))
    far_shifts = far_size - 1
    slots = 2 if far_shifts else 1
    shifts = (near_shifts, far_shifts)[:slots]

    near_position = jnp.where(seq_index < half, seq_index, (seq_index - half) % near_size)
    far_position = seq_index // STRIDE % far_size
    far_match = (seq_index % STRIDE == far_offset // block_rate).astype(jnp.int32)
    side = seq_index % 2
    full_places = [(mine ^ j) * share for j in range(pieces)]
    half_places = [[place + side * half_share, place + (1 - side) * half_share] for place in full_places]
    scalars = full_places + sum(half_places, []) + [near_position, far_position]
    meta = jnp.concatenate(
        [jnp.stack([jnp.asarray(scalar, jnp.int32) for scalar in scalars])]
        + [near_offset, far_offset % block_rate, far_match]
    )
    place_at = 3 * pieces
    slot_at = place_at + 2
    match_at = slot_at + 2 * HEADS

    scalar_spec = pl.BlockSpec(memory_space=pltpu.SMEM)
    whole = pl.BlockSpec(memory_space=pltpu.VMEM)
    shape = jax.ShapeDtypeStruct
    pairs = HEADS // 2

    def call(kernel, args, results, flops, name, scratch=(), scalars=None, spec=whole, limit=VMEM_LIMIT):
        return pl.pallas_call(
            kernel,
            in_specs=[scalar_spec] + [spec] * len(args),
            out_specs=[whole] * len(results),
            out_shape=results,
            scratch_shapes=list(scratch),
            compiler_params=pltpu.CompilerParams(vmem_limit_bytes=limit),
            cost_estimate=pl.CostEstimate(
                flops=MODEL_FLOPS[name[:3]], bytes_accessed=1000, transcendentals=0
            ),
            name=name,
        )(meta if scalars is None else scalars, *args)

    local = [qkv_weight]
    arrived = {}
    bits = range(2, pieces, 2)
    if pieces > 1:
        local.append(swap(qkv_weight, "fsdp", 1))
    if pieces > 2:
        *sent, own_q = call(
            cut_kernel,
            [qkv_weight],
            [shape((half_share, 2 * PAIR), BF16)] * pairs + [shape((share, WIDTH), BF16)],
            0,
            "cut",
            [pltpu.SemaphoreType.DMA((2 * pairs + 1,))],
            side.astype(jnp.int32).reshape(1),
            pl.BlockSpec(memory_space=pl.ANY),
            60*2**20,
        )
        first = [[swap(sent[0], "fsdp", bit) for bit in bits]]
        known = {"A": first[0][0], "core": local[-1]}
        first.append([swap(sent[1], "fsdp", bit) for bit in bits])
        known["B"] = first[1][0]
        crossed_x = [swap(own_q, "fsdp", bit) for bit in bits]
    else:
        first, crossed_x, known = [[] for _ in range(pairs)], [], {}

    kvs, packs_in = [], []
    for pair in range(pairs):
        crossed, kv_places = [], []
        tag = "AB"[pair]
        for direct, bit in zip(first[pair], bits):
            passed = swap(direct, "seq", 1)
            passed = after(passed, *(known[name] for name in (('B',), ('kvA',))[pair]))
            known["p" + tag] = passed
            crossed += [direct, swap(direct, "fsdp", 1), passed, swap(passed, "fsdp", 1)]
            for half_number in range(2):
                for piece in (bit, bit ^ 1):
                    kv_places.append(pieces + 2 * piece + half_number)
        kv, *packs = call(
            functools.partial(kv_kernel, pair, list(range(len(local))), kv_places, slots, slot_at),
            [sequence, *local, *crossed],
            [shape((row_count, 2 * PAIR), BF16)] + [shape((BLOCK, 2 * PAIR), BF16)] * slots,
            2 * row_count * share * (pieces - len(local)) * 2 * PAIR,
            f"project_kv{pair}",
        )
        kvs.append(kv)
        known["kv" + tag] = kv
        known["k" + tag] = packs[0]
        packs[0] = after(packs[0], *(known[name] for name in ((), ('kA',))[pair]))
        packs_in.append([])
        for pack, place, count, unit in zip(packs, (near_at, far_at), shifts, (1, STRIDE)):
            for step in range(1, count + 1):
                packs_in[pair].append(
                    lax.ppermute(pack, "seq", shift_pairs(seq_size, place, step * unit))
                )
        for step, pack in enumerate(packs_in[pair]):
            known[f"n{step + 1}{tag}"] = pack

    crossed_q, q_places = [], []
    for direct, bit in zip(crossed_x, bits):
        direct = after(direct, known['kvB'])
        crossed_q += [direct, swap(direct, "fsdp", 1)]
        q_places += [bit, bit ^ 1]

    state_types = [BF16, F32, F32, F32]
    outs = []
    for pair in range(pairs):
        out, *state = call(
            functools.partial(attend_kernel, pair, list(range(len(local))), q_places, slots, slot_at, match_at),
            [sequence, *local, *crossed_q, kvs[pair]],
            [shape((row_count, PAIR), BF16)] + [shape((BLOCK, PAIR), kind) for kind in state_types] * slots,
            2 * row_count * share * (pieces - len(local)) * PAIR + 4 * row_count * row_count * PAIR,
            f"attend_local{pair}",
            [pltpu.VMEM((row_count, PAIR), kind) for kind in state_types],
        )
        outs.append((out, state))
        known["o" + "AB"[pair]] = out
    merged = []
    for pair, (out, state) in enumerate(outs):
        before = merged + [out] if pair == pairs - 1 else [out]
        (out,) = call(
            functools.partial(merge_kernel, pair, shifts, slot_at, match_at, place_at),
            [state[0], *state[1:], *packs_in[pair], *before],
            [shape((row_count, PAIR * len(before)), BF16)],
            4 * BLOCK * BLOCK * PAIR * sum(shifts),
            f"merge_near{pair}",
        )
        merged.append(out)
    return merged[-1][None]


def solution(mesh):
    in_specs = (P("fsdp", "seq", None), P("fsdp", None), P(), P())
    out_specs = P("fsdp", "seq", None)
    return jax.shard_map(body, mesh=mesh, in_specs=in_specs, out_specs=out_specs, check_vma=False)
```

```python
import functools
import math

import jax
import jax.numpy as jnp
from jax import lax
from jax.experimental import pallas as pl
from jax.experimental.pallas import tpu as pltpu
from jax.sharding import PartitionSpec as P

HEADS = 4
HEAD_DIM = 128
BLOCK = 128
STRIDE = 8
WIDTH = HEADS * HEAD_DIM
PAIR = 2 * HEAD_DIM
NEG = -1e30
SCALE2 = HEAD_DIM ** (-0.5) * math.log2(math.e)
VMEM_LIMIT = 24 * 1024 * 1024

MODEL_FLOPS = {"project_own": 3680000, "project_mid": 1610000, "project_kv": 2990000, "attend_local": 6325000, "merge_near": 2990000}
NEAR_ORDER = (2, 3, 1)
F32 = jnp.float32
BF16 = jnp.bfloat16


def near_place(index, half, size):
    if index < half:
        return 0, index
    return 1 + (index - half) // size, (index - half) % size


def earlier_pairs(count, place, bits):
    where = {place(i): i for i in range(count)}
    pairs = []
    for source in range(count):
        run, spot = place(source)
        if spot ^ bits > spot and (run, spot ^ bits) in where:
            pairs.append((source, where[run, spot ^ bits]))
    return pairs


def swap(value, axis, bit):
    count = lax.axis_size(axis)
    return lax.ppermute(value, axis, [(i, i ^ bit) for i in range(count)])


def after(value, *others):
    return lax.optimization_barrier((value,) + others)[0]


def rows_of(block):
    return pl.ds(pl.multiple_of(block * BLOCK, BLOCK), BLOCK)


def qk(query, key):
    return lax.dot_general(query, key, (((1,), (1,)), ((), ())), preferred_element_type=F32)


def pv(weights, value):
    return jnp.dot(weights.astype(BF16), value, preferred_element_type=F32)


def add_up(tokens, places, weights):
    total = None
    for place, weight in zip(places, weights):
        depth = weight.shape[0]
        columns = pl.ds(pl.multiple_of(place, depth), depth)
        term = jnp.dot(tokens[:, columns], weight[...], preferred_element_type=F32)
        total = term if total is None else total + term
    return total


def own_kernel(count, meta, tokens, *refs):
    weights, out = refs[:count], refs[count]
    for j in range(out.shape[1] // PAIR):
        lanes = slice(j * PAIR, (j + 1) * PAIR)
        out[:, lanes] = add_up(tokens, [meta[at] for at in range(count)], [weight.at[:, lanes] for weight in weights])


def mid_kernel(places_at, side_at, meta, tokens, partial, *refs):
    halves, out, joined = refs[:-2], refs[-2], refs[-1]
    rows = halves[0].shape[0]
    side = meta[side_at]
    for j, at in enumerate(places_at):
        for half in range(2):
            first = pl.multiple_of((side ^ half) * rows, rows)
            joined[j, pl.ds(first, rows), :] = halves[2 * j + half][...]
    places = [meta[at] for at in places_at]
    for j in range(out.shape[1] // PAIR):
        lanes = slice(j * PAIR, (j + 1) * PAIR)
        total = partial[:, WIDTH + j * PAIR : WIDTH + (j + 1) * PAIR]
        out[:, lanes] = total + add_up(tokens, places, [joined.at[i, :, lanes] for i in range(len(places))])


def kv_kernel(first, places_at, slots, slot_at, meta, tokens, partial, *refs):
    weights, kv, packs = refs[: len(places_at)], refs[len(places_at)], refs[len(places_at) + 1 :]
    places = [meta[at] for at in places_at]
    for j in range(2 * WIDTH // PAIR):
        lanes = slice(j * PAIR, (j + 1) * PAIR)
        total = partial[:, first + j * PAIR : first + (j + 1) * PAIR]
        if weights:
            total = total + add_up(tokens, places, [weight.at[:, lanes] for weight in weights])
        kv[:, lanes] = total.astype(BF16)
    for slot in range(slots):
        for head in range(HEADS):
            rows = rows_of(meta[slot_at + HEADS * slot + head])
            for field in range(2):
                lanes = slice(field * WIDTH + head * HEAD_DIM, field * WIDTH + (head + 1) * HEAD_DIM)
                packs[slot][:, lanes] = kv[rows, lanes]


def with_ones(value):
    return jnp.concatenate([value, jnp.ones(value.shape, BF16)], axis=1)


def attend_kernel(bases_at, slots, slot_at, match_at, meta, tokens, partial, *refs):
    weights, refs = refs[: len(bases_at)], refs[len(bases_at) :]
    kv, out, refs = refs[0], refs[1], refs[2:]
    state, scratch = refs[: 4 * slots], refs[4 * slots :]
    query, acc_all, top_all, sum_all = scratch
    blocks = query.shape[0] // BLOCK
    row = lax.broadcasted_iota(jnp.int32, (BLOCK, BLOCK), 0)
    column = lax.broadcasted_iota(jnp.int32, (BLOCK, BLOCK), 1)
    causal = column <= row
    share = weights[0].shape[1] if weights else 0
    places = [meta[at] + i * share for at in bases_at for i in range(2)]
    for pair in range(HEADS // 2):
        lanes = slice(pair * PAIR, (pair + 1) * PAIR)
        total = partial[:, lanes]
        if weights:
            parts = [weight.at[i, :, lanes] for weight in weights for i in range(2)]
            total = total + add_up(tokens, places, parts)
        query[:, lanes] = total.astype(BF16)

    def lanes_of(head):
        return slice(head * HEAD_DIM, (head + 1) * HEAD_DIM)

    def score(head, b):
        rows = slice(b * BLOCK, (b + 1) * BLOCK)
        return qk(query[rows, lanes_of(head)], kv[: (b + 1) * BLOCK, lanes_of(head)])

    def weigh(head, b, scores):
        near_block = meta[slot_at + head]
        far_block = meta[slot_at + HEADS + head]
        times = (
            1
            + jnp.where(near_block == b, 1, 0)
            + jnp.where(far_block == b, meta[match_at + head], 0)
        ).astype(F32)
        diagonal = jnp.where(causal, scores[:, b * BLOCK :], NEG)
        top = jnp.max(diagonal, axis=1, keepdims=True)
        if b:
            top = jnp.maximum(top, jnp.max(scores[:, : b * BLOCK], axis=1, keepdims=True))
        weight = (jnp.exp2((diagonal - top) * SCALE2) * times).astype(BF16)
        if b:
            before = jnp.exp2((scores[:, : b * BLOCK] - top) * SCALE2).astype(BF16)
            weight = jnp.concatenate([before, weight], axis=1)
        return top, weight

    def finish(head, b, top, weight):
        lanes = lanes_of(head)
        rows = slice(b * BLOCK, (b + 1) * BLOCK)
        value = kv[: (b + 1) * BLOCK, WIDTH + head * HEAD_DIM : WIDTH + (head + 1) * HEAD_DIM]
        both = jnp.dot(weight, with_ones(value), preferred_element_type=F32)
        acc, summed = both[:, :HEAD_DIM], both[:, HEAD_DIM:]
        out[rows, lanes] = (acc / summed).astype(BF16)
        acc_all[rows, lanes] = acc
        top_all[rows, lanes] = jnp.broadcast_to(top, (BLOCK, HEAD_DIM))
        sum_all[rows, lanes] = summed
        if b == blocks - 1:
            for slot in range(slots):
                rows = rows_of(meta[slot_at + slot * HEADS + head])
                for target, source in zip(state[4 * slot :], scratch):
                    target[:, lanes] = source[rows, lanes]

    tasks = [(head, b) for head in range(HEADS) for b in range(blocks)]
    scored, weighed = {}, {}
    for step in range(len(tasks) + 2):
        if step < len(tasks):
            scored[step] = score(*tasks[step])
        if 0 <= step - 1 < len(tasks):
            weighed[step - 1] = weigh(*tasks[step - 1], scored.pop(step - 1))
        if 0 <= step - 2 < len(tasks):
            finish(*tasks[step - 2], *weighed.pop(step - 2))


def merge_kernel(shifts, slot_at, match_at, place_at, meta, *refs):
    slots = len(shifts)
    state = refs[: 4 * slots]
    packs = refs[4 * slots : 4 * slots + sum(shifts)]
    out, results, sems = refs[4 * slots + sum(shifts) + 1 :]
    lanes = [slice(head * HEAD_DIM, (head + 1) * HEAD_DIM) for head in range(HEADS)]
    values = [slice(WIDTH + head * HEAD_DIM, WIDTH + (head + 1) * HEAD_DIM) for head in range(HEADS)]
    earlier = [None] * HEADS
    for slot, count in enumerate(shifts):
        fields = packs[sum(shifts[:slot]) : sum(shifts[: slot + 1])]
        query, acc_ref, top_ref, sum_ref = state[4 * slot : 4 * slot + 4]
        place = meta[place_at + slot]
        scores, weights = [], []
        for head in range(HEADS):
            parts = []
            for step, field in enumerate(fields):
                seen = place ^ (step + 1) < place
                if slot:
                    seen = seen & (meta[match_at + head] == 1)
                parts.append(jnp.where(seen, qk(query[:, lanes[head]], field[:, lanes[head]]), NEG))
            scores.append(jnp.concatenate(parts, axis=1))
        for head in range(HEADS):
            acc, top, summed = (ref[:, lanes[head]] for ref in (acc_ref, top_ref, sum_ref))
            if slot:
                same = meta[slot_at + head] == meta[slot_at + HEADS + head]
                acc, top, summed = (
                    jnp.where(same, new, old) for new, old in zip(earlier[head], (acc, top, summed))
                )
            best = jnp.maximum(top, jnp.max(scores[head], axis=1, keepdims=True))
            decay = jnp.exp2((top - best) * SCALE2)
            weight = jnp.exp2((scores[head] - best[:, :1]) * SCALE2).astype(BF16)
            weights.append((acc * decay, best, summed * decay, weight))
        copies = []
        for head in range(HEADS):
            acc, best, summed, weight = weights[head]
            value = jnp.concatenate([field[:, values[head]] for field in fields], axis=0)
            both = jnp.dot(weight, with_ones(value), preferred_element_type=F32)
            acc = acc + both[:, :HEAD_DIM]
            summed = summed + both[:, HEAD_DIM:]
            earlier[head] = (acc, best, summed)
            results[slot, :, lanes[head]] = (acc / summed).astype(BF16)
            rows = rows_of(meta[slot_at + slot * HEADS + head])
            copies.append(
                pltpu.make_async_copy(
                    results.at[slot, :, lanes[head]], out.at[rows, lanes[head]], sems.at[head]
                )
            )
            copies[-1].start()
        for copy in copies:
            copy.wait()


def body(tokens, qkv_weight, near_offset, far_offset):
    sequence = tokens[0]
    row_count, depth = sequence.shape
    share = qkv_weight.shape[0]
    quarter = share // 4
    block_rate = row_count // BLOCK
    seq_size = lax.axis_size("seq")
    seq_index = lax.axis_index("seq")
    pieces = lax.axis_size("fsdp")
    mine = lax.axis_index("fsdp")
    near_size = min(16, seq_size)
    half = near_size // 2
    far_size = max(1, min(16, seq_size // STRIDE))
    near_at = lambda i: near_place(i, half, near_size)
    far_at = lambda i: (i // (STRIDE * far_size) * STRIDE + i % STRIDE, i // STRIDE % far_size)
    reach = max(near_at(i)[1] for i in range(seq_size))
    near_shifts = (1 << reach.bit_length()) - 1
    far_shifts = (1 << (far_size - 1).bit_length()) - 1
    slots = 2 if far_shifts else 1
    shifts = (near_shifts, far_shifts)[:slots]

    near_position = jnp.where(seq_index < half, seq_index, (seq_index - half) % near_size)
    far_position = seq_index // STRIDE % far_size
    far_match = (seq_index % STRIDE == far_offset // block_rate).astype(jnp.int32)
    side = seq_index % 2
    full_places = [(mine ^ j) * share for j in range(pieces)]
    scalars = full_places + [place + 2 * quarter for place in full_places]
    scalars += [near_position, far_position, side]
    scalars += [(mine ^ bit) // 2 * 2 * share for bit in range(2, pieces, 2)]
    meta = jnp.concatenate(
        [jnp.stack([jnp.asarray(scalar, jnp.int32) for scalar in scalars])]
        + [near_offset, far_offset % block_rate, far_match]
    )
    place_at = 2 * pieces
    side_at = place_at + 2
    base_at = side_at
    slot_at = side_at + max(1, pieces // 2)
    match_at = slot_at + 2 * HEADS

    scalar_spec = pl.BlockSpec(memory_space=pltpu.SMEM)
    whole = pl.BlockSpec(memory_space=pltpu.VMEM)
    shape = jax.ShapeDtypeStruct

    def call(kernel, args, results, name, scratch=()):
        return pl.pallas_call(
            kernel,
            in_specs=[scalar_spec] + [whole] * len(args),
            out_specs=[whole] * len(results),
            out_shape=results,
            scratch_shapes=list(scratch),
            compiler_params=pltpu.CompilerParams(vmem_limit_bytes=VMEM_LIMIT),
            cost_estimate=pl.CostEstimate(flops=MODEL_FLOPS[name], bytes_accessed=1000, transcendentals=0),
            name=name,
        )(meta, *args)

    local = [qkv_weight]
    bits = range(2, pieces, 2)
    known = {}
    if pieces > 1:
        local.append(swap(qkv_weight, "fsdp", 1))
        known["core"] = local[-1]
    crossed_mid, mid_places, crossed_kv, kv_places, crossed_q, q_places = [], [], [], [], [], []
    (partial,) = call(
        functools.partial(own_kernel, len(local)),
        [sequence, *local],
        [shape((row_count, 3 * WIDTH), F32)],
        "project_own",
    )
    known["partial"] = partial
    kv_part, kv_first = partial, WIDTH
    passing = []
    for bit in bits:
        cut = lax.dynamic_slice(qkv_weight, (side * quarter, WIDTH), (quarter, 2 * WIDTH))
        known["cutM"] = cut
        direct = swap(cut, "fsdp", bit)
        known["M"] = direct
        rest_cut = after(qkv_weight, known['cutM'])[2 * quarter :, WIDTH:]
        known["cutD"] = rest_cut
        rest = swap(rest_cut, "fsdp", bit)
        known["D"] = rest
        passed = swap(direct, "seq", 1)
        known["Y"] = passed
        passed = after(passed, known['partial'])
        crossed_mid += [direct, passed, swap(direct, "fsdp", 1), swap(passed, "fsdp", 1)]
        mid_places += [bit, bit ^ 1]
        passing.append(rest)
        kv_places += [pieces + bit, pieces + (bit ^ 1)]
        nq = 1
        cut_q = after(qkv_weight, known['cutD'])
        qs = [swap(cut_q[i * share // nq : (i + 1) * share // nq, :WIDTH], "fsdp", bit) for i in range(nq)]
    if crossed_mid:
        (kv_part,) = call(
            functools.partial(mid_kernel, mid_places, side_at),
            [sequence, partial, *crossed_mid],
            [shape((row_count, 2 * WIDTH), F32)],
            "project_mid",
            [pltpu.VMEM((len(mid_places), 2 * quarter, 2 * WIDTH), BF16)],
        )
        kv_first = 0
        known["mid"] = kv_part
    for rest in passing:
        rest = after(rest, known['mid'])
        crossed_kv += [rest, swap(rest, "fsdp", 1)]
    kv, *packs = call(
        functools.partial(kv_kernel, kv_first, kv_places, slots, slot_at),
        [sequence, kv_part, *crossed_kv],
        [shape((row_count, 2 * WIDTH), BF16)] + [shape((BLOCK, 2 * WIDTH), BF16)] * slots,
        "project_kv",
    )
    known["kv"] = kv
    known["pack"] = packs[0]
    received = []
    for pack, place, count, unit in zip(packs, (near_at, far_at), shifts, (1, STRIDE)):
        for step in NEAR_ORDER if count == len(NEAR_ORDER) else range(1, count + 1):
            received.append((step, lax.ppermute(pack, "seq", earlier_pairs(seq_size, place, step))))
        known |= {f"n{step}": r for step, r in received}
    received = [r for _, r in sorted(received[:shifts[0]], key=lambda v: v[0])] + [r for _, r in received[shifts[0]:]]
    for bit in bits:
        for i, q in enumerate(qs):
            q = after(q, known['kv'])
            both = lax.all_to_all(
                jnp.broadcast_to(q[None], (2,) + q.shape), "fsdp", 0, 0,
                axis_index_groups=[[i, i + 1] for i in range(0, pieces, 2)],
            )
            crossed_q += [both]
    nq = 1
    q_where = [base_at + bit // 2 for bit in bits]
    state_types = [BF16, F32, F32, F32]
    partial_out, *state = call(
        functools.partial(attend_kernel, q_where, slots, slot_at, match_at),
        [sequence, partial, *crossed_q, kv],
        [shape((row_count, WIDTH), BF16)] + [shape((BLOCK, WIDTH), kind) for kind in state_types] * slots,
        "attend_local",
        [pltpu.VMEM((row_count, WIDTH), kind) for kind in state_types],
    )
    count = 4 * slots + sum(shifts)
    merged = pl.pallas_call(
        functools.partial(merge_kernel, shifts, slot_at, match_at, place_at),
        in_specs=[scalar_spec] + [whole] * count + [pl.BlockSpec(memory_space=pl.ANY)],
        out_specs=pl.BlockSpec(memory_space=pl.ANY),
        out_shape=shape((row_count, WIDTH), BF16),
        scratch_shapes=[pltpu.VMEM((slots, BLOCK, WIDTH), BF16), pltpu.SemaphoreType.DMA((HEADS,))],
        input_output_aliases={count + 1: 0},
        compiler_params=pltpu.CompilerParams(vmem_limit_bytes=VMEM_LIMIT),
        cost_estimate=pl.CostEstimate(flops=MODEL_FLOPS["merge_near"], bytes_accessed=1000, transcendentals=0),
        name="merge_near",
    )(meta, *state, *received, partial_out)
    return merged[None]


def solution(mesh):
    in_specs = (P("fsdp", "seq", None), P("fsdp", None), P(), P())
    out_specs = P("fsdp", "seq", None)
    return jax.shard_map(body, mesh=mesh, in_specs=in_specs, out_specs=out_specs, check_vma=False)
```

```python
import functools
import math

import jax
import jax.numpy as jnp
from jax import lax
from jax.experimental import pallas as pl
from jax.experimental.pallas import tpu as pltpu
from jax.sharding import PartitionSpec as P

HEADS = 4
HEAD_DIM = 128
BLOCK = 128
STRIDE = 8
WIDTH = HEADS * HEAD_DIM
PAIR = 2 * HEAD_DIM
NEG = -1e30
SCALE2 = HEAD_DIM ** (-0.5) * math.log2(math.e)
VMEM_LIMIT = 24 * 1024 * 1024

MODEL_FLOPS = {"project_pack": 689999, "project_own": 3680000, "project_mid": 1610000, "project_kv": 2990000, "attend_local": 6325000, "merge_near": 2990000}
NEAR_ORDER = (2, 3, 1)
F32 = jnp.float32
BF16 = jnp.bfloat16


def near_place(index, half, size):
    if index < half:
        return 0, index
    return 1 + (index - half) // size, (index - half) % size


def earlier_pairs(count, place, bits):
    where = {place(i): i for i in range(count)}
    pairs = []
    for source in range(count):
        run, spot = place(source)
        if spot ^ bits > spot and (run, spot ^ bits) in where:
            pairs.append((source, where[run, spot ^ bits]))
    return pairs


def swap(value, axis, bit):
    count = lax.axis_size(axis)
    return lax.ppermute(value, axis, [(i, i ^ bit) for i in range(count)])


def after(value, *others):
    return lax.optimization_barrier((value,) + others)[0]


def rows_of(block):
    return pl.ds(pl.multiple_of(block * BLOCK, BLOCK), BLOCK)


def qk(query, key):
    return lax.dot_general(query, key, (((1,), (1,)), ((), ())), preferred_element_type=F32)


def pv(weights, value):
    return jnp.dot(weights.astype(BF16), value, preferred_element_type=F32)


def add_up(tokens, places, weights):
    total = None
    for place, weight in zip(places, weights):
        depth = weight.shape[0]
        columns = pl.ds(pl.multiple_of(place, depth), depth)
        term = jnp.dot(tokens[:, columns], weight[...], preferred_element_type=F32)
        total = term if total is None else total + term
    return total


def own_kernel(count, meta, tokens, *refs):
    weights, out = refs[:count], refs[count]
    for j in range(out.shape[1] // PAIR):
        lanes = slice(j * PAIR, (j + 1) * PAIR)
        out[:, lanes] = add_up(tokens, [meta[at] for at in range(count)], [weight.at[:, lanes] for weight in weights])


def pack_kernel(layout, base_at, slots, slot_at, meta, tokens, partial, *refs):
    arrived, packs, joined = refs[: len(layout)], refs[len(layout) : -1], refs[-1]
    for at, array in zip(layout, arrived):
        rows = array.shape[0]
        joined[pl.ds(pl.multiple_of(meta[at], rows), rows), :] = array[...]
    columns = pl.ds(pl.multiple_of(meta[base_at], joined.shape[0]), joined.shape[0])
    for slot in range(slots):
        for head in range(HEADS):
            rows = rows_of(meta[slot_at + HEADS * slot + head])
            lanes = [slice(start, start + HEAD_DIM) for start in (head * HEAD_DIM, WIDTH + head * HEAD_DIM)]
            weight = jnp.concatenate([joined[:, part] for part in lanes], axis=1)
            product = jnp.dot(tokens[rows, columns], weight, preferred_element_type=F32)
            for field, part in enumerate(lanes):
                own = partial[rows, WIDTH + part.start : WIDTH + part.stop]
                total = own + product[:, field * HEAD_DIM : (field + 1) * HEAD_DIM]
                packs[slot][:, part] = total.astype(BF16)


def kv_kernel(base_at, meta, tokens, partial, joined, kv):
    columns = pl.ds(pl.multiple_of(meta[base_at], joined.shape[0]), joined.shape[0])
    for j in range(2 * WIDTH // PAIR):
        lanes = slice(j * PAIR, (j + 1) * PAIR)
        product = jnp.dot(tokens[:, columns], joined[:, lanes], preferred_element_type=F32)
        kv[:, lanes] = (partial[:, WIDTH + j * PAIR : WIDTH + (j + 1) * PAIR] + product).astype(BF16)


def with_ones(value):
    return jnp.concatenate([value, jnp.ones(value.shape, BF16)], axis=1)


def attend_kernel(bases_at, slots, slot_at, match_at, meta, tokens, partial, *refs):
    weights, refs = refs[: len(bases_at)], refs[len(bases_at) :]
    kv, out, refs = refs[0], refs[1], refs[2:]
    state, scratch = refs[: 4 * slots], refs[4 * slots :]
    query, acc_all, top_all, sum_all = scratch
    blocks = query.shape[0] // BLOCK
    row = lax.broadcasted_iota(jnp.int32, (BLOCK, BLOCK), 0)
    column = lax.broadcasted_iota(jnp.int32, (BLOCK, BLOCK), 1)
    causal = column <= row
    share = weights[0].shape[1] if weights else 0
    places = [meta[at] + i * share for at in bases_at for i in range(2)]
    for pair in range(HEADS // 2):
        lanes = slice(pair * PAIR, (pair + 1) * PAIR)
        total = partial[:, lanes]
        if weights:
            parts = [weight.at[i, :, lanes] for weight in weights for i in range(2)]
            total = total + add_up(tokens, places, parts)
        query[:, lanes] = total.astype(BF16)

    def lanes_of(head):
        return slice(head * HEAD_DIM, (head + 1) * HEAD_DIM)

    def score(head, b):
        rows = slice(b * BLOCK, (b + 1) * BLOCK)
        return qk(query[rows, lanes_of(head)], kv[: (b + 1) * BLOCK, lanes_of(head)])

    def weigh(head, b, scores):
        near_block = meta[slot_at + head]
        far_block = meta[slot_at + HEADS + head]
        times = (
            1
            + jnp.where(near_block == b, 1, 0)
            + jnp.where(far_block == b, meta[match_at + head], 0)
        ).astype(F32)
        diagonal = jnp.where(causal, scores[:, b * BLOCK :], NEG)
        top = jnp.max(diagonal, axis=1, keepdims=True)
        if b:
            top = jnp.maximum(top, jnp.max(scores[:, : b * BLOCK], axis=1, keepdims=True))
        weight = (jnp.exp2((diagonal - top) * SCALE2) * times).astype(BF16)
        if b:
            before = jnp.exp2((scores[:, : b * BLOCK] - top) * SCALE2).astype(BF16)
            weight = jnp.concatenate([before, weight], axis=1)
        return top, weight

    def finish(head, b, top, weight):
        lanes = lanes_of(head)
        rows = slice(b * BLOCK, (b + 1) * BLOCK)
        value = kv[: (b + 1) * BLOCK, WIDTH + head * HEAD_DIM : WIDTH + (head + 1) * HEAD_DIM]
        both = jnp.dot(weight, with_ones(value), preferred_element_type=F32)
        acc, summed = both[:, :HEAD_DIM], both[:, HEAD_DIM:]
        out[rows, lanes] = (acc / summed).astype(BF16)
        acc_all[rows, lanes] = acc
        top_all[rows, lanes] = jnp.broadcast_to(top, (BLOCK, HEAD_DIM))
        sum_all[rows, lanes] = summed
        if b == blocks - 1:
            for slot in range(slots):
                rows = rows_of(meta[slot_at + slot * HEADS + head])
                for target, source in zip(state[4 * slot :], scratch):
                    target[:, lanes] = source[rows, lanes]

    tasks = [(head, b) for head in range(HEADS) for b in range(blocks)]
    scored, weighed = {}, {}
    for step in range(len(tasks) + 2):
        if step < len(tasks):
            scored[step] = score(*tasks[step])
        if 0 <= step - 1 < len(tasks):
            weighed[step - 1] = weigh(*tasks[step - 1], scored.pop(step - 1))
        if 0 <= step - 2 < len(tasks):
            finish(*tasks[step - 2], *weighed.pop(step - 2))


def merge_kernel(shifts, slot_at, match_at, place_at, meta, *refs):
    slots = len(shifts)
    state = refs[: 4 * slots]
    packs = refs[4 * slots : 4 * slots + sum(shifts)]
    out, results, sems = refs[4 * slots + sum(shifts) + 1 :]
    lanes = [slice(head * HEAD_DIM, (head + 1) * HEAD_DIM) for head in range(HEADS)]
    values = [slice(WIDTH + head * HEAD_DIM, WIDTH + (head + 1) * HEAD_DIM) for head in range(HEADS)]
    earlier = [None] * HEADS
    for slot, count in enumerate(shifts):
        fields = packs[sum(shifts[:slot]) : sum(shifts[: slot + 1])]
        query, acc_ref, top_ref, sum_ref = state[4 * slot : 4 * slot + 4]
        place = meta[place_at + slot]
        scores, weights = [], []
        for head in range(HEADS):
            parts = []
            for step, field in enumerate(fields):
                seen = place ^ (step + 1) < place
                if slot:
                    seen = seen & (meta[match_at + head] == 1)
                parts.append(jnp.where(seen, qk(query[:, lanes[head]], field[:, lanes[head]]), NEG))
            scores.append(jnp.concatenate(parts, axis=1))
        for head in range(HEADS):
            acc, top, summed = (ref[:, lanes[head]] for ref in (acc_ref, top_ref, sum_ref))
            if slot:
                same = meta[slot_at + head] == meta[slot_at + HEADS + head]
                acc, top, summed = (
                    jnp.where(same, new, old) for new, old in zip(earlier[head], (acc, top, summed))
                )
            best = jnp.maximum(top, jnp.max(scores[head], axis=1, keepdims=True))
            decay = jnp.exp2((top - best) * SCALE2)
            weight = jnp.exp2((scores[head] - best[:, :1]) * SCALE2).astype(BF16)
            weights.append((acc * decay, best, summed * decay, weight))
        copies = []
        for head in range(HEADS):
            acc, best, summed, weight = weights[head]
            value = jnp.concatenate([field[:, values[head]] for field in fields], axis=0)
            both = jnp.dot(weight, with_ones(value), preferred_element_type=F32)
            acc = acc + both[:, :HEAD_DIM]
            summed = summed + both[:, HEAD_DIM:]
            earlier[head] = (acc, best, summed)
            results[slot, :, lanes[head]] = (acc / summed).astype(BF16)
            rows = rows_of(meta[slot_at + slot * HEADS + head])
            copies.append(
                pltpu.make_async_copy(
                    results.at[slot, :, lanes[head]], out.at[rows, lanes[head]], sems.at[head]
                )
            )
            copies[-1].start()
        for copy in copies:
            copy.wait()


def body(tokens, qkv_weight, near_offset, far_offset):
    sequence = tokens[0]
    row_count, depth = sequence.shape
    share = qkv_weight.shape[0]
    block_rate = row_count // BLOCK
    seq_size = lax.axis_size("seq")
    seq_index = lax.axis_index("seq")
    pieces = lax.axis_size("fsdp")
    mine = lax.axis_index("fsdp")
    near_size = min(16, seq_size)
    half = near_size // 2
    far_size = max(1, min(16, seq_size // STRIDE))
    near_at = lambda i: near_place(i, half, near_size)
    far_at = lambda i: (i // (STRIDE * far_size) * STRIDE + i % STRIDE, i // STRIDE % far_size)
    reach = max(near_at(i)[1] for i in range(seq_size))
    near_shifts = (1 << reach.bit_length()) - 1
    far_shifts = (1 << (far_size - 1).bit_length()) - 1
    slots = 2 if far_shifts else 1
    shifts = (near_shifts, far_shifts)[:slots]

    near_position = jnp.where(seq_index < half, seq_index, (seq_index - half) % near_size)
    far_position = seq_index // STRIDE % far_size
    far_match = (seq_index % STRIDE == far_offset // block_rate).astype(jnp.int32)
    spans = [(0, share // 4), (share // 2, share // 8)] if seq_size % 4 == 0 else []
    direct_from = spans[-1][0] + 2 * spans[-1][1] if spans else 0
    full_places = [(mine ^ j) * share for j in range(pieces)]
    scalars = list(full_places)
    place_at = len(scalars)
    scalars += [near_position, far_position]
    base_at = len(scalars)
    scalars += [(mine ^ bit) // 2 * 2 * share for bit in range(2, pieces, 2)]
    slot_at = len(scalars)
    match_at = slot_at + 2 * HEADS
    offsets_at = match_at + HEADS
    offsets = []
    for core in range(2):
        first = (mine % 2 ^ core) * share
        for number, (start, rows) in enumerate(spans):
            side = seq_index // (1 << number) % 2
            offsets += [first + start + side * rows, first + start + (1 - side) * rows]
        offsets.append(first + direct_from)
    as_array = lambda values: jnp.stack([jnp.asarray(value, jnp.int32) for value in values])
    meta = jnp.concatenate(
        [as_array(scalars), near_offset, far_offset % block_rate, far_match, as_array(offsets)]
    )

    scalar_spec = pl.BlockSpec(memory_space=pltpu.SMEM)
    whole = pl.BlockSpec(memory_space=pltpu.VMEM)
    shape = jax.ShapeDtypeStruct

    def call(kernel, args, results, name, scratch=()):
        return pl.pallas_call(
            kernel,
            in_specs=[scalar_spec] + [whole] * len(args),
            out_specs=[whole] * len(results),
            out_shape=results,
            scratch_shapes=list(scratch),
            compiler_params=pltpu.CompilerParams(vmem_limit_bytes=VMEM_LIMIT),
            cost_estimate=pl.CostEstimate(flops=MODEL_FLOPS[name], bytes_accessed=1000, transcendentals=0),
            name=name,
        )(meta, *args)

    local = [qkv_weight]
    bits = range(2, pieces, 2)
    known = {}
    if pieces > 1:
        local.append(swap(qkv_weight, "fsdp", 1))
        known["core"] = local[-1]
    (partial,) = call(
        functools.partial(own_kernel, len(local)),
        [sequence, *local],
        [shape((row_count, 3 * WIDTH), F32)],
        "project_own",
    )
    known["partial"] = partial
    direct_rows, queries = [], []
    for bit in bits:
        mine_rows, other_rows = [], []
        for number, (start, rows) in enumerate(spans):
            tag = str(number)
            side = seq_index // (1 << number) % 2
            cut = lax.dynamic_slice(
                qkv_weight, (start + side * rows, WIDTH), (rows, 2 * WIDTH)
            )
            known["c" + tag] = cut
            direct = swap(cut, "fsdp", bit)
            known["x" + tag] = direct
            across = swap(direct, "fsdp", 1)
            known["f" + tag] = across
            passed = swap(direct, "seq", 1 << number)
            known["y" + tag] = passed
            mine_rows += [direct, passed]
            other_rows += [across, swap(passed, "fsdp", 1)]
            known["q" + tag] = other_rows[-1]
        cut = after(qkv_weight, known['c1'])[direct_from:, WIDTH:]
        known["cD"] = cut
        rest = swap(cut, "fsdp", bit)
        known["xD"] = rest
        rest = rest
        known["fD"] = swap(rest, "fsdp", 1)
        direct_rows.append(mine_rows + [rest] + other_rows + [known["fD"]])
        cut = after(qkv_weight, known['cD'])[:, :WIDTH]
        known["cQ"] = cut
        queries.append(swap(cut, "fsdp", bit))
    assert len(bits) <= 1
    if bits:
        layout = [offsets_at + i for i in range(len(direct_rows[0]))]
        *packs, joined = call(
            functools.partial(pack_kernel, layout, base_at, slots, slot_at),
            [sequence, partial, *direct_rows[0]],
            [shape((BLOCK, 2 * WIDTH), BF16)] * slots + [shape((2 * share, 2 * WIDTH), BF16)],
            "project_pack",
        )
        known["pack"] = packs[0]
        (kv,) = call(
            functools.partial(kv_kernel, base_at),
            [sequence, after(partial, known['pack']), joined],
            [shape((row_count, 2 * WIDTH), BF16)],
            "project_kv",
        )
    else:
        kv = partial[:, WIDTH:].astype(BF16)
        blocks = kv.reshape(block_rate, BLOCK, 2, HEADS, HEAD_DIM)
        packs = []
        for offset in (near_offset, far_offset % block_rate)[:slots]:
            picked = blocks[offset, :, :, jnp.arange(HEADS)]
            packs.append(picked.transpose(1, 2, 0, 3).reshape(BLOCK, 2 * WIDTH))
    known["kv"] = kv
    received = []
    for pack, place, count, unit in zip(packs, (near_at, far_at), shifts, (1, STRIDE)):
        for step in NEAR_ORDER if count == len(NEAR_ORDER) else range(1, count + 1):
            received.append((step, lax.ppermute(pack, "seq", earlier_pairs(seq_size, place, step))))
        known |= {f"n{step}": r for step, r in received}
    received = [r for _, r in sorted(received[:shifts[0]], key=lambda v: v[0])] + [r for _, r in received[shifts[0]:]]
    crossed_q = []
    for direct in queries:
        direct = after(direct, known['kv'])
        crossed_q.append(
            lax.all_to_all(
                jnp.broadcast_to(direct[None], (2,) + direct.shape),
                "fsdp",
                0,
                0,
                axis_index_groups=[[i, i + 1] for i in range(0, pieces, 2)],
            )
        )
    q_where = [base_at + number for number in range(len(queries))]
    state_types = [BF16, F32, F32, F32]
    partial_out, *state = call(
        functools.partial(attend_kernel, q_where, slots, slot_at, match_at),
        [sequence, partial, *crossed_q, kv],
        [shape((row_count, WIDTH), BF16)] + [shape((BLOCK, WIDTH), kind) for kind in state_types] * slots,
        "attend_local",
        [pltpu.VMEM((row_count, WIDTH), kind) for kind in state_types],
    )
    count = 4 * slots + sum(shifts)
    merged = pl.pallas_call(
        functools.partial(merge_kernel, shifts, slot_at, match_at, place_at),
        in_specs=[scalar_spec] + [whole] * count + [pl.BlockSpec(memory_space=pl.ANY)],
        out_specs=pl.BlockSpec(memory_space=pl.ANY),
        out_shape=shape((row_count, WIDTH), BF16),
        scratch_shapes=[pltpu.VMEM((slots, BLOCK, WIDTH), BF16), pltpu.SemaphoreType.DMA((HEADS,))],
        input_output_aliases={count + 1: 0},
        compiler_params=pltpu.CompilerParams(vmem_limit_bytes=VMEM_LIMIT),
        cost_estimate=pl.CostEstimate(flops=MODEL_FLOPS["merge_near"], bytes_accessed=1000, transcendentals=0),
        name="merge_near",
    )(meta, *state, *received, partial_out)
    return merged[None]


def solution(mesh):
    in_specs = (P("fsdp", "seq", None), P("fsdp", None), P(), P())
    out_specs = P("fsdp", "seq", None)
    return jax.shard_map(body, mesh=mesh, in_specs=in_specs, out_specs=out_specs, check_vma=False)
```

```python
import functools
import math

import jax
import jax.numpy as jnp
from jax import lax
from jax.experimental import pallas as pl
from jax.experimental.pallas import tpu as pltpu
from jax.sharding import PartitionSpec as P

HEADS = 4
HEAD_DIM = 128
BLOCK = 128
STRIDE = 8
WIDTH = HEADS * HEAD_DIM
PAIR = 2 * HEAD_DIM
NEG = -1e30
SCALE2 = HEAD_DIM ** (-0.5) * math.log2(math.e)
VMEM_LIMIT = 24 * 1024 * 1024

MODEL_FLOPS = {"project_pack": 689999, "project_own": 3680000, "project_mid": 1610000, "project_kv": 2990000, "attend_local": 6325000, "merge_near": 2990000}
ORDER = {
    'c1': ('c0',),
    'cD': ('c1',),
    'cQ': ('cD',),
    'p0': ('partial', 'xD'),
    'p1': ('partial',),
    'q': ('kv',),
    'kv': ('pack',),
}
NEAR_ORDER = (2, 3, 1)
F32 = jnp.float32
BF16 = jnp.bfloat16


def near_place(index, half, size):
    if index < half:
        return 0, index
    return 1 + (index - half) // size, (index - half) % size


def earlier_pairs(count, place, bits):
    where = {place(i): i for i in range(count)}
    pairs = []
    for source in range(count):
        run, spot = place(source)
        if spot ^ bits > spot and (run, spot ^ bits) in where:
            pairs.append((source, where[run, spot ^ bits]))
    return pairs


def swap(value, axis, bit):
    count = lax.axis_size(axis)
    return lax.ppermute(value, axis, [(i, i ^ bit) for i in range(count)])


def after(value, *others):
    return lax.optimization_barrier((value,) + others)[0]


def ordered(name, value, known):
    others = [known[other] for other in ORDER.get(name, ()) if other in known]
    return after(value, *others) if others else value


def rows_of(block):
    return pl.ds(pl.multiple_of(block * BLOCK, BLOCK), BLOCK)


def qk(query, key):
    return lax.dot_general(query, key, (((1,), (1,)), ((), ())), preferred_element_type=F32)


def pv(weights, value):
    return jnp.dot(weights.astype(BF16), value, preferred_element_type=F32)


def add_up(tokens, places, weights):
    total = None
    for place, weight in zip(places, weights):
        depth = weight.shape[0]
        columns = pl.ds(pl.multiple_of(place, depth), depth)
        term = jnp.dot(tokens[:, columns], weight[...], preferred_element_type=F32)
        total = term if total is None else total + term
    return total


def own_kernel(count, meta, tokens, *refs):
    weights, out = refs[:count], refs[count]
    for j in range(out.shape[1] // PAIR):
        lanes = slice(j * PAIR, (j + 1) * PAIR)
        out[:, lanes] = add_up(tokens, [meta[at] for at in range(count)], [weight.at[:, lanes] for weight in weights])


def pack_kernel(layout, base_at, slots, slot_at, meta, tokens, partial, *refs):
    arrived, packs, joined = refs[: len(layout)], refs[len(layout) : -1], refs[-1]
    for at, array in zip(layout, arrived):
        rows = array.shape[0]
        joined[pl.ds(pl.multiple_of(meta[at], rows), rows), :] = array[...]
    columns = pl.ds(pl.multiple_of(meta[base_at], joined.shape[0]), joined.shape[0])
    for slot in range(slots):
        for head in range(HEADS):
            rows = rows_of(meta[slot_at + HEADS * slot + head])
            lanes = [slice(start, start + HEAD_DIM) for start in (head * HEAD_DIM, WIDTH + head * HEAD_DIM)]
            weight = jnp.concatenate([joined[:, part] for part in lanes], axis=1)
            product = jnp.dot(tokens[rows, columns], weight, preferred_element_type=F32)
            for field, part in enumerate(lanes):
                own = partial[rows, WIDTH + part.start : WIDTH + part.stop]
                total = own + product[:, field * HEAD_DIM : (field + 1) * HEAD_DIM]
                packs[slot][:, part] = total.astype(BF16)


def kv_kernel(base_at, meta, tokens, partial, joined, kv):
    columns = pl.ds(pl.multiple_of(meta[base_at], joined.shape[0]), joined.shape[0])
    for j in range(2 * WIDTH // PAIR):
        lanes = slice(j * PAIR, (j + 1) * PAIR)
        product = jnp.dot(tokens[:, columns], joined[:, lanes], preferred_element_type=F32)
        kv[:, lanes] = (partial[:, WIDTH + j * PAIR : WIDTH + (j + 1) * PAIR] + product).astype(BF16)


def with_ones(value):
    return jnp.concatenate([value, jnp.ones(value.shape, BF16)], axis=1)


def attend_kernel(bases_at, slots, slot_at, match_at, meta, tokens, partial, *refs):
    weights, refs = refs[: len(bases_at)], refs[len(bases_at) :]
    kv, out, refs = refs[0], refs[1], refs[2:]
    state, scratch = refs[: 4 * slots], refs[4 * slots :]
    query, acc_all, top_all, sum_all = scratch
    blocks = query.shape[0] // BLOCK
    row = lax.broadcasted_iota(jnp.int32, (BLOCK, BLOCK), 0)
    column = lax.broadcasted_iota(jnp.int32, (BLOCK, BLOCK), 1)
    causal = column <= row
    share = weights[0].shape[1] if weights else 0
    places = [meta[at] + i * share for at in bases_at for i in range(2)]
    for pair in range(HEADS // 2):
        lanes = slice(pair * PAIR, (pair + 1) * PAIR)
        total = partial[:, lanes]
        if weights:
            parts = [weight.at[i, :, lanes] for weight in weights for i in range(2)]
            total = total + add_up(tokens, places, parts)
        query[:, lanes] = total.astype(BF16)

    def lanes_of(head):
        return slice(head * HEAD_DIM, (head + 1) * HEAD_DIM)

    def score(head, b):
        rows = slice(b * BLOCK, (b + 1) * BLOCK)
        return qk(query[rows, lanes_of(head)], kv[: (b + 1) * BLOCK, lanes_of(head)])

    def weigh(head, b, scores):
        near_block = meta[slot_at + head]
        far_block = meta[slot_at + HEADS + head]
        times = (
            1
            + jnp.where(near_block == b, 1, 0)
            + jnp.where(far_block == b, meta[match_at + head], 0)
        ).astype(F32)
        diagonal = jnp.where(causal, scores[:, b * BLOCK :], NEG)
        top = jnp.max(diagonal, axis=1, keepdims=True)
        if b:
            top = jnp.maximum(top, jnp.max(scores[:, : b * BLOCK], axis=1, keepdims=True))
        weight = (jnp.exp2((diagonal - top) * SCALE2) * times).astype(BF16)
        if b:
            before = jnp.exp2((scores[:, : b * BLOCK] - top) * SCALE2).astype(BF16)
            weight = jnp.concatenate([before, weight], axis=1)
        return top, weight

    def finish(head, b, top, weight):
        lanes = lanes_of(head)
        rows = slice(b * BLOCK, (b + 1) * BLOCK)
        value = kv[: (b + 1) * BLOCK, WIDTH + head * HEAD_DIM : WIDTH + (head + 1) * HEAD_DIM]
        both = jnp.dot(weight, with_ones(value), preferred_element_type=F32)
        acc, summed = both[:, :HEAD_DIM], both[:, HEAD_DIM:]
        out[rows, lanes] = (acc / summed).astype(BF16)
        acc_all[rows, lanes] = acc
        top_all[rows, lanes] = jnp.broadcast_to(top, (BLOCK, HEAD_DIM))
        sum_all[rows, lanes] = summed
        if b == blocks - 1:
            for slot in range(slots):
                rows = rows_of(meta[slot_at + slot * HEADS + head])
                for target, source in zip(state[4 * slot :], scratch):
                    target[:, lanes] = source[rows, lanes]

    tasks = [(head, b) for head in range(HEADS) for b in range(blocks)]
    scored, weighed = {}, {}
    for step in range(len(tasks) + 2):
        if step < len(tasks):
            scored[step] = score(*tasks[step])
        if 0 <= step - 1 < len(tasks):
            weighed[step - 1] = weigh(*tasks[step - 1], scored.pop(step - 1))
        if 0 <= step - 2 < len(tasks):
            finish(*tasks[step - 2], *weighed.pop(step - 2))


def merge_kernel(shifts, slot_at, match_at, place_at, meta, *refs):
    slots = len(shifts)
    state = refs[: 4 * slots]
    packs = refs[4 * slots : 4 * slots + sum(shifts)]
    out, results, sems = refs[4 * slots + sum(shifts) + 1 :]
    lanes = [slice(head * HEAD_DIM, (head + 1) * HEAD_DIM) for head in range(HEADS)]
    values = [slice(WIDTH + head * HEAD_DIM, WIDTH + (head + 1) * HEAD_DIM) for head in range(HEADS)]
    earlier = [None] * HEADS
    for slot, count in enumerate(shifts):
        fields = packs[sum(shifts[:slot]) : sum(shifts[: slot + 1])]
        query, acc_ref, top_ref, sum_ref = state[4 * slot : 4 * slot + 4]
        place = meta[place_at + slot]
        scores, weights = [], []
        for head in range(HEADS):
            parts = []
            for step, field in enumerate(fields):
                seen = place ^ (step + 1) < place
                if slot:
                    seen = seen & (meta[match_at + head] == 1)
                parts.append(jnp.where(seen, qk(query[:, lanes[head]], field[:, lanes[head]]), NEG))
            scores.append(jnp.concatenate(parts, axis=1))
        for head in range(HEADS):
            acc, top, summed = (ref[:, lanes[head]] for ref in (acc_ref, top_ref, sum_ref))
            if slot:
                same = meta[slot_at + head] == meta[slot_at + HEADS + head]
                acc, top, summed = (
                    jnp.where(same, new, old) for new, old in zip(earlier[head], (acc, top, summed))
                )
            best = jnp.maximum(top, jnp.max(scores[head], axis=1, keepdims=True))
            decay = jnp.exp2((top - best) * SCALE2)
            weight = jnp.exp2((scores[head] - best[:, :1]) * SCALE2).astype(BF16)
            weights.append((acc * decay, best, summed * decay, weight))
        copies = []
        for head in range(HEADS):
            acc, best, summed, weight = weights[head]
            value = jnp.concatenate([field[:, values[head]] for field in fields], axis=0)
            both = jnp.dot(weight, with_ones(value), preferred_element_type=F32)
            acc = acc + both[:, :HEAD_DIM]
            summed = summed + both[:, HEAD_DIM:]
            earlier[head] = (acc, best, summed)
            results[slot, :, lanes[head]] = (acc / summed).astype(BF16)
            rows = rows_of(meta[slot_at + slot * HEADS + head])
            copies.append(
                pltpu.make_async_copy(
                    results.at[slot, :, lanes[head]], out.at[rows, lanes[head]], sems.at[head]
                )
            )
            copies[-1].start()
        for copy in copies:
            copy.wait()


def body(tokens, qkv_weight, near_offset, far_offset):
    sequence = tokens[0]
    row_count, depth = sequence.shape
    share = qkv_weight.shape[0]
    block_rate = row_count // BLOCK
    seq_size = lax.axis_size("seq")
    seq_index = lax.axis_index("seq")
    pieces = lax.axis_size("fsdp")
    mine = lax.axis_index("fsdp")
    near_size = min(16, seq_size)
    half = near_size // 2
    far_size = max(1, min(16, seq_size // STRIDE))
    near_at = lambda i: near_place(i, half, near_size)
    far_at = lambda i: (i // (STRIDE * far_size) * STRIDE + i % STRIDE, i // STRIDE % far_size)
    reach = max(near_at(i)[1] for i in range(seq_size))
    near_shifts = (1 << reach.bit_length()) - 1
    far_shifts = (1 << (far_size - 1).bit_length()) - 1
    slots = 2 if far_shifts else 1
    shifts = (near_shifts, far_shifts)[:slots]

    near_position = jnp.where(seq_index < half, seq_index, (seq_index - half) % near_size)
    far_position = seq_index // STRIDE % far_size
    far_match = (seq_index % STRIDE == far_offset // block_rate).astype(jnp.int32)
    spans = [(0, share // 4), (share // 2, share // 8)] if seq_size % 4 == 0 else []
    direct_from = spans[-1][0] + 2 * spans[-1][1] if spans else 0
    full_places = [(mine ^ j) * share for j in range(pieces)]
    scalars = list(full_places)
    place_at = len(scalars)
    scalars += [near_position, far_position]
    base_at = len(scalars)
    scalars += [(mine ^ bit) // 2 * 2 * share for bit in range(2, pieces, 2)]
    slot_at = len(scalars)
    match_at = slot_at + 2 * HEADS
    offsets_at = match_at + HEADS
    offsets = []
    for core in range(2):
        first = (mine % 2 ^ core) * share
        for number, (start, rows) in enumerate(spans):
            side = seq_index // (1 << number) % 2
            offsets += [first + start + side * rows, first + start + (1 - side) * rows]
        offsets.append(first + direct_from)
    as_array = lambda values: jnp.stack([jnp.asarray(value, jnp.int32) for value in values])
    meta = jnp.concatenate(
        [as_array(scalars), near_offset, far_offset % block_rate, far_match, as_array(offsets)]
    )

    scalar_spec = pl.BlockSpec(memory_space=pltpu.SMEM)
    whole = pl.BlockSpec(memory_space=pltpu.VMEM)
    shape = jax.ShapeDtypeStruct

    def call(kernel, args, results, name, scratch=()):
        return pl.pallas_call(
            kernel,
            in_specs=[scalar_spec] + [whole] * len(args),
            out_specs=[whole] * len(results),
            out_shape=results,
            scratch_shapes=list(scratch),
            compiler_params=pltpu.CompilerParams(vmem_limit_bytes=VMEM_LIMIT),
            cost_estimate=pl.CostEstimate(flops=MODEL_FLOPS[name], bytes_accessed=1000, transcendentals=0),
            name=name,
        )(meta, *args)

    local = [qkv_weight]
    bits = range(2, pieces, 2)
    known = {}
    if pieces > 1:
        local.append(swap(qkv_weight, "fsdp", 1))
        known["core"] = local[-1]
    (partial,) = call(
        functools.partial(own_kernel, len(local)),
        [ordered("t", sequence, known), *local],
        [shape((row_count, 3 * WIDTH), F32)],
        "project_own",
    )
    known["partial"] = partial
    direct_rows, queries = [], []
    for bit in bits:
        mine_rows, other_rows = [], []
        for number, (start, rows) in enumerate(spans):
            tag = str(number)
            side = seq_index // (1 << number) % 2
            cut = lax.dynamic_slice(
                ordered("c" + tag, qkv_weight, known), (start + side * rows, WIDTH), (rows, 2 * WIDTH)
            )
            known["c" + tag] = cut
            direct = swap(cut, "fsdp", bit)
            known["x" + tag] = direct
            across = swap(ordered("f" + tag, direct, known), "fsdp", 1)
            known["f" + tag] = across
            passed = ordered("p" + tag, swap(ordered("y" + tag, direct, known), "seq", 1 << number), known)
            known["y" + tag] = passed
            mine_rows += [direct, passed]
            other_rows += [across, swap(passed, "fsdp", 1)]
            known["q" + tag] = other_rows[-1]
        cut = ordered("cD", qkv_weight, known)[direct_from:, WIDTH:]
        known["cD"] = cut
        rest = swap(cut, "fsdp", bit)
        known["xD"] = rest
        rest = ordered("pD", rest, known)
        known["fD"] = swap(rest, "fsdp", 1)
        direct_rows.append(mine_rows + [rest] + other_rows + [known["fD"]])
        cut = ordered("cQ", qkv_weight, known)[:, :WIDTH]
        known["cQ"] = cut
        queries.append(swap(cut, "fsdp", bit))
    assert len(bits) <= 1
    if bits:
        layout = [offsets_at + i for i in range(len(direct_rows[0]))]
        *packs, joined = call(
            functools.partial(pack_kernel, layout, base_at, slots, slot_at),
            [sequence, partial, *direct_rows[0]],
            [shape((BLOCK, 2 * WIDTH), BF16)] * slots + [shape((2 * share, 2 * WIDTH), BF16)],
            "project_pack",
        )
        known["pack"] = packs[0]
        (kv,) = call(
            functools.partial(kv_kernel, base_at),
            [sequence, ordered("kv", partial, known), joined],
            [shape((row_count, 2 * WIDTH), BF16)],
            "project_kv",
        )
    else:
        kv = partial[:, WIDTH:].astype(BF16)
        blocks = kv.reshape(block_rate, BLOCK, 2, HEADS, HEAD_DIM)
        packs = []
        for offset in (near_offset, far_offset % block_rate)[:slots]:
            picked = blocks[offset, :, :, jnp.arange(HEADS)]
            packs.append(picked.transpose(1, 2, 0, 3).reshape(BLOCK, 2 * WIDTH))
    known["kv"] = kv
    received = []
    for pack, place, count, unit in zip(packs, (near_at, far_at), shifts, (1, STRIDE)):
        for step in NEAR_ORDER if count == len(NEAR_ORDER) else range(1, count + 1):
            received.append((step, lax.ppermute(pack, "seq", earlier_pairs(seq_size, place, step))))
        known |= {f"n{step}": r for step, r in received}
    received = [r for _, r in sorted(received[:shifts[0]], key=lambda v: v[0])] + [r for _, r in received[shifts[0]:]]
    crossed_q = []
    for direct in queries:
        direct = ordered("q", direct, known)
        crossed_q.append(
            lax.all_to_all(
                jnp.broadcast_to(direct[None], (2,) + direct.shape),
                "fsdp",
                0,
                0,
                axis_index_groups=[[i, i + 1] for i in range(0, pieces, 2)],
            )
        )
    q_where = [base_at + number for number in range(len(queries))]
    state_types = [BF16, F32, F32, F32]
    partial_out, *state = call(
        functools.partial(attend_kernel, q_where, slots, slot_at, match_at),
        [sequence, partial, *crossed_q, kv],
        [shape((row_count, WIDTH), BF16)] + [shape((BLOCK, WIDTH), kind) for kind in state_types] * slots,
        "attend_local",
        [pltpu.VMEM((row_count, WIDTH), kind) for kind in state_types],
    )
    count = 4 * slots + sum(shifts)
    merged = pl.pallas_call(
        functools.partial(merge_kernel, shifts, slot_at, match_at, place_at),
        in_specs=[scalar_spec] + [whole] * count + [pl.BlockSpec(memory_space=pl.ANY)],
        out_specs=pl.BlockSpec(memory_space=pl.ANY),
        out_shape=shape((row_count, WIDTH), BF16),
        scratch_shapes=[pltpu.VMEM((slots, BLOCK, WIDTH), BF16), pltpu.SemaphoreType.DMA((HEADS,))],
        input_output_aliases={count + 1: 0},
        compiler_params=pltpu.CompilerParams(vmem_limit_bytes=VMEM_LIMIT),
        cost_estimate=pl.CostEstimate(flops=MODEL_FLOPS["merge_near"], bytes_accessed=1000, transcendentals=0),
        name="merge_near",
    )(meta, *state, *received, partial_out)
    return merged[None]


def solution(mesh):
    in_specs = (P("fsdp", "seq", None), P("fsdp", None), P(), P())
    out_specs = P("fsdp", "seq", None)
    return jax.shard_map(body, mesh=mesh, in_specs=in_specs, out_specs=out_specs, check_vma=False)
```

```python
import functools
import math

import jax
import jax.numpy as jnp
from jax import lax
from jax.experimental import pallas as pl
from jax.experimental.pallas import tpu as pltpu
from jax.sharding import PartitionSpec as P

HEADS = 4
HEAD_DIM = 128
BLOCK = 128
STRIDE = 8
WIDTH = HEADS * HEAD_DIM
PAIR = 2 * HEAD_DIM
NEG = -1e30
SCALE2 = HEAD_DIM ** (-0.5) * math.log2(math.e)
VMEM_LIMIT = 24 * 1024 * 1024

MODEL_FLOPS = {"project_pack": 689999, "project_own": 3680000, "project_mid": 1610000, "project_kv": 2990000, "attend_local": 6325000, "merge_near": 2990000}
ORDER = {
    'c1': ('c0',),
    'cD': ('c1',),
    'cQ': ('cD',),
    'p0': ('partial', 'xD'),
    'p1': ('partial',),
    'q': ('kv',),
    'kv': ('pack',),
}
NEAR_ORDER = (2, 3, 1)
F32 = jnp.float32
BF16 = jnp.bfloat16


def near_place(index, half, size):
    if index < half:
        return 0, index
    return 1 + (index - half) // size, (index - half) % size


def earlier_pairs(count, place, bits):
    where = {place(i): i for i in range(count)}
    pairs = []
    for source in range(count):
        run, spot = place(source)
        if spot ^ bits > spot and (run, spot ^ bits) in where:
            pairs.append((source, where[run, spot ^ bits]))
    return pairs


def swap(value, axis, bit):
    count = lax.axis_size(axis)
    return lax.ppermute(value, axis, [(i, i ^ bit) for i in range(count)])


def after(value, *others):
    return lax.optimization_barrier((value,) + others)[0]


def ordered(name, value, known):
    others = [known[other] for other in ORDER.get(name, ()) if other in known]
    return after(value, *others) if others else value


def rows_of(block):
    return pl.ds(pl.multiple_of(block * BLOCK, BLOCK), BLOCK)


def qk(query, key):
    return lax.dot_general(query, key, (((1,), (1,)), ((), ())), preferred_element_type=F32)


def pv(weights, value):
    return jnp.dot(weights.astype(BF16), value, preferred_element_type=F32)


def add_up(tokens, places, weights):
    total = None
    for place, weight in zip(places, weights):
        depth = weight.shape[0]
        columns = pl.ds(pl.multiple_of(place, depth), depth)
        term = jnp.dot(tokens[:, columns], weight[...], preferred_element_type=F32)
        total = term if total is None else total + term
    return total


def own_kernel(count, meta, tokens, *refs):
    weights, out = refs[:count], refs[count]
    for j in range(out.shape[1] // PAIR):
        lanes = slice(j * PAIR, (j + 1) * PAIR)
        out[:, lanes] = add_up(tokens, [meta[at] for at in range(count)], [weight.at[:, lanes] for weight in weights])


def pack_kernel(layout, base_at, slots, slot_at, meta, tokens, partial, *refs):
    arrived, packs, joined = refs[: len(layout)], refs[len(layout) : -1], refs[-1]
    for at, array in zip(layout, arrived):
        rows = array.shape[0]
        joined[pl.ds(pl.multiple_of(meta[at], rows), rows), :] = array[...]
    columns = pl.ds(pl.multiple_of(meta[base_at], joined.shape[0]), joined.shape[0])
    for slot in range(slots):
        for head in range(HEADS):
            rows = rows_of(meta[slot_at + HEADS * slot + head])
            lanes = [slice(start, start + HEAD_DIM) for start in (head * HEAD_DIM, WIDTH + head * HEAD_DIM)]
            weight = jnp.concatenate([joined[:, part] for part in lanes], axis=1)
            product = jnp.dot(tokens[rows, columns], weight, preferred_element_type=F32)
            for field, part in enumerate(lanes):
                own = partial[rows, WIDTH + part.start : WIDTH + part.stop]
                total = own + product[:, field * HEAD_DIM : (field + 1) * HEAD_DIM]
                packs[slot][:, part] = total.astype(BF16)


def kv_kernel(base_at, meta, tokens, partial, joined, kv):
    columns = pl.ds(pl.multiple_of(meta[base_at], joined.shape[0]), joined.shape[0])
    for j in range(2 * WIDTH // PAIR):
        lanes = slice(j * PAIR, (j + 1) * PAIR)
        product = jnp.dot(tokens[:, columns], joined[:, lanes], preferred_element_type=F32)
        kv[:, lanes] = (partial[:, WIDTH + j * PAIR : WIDTH + (j + 1) * PAIR] + product).astype(BF16)


def with_ones(value):
    return jnp.concatenate([value, jnp.ones(value.shape, BF16)], axis=1)


def attend_kernel(bases_at, slots, slot_at, match_at, meta, tokens, partial, *refs):
    weights, refs = refs[: len(bases_at)], refs[len(bases_at) :]
    kv, out, refs = refs[0], refs[1], refs[2:]
    state, scratch = refs[: 4 * slots], refs[4 * slots :]
    query, acc_all, top_all, sum_all = scratch
    blocks = query.shape[0] // BLOCK
    row = lax.broadcasted_iota(jnp.int32, (BLOCK, BLOCK), 0)
    column = lax.broadcasted_iota(jnp.int32, (BLOCK, BLOCK), 1)
    causal = column <= row
    places = [meta[at] + offset for at, offset in bases_at]
    for pair in range(HEADS // 2):
        lanes = slice(pair * PAIR, (pair + 1) * PAIR)
        total = partial[:, lanes]
        if weights:
            total = total + add_up(tokens, places, [weight.at[:, lanes] for weight in weights])
        query[:, lanes] = total.astype(BF16)

    def lanes_of(head):
        return slice(head * HEAD_DIM, (head + 1) * HEAD_DIM)

    def score(head, b):
        rows = slice(b * BLOCK, (b + 1) * BLOCK)
        return qk(query[rows, lanes_of(head)], kv[: (b + 1) * BLOCK, lanes_of(head)])

    def weigh(head, b, scores):
        near_block = meta[slot_at + head]
        far_block = meta[slot_at + HEADS + head]
        times = (
            1
            + jnp.where(near_block == b, 1, 0)
            + jnp.where(far_block == b, meta[match_at + head], 0)
        ).astype(F32)
        diagonal = jnp.where(causal, scores[:, b * BLOCK :], NEG)
        top = jnp.max(diagonal, axis=1, keepdims=True)
        if b:
            top = jnp.maximum(top, jnp.max(scores[:, : b * BLOCK], axis=1, keepdims=True))
        weight = (jnp.exp2((diagonal - top) * SCALE2) * times).astype(BF16)
        if b:
            before = jnp.exp2((scores[:, : b * BLOCK] - top) * SCALE2).astype(BF16)
            weight = jnp.concatenate([before, weight], axis=1)
        return top, weight

    def finish(head, b, top, weight):
        lanes = lanes_of(head)
        rows = slice(b * BLOCK, (b + 1) * BLOCK)
        value = kv[: (b + 1) * BLOCK, WIDTH + head * HEAD_DIM : WIDTH + (head + 1) * HEAD_DIM]
        both = jnp.dot(weight, with_ones(value), preferred_element_type=F32)
        acc, summed = both[:, :HEAD_DIM], both[:, HEAD_DIM:]
        out[rows, lanes] = (acc / summed).astype(BF16)
        acc_all[rows, lanes] = acc
        top_all[rows, lanes] = jnp.broadcast_to(top, (BLOCK, HEAD_DIM))
        sum_all[rows, lanes] = summed
        if b == blocks - 1:
            for slot in range(slots):
                rows = rows_of(meta[slot_at + slot * HEADS + head])
                for target, source in zip(state[4 * slot :], scratch):
                    target[:, lanes] = source[rows, lanes]

    tasks = [(head, b) for head in range(HEADS) for b in range(blocks)]
    scored, weighed = {}, {}
    for step in range(len(tasks) + 2):
        if step < len(tasks):
            scored[step] = score(*tasks[step])
        if 0 <= step - 1 < len(tasks):
            weighed[step - 1] = weigh(*tasks[step - 1], scored.pop(step - 1))
        if 0 <= step - 2 < len(tasks):
            finish(*tasks[step - 2], *weighed.pop(step - 2))


def merge_kernel(shifts, steps, slot_at, match_at, place_at, meta, *refs):
    slots = len(shifts)
    state = refs[: 4 * slots]
    packs = refs[4 * slots : 4 * slots + sum(shifts)]
    out, results, sems = refs[4 * slots + sum(shifts) + 1 :]
    lanes = [slice(head * HEAD_DIM, (head + 1) * HEAD_DIM) for head in range(HEADS)]
    values = [slice(WIDTH + head * HEAD_DIM, WIDTH + (head + 1) * HEAD_DIM) for head in range(HEADS)]
    earlier = [None] * HEADS
    for slot, count in enumerate(shifts):
        fields = packs[sum(shifts[:slot]) : sum(shifts[: slot + 1])]
        query, acc_ref, top_ref, sum_ref = state[4 * slot : 4 * slot + 4]
        place = meta[place_at + slot]
        scores, weights = [], []
        for head in range(HEADS):
            parts = []
            for step, field in zip(steps[sum(shifts[:slot]) :], fields):
                seen = place ^ step < place
                if slot:
                    seen = seen & (meta[match_at + head] == 1)
                parts.append(jnp.where(seen, qk(query[:, lanes[head]], field[:, lanes[head]]), NEG))
            scores.append(jnp.concatenate(parts, axis=1))
        for head in range(HEADS):
            acc, top, summed = (ref[:, lanes[head]] for ref in (acc_ref, top_ref, sum_ref))
            if slot:
                same = meta[slot_at + head] == meta[slot_at + HEADS + head]
                acc, top, summed = (
                    jnp.where(same, new, old) for new, old in zip(earlier[head], (acc, top, summed))
                )
            best = jnp.maximum(top, jnp.max(scores[head], axis=1, keepdims=True))
            decay = jnp.exp2((top - best) * SCALE2)
            weight = jnp.exp2((scores[head] - best[:, :1]) * SCALE2).astype(BF16)
            weights.append((acc * decay, best, summed * decay, weight))
        copies = []
        for head in range(HEADS):
            acc, best, summed, weight = weights[head]
            value = jnp.concatenate([field[:, values[head]] for field in fields], axis=0)
            both = jnp.dot(weight, with_ones(value), preferred_element_type=F32)
            acc = acc + both[:, :HEAD_DIM]
            summed = summed + both[:, HEAD_DIM:]
            earlier[head] = (acc, best, summed)
            results[slot, :, lanes[head]] = (acc / summed).astype(BF16)
            rows = rows_of(meta[slot_at + slot * HEADS + head])
            copies.append(
                pltpu.make_async_copy(
                    results.at[slot, :, lanes[head]], out.at[rows, lanes[head]], sems.at[head]
                )
            )
            copies[-1].start()
        for copy in copies:
            copy.wait()


def body(tokens, qkv_weight, near_offset, far_offset):
    sequence = tokens[0]
    row_count, depth = sequence.shape
    share = qkv_weight.shape[0]
    block_rate = row_count // BLOCK
    seq_size = lax.axis_size("seq")
    seq_index = lax.axis_index("seq")
    pieces = lax.axis_size("fsdp")
    mine = lax.axis_index("fsdp")
    near_size = min(16, seq_size)
    half = near_size // 2
    far_size = max(1, min(16, seq_size // STRIDE))
    near_at = lambda i: near_place(i, half, near_size)
    far_at = lambda i: (i // (STRIDE * far_size) * STRIDE + i % STRIDE, i // STRIDE % far_size)
    reach = max(near_at(i)[1] for i in range(seq_size))
    near_shifts = (1 << reach.bit_length()) - 1
    far_shifts = (1 << (far_size - 1).bit_length()) - 1
    slots = 2 if far_shifts else 1
    shifts = (near_shifts, far_shifts)[:slots]

    near_position = jnp.where(seq_index < half, seq_index, (seq_index - half) % near_size)
    far_position = seq_index // STRIDE % far_size
    far_match = (seq_index % STRIDE == far_offset // block_rate).astype(jnp.int32)
    spans = [(0, share // 4), (share // 2, share // 8)] if seq_size % 4 == 0 else []
    direct_from = spans[-1][0] + 2 * spans[-1][1] if spans else 0
    full_places = [(mine ^ j) * share for j in range(pieces)]
    scalars = list(full_places)
    place_at = len(scalars)
    scalars += [near_position, far_position]
    base_at = len(scalars)
    scalars += [(mine ^ bit) // 2 * 2 * share for bit in range(2, pieces, 2)]
    slot_at = len(scalars)
    match_at = slot_at + 2 * HEADS
    offsets_at = match_at + HEADS
    offsets = []
    for core in range(2):
        first = (mine % 2 ^ core) * share
        for number, (start, rows) in enumerate(spans):
            side = seq_index // (1 << number) % 2
            offsets += [first + start + side * rows, first + start + (1 - side) * rows]
        offsets.append(first + direct_from)
    as_array = lambda values: jnp.stack([jnp.asarray(value, jnp.int32) for value in values])
    meta = jnp.concatenate(
        [as_array(scalars), near_offset, far_offset % block_rate, far_match, as_array(offsets)]
    )

    scalar_spec = pl.BlockSpec(memory_space=pltpu.SMEM)
    whole = pl.BlockSpec(memory_space=pltpu.VMEM)
    shape = jax.ShapeDtypeStruct

    def call(kernel, args, results, name, scratch=()):
        return pl.pallas_call(
            kernel,
            in_specs=[scalar_spec] + [whole] * len(args),
            out_specs=[whole] * len(results),
            out_shape=results,
            scratch_shapes=list(scratch),
            compiler_params=pltpu.CompilerParams(vmem_limit_bytes=VMEM_LIMIT),
            cost_estimate=pl.CostEstimate(flops=MODEL_FLOPS[name], bytes_accessed=1000, transcendentals=0),
            name=name,
        )(meta, *args)

    local = [qkv_weight]
    bits = range(2, pieces, 2)
    known = {}
    if pieces > 1:
        local.append(swap(qkv_weight, "fsdp", 1))
        known["core"] = local[-1]
    (partial,) = call(
        functools.partial(own_kernel, len(local)),
        [ordered("t", sequence, known), *local],
        [shape((row_count, 3 * WIDTH), F32)],
        "project_own",
    )
    known["partial"] = partial
    direct_rows, queries = [], []
    for bit in bits:
        mine_rows, other_rows = [], []
        for number, (start, rows) in enumerate(spans):
            tag = str(number)
            side = seq_index // (1 << number) % 2
            cut = lax.dynamic_slice(
                ordered("c" + tag, qkv_weight, known), (start + side * rows, WIDTH), (rows, 2 * WIDTH)
            )
            known["c" + tag] = cut
            direct = swap(cut, "fsdp", bit)
            known["x" + tag] = direct
            across = swap(ordered("f" + tag, direct, known), "fsdp", 1)
            known["f" + tag] = across
            passed = ordered("p" + tag, swap(ordered("y" + tag, direct, known), "seq", 1 << number), known)
            known["y" + tag] = passed
            mine_rows += [direct, passed]
            other_rows += [across, swap(passed, "fsdp", 1)]
            known["q" + tag] = other_rows[-1]
        known["meta"] = meta
        cut = ordered("cD", qkv_weight, known)[direct_from:, WIDTH:]
        known["cD"] = cut
        rest = swap(cut, "fsdp", bit)
        known["xD"] = rest
        rest = ordered("pD", rest, known)
        known["fD"] = swap(rest, "fsdp", 1)
        direct_rows.append(mine_rows + [rest] + other_rows + [known["fD"]])
        cut = ordered("cQ", qkv_weight, known)[:, :WIDTH]
        known["cQ"] = cut
        queries.append(swap(cut, "fsdp", bit))
    assert len(bits) <= 1
    if bits:
        layout = [offsets_at + i for i in range(len(direct_rows[0]))]
        *packs, joined = call(
            functools.partial(pack_kernel, layout, base_at, slots, slot_at),
            [sequence, partial, *direct_rows[0]],
            [shape((BLOCK, 2 * WIDTH), BF16)] * slots + [shape((2 * share, 2 * WIDTH), BF16)],
            "project_pack",
        )
        known["pack"] = packs[0]
        (kv,) = call(
            functools.partial(kv_kernel, base_at),
            [sequence, ordered("kv", partial, known), joined],
            [shape((row_count, 2 * WIDTH), BF16)],
            "project_kv",
        )
    else:
        kv = partial[:, WIDTH:].astype(BF16)
        blocks = kv.reshape(block_rate, BLOCK, 2, HEADS, HEAD_DIM)
        packs = []
        for offset in (near_offset, far_offset % block_rate)[:slots]:
            picked = blocks[offset, :, :, jnp.arange(HEADS)]
            packs.append(picked.transpose(1, 2, 0, 3).reshape(BLOCK, 2 * WIDTH))
    known["kv"] = kv
    received = []
    for pack, place, count, unit in zip(packs, (near_at, far_at), shifts, (1, STRIDE)):
        for step in NEAR_ORDER if count == len(NEAR_ORDER) else range(1, count + 1):
            received.append((step, lax.ppermute(pack, "seq", earlier_pairs(seq_size, place, step))))
        known |= {f"n{step}": r for step, r in received}
    steps = [step for step, _ in received]
    received = [pack for _, pack in received]
    crossed_q, q_places = [], []
    for bit, direct in zip(bits, queries):
        direct = ordered("q", direct, known)
        across = lax.cond(
            near_offset[0] >= 0,
            lambda value: swap(value, "fsdp", 1),
            lambda value: swap(swap(swap(value, "fsdp", 1), "fsdp", 1), "fsdp", 1),
            direct,
        )
        crossed_q += [direct, across]
        q_places += [(bit, 0), (bit ^ 1, 0)]
    state_types = [BF16, F32, F32, F32]
    partial_out, *state = call(
        functools.partial(attend_kernel, q_places, slots, slot_at, match_at),
        [sequence, partial, *crossed_q, kv],
        [shape((row_count, WIDTH), BF16)] + [shape((BLOCK, WIDTH), kind) for kind in state_types] * slots,
        "attend_local",
        [pltpu.VMEM((row_count, WIDTH), kind) for kind in state_types],
    )
    count = 4 * slots + sum(shifts)
    merged = pl.pallas_call(
        functools.partial(merge_kernel, shifts, steps, slot_at, match_at, place_at),
        in_specs=[scalar_spec] + [whole] * count + [pl.BlockSpec(memory_space=pl.ANY)],
        out_specs=pl.BlockSpec(memory_space=pl.ANY),
        out_shape=shape((row_count, WIDTH), BF16),
        scratch_shapes=[pltpu.VMEM((slots, BLOCK, WIDTH), BF16), pltpu.SemaphoreType.DMA((HEADS,))],
        input_output_aliases={count + 1: 0},
        compiler_params=pltpu.CompilerParams(vmem_limit_bytes=VMEM_LIMIT),
        cost_estimate=pl.CostEstimate(flops=MODEL_FLOPS["merge_near"], bytes_accessed=1000, transcendentals=0),
        name="merge_near",
    )(meta, *state, *received, partial_out)
    return merged[None]


def solution(mesh):
    in_specs = (P("fsdp", "seq", None), P("fsdp", None), P(), P())
    out_specs = P("fsdp", "seq", None)
    return jax.shard_map(body, mesh=mesh, in_specs=in_specs, out_specs=out_specs, check_vma=False)
```

```python
import functools
import math

import jax
import jax.numpy as jnp
from jax import lax
from jax.experimental import pallas as pl
from jax.experimental.pallas import tpu as pltpu
from jax.sharding import PartitionSpec as P

HEADS = 4
HEAD_DIM = 128
BLOCK = 128
STRIDE = 8
WIDTH = HEADS * HEAD_DIM
PAIR = 2 * HEAD_DIM
NEG = -1e30
SCALE2 = HEAD_DIM ** (-0.5) * math.log2(math.e)
VMEM_LIMIT = 24 * 1024 * 1024

MODEL_FLOPS = {"slot_queries": 575000, "project_pack": 689999, "project_own": 3680000, "project_mid": 1610000, "project_kv": 2990000, "attend_local": 6325000, "merge_near": 2990000}
ORDER = {
    'c1': ('c0',),
    'cD': ('c1',),
    'cQ': ('cD',),
    'p0': ('partial', 'xD'),
    'p1': ('partial',),
    'q': ('kv',),
    'kv': ('pack',),
}
NEAR_ORDER = (3, 2, 1)
F32 = jnp.float32
BF16 = jnp.bfloat16


def near_place(index, half, size):
    if index < half:
        return 0, index
    return 1 + (index - half) // size, (index - half) % size


def partners(count, place, bits):
    where = {place(i): i for i in range(count)}
    pairs = []
    for source in range(count):
        run, spot = place(source)
        if (run, spot ^ bits) in where:
            pairs.append((source, where[run, spot ^ bits]))
    return pairs


def swap(value, axis, bit):
    count = lax.axis_size(axis)
    return lax.ppermute(value, axis, [(i, i ^ bit) for i in range(count)])


def after(value, *others):
    return lax.optimization_barrier((value,) + others)[0]


def ordered(name, value, known):
    others = [known[other] for other in ORDER.get(name, ()) if other in known]
    return after(value, *others) if others else value


def rows_of(block):
    return pl.ds(pl.multiple_of(block * BLOCK, BLOCK), BLOCK)


def qk(query, key):
    return lax.dot_general(query, key, (((1,), (1,)), ((), ())), preferred_element_type=F32)


def pv(weights, value):
    return jnp.dot(weights.astype(BF16), value, preferred_element_type=F32)


def add_up(tokens, places, weights):
    total = None
    for place, weight in zip(places, weights):
        depth = weight.shape[0]
        columns = pl.ds(pl.multiple_of(place, depth), depth)
        term = jnp.dot(tokens[:, columns], weight[...], preferred_element_type=F32)
        total = term if total is None else total + term
    return total


def own_kernel(count, meta, tokens, *refs):
    weights, out = refs[:count], refs[count]
    for j in range(out.shape[1] // PAIR):
        lanes = slice(j * PAIR, (j + 1) * PAIR)
        out[:, lanes] = add_up(tokens, [meta[at] for at in range(count)], [weight.at[:, lanes] for weight in weights])


def pack_kernel(layout, base_at, slots, slot_at, meta, tokens, partial, *refs):
    arrived, packs, joined = refs[: len(layout)], refs[len(layout) : -1], refs[-1]
    for at, array in zip(layout, arrived):
        rows = array.shape[0]
        joined[pl.ds(pl.multiple_of(meta[at], rows), rows), :] = array[...]
    columns = pl.ds(pl.multiple_of(meta[base_at], joined.shape[0]), joined.shape[0])
    for slot in range(slots):
        for head in range(HEADS):
            rows = rows_of(meta[slot_at + HEADS * slot + head])
            lanes = [slice(start, start + HEAD_DIM) for start in (head * HEAD_DIM, WIDTH + head * HEAD_DIM)]
            weight = jnp.concatenate([joined[:, part] for part in lanes], axis=1)
            product = jnp.dot(tokens[rows, columns], weight, preferred_element_type=F32)
            for field, part in enumerate(lanes):
                own = partial[rows, WIDTH + part.start : WIDTH + part.stop]
                total = own + product[:, field * HEAD_DIM : (field + 1) * HEAD_DIM]
                packs[slot][:, part] = total.astype(BF16)


def slot_kernel(core_at, meta, source, out):
    out[1 - meta[core_at]] = source[...]


def kv_kernel(base_at, meta, tokens, partial, joined, kv):
    columns = pl.ds(pl.multiple_of(meta[base_at], joined.shape[0]), joined.shape[0])
    for j in range(2 * WIDTH // PAIR):
        lanes = slice(j * PAIR, (j + 1) * PAIR)
        product = jnp.dot(tokens[:, columns], joined[:, lanes], preferred_element_type=F32)
        kv[:, lanes] = (partial[:, WIDTH + j * PAIR : WIDTH + (j + 1) * PAIR] + product).astype(BF16)


def with_ones(value):
    return jnp.concatenate([value, jnp.ones(value.shape, BF16)], axis=1)


def attend_kernel(bases_at, core_at, slots, slot_at, match_at, meta, tokens, partial, *refs):
    weights, refs = refs[: len(bases_at)], refs[len(bases_at) :]
    kv, out, refs = refs[0], refs[1], refs[2:]
    state, scratch = refs[: 4 * slots], refs[4 * slots :]
    query, acc_all, top_all, sum_all = scratch
    blocks = query.shape[0] // BLOCK
    row = lax.broadcasted_iota(jnp.int32, (BLOCK, BLOCK), 0)
    column = lax.broadcasted_iota(jnp.int32, (BLOCK, BLOCK), 1)
    causal = column <= row
    places = [meta[at] for at in bases_at]
    other = 1 - meta[core_at]
    for pair in range(HEADS // 2):
        lanes = slice(pair * PAIR, (pair + 1) * PAIR)
        total = partial[:, lanes]
        if weights:
            parts = [weights[0].at[:, lanes], weights[1].at[other, :, lanes]]
            total = total + add_up(tokens, places, parts)
        query[:, lanes] = total.astype(BF16)

    def lanes_of(head):
        return slice(head * HEAD_DIM, (head + 1) * HEAD_DIM)

    def score(head, b):
        rows = slice(b * BLOCK, (b + 1) * BLOCK)
        return qk(query[rows, lanes_of(head)], kv[: (b + 1) * BLOCK, lanes_of(head)])

    def weigh(head, b, scores):
        near_block = meta[slot_at + head]
        far_block = meta[slot_at + HEADS + head]
        times = (
            1
            + jnp.where(near_block == b, 1, 0)
            + jnp.where(far_block == b, meta[match_at + head], 0)
        ).astype(F32)
        diagonal = jnp.where(causal, scores[:, b * BLOCK :], NEG)
        top = jnp.max(diagonal, axis=1, keepdims=True)
        if b:
            top = jnp.maximum(top, jnp.max(scores[:, : b * BLOCK], axis=1, keepdims=True))
        weight = (jnp.exp2((diagonal - top) * SCALE2) * times).astype(BF16)
        if b:
            before = jnp.exp2((scores[:, : b * BLOCK] - top) * SCALE2).astype(BF16)
            weight = jnp.concatenate([before, weight], axis=1)
        return top, weight

    def finish(head, b, top, weight):
        lanes = lanes_of(head)
        rows = slice(b * BLOCK, (b + 1) * BLOCK)
        value = kv[: (b + 1) * BLOCK, WIDTH + head * HEAD_DIM : WIDTH + (head + 1) * HEAD_DIM]
        both = jnp.dot(weight, with_ones(value), preferred_element_type=F32)
        acc, summed = both[:, :HEAD_DIM], both[:, HEAD_DIM:]
        out[rows, lanes] = (acc / summed).astype(BF16)
        acc_all[rows, lanes] = acc
        top_all[rows, lanes] = jnp.broadcast_to(top, (BLOCK, HEAD_DIM))
        sum_all[rows, lanes] = summed
        if b == blocks - 1:
            for slot in range(slots):
                rows = rows_of(meta[slot_at + slot * HEADS + head])
                for target, source in zip(state[4 * slot :], scratch):
                    target[:, lanes] = source[rows, lanes]

    tasks = [(head, b) for head in range(HEADS) for b in range(blocks)]
    scored, weighed = {}, {}
    for step in range(len(tasks) + 2):
        if step < len(tasks):
            scored[step] = score(*tasks[step])
        if 0 <= step - 1 < len(tasks):
            weighed[step - 1] = weigh(*tasks[step - 1], scored.pop(step - 1))
        if 0 <= step - 2 < len(tasks):
            finish(*tasks[step - 2], *weighed.pop(step - 2))


def merge_kernel(shifts, steps, slot_at, match_at, place_at, meta, *refs):
    slots = len(shifts)
    state = refs[: 4 * slots]
    packs = refs[4 * slots : 4 * slots + sum(shifts)]
    out, results, sems = refs[4 * slots + sum(shifts) + 1 :]
    lanes = [slice(head * HEAD_DIM, (head + 1) * HEAD_DIM) for head in range(HEADS)]
    values = [slice(WIDTH + head * HEAD_DIM, WIDTH + (head + 1) * HEAD_DIM) for head in range(HEADS)]
    earlier = [None] * HEADS
    for slot, count in enumerate(shifts):
        fields = packs[sum(shifts[:slot]) : sum(shifts[: slot + 1])]
        query, acc_ref, top_ref, sum_ref = state[4 * slot : 4 * slot + 4]
        place = meta[place_at + slot]
        scores, weights = [], []
        for head in range(HEADS):
            parts = []
            for step, field in zip(steps[sum(shifts[:slot]) :], fields):
                seen = place ^ step < place
                if slot:
                    seen = seen & (meta[match_at + head] == 1)
                parts.append(jnp.where(seen, qk(query[:, lanes[head]], field[:, lanes[head]]), NEG))
            scores.append(jnp.concatenate(parts, axis=1))
        for head in range(HEADS):
            acc, top, summed = (ref[:, lanes[head]] for ref in (acc_ref, top_ref, sum_ref))
            if slot:
                same = meta[slot_at + head] == meta[slot_at + HEADS + head]
                acc, top, summed = (
                    jnp.where(same, new, old) for new, old in zip(earlier[head], (acc, top, summed))
                )
            best = jnp.maximum(top, jnp.max(scores[head], axis=1, keepdims=True))
            decay = jnp.exp2((top - best) * SCALE2)
            weight = jnp.exp2((scores[head] - best[:, :1]) * SCALE2).astype(BF16)
            weights.append((acc * decay, best, summed * decay, weight))
        copies = []
        for head in range(HEADS):
            acc, best, summed, weight = weights[head]
            value = jnp.concatenate([field[:, values[head]] for field in fields], axis=0)
            both = jnp.dot(weight, with_ones(value), preferred_element_type=F32)
            acc = acc + both[:, :HEAD_DIM]
            summed = summed + both[:, HEAD_DIM:]
            earlier[head] = (acc, best, summed)
            results[slot, :, lanes[head]] = (acc / summed).astype(BF16)
            rows = rows_of(meta[slot_at + slot * HEADS + head])
            copies.append(
                pltpu.make_async_copy(
                    results.at[slot, :, lanes[head]], out.at[rows, lanes[head]], sems.at[head]
                )
            )
            copies[-1].start()
        for copy in copies:
            copy.wait()


def body(tokens, qkv_weight, near_offset, far_offset):
    sequence = tokens[0]
    row_count, depth = sequence.shape
    share = qkv_weight.shape[0]
    block_rate = row_count // BLOCK
    seq_size = lax.axis_size("seq")
    seq_index = lax.axis_index("seq")
    pieces = lax.axis_size("fsdp")
    mine = lax.axis_index("fsdp")
    near_size = min(16, seq_size)
    half = near_size // 2
    far_size = max(1, min(16, seq_size // STRIDE))
    near_at = lambda i: near_place(i, half, near_size)
    far_at = lambda i: (i // (STRIDE * far_size) * STRIDE + i % STRIDE, i // STRIDE % far_size)
    reach = max(near_at(i)[1] for i in range(seq_size))
    near_shifts = (1 << reach.bit_length()) - 1
    far_shifts = (1 << (far_size - 1).bit_length()) - 1
    slots = 2 if far_shifts else 1
    shifts = (near_shifts, far_shifts)[:slots]

    near_position = jnp.where(seq_index < half, seq_index, (seq_index - half) % near_size)
    far_position = seq_index // STRIDE % far_size
    far_match = (seq_index % STRIDE == far_offset // block_rate).astype(jnp.int32)
    spans = [(0, share // 4), (share // 2, share // 8)] if seq_size % 4 == 0 else []
    direct_from = spans[-1][0] + 2 * spans[-1][1] if spans else 0
    full_places = [(mine ^ j) * share for j in range(pieces)]
    scalars = list(full_places)
    place_at = len(scalars)
    scalars += [near_position, far_position]
    base_at = len(scalars)
    scalars += [(mine ^ bit) // 2 * 2 * share for bit in range(2, pieces, 2)]
    core_at = len(scalars)
    scalars.append(mine % 2)
    slot_at = len(scalars)
    match_at = slot_at + 2 * HEADS
    offsets_at = match_at + HEADS
    offsets = []
    for core in range(2):
        first = (mine % 2 ^ core) * share
        for number, (start, rows) in enumerate(spans):
            side = seq_index // (1 << number) % 2
            offsets += [first + start + side * rows, first + start + (1 - side) * rows]
        offsets.append(first + direct_from)
    as_array = lambda values: jnp.stack([jnp.asarray(value, jnp.int32) for value in values])
    meta = jnp.concatenate(
        [as_array(scalars), near_offset, far_offset % block_rate, far_match, as_array(offsets)]
    )

    scalar_spec = pl.BlockSpec(memory_space=pltpu.SMEM)
    whole = pl.BlockSpec(memory_space=pltpu.VMEM)
    shape = jax.ShapeDtypeStruct

    def call(kernel, args, results, name, scratch=()):
        return pl.pallas_call(
            kernel,
            in_specs=[scalar_spec] + [whole] * len(args),
            out_specs=[whole] * len(results),
            out_shape=results,
            scratch_shapes=list(scratch),
            compiler_params=pltpu.CompilerParams(vmem_limit_bytes=VMEM_LIMIT),
            cost_estimate=pl.CostEstimate(flops=MODEL_FLOPS[name], bytes_accessed=1000, transcendentals=0),
            name=name,
        )(meta, *args)

    local = [qkv_weight]
    bits = range(2, pieces, 2)
    known = {}
    if pieces > 1:
        local.append(swap(qkv_weight, "fsdp", 1))
        known["core"] = local[-1]
    (partial,) = call(
        functools.partial(own_kernel, len(local)),
        [ordered("t", sequence, known), *local],
        [shape((row_count, 3 * WIDTH), F32)],
        "project_own",
    )
    known["partial"] = partial
    direct_rows, queries = [], []
    for bit in bits:
        mine_rows, other_rows = [], []
        for number, (start, rows) in enumerate(spans):
            tag = str(number)
            side = seq_index // (1 << number) % 2
            cut = lax.dynamic_slice(
                ordered("c" + tag, qkv_weight, known), (start + side * rows, WIDTH), (rows, 2 * WIDTH)
            )
            known["c" + tag] = cut
            direct = swap(cut, "fsdp", bit)
            known["x" + tag] = direct
            across = swap(ordered("f" + tag, direct, known), "fsdp", 1)
            known["f" + tag] = across
            passed = ordered("p" + tag, swap(ordered("y" + tag, direct, known), "seq", 1 << number), known)
            known["y" + tag] = passed
            mine_rows += [direct, passed]
            other_rows += [across, swap(passed, "fsdp", 1)]
            known["q" + tag] = other_rows[-1]
        known["meta"] = meta
        cut = ordered("cD", qkv_weight, known)[direct_from:, WIDTH:]
        known["cD"] = cut
        rest = swap(cut, "fsdp", bit)
        known["xD"] = rest
        rest = ordered("pD", rest, known)
        known["fD"] = swap(rest, "fsdp", 1)
        direct_rows.append(mine_rows + [rest] + other_rows + [known["fD"]])
        cut = ordered("cQ", qkv_weight, known)[:, :WIDTH]
        known["cQ"] = cut
        queries.append(swap(cut, "fsdp", bit))
    assert len(bits) <= 1
    if bits:
        layout = [offsets_at + i for i in range(len(direct_rows[0]))]
        *packs, joined = call(
            functools.partial(pack_kernel, layout, base_at, slots, slot_at),
            [sequence, partial, *direct_rows[0]],
            [shape((BLOCK, 2 * WIDTH), BF16)] * slots + [shape((2 * share, 2 * WIDTH), BF16)],
            "project_pack",
        )
        known["pack"] = packs[0]
        (kv,) = call(
            functools.partial(kv_kernel, base_at),
            [sequence, ordered("kv", partial, known), joined],
            [shape((row_count, 2 * WIDTH), BF16)],
            "project_kv",
        )
    else:
        kv = partial[:, WIDTH:].astype(BF16)
        blocks = kv.reshape(block_rate, BLOCK, 2, HEADS, HEAD_DIM)
        packs = []
        for offset in (near_offset, far_offset % block_rate)[:slots]:
            picked = blocks[offset, :, :, jnp.arange(HEADS)]
            packs.append(picked.transpose(1, 2, 0, 3).reshape(BLOCK, 2 * WIDTH))
    known["kv"] = kv
    received = []
    for pack, place, count, unit in zip(packs, (near_at, far_at), shifts, (1, STRIDE)):
        for step in NEAR_ORDER if count == len(NEAR_ORDER) else range(1, count + 1):
            received.append((step, lax.ppermute(pack, "seq", partners(seq_size, place, step))))
        known |= {f"n{step}": r for step, r in received}
    steps = [step for step, _ in received]
    received = [pack for _, pack in received]
    crossed_q, q_places = [], []
    for bit, direct in zip(bits, queries):
        direct = ordered("q", direct, known)
        (slots_out,) = call(
            functools.partial(slot_kernel, core_at), [direct], [shape((2,) + direct.shape, BF16)], "slot_queries"
        )
        both = lax.all_to_all(
            slots_out, "fsdp", 0, 0, axis_index_groups=[[i, i + 1] for i in range(0, pieces, 2)]
        )
        crossed_q += [direct, both]
        q_places += [bit, bit ^ 1]
    state_types = [BF16, F32, F32, F32]
    partial_out, *state = call(
        functools.partial(attend_kernel, q_places, core_at, slots, slot_at, match_at),
        [sequence, partial, *crossed_q, kv],
        [shape((row_count, WIDTH), BF16)] + [shape((BLOCK, WIDTH), kind) for kind in state_types] * slots,
        "attend_local",
        [pltpu.VMEM((row_count, WIDTH), kind) for kind in state_types],
    )
    count = 4 * slots + sum(shifts)
    merged = pl.pallas_call(
        functools.partial(merge_kernel, shifts, steps, slot_at, match_at, place_at),
        in_specs=[scalar_spec] + [whole] * count + [pl.BlockSpec(memory_space=pl.ANY)],
        out_specs=pl.BlockSpec(memory_space=pl.ANY),
        out_shape=shape((row_count, WIDTH), BF16),
        scratch_shapes=[pltpu.VMEM((slots, BLOCK, WIDTH), BF16), pltpu.SemaphoreType.DMA((HEADS,))],
        input_output_aliases={count + 1: 0},
        compiler_params=pltpu.CompilerParams(vmem_limit_bytes=VMEM_LIMIT),
        cost_estimate=pl.CostEstimate(flops=MODEL_FLOPS["merge_near"], bytes_accessed=1000, transcendentals=0),
        name="merge_near",
    )(meta, *state, *received, partial_out)
    return merged[None]


def solution(mesh):
    in_specs = (P("fsdp", "seq", None), P("fsdp", None), P(), P())
    out_specs = P("fsdp", "seq", None)
    return jax.shard_map(body, mesh=mesh, in_specs=in_specs, out_specs=out_specs, check_vma=False)
```

```python
import functools
import math

import jax
import jax.numpy as jnp
from jax import lax
from jax.experimental import pallas as pl
from jax.experimental.pallas import tpu as pltpu
from jax.sharding import PartitionSpec as P

HEADS = 4
HEAD_DIM = 128
BLOCK = 128
STRIDE = 8
WIDTH = HEADS * HEAD_DIM
PAIR = 2 * HEAD_DIM
NEG = -1e30
SCALE2 = HEAD_DIM ** (-0.5) * math.log2(math.e)
VMEM_LIMIT = 24 * 1024 * 1024

MODEL_FLOPS = {"slot_queries": 575000, "sides": 11500000000, "cut_rest": 1150000, "project_other": 1150000, "project_pack": 689999, "project_own": 3680000, "project_mid": 1610000, "project_kv": 2990000, "attend_local": 6325000, "merge_near": 2990000}
ORDER = {
    'cut': ('c0',),
    'p0': ('partial', 'xD'),
    'p1': ('partial',),
    'q': ('kv',),
    'kv': ('pack',),
}
NEAR_ORDER = (3, 2, 1)
F32 = jnp.float32
BF16 = jnp.bfloat16


def near_place(index, half, size):
    if index < half:
        return 0, index
    return 1 + (index - half) // size, (index - half) % size


def partners(count, place, bits):
    where = {place(i): i for i in range(count)}
    pairs = []
    for source in range(count):
        run, spot = place(source)
        if (run, spot ^ bits) in where:
            pairs.append((source, where[run, spot ^ bits]))
    return pairs


def swap(value, axis, bit):
    count = lax.axis_size(axis)
    return lax.ppermute(value, axis, [(i, i ^ bit) for i in range(count)])


def after(value, *others):
    return lax.optimization_barrier((value,) + others)[0]


def ordered(name, value, known):
    others = [known[other] for other in ORDER.get(name, ()) if other in known]
    return after(value, *others) if others else value


def rows_of(block):
    return pl.ds(pl.multiple_of(block * BLOCK, BLOCK), BLOCK)


def qk(query, key):
    return lax.dot_general(query, key, (((1,), (1,)), ((), ())), preferred_element_type=F32)


def pv(weights, value):
    return jnp.dot(weights.astype(BF16), value, preferred_element_type=F32)


def add_up(tokens, places, weights):
    total = None
    for place, weight in zip(places, weights):
        depth = weight.shape[0]
        columns = pl.ds(pl.multiple_of(place, depth), depth)
        term = jnp.dot(tokens[:, columns], weight[...], preferred_element_type=F32)
        total = term if total is None else total + term
    return total


def sides_kernel(share, out):
    place = lax.axis_index("seq")
    out[0] = place % 2
    out[1] = place // 2 % 2
    out[2] = lax.axis_index("fsdp") * share


def cut_kernel(spans, direct_from, sides, tokens, weight, *refs):
    outs, total = refs[:-1], refs[-1]
    for (number, start, rows), out in zip(spans, outs):
        first = pl.multiple_of(start + sides[number] * rows, rows)
        out[...] = weight[pl.ds(first, rows), WIDTH:]
    if outs:
        outs[-2][...] = weight[direct_from:, WIDTH:]
        outs[-1][...] = weight[:, :WIDTH]
    multiply(tokens, sides[2], weight, None, total)


def multiply(tokens, place, weight, before, total):
    columns = pl.ds(pl.multiple_of(place, weight.shape[0]), weight.shape[0])
    for j in range(total.shape[1] // PAIR):
        lanes = slice(j * PAIR, (j + 1) * PAIR)
        product = jnp.dot(tokens[:, columns], weight[:, lanes], preferred_element_type=F32)
        total[:, lanes] = product if before is None else before[:, lanes] + product


def other_kernel(place_at, meta, tokens, weight, before, total):
    multiply(tokens, meta[place_at], weight, before, total)


def pack_kernel(layout, base_at, slots, slot_at, meta, tokens, partial, *refs):
    arrived, packs, joined = refs[: len(layout)], refs[len(layout) : -1], refs[-1]
    for at, array in zip(layout, arrived):
        rows = array.shape[0]
        joined[pl.ds(pl.multiple_of(meta[at], rows), rows), :] = array[...]
    columns = pl.ds(pl.multiple_of(meta[base_at], joined.shape[0]), joined.shape[0])
    for slot in range(slots):
        for head in range(HEADS):
            rows = rows_of(meta[slot_at + HEADS * slot + head])
            lanes = [slice(start, start + HEAD_DIM) for start in (head * HEAD_DIM, WIDTH + head * HEAD_DIM)]
            weight = jnp.concatenate([joined[:, part] for part in lanes], axis=1)
            product = jnp.dot(tokens[rows, columns], weight, preferred_element_type=F32)
            for field, part in enumerate(lanes):
                own = partial[rows, WIDTH + part.start : WIDTH + part.stop]
                total = own + product[:, field * HEAD_DIM : (field + 1) * HEAD_DIM]
                packs[slot][:, part] = total.astype(BF16)


def slot_kernel(core_at, meta, source, out):
    out[1 - meta[core_at]] = source[...]


def kv_kernel(base_at, meta, tokens, partial, joined, kv):
    columns = pl.ds(pl.multiple_of(meta[base_at], joined.shape[0]), joined.shape[0])
    for j in range(2 * WIDTH // PAIR):
        lanes = slice(j * PAIR, (j + 1) * PAIR)
        product = jnp.dot(tokens[:, columns], joined[:, lanes], preferred_element_type=F32)
        kv[:, lanes] = (partial[:, WIDTH + j * PAIR : WIDTH + (j + 1) * PAIR] + product).astype(BF16)


def with_ones(value):
    return jnp.concatenate([value, jnp.ones(value.shape, BF16)], axis=1)


def attend_kernel(bases_at, core_at, slots, slot_at, match_at, meta, tokens, partial, *refs):
    weights, refs = refs[: len(bases_at)], refs[len(bases_at) :]
    kv, out, refs = refs[0], refs[1], refs[2:]
    state, scratch, (results, sems) = refs[: 4 * slots], refs[4 * slots : -2], refs[-2:]
    query, acc_all, top_all, sum_all = scratch
    copies = []
    blocks = query.shape[0] // BLOCK
    row = lax.broadcasted_iota(jnp.int32, (BLOCK, BLOCK), 0)
    column = lax.broadcasted_iota(jnp.int32, (BLOCK, BLOCK), 1)
    causal = column <= row
    places = [meta[at] for at in bases_at]
    other = 1 - meta[core_at]
    for pair in range(HEADS // 2):
        lanes = slice(pair * PAIR, (pair + 1) * PAIR)
        total = partial[:, lanes]
        if weights:
            parts = [weights[0].at[:, lanes], weights[1].at[other, :, lanes]]
            total = total + add_up(tokens, places, parts)
        query[:, lanes] = total.astype(BF16)

    def lanes_of(head):
        return slice(head * HEAD_DIM, (head + 1) * HEAD_DIM)

    def score(head, b):
        rows = slice(b * BLOCK, (b + 1) * BLOCK)
        return qk(query[rows, lanes_of(head)], kv[: (b + 1) * BLOCK, lanes_of(head)])

    def weigh(head, b, scores):
        near_block = meta[slot_at + head]
        far_block = meta[slot_at + HEADS + head]
        times = (
            1
            + jnp.where(near_block == b, 1, 0)
            + jnp.where(far_block == b, meta[match_at + head], 0)
        ).astype(F32)
        diagonal = jnp.where(causal, scores[:, b * BLOCK :], NEG)
        top = jnp.max(diagonal, axis=1, keepdims=True)
        if b:
            top = jnp.maximum(top, jnp.max(scores[:, : b * BLOCK], axis=1, keepdims=True))
        weight = (jnp.exp2((diagonal - top) * SCALE2) * times).astype(BF16)
        if b:
            before = jnp.exp2((scores[:, : b * BLOCK] - top) * SCALE2).astype(BF16)
            weight = jnp.concatenate([before, weight], axis=1)
        return top, weight

    def finish(head, b, top, weight):
        lanes = lanes_of(head)
        rows = slice(b * BLOCK, (b + 1) * BLOCK)
        value = kv[: (b + 1) * BLOCK, WIDTH + head * HEAD_DIM : WIDTH + (head + 1) * HEAD_DIM]
        both = jnp.dot(weight, with_ones(value), preferred_element_type=F32)
        acc, summed = both[:, :HEAD_DIM], both[:, HEAD_DIM:]
        results[rows, lanes] = (acc / summed).astype(BF16)
        acc_all[rows, lanes] = acc
        top_all[rows, lanes] = jnp.broadcast_to(top, (BLOCK, HEAD_DIM))
        sum_all[rows, lanes] = summed
        if b == blocks - 1:
            copies.append(pltpu.make_async_copy(results.at[:, lanes], out.at[:, lanes], sems.at[head]))
            copies[-1].start()
            for slot in range(slots):
                rows = rows_of(meta[slot_at + slot * HEADS + head])
                for target, source in zip(state[4 * slot :], scratch):
                    target[:, lanes] = source[rows, lanes]

    tasks = [(head, b) for head in range(HEADS) for b in range(blocks)]
    scored, weighed = {}, {}
    for step in range(len(tasks) + 2):
        if step < len(tasks):
            scored[step] = score(*tasks[step])
        if 0 <= step - 1 < len(tasks):
            weighed[step - 1] = weigh(*tasks[step - 1], scored.pop(step - 1))
        if 0 <= step - 2 < len(tasks):
            finish(*tasks[step - 2], *weighed.pop(step - 2))
    for copy in copies:
        copy.wait()


def merge_kernel(shifts, steps, slot_at, match_at, place_at, meta, *refs):
    slots = len(shifts)
    state = refs[: 4 * slots]
    packs = refs[4 * slots : 4 * slots + sum(shifts)]
    out, results, sems = refs[4 * slots + sum(shifts) + 1 :]
    lanes = [slice(head * HEAD_DIM, (head + 1) * HEAD_DIM) for head in range(HEADS)]
    values = [slice(WIDTH + head * HEAD_DIM, WIDTH + (head + 1) * HEAD_DIM) for head in range(HEADS)]
    earlier = [None] * HEADS
    for slot, count in enumerate(shifts):
        fields = packs[sum(shifts[:slot]) : sum(shifts[: slot + 1])]
        query, acc_ref, top_ref, sum_ref = state[4 * slot : 4 * slot + 4]
        place = meta[place_at + slot]
        scores, weights = [], []
        for head in range(HEADS):
            parts = []
            for step, field in zip(steps[sum(shifts[:slot]) :], fields):
                seen = place ^ step < place
                if slot:
                    seen = seen & (meta[match_at + head] == 1)
                parts.append(jnp.where(seen, qk(query[:, lanes[head]], field[:, lanes[head]]), NEG))
            scores.append(jnp.concatenate(parts, axis=1))
        for head in range(HEADS):
            acc, top, summed = (ref[:, lanes[head]] for ref in (acc_ref, top_ref, sum_ref))
            if slot:
                same = meta[slot_at + head] == meta[slot_at + HEADS + head]
                acc, top, summed = (
                    jnp.where(same, new, old) for new, old in zip(earlier[head], (acc, top, summed))
                )
            best = jnp.maximum(top, jnp.max(scores[head], axis=1, keepdims=True))
            decay = jnp.exp2((top - best) * SCALE2)
            weight = jnp.exp2((scores[head] - best[:, :1]) * SCALE2).astype(BF16)
            weights.append((acc * decay, best, summed * decay, weight))
        copies = []
        for head in range(HEADS):
            acc, best, summed, weight = weights[head]
            value = jnp.concatenate([field[:, values[head]] for field in fields], axis=0)
            both = jnp.dot(weight, with_ones(value), preferred_element_type=F32)
            acc = acc + both[:, :HEAD_DIM]
            summed = summed + both[:, HEAD_DIM:]
            earlier[head] = (acc, best, summed)
            results[slot, :, lanes[head]] = (acc / summed).astype(BF16)
            rows = rows_of(meta[slot_at + slot * HEADS + head])
            copies.append(
                pltpu.make_async_copy(
                    results.at[slot, :, lanes[head]], out.at[rows, lanes[head]], sems.at[head]
                )
            )
            copies[-1].start()
        for copy in copies:
            copy.wait()


def body(tokens, qkv_weight, near_offset, far_offset):
    sequence = tokens[0]
    row_count, depth = sequence.shape
    share = qkv_weight.shape[0]
    block_rate = row_count // BLOCK
    seq_size = lax.axis_size("seq")
    seq_index = lax.axis_index("seq")
    pieces = lax.axis_size("fsdp")
    mine = lax.axis_index("fsdp")
    near_size = min(16, seq_size)
    half = near_size // 2
    far_size = max(1, min(16, seq_size // STRIDE))
    near_at = lambda i: near_place(i, half, near_size)
    far_at = lambda i: (i // (STRIDE * far_size) * STRIDE + i % STRIDE, i // STRIDE % far_size)
    reach = max(near_at(i)[1] for i in range(seq_size))
    near_shifts = (1 << reach.bit_length()) - 1
    far_shifts = (1 << (far_size - 1).bit_length()) - 1
    slots = 2 if far_shifts else 1
    shifts = (near_shifts, far_shifts)[:slots]

    near_position = jnp.where(seq_index < half, seq_index, (seq_index - half) % near_size)
    far_position = seq_index // STRIDE % far_size
    far_match = (seq_index % STRIDE == far_offset // block_rate).astype(jnp.int32)
    spans = [(0, share // 4), (share // 2, share // 8)] if seq_size % 4 == 0 else []
    direct_from = spans[-1][0] + 2 * spans[-1][1] if spans else 0
    full_places = [(mine ^ j) * share for j in range(pieces)]
    scalars = list(full_places)
    place_at = len(scalars)
    scalars += [near_position, far_position]
    base_at = len(scalars)
    scalars += [(mine ^ bit) // 2 * 2 * share for bit in range(2, pieces, 2)]
    core_at = len(scalars)
    scalars.append(mine % 2)
    slot_at = len(scalars)
    match_at = slot_at + 2 * HEADS
    offsets_at = match_at + HEADS
    offsets = []
    for core in range(2):
        first = (mine % 2 ^ core) * share
        for number, (start, rows) in enumerate(spans):
            side = seq_index // (1 << number) % 2
            offsets += [first + start + side * rows, first + start + (1 - side) * rows]
        offsets.append(first + direct_from)
    as_array = lambda values: jnp.stack([jnp.asarray(value, jnp.int32) for value in values])
    meta = jnp.concatenate(
        [as_array(scalars), near_offset, far_offset % block_rate, far_match, as_array(offsets)]
    )

    scalar_spec = pl.BlockSpec(memory_space=pltpu.SMEM)
    whole = pl.BlockSpec(memory_space=pltpu.VMEM)
    shape = jax.ShapeDtypeStruct

    def call(kernel, args, results, name, scratch=(), scalars=None, first_out=None):
        return pl.pallas_call(
            kernel,
            in_specs=[scalar_spec] + [whole] * len(args),
            out_specs=[first_out or whole] + [whole] * (len(results) - 1),
            out_shape=results,
            scratch_shapes=list(scratch),
            compiler_params=pltpu.CompilerParams(vmem_limit_bytes=VMEM_LIMIT),
            cost_estimate=pl.CostEstimate(flops=MODEL_FLOPS[name], bytes_accessed=1000, transcendentals=0),
            name=name,
        )(meta if scalars is None else scalars, *args)

    local = [qkv_weight]
    bits = range(2, pieces, 2)
    known = {}
    if pieces > 1:
        local.append(swap(qkv_weight, "fsdp", 1))
        known["core"] = local[-1]
    sides = pl.pallas_call(
        functools.partial(sides_kernel, share),
        out_specs=scalar_spec,
        out_shape=shape((3,), jnp.int32),
        cost_estimate=pl.CostEstimate(flops=MODEL_FLOPS["sides"], bytes_accessed=1000, transcendentals=0),
        name="sides",
    )()
    known["sides"] = sides
    first_cut = [
        lax.dynamic_slice(ordered("first", qkv_weight, known), (start + seq_index % 2 * rows, WIDTH), (rows, 2 * WIDTH))
        for start, rows in spans[:1]
        if bits
    ]
    known |= {"c0": value for value in first_cut}
    rest_spans = [(number, *span) for number, span in enumerate(spans)][1:] if bits else []
    cut_shapes = [shape((rows, 2 * WIDTH), BF16) for _, _, rows in rest_spans]
    if bits:
        cut_shapes += [shape((share - direct_from, 2 * WIDTH), BF16), shape((share, WIDTH), BF16)]
    *cuts, partial = call(
        functools.partial(cut_kernel, rest_spans, direct_from),
        [sequence, ordered("cut", qkv_weight, known)],
        cut_shapes + [shape((row_count, 3 * WIDTH), F32)],
        "cut_rest",
        scalars=sides,
    )
    if pieces > 1:
        (partial,) = call(
            functools.partial(other_kernel, 1),
            [sequence, ordered("o", local[1], known), partial],
            [shape((row_count, 3 * WIDTH), F32)],
            "project_other",
        )
    known["partial"] = partial
    direct_rows, queries = [], []
    for bit in bits:
        mine_rows, other_rows = [], []
        *span_cuts, direct_cut, query_cut = first_cut + cuts
        for number, (start, rows) in enumerate(spans):
            tag = str(number)
            cut = span_cuts[number]
            known["c" + tag] = cut
            direct = swap(cut, "fsdp", bit)
            known["x" + tag] = direct
            across = swap(ordered("f" + tag, direct, known), "fsdp", 1)
            known["f" + tag] = across
            passed = ordered("p" + tag, swap(ordered("y" + tag, direct, known), "seq", 1 << number), known)
            known["y" + tag] = passed
            mine_rows += [direct, passed]
            other_rows += [across, swap(passed, "fsdp", 1)]
            known["q" + tag] = other_rows[-1]
        cut = direct_cut
        known["cD"] = cut
        rest = swap(cut, "fsdp", bit)
        known["xD"] = rest
        rest = ordered("pD", rest, known)
        known["fD"] = swap(rest, "fsdp", 1)
        direct_rows.append(mine_rows + [rest] + other_rows + [known["fD"]])
        cut = query_cut
        known["cQ"] = cut
        queries.append(swap(cut, "fsdp", bit))
    assert len(bits) <= 1
    if bits:
        layout = [offsets_at + i for i in range(len(direct_rows[0]))]
        *packs, joined = call(
            functools.partial(pack_kernel, layout, base_at, slots, slot_at),
            [sequence, partial, *direct_rows[0]],
            [shape((BLOCK, 2 * WIDTH), BF16)] * slots + [shape((2 * share, 2 * WIDTH), BF16)],
            "project_pack",
        )
        known["pack"] = packs[0]
        (kv,) = call(
            functools.partial(kv_kernel, base_at),
            [sequence, ordered("kv", partial, known), joined],
            [shape((row_count, 2 * WIDTH), BF16)],
            "project_kv",
        )
    else:
        kv = partial[:, WIDTH:].astype(BF16)
        blocks = kv.reshape(block_rate, BLOCK, 2, HEADS, HEAD_DIM)
        packs = []
        for offset in (near_offset, far_offset % block_rate)[:slots]:
            picked = blocks[offset, :, :, jnp.arange(HEADS)]
            packs.append(picked.transpose(1, 2, 0, 3).reshape(BLOCK, 2 * WIDTH))
    known["kv"] = kv
    received = []
    for pack, place, count, unit in zip(packs, (near_at, far_at), shifts, (1, STRIDE)):
        for step in NEAR_ORDER if count == len(NEAR_ORDER) else range(1, count + 1):
            received.append((step, lax.ppermute(pack, "seq", partners(seq_size, place, step))))
        known |= {f"n{step}": r for step, r in received}
    steps = [step for step, _ in received]
    received = [pack for _, pack in received]
    crossed_q, q_places = [], []
    for bit, direct in zip(bits, queries):
        direct = ordered("q", direct, known)
        (slots_out,) = call(
            functools.partial(slot_kernel, core_at), [direct], [shape((2,) + direct.shape, BF16)], "slot_queries"
        )
        both = lax.all_to_all(
            slots_out, "fsdp", 0, 0, axis_index_groups=[[i, i + 1] for i in range(0, pieces, 2)]
        )
        crossed_q += [direct, both]
        q_places += [bit, bit ^ 1]
    state_types = [BF16, F32, F32, F32]
    partial_out, *state = call(
        functools.partial(attend_kernel, q_places, core_at, slots, slot_at, match_at),
        [sequence, partial, *crossed_q, kv],
        [shape((row_count, WIDTH), BF16)] + [shape((BLOCK, WIDTH), kind) for kind in state_types] * slots,
        "attend_local",
        [pltpu.VMEM((row_count, WIDTH), kind) for kind in state_types]
        + [pltpu.VMEM((row_count, WIDTH), BF16), pltpu.SemaphoreType.DMA((HEADS,))],
        first_out=pl.BlockSpec(memory_space=pl.ANY),
    )
    count = 4 * slots + sum(shifts)
    merged = pl.pallas_call(
        functools.partial(merge_kernel, shifts, steps, slot_at, match_at, place_at),
        in_specs=[scalar_spec] + [whole] * count + [pl.BlockSpec(memory_space=pl.ANY)],
        out_specs=pl.BlockSpec(memory_space=pl.ANY),
        out_shape=shape((row_count, WIDTH), BF16),
        scratch_shapes=[pltpu.VMEM((slots, BLOCK, WIDTH), BF16), pltpu.SemaphoreType.DMA((HEADS,))],
        input_output_aliases={count + 1: 0},
        compiler_params=pltpu.CompilerParams(vmem_limit_bytes=VMEM_LIMIT),
        cost_estimate=pl.CostEstimate(flops=MODEL_FLOPS["merge_near"], bytes_accessed=1000, transcendentals=0),
        name="merge_near",
    )(meta, *state, *received, partial_out)
    return merged[None]


def solution(mesh):
    in_specs = (P("fsdp", "seq", None), P("fsdp", None), P(), P())
    out_specs = P("fsdp", "seq", None)
    return jax.shard_map(body, mesh=mesh, in_specs=in_specs, out_specs=out_specs, check_vma=False)
```

```python
import functools
import math

import jax
import jax.numpy as jnp
from jax import lax
from jax.experimental import pallas as pl
from jax.experimental.pallas import tpu as pltpu
from jax.sharding import PartitionSpec as P

HEADS = 4
HEAD_DIM = 128
BLOCK = 128
STRIDE = 8
WIDTH = HEADS * HEAD_DIM
PAIR = 2 * HEAD_DIM
NEG = -1e30
SCALE2 = HEAD_DIM ** (-0.5) * math.log2(math.e)
VMEM_LIMIT = 24 * 1024 * 1024

MODEL_FLOPS = {"slot_queries": 575000, "project_pack": 689999, "project_own": 3680000, "project_mid": 1610000, "project_kv": 2990000, "attend_local": 6325000, "merge_near": 2990000}
ORDER = {
    'c1': ('c0',),
    'cD': ('c1',),
    'cQ': ('cD',),
    'p0': ('partial', 'xD'),
    'p1': ('partial',),
    'q': ('kv',),
    'kv': ('pack',),
}
NEAR_ORDER = (3, 2, 1)
F32 = jnp.float32
BF16 = jnp.bfloat16


def near_place(index, half, size):
    if index < half:
        return 0, index
    return 1 + (index - half) // size, (index - half) % size


def partners(count, place, bits):
    where = {place(i): i for i in range(count)}
    pairs = []
    for source in range(count):
        run, spot = place(source)
        if (run, spot ^ bits) in where:
            pairs.append((source, where[run, spot ^ bits]))
    return pairs


def swap(value, axis, bit):
    count = lax.axis_size(axis)
    return lax.ppermute(value, axis, [(i, i ^ bit) for i in range(count)])


def after(value, *others):
    return lax.optimization_barrier((value,) + others)[0]


def ordered(name, value, known):
    others = [known[other] for other in ORDER.get(name, ()) if other in known]
    return after(value, *others) if others else value


def rows_of(block):
    return pl.ds(pl.multiple_of(block * BLOCK, BLOCK), BLOCK)


def qk(query, key):
    return lax.dot_general(query, key, (((1,), (1,)), ((), ())), preferred_element_type=F32)


def pv(weights, value):
    return jnp.dot(weights.astype(BF16), value, preferred_element_type=F32)


def add_up(tokens, places, weights):
    total = None
    for place, weight in zip(places, weights):
        depth = weight.shape[0]
        columns = pl.ds(pl.multiple_of(place, depth), depth)
        term = jnp.dot(tokens[:, columns], weight[...], preferred_element_type=F32)
        total = term if total is None else total + term
    return total


def own_kernel(count, meta, tokens, *refs):
    weights, out = refs[:count], refs[count]
    for j in range(out.shape[1] // PAIR):
        lanes = slice(j * PAIR, (j + 1) * PAIR)
        out[:, lanes] = add_up(tokens, [meta[at] for at in range(count)], [weight.at[:, lanes] for weight in weights])


def pack_kernel(layout, base_at, slots, slot_at, meta, tokens, partial, *refs):
    arrived, packs, joined = refs[: len(layout)], refs[len(layout) : -1], refs[-1]
    for at, array in zip(layout, arrived):
        rows = array.shape[0]
        joined[pl.ds(pl.multiple_of(meta[at], rows), rows), :] = array[...]
    columns = pl.ds(pl.multiple_of(meta[base_at], joined.shape[0]), joined.shape[0])
    for slot in range(slots):
        for head in range(HEADS):
            rows = rows_of(meta[slot_at + HEADS * slot + head])
            lanes = [slice(start, start + HEAD_DIM) for start in (head * HEAD_DIM, WIDTH + head * HEAD_DIM)]
            weight = jnp.concatenate([joined[:, part] for part in lanes], axis=1)
            product = jnp.dot(tokens[rows, columns], weight, preferred_element_type=F32)
            for field, part in enumerate(lanes):
                own = partial[rows, WIDTH + part.start : WIDTH + part.stop]
                total = own + product[:, field * HEAD_DIM : (field + 1) * HEAD_DIM]
                packs[slot][:, part] = total.astype(BF16)


def slot_kernel(core_at, meta, source, out):
    out[1 - meta[core_at]] = source[...]


def kv_kernel(base_at, meta, tokens, partial, joined, kv):
    columns = pl.ds(pl.multiple_of(meta[base_at], joined.shape[0]), joined.shape[0])
    for j in range(2 * WIDTH // PAIR):
        lanes = slice(j * PAIR, (j + 1) * PAIR)
        product = jnp.dot(tokens[:, columns], joined[:, lanes], preferred_element_type=F32)
        kv[:, lanes] = (partial[:, WIDTH + j * PAIR : WIDTH + (j + 1) * PAIR] + product).astype(BF16)


def with_ones(value):
    return jnp.concatenate([value, jnp.ones(value.shape, BF16)], axis=1)


def attend_kernel(bases_at, core_at, slots, slot_at, match_at, meta, tokens, partial, *refs):
    weights, refs = refs[: len(bases_at)], refs[len(bases_at) :]
    kv, out, refs = refs[0], refs[1], refs[2:]
    state, scratch = refs[: 4 * slots], refs[4 * slots :]
    query, acc_all, top_all, sum_all = scratch
    blocks = query.shape[0] // BLOCK
    GROUP = 2 if blocks % 2 == 0 else 1
    row = lax.broadcasted_iota(jnp.int32, (BLOCK, BLOCK), 0)
    column = lax.broadcasted_iota(jnp.int32, (BLOCK, BLOCK), 1)
    causal = column <= row
    places = [meta[at] for at in bases_at]
    other = 1 - meta[core_at]
    for pair in range(HEADS // 2):
        lanes = slice(pair * PAIR, (pair + 1) * PAIR)
        total = partial[:, lanes]
        if weights:
            parts = [weights[0].at[:, lanes], weights[1].at[other, :, lanes]]
            total = total + add_up(tokens, places, parts)
        query[:, lanes] = total.astype(BF16)

    def lanes_of(head):
        return slice(head * HEAD_DIM, (head + 1) * HEAD_DIM)

    def rows_at(b):
        return slice(b * BLOCK, (b + 1) * BLOCK)

    def score(head, group):
        first, last = group * GROUP, (group + 1) * GROUP
        rows = slice(first * BLOCK, last * BLOCK)
        return qk(query[rows, lanes_of(head)], kv[: last * BLOCK, lanes_of(head)])

    def weigh(head, group, scores):
        near_block = meta[slot_at + head]
        far_block = meta[slot_at + HEADS + head]
        tops, weights = [], []
        for i in range(GROUP):
            b = group * GROUP + i
            mine = scores[rows_at(i)]
            times = (
                1
                + jnp.where(near_block == b, 1, 0)
                + jnp.where(far_block == b, meta[match_at + head], 0)
            ).astype(F32)
            diagonal = jnp.where(causal, mine[:, rows_at(b)], NEG)
            top = jnp.max(diagonal, axis=1, keepdims=True)
            if b:
                top = jnp.maximum(top, jnp.max(mine[:, : b * BLOCK], axis=1, keepdims=True))
            parts = [(jnp.exp2((diagonal - top) * SCALE2) * times).astype(BF16)]
            if b:
                parts.insert(0, jnp.exp2((mine[:, : b * BLOCK] - top) * SCALE2).astype(BF16))
            if i < GROUP - 1:
                parts.append(jnp.zeros((BLOCK, (GROUP - 1 - i) * BLOCK), BF16))
            tops.append(top)
            weights.append(jnp.concatenate(parts, axis=1))
        return tops, jnp.concatenate(weights, axis=0)

    def finish(head, group, tops, weight):
        lanes = lanes_of(head)
        keys = (group + 1) * GROUP * BLOCK
        value = kv[:keys, WIDTH + head * HEAD_DIM : WIDTH + (head + 1) * HEAD_DIM]
        both = jnp.dot(weight, with_ones(value), preferred_element_type=F32)
        rows = slice(group * GROUP * BLOCK, keys)
        acc, summed = both[:, :HEAD_DIM], both[:, HEAD_DIM:]
        out[rows, lanes] = (acc / summed).astype(BF16)
        acc_all[rows, lanes] = acc
        sum_all[rows, lanes] = summed
        for i, top in enumerate(tops):
            top_all[rows_at(group * GROUP + i), lanes] = jnp.broadcast_to(top, (BLOCK, HEAD_DIM))
        if group == blocks // GROUP - 1:
            for slot in range(slots):
                rows = rows_of(meta[slot_at + slot * HEADS + head])
                for target, source in zip(state[4 * slot :], scratch):
                    target[:, lanes] = source[rows, lanes]

    tasks = [(head, group) for head in range(HEADS) for group in range(blocks // GROUP)]
    scored, weighed = {}, {}
    for step in range(len(tasks) + 2):
        if step < len(tasks):
            scored[step] = score(*tasks[step])
        if 0 <= step - 1 < len(tasks):
            weighed[step - 1] = weigh(*tasks[step - 1], scored.pop(step - 1))
        if 0 <= step - 2 < len(tasks):
            finish(*tasks[step - 2], *weighed.pop(step - 2))


def merge_kernel(shifts, steps, slot_at, match_at, place_at, meta, *refs):
    slots = len(shifts)
    state = refs[: 4 * slots]
    packs = refs[4 * slots : 4 * slots + sum(shifts)]
    out, results, sems = refs[4 * slots + sum(shifts) + 1 :]
    lanes = [slice(head * HEAD_DIM, (head + 1) * HEAD_DIM) for head in range(HEADS)]
    values = [slice(WIDTH + head * HEAD_DIM, WIDTH + (head + 1) * HEAD_DIM) for head in range(HEADS)]
    earlier = [None] * HEADS
    for slot, count in enumerate(shifts):
        fields = packs[sum(shifts[:slot]) : sum(shifts[: slot + 1])]
        query, acc_ref, top_ref, sum_ref = state[4 * slot : 4 * slot + 4]
        place = meta[place_at + slot]
        scores, weights = [], []
        for head in range(HEADS):
            keys = jnp.concatenate([field[:, lanes[head]] for field in fields], axis=0)
            score = qk(query[:, lanes[head]], keys)
            parts = []
            for number, step in enumerate(steps[sum(shifts[:slot]) : sum(shifts[: slot + 1])]):
                seen = place ^ step < place
                if slot:
                    seen = seen & (meta[match_at + head] == 1)
                part = score[:, number * BLOCK : (number + 1) * BLOCK]
                parts.append(jnp.where(seen, part, NEG))
            scores.append(jnp.concatenate(parts, axis=1))
        for head in range(HEADS):
            acc, top, summed = (ref[:, lanes[head]] for ref in (acc_ref, top_ref, sum_ref))
            if slot:
                same = meta[slot_at + head] == meta[slot_at + HEADS + head]
                acc, top, summed = (
                    jnp.where(same, new, old) for new, old in zip(earlier[head], (acc, top, summed))
                )
            best = jnp.maximum(top, jnp.max(scores[head], axis=1, keepdims=True))
            decay = jnp.exp2((top - best) * SCALE2)
            weight = jnp.exp2((scores[head] - best[:, :1]) * SCALE2).astype(BF16)
            weights.append((acc * decay, best, summed * decay, weight))
        copies = []
        for head in range(HEADS):
            acc, best, summed, weight = weights[head]
            value = jnp.concatenate([field[:, values[head]] for field in fields], axis=0)
            both = jnp.dot(weight, with_ones(value), preferred_element_type=F32)
            acc = acc + both[:, :HEAD_DIM]
            summed = summed + both[:, HEAD_DIM:]
            earlier[head] = (acc, best, summed)
            results[slot, :, lanes[head]] = (acc / summed).astype(BF16)
            rows = rows_of(meta[slot_at + slot * HEADS + head])
            copies.append(
                pltpu.make_async_copy(
                    results.at[slot, :, lanes[head]], out.at[rows, lanes[head]], sems.at[head]
                )
            )
            copies[-1].start()
        for copy in copies:
            copy.wait()


def body(tokens, qkv_weight, near_offset, far_offset):
    sequence = tokens[0]
    row_count, depth = sequence.shape
    share = qkv_weight.shape[0]
    block_rate = row_count // BLOCK
    seq_size = lax.axis_size("seq")
    seq_index = lax.axis_index("seq")
    pieces = lax.axis_size("fsdp")
    mine = lax.axis_index("fsdp")
    near_size = min(16, seq_size)
    half = near_size // 2
    far_size = max(1, min(16, seq_size // STRIDE))
    near_at = lambda i: near_place(i, half, near_size)
    far_at = lambda i: (i // (STRIDE * far_size) * STRIDE + i % STRIDE, i // STRIDE % far_size)
    reach = max(near_at(i)[1] for i in range(seq_size))
    near_shifts = (1 << reach.bit_length()) - 1
    far_shifts = (1 << (far_size - 1).bit_length()) - 1
    slots = 2 if far_shifts else 1
    shifts = (near_shifts, far_shifts)[:slots]

    near_position = jnp.where(seq_index < half, seq_index, (seq_index - half) % near_size)
    far_position = seq_index // STRIDE % far_size
    far_match = (seq_index % STRIDE == far_offset // block_rate).astype(jnp.int32)
    spans = [(0, share // 4), (share // 2, share // 8)] if seq_size % 4 == 0 else []
    direct_from = spans[-1][0] + 2 * spans[-1][1] if spans else 0
    full_places = [(mine ^ j) * share for j in range(pieces)]
    scalars = list(full_places)
    place_at = len(scalars)
    scalars += [near_position, far_position]
    base_at = len(scalars)
    scalars += [(mine ^ bit) // 2 * 2 * share for bit in range(2, pieces, 2)]
    core_at = len(scalars)
    scalars.append(mine % 2)
    slot_at = len(scalars)
    match_at = slot_at + 2 * HEADS
    offsets_at = match_at + HEADS
    offsets = []
    for core in range(2):
        first = (mine % 2 ^ core) * share
        for number, (start, rows) in enumerate(spans):
            side = seq_index // (1 << number) % 2
            offsets += [first + start + side * rows, first + start + (1 - side) * rows]
        offsets.append(first + direct_from)
    as_array = lambda values: jnp.stack([jnp.asarray(value, jnp.int32) for value in values])
    meta = jnp.concatenate(
        [as_array(scalars), near_offset, far_offset % block_rate, far_match, as_array(offsets)]
    )

    scalar_spec = pl.BlockSpec(memory_space=pltpu.SMEM)
    whole = pl.BlockSpec(memory_space=pltpu.VMEM)
    shape = jax.ShapeDtypeStruct

    def call(kernel, args, results, name, scratch=()):
        return pl.pallas_call(
            kernel,
            in_specs=[scalar_spec] + [whole] * len(args),
            out_specs=[whole] * len(results),
            out_shape=results,
            scratch_shapes=list(scratch),
            compiler_params=pltpu.CompilerParams(vmem_limit_bytes=VMEM_LIMIT),
            cost_estimate=pl.CostEstimate(flops=MODEL_FLOPS[name], bytes_accessed=1000, transcendentals=0),
            name=name,
        )(meta, *args)

    local = [qkv_weight]
    bits = range(2, pieces, 2)
    known = {}
    if pieces > 1:
        local.append(swap(qkv_weight, "fsdp", 1))
        known["core"] = local[-1]
    (partial,) = call(
        functools.partial(own_kernel, len(local)),
        [ordered("t", sequence, known), *local],
        [shape((row_count, 3 * WIDTH), F32)],
        "project_own",
    )
    known["partial"] = partial
    direct_rows, queries = [], []
    for bit in bits:
        mine_rows, other_rows = [], []
        for number, (start, rows) in enumerate(spans):
            tag = str(number)
            side = seq_index // (1 << number) % 2
            cut = lax.dynamic_slice(
                ordered("c" + tag, qkv_weight, known), (start + side * rows, WIDTH), (rows, 2 * WIDTH)
            )
            known["c" + tag] = cut
            direct = swap(cut, "fsdp", bit)
            known["x" + tag] = direct
            across = swap(ordered("f" + tag, direct, known), "fsdp", 1)
            known["f" + tag] = across
            passed = ordered("p" + tag, swap(ordered("y" + tag, direct, known), "seq", 1 << number), known)
            known["y" + tag] = passed
            mine_rows += [direct, passed]
            other_rows += [across, swap(passed, "fsdp", 1)]
            known["q" + tag] = other_rows[-1]
        known["meta"] = meta
        cut = ordered("cD", qkv_weight, known)[direct_from:, WIDTH:]
        known["cD"] = cut
        rest = swap(cut, "fsdp", bit)
        known["xD"] = rest
        rest = ordered("pD", rest, known)
        known["fD"] = swap(rest, "fsdp", 1)
        direct_rows.append(mine_rows + [rest] + other_rows + [known["fD"]])
        cut = ordered("cQ", qkv_weight, known)[:, :WIDTH]
        known["cQ"] = cut
        queries.append(swap(cut, "fsdp", bit))
    assert len(bits) <= 1
    if bits:
        layout = [offsets_at + i for i in range(len(direct_rows[0]))]
        *packs, joined = call(
            functools.partial(pack_kernel, layout, base_at, slots, slot_at),
            [sequence, partial, *direct_rows[0]],
            [shape((BLOCK, 2 * WIDTH), BF16)] * slots + [shape((2 * share, 2 * WIDTH), BF16)],
            "project_pack",
        )
        known["pack"] = packs[0]
        (kv,) = call(
            functools.partial(kv_kernel, base_at),
            [sequence, ordered("kv", partial, known), joined],
            [shape((row_count, 2 * WIDTH), BF16)],
            "project_kv",
        )
    else:
        kv = partial[:, WIDTH:].astype(BF16)
        blocks = kv.reshape(block_rate, BLOCK, 2, HEADS, HEAD_DIM)
        packs = []
        for offset in (near_offset, far_offset % block_rate)[:slots]:
            picked = blocks[offset, :, :, jnp.arange(HEADS)]
            packs.append(picked.transpose(1, 2, 0, 3).reshape(BLOCK, 2 * WIDTH))
    known["kv"] = kv
    received = []
    for pack, place, count, unit in zip(packs, (near_at, far_at), shifts, (1, STRIDE)):
        for step in NEAR_ORDER if count == len(NEAR_ORDER) else range(1, count + 1):
            received.append((step, lax.ppermute(pack, "seq", partners(seq_size, place, step))))
        known |= {f"n{step}": r for step, r in received}
    steps = [step for step, _ in received]
    received = [pack for _, pack in received]
    crossed_q, q_places = [], []
    for bit, direct in zip(bits, queries):
        direct = ordered("q", direct, known)
        (slots_out,) = call(
            functools.partial(slot_kernel, core_at), [direct], [shape((2,) + direct.shape, BF16)], "slot_queries"
        )
        both = lax.all_to_all(
            slots_out, "fsdp", 0, 0, axis_index_groups=[[i, i + 1] for i in range(0, pieces, 2)]
        )
        crossed_q += [direct, both]
        q_places += [bit, bit ^ 1]
    state_types = [BF16, F32, F32, F32]
    partial_out, *state = call(
        functools.partial(attend_kernel, q_places, core_at, slots, slot_at, match_at),
        [sequence, partial, *crossed_q, kv],
        [shape((row_count, WIDTH), BF16)] + [shape((BLOCK, WIDTH), kind) for kind in state_types] * slots,
        "attend_local",
        [pltpu.VMEM((row_count, WIDTH), kind) for kind in state_types],
    )
    count = 4 * slots + sum(shifts)
    merged = pl.pallas_call(
        functools.partial(merge_kernel, shifts, steps, slot_at, match_at, place_at),
        in_specs=[scalar_spec] + [whole] * count + [pl.BlockSpec(memory_space=pl.ANY)],
        out_specs=pl.BlockSpec(memory_space=pl.ANY),
        out_shape=shape((row_count, WIDTH), BF16),
        scratch_shapes=[pltpu.VMEM((slots, BLOCK, WIDTH), BF16), pltpu.SemaphoreType.DMA((HEADS,))],
        input_output_aliases={count + 1: 0},
        compiler_params=pltpu.CompilerParams(vmem_limit_bytes=VMEM_LIMIT),
        cost_estimate=pl.CostEstimate(flops=MODEL_FLOPS["merge_near"], bytes_accessed=1000, transcendentals=0),
        name="merge_near",
    )(meta, *state, *received, partial_out)
    return merged[None]


def solution(mesh):
    in_specs = (P("fsdp", "seq", None), P("fsdp", None), P(), P())
    out_specs = P("fsdp", "seq", None)
    return jax.shard_map(body, mesh=mesh, in_specs=in_specs, out_specs=out_specs, check_vma=False)
```

```python
import functools
import math

import jax
import jax.numpy as jnp
from jax import lax
from jax.experimental import pallas as pl
from jax.experimental.pallas import tpu as pltpu
from jax.sharding import PartitionSpec as P

HEADS = 4
HEAD_DIM = 128
BLOCK = 128
STRIDE = 8
WIDTH = HEADS * HEAD_DIM
PAIR = 2 * HEAD_DIM
NEG = -1e30
SCALE2 = HEAD_DIM ** (-0.5) * math.log2(math.e)
VMEM_LIMIT = 24 * 1024 * 1024

MODEL_FLOPS = {"slot_queries": 575000, "project_pack": 689999, "project_own": 3680000, "project_mid": 1610000, "project_kv": 2990000, "attend_local": 6325000, "merge_near": 2990000}
ORDER = {
    'c1': ('c0',),
    'cD': ('c1',),
    'cQ': ('cD',),
    'p0': ('partial', 'xD'),
    'p1': ('partial',),
    'q': ('kv',),
    'kv': ('pack',),
}
NEAR_ORDER = (3, 2, 1)
F32 = jnp.float32
BF16 = jnp.bfloat16


def near_place(index, half, size):
    if index < half:
        return 0, index
    return 1 + (index - half) // size, (index - half) % size


def partners(count, place, bits):
    where = {place(i): i for i in range(count)}
    pairs = []
    for source in range(count):
        run, spot = place(source)
        if (run, spot ^ bits) in where:
            pairs.append((source, where[run, spot ^ bits]))
    return pairs


def swap(value, axis, bit):
    count = lax.axis_size(axis)
    return lax.ppermute(value, axis, [(i, i ^ bit) for i in range(count)])


def after(value, *others):
    return lax.optimization_barrier((value,) + others)[0]


def ordered(name, value, known):
    others = [known[other] for other in ORDER.get(name, ()) if other in known]
    return after(value, *others) if others else value


def rows_of(block):
    return pl.ds(pl.multiple_of(block * BLOCK, BLOCK), BLOCK)


def qk(query, key):
    return lax.dot_general(query, key, (((1,), (1,)), ((), ())), preferred_element_type=F32)


def pv(weights, value):
    return jnp.dot(weights.astype(BF16), value, preferred_element_type=F32)


def add_up(tokens, places, weights):
    total = None
    for place, weight in zip(places, weights):
        depth = weight.shape[0]
        columns = pl.ds(pl.multiple_of(place, depth), depth)
        term = jnp.dot(tokens[:, columns], weight[...], preferred_element_type=F32)
        total = term if total is None else total + term
    return total


def own_kernel(count, meta, tokens, *refs):
    weights, out = refs[:count], refs[count]
    for j in range(out.shape[1] // PAIR):
        lanes = slice(j * PAIR, (j + 1) * PAIR)
        out[:, lanes] = add_up(tokens, [meta[at] for at in range(count)], [weight.at[:, lanes] for weight in weights])


def pack_kernel(layout, base_at, slots, slot_at, meta, tokens, partial, *refs):
    arrived, packs, joined = refs[: len(layout)], refs[len(layout) : -1], refs[-1]
    for at, array in zip(layout, arrived):
        rows = array.shape[0]
        joined[pl.ds(pl.multiple_of(meta[at], rows), rows), :] = array[...]
    columns = pl.ds(pl.multiple_of(meta[base_at], joined.shape[0]), joined.shape[0])
    for slot in range(slots):
        for head in range(HEADS):
            rows = rows_of(meta[slot_at + HEADS * slot + head])
            lanes = [slice(start, start + HEAD_DIM) for start in (head * HEAD_DIM, WIDTH + head * HEAD_DIM)]
            weight = jnp.concatenate([joined[:, part] for part in lanes], axis=1)
            product = jnp.dot(tokens[rows, columns], weight, preferred_element_type=F32)
            for field, part in enumerate(lanes):
                own = partial[rows, WIDTH + part.start : WIDTH + part.stop]
                total = own + product[:, field * HEAD_DIM : (field + 1) * HEAD_DIM]
                packs[slot][:, part] = total.astype(BF16)


def slot_kernel(core_at, meta, source, out):
    out[1 - meta[core_at]] = source[...]


def kv_kernel(base_at, meta, tokens, partial, joined, kv):
    columns = pl.ds(pl.multiple_of(meta[base_at], joined.shape[0]), joined.shape[0])
    for j in range(2 * WIDTH // PAIR):
        lanes = slice(j * PAIR, (j + 1) * PAIR)
        product = jnp.dot(tokens[:, columns], joined[:, lanes], preferred_element_type=F32)
        kv[:, lanes] = (partial[:, WIDTH + j * PAIR : WIDTH + (j + 1) * PAIR] + product).astype(BF16)


def with_ones(value):
    return jnp.concatenate([value, jnp.ones(value.shape, BF16)], axis=1)


def attend_kernel(bases_at, core_at, slots, slot_at, match_at, meta, tokens, partial, *refs):
    weights, refs = refs[: len(bases_at)], refs[len(bases_at) :]
    kv, out, refs = refs[0], refs[1], refs[2:]
    state, scratch = refs[: 4 * slots], refs[4 * slots :]
    query, acc_all, top_all, sum_all = scratch
    blocks = query.shape[0] // BLOCK
    GROUP = 2 if blocks % 2 == 0 else 1
    row = lax.broadcasted_iota(jnp.int32, (BLOCK, BLOCK), 0)
    column = lax.broadcasted_iota(jnp.int32, (BLOCK, BLOCK), 1)
    causal = column <= row
    places = [meta[at] for at in bases_at]
    other = 1 - meta[core_at]
    for pair in range(HEADS // 2):
        lanes = slice(pair * PAIR, (pair + 1) * PAIR)
        total = partial[:, lanes]
        if weights:
            parts = [weights[0].at[:, lanes], weights[1].at[other, :, lanes]]
            total = total + add_up(tokens, places, parts)
        query[:, lanes] = total.astype(BF16)

    def lanes_of(head):
        return slice(head * HEAD_DIM, (head + 1) * HEAD_DIM)

    def rows_at(b):
        return slice(b * BLOCK, (b + 1) * BLOCK)

    def score(head, group):
        first, last = group * GROUP, (group + 1) * GROUP
        rows = slice(first * BLOCK, last * BLOCK)
        return qk(query[rows, lanes_of(head)], kv[: last * BLOCK, lanes_of(head)])

    def weigh(head, group, scores):
        near_block = meta[slot_at + head]
        far_block = meta[slot_at + HEADS + head]
        tops, weights = [], []
        for i in range(GROUP):
            b = group * GROUP + i
            mine = scores[rows_at(i)]
            times = (
                1
                + jnp.where(near_block == b, 1, 0)
                + jnp.where(far_block == b, meta[match_at + head], 0)
            ).astype(F32)
            diagonal = jnp.where(causal, mine[:, rows_at(b)], NEG)
            top = jnp.max(diagonal, axis=1, keepdims=True)
            if b:
                top = jnp.maximum(top, jnp.max(mine[:, : b * BLOCK], axis=1, keepdims=True))
            parts = [(jnp.exp2((diagonal - top) * SCALE2) * times).astype(BF16)]
            if b:
                parts.insert(0, jnp.exp2((mine[:, : b * BLOCK] - top) * SCALE2).astype(BF16))
            if i < GROUP - 1:
                parts.append(jnp.zeros((BLOCK, (GROUP - 1 - i) * BLOCK), BF16))
            tops.append(top)
            weights.append(jnp.concatenate(parts, axis=1))
        return tops, jnp.concatenate(weights, axis=0)

    def finish(head, group, tops, weight):
        lanes = lanes_of(head)
        keys = (group + 1) * GROUP * BLOCK
        value = kv[:keys, WIDTH + head * HEAD_DIM : WIDTH + (head + 1) * HEAD_DIM]
        both = jnp.dot(weight, with_ones(value), preferred_element_type=F32)
        rows = slice(group * GROUP * BLOCK, keys)
        acc, summed = both[:, :HEAD_DIM], both[:, HEAD_DIM:]
        out[rows, lanes] = (acc / summed).astype(BF16)
        acc_all[rows, lanes] = acc
        sum_all[rows, lanes] = summed
        for i, top in enumerate(tops):
            top_all[rows_at(group * GROUP + i), lanes] = jnp.broadcast_to(top, (BLOCK, HEAD_DIM))
        if group == blocks // GROUP - 1:
            for slot in range(slots):
                rows = rows_of(meta[slot_at + slot * HEADS + head])
                for target, source in zip(state[4 * slot :], scratch):
                    target[:, lanes] = source[rows, lanes]

    tasks = [(head, group) for head in range(HEADS) for group in range(blocks // GROUP)]
    scored, weighed = {}, {}
    for step in range(len(tasks) + 2):
        if step < len(tasks):
            scored[step] = score(*tasks[step])
        if 0 <= step - 1 < len(tasks):
            weighed[step - 1] = weigh(*tasks[step - 1], scored.pop(step - 1))
        if 0 <= step - 2 < len(tasks):
            finish(*tasks[step - 2], *weighed.pop(step - 2))


def merge_kernel(shifts, steps, slot_at, match_at, place_at, meta, *refs):
    slots = len(shifts)
    state = refs[: 4 * slots]
    packs = refs[4 * slots : 4 * slots + sum(shifts)]
    out, results, sems = refs[4 * slots + sum(shifts) + 1 :]
    if slots == 1:
        pl.when(meta[place_at] > 0)(lambda: merge_slots(
            shifts, steps, slot_at, match_at, place_at, meta, state, packs, out, results, sems
        ))
    else:
        merge_slots(shifts, steps, slot_at, match_at, place_at, meta, state, packs, out, results, sems)


def merge_slots(shifts, steps, slot_at, match_at, place_at, meta, state, packs, out, results, sems):
    lanes = [slice(head * HEAD_DIM, (head + 1) * HEAD_DIM) for head in range(HEADS)]
    values = [slice(WIDTH + head * HEAD_DIM, WIDTH + (head + 1) * HEAD_DIM) for head in range(HEADS)]
    earlier = [None] * HEADS
    for slot, count in enumerate(shifts):
        fields = packs[sum(shifts[:slot]) : sum(shifts[: slot + 1])]
        query, acc_ref, top_ref, sum_ref = state[4 * slot : 4 * slot + 4]
        place = meta[place_at + slot]
        scores, weights = [], []
        for head in range(HEADS):
            keys = jnp.concatenate([field[:, lanes[head]] for field in fields], axis=0)
            score = qk(query[:, lanes[head]], keys)
            parts = []
            for number, step in enumerate(steps[sum(shifts[:slot]) : sum(shifts[: slot + 1])]):
                seen = place ^ step < place
                if slot:
                    seen = seen & (meta[match_at + head] == 1)
                part = score[:, number * BLOCK : (number + 1) * BLOCK]
                parts.append(jnp.where(seen, part, NEG))
            scores.append(jnp.concatenate(parts, axis=1))
        for head in range(HEADS):
            acc, top, summed = (ref[:, lanes[head]] for ref in (acc_ref, top_ref, sum_ref))
            if slot:
                same = meta[slot_at + head] == meta[slot_at + HEADS + head]
                acc, top, summed = (
                    jnp.where(same, new, old) for new, old in zip(earlier[head], (acc, top, summed))
                )
            best = jnp.maximum(top, jnp.max(scores[head], axis=1, keepdims=True))
            decay = jnp.exp2((top - best) * SCALE2)
            weight = jnp.exp2((scores[head] - best[:, :1]) * SCALE2).astype(BF16)
            weights.append((acc * decay, best, summed * decay, weight))
        copies = []
        for head in range(HEADS):
            acc, best, summed, weight = weights[head]
            value = jnp.concatenate([field[:, values[head]] for field in fields], axis=0)
            both = jnp.dot(weight, with_ones(value), preferred_element_type=F32)
            acc = acc + both[:, :HEAD_DIM]
            summed = summed + both[:, HEAD_DIM:]
            earlier[head] = (acc, best, summed)
            results[slot, :, lanes[head]] = (acc / summed).astype(BF16)
            rows = rows_of(meta[slot_at + slot * HEADS + head])
            copies.append(
                pltpu.make_async_copy(
                    results.at[slot, :, lanes[head]], out.at[rows, lanes[head]], sems.at[head]
                )
            )
            copies[-1].start()
        for copy in copies:
            copy.wait()


def body(tokens, qkv_weight, near_offset, far_offset):
    sequence = tokens[0]
    row_count, depth = sequence.shape
    share = qkv_weight.shape[0]
    block_rate = row_count // BLOCK
    seq_size = lax.axis_size("seq")
    seq_index = lax.axis_index("seq")
    pieces = lax.axis_size("fsdp")
    mine = lax.axis_index("fsdp")
    near_size = min(16, seq_size)
    half = near_size // 2
    far_size = max(1, min(16, seq_size // STRIDE))
    near_at = lambda i: near_place(i, half, near_size)
    far_at = lambda i: (i // (STRIDE * far_size) * STRIDE + i % STRIDE, i // STRIDE % far_size)
    reach = max(near_at(i)[1] for i in range(seq_size))
    near_shifts = (1 << reach.bit_length()) - 1
    far_shifts = (1 << (far_size - 1).bit_length()) - 1
    slots = 2 if far_shifts else 1
    shifts = (near_shifts, far_shifts)[:slots]

    near_position = jnp.where(seq_index < half, seq_index, (seq_index - half) % near_size)
    far_position = seq_index // STRIDE % far_size
    far_match = (seq_index % STRIDE == far_offset // block_rate).astype(jnp.int32)
    spans = [(0, share // 4), (share // 2, share // 8)] if seq_size % 4 == 0 else []
    direct_from = spans[-1][0] + 2 * spans[-1][1] if spans else 0
    full_places = [(mine ^ j) * share for j in range(pieces)]
    scalars = list(full_places)
    place_at = len(scalars)
    scalars += [near_position, far_position]
    base_at = len(scalars)
    scalars += [(mine ^ bit) // 2 * 2 * share for bit in range(2, pieces, 2)]
    core_at = len(scalars)
    scalars.append(mine % 2)
    slot_at = len(scalars)
    match_at = slot_at + 2 * HEADS
    offsets_at = match_at + HEADS
    offsets = []
    for core in range(2):
        first = (mine % 2 ^ core) * share
        for number, (start, rows) in enumerate(spans):
            side = seq_index // (1 << number) % 2
            offsets += [first + start + side * rows, first + start + (1 - side) * rows]
        offsets.append(first + direct_from)
    as_array = lambda values: jnp.stack([jnp.asarray(value, jnp.int32) for value in values])
    meta = jnp.concatenate(
        [as_array(scalars), near_offset, far_offset % block_rate, far_match, as_array(offsets)]
    )

    scalar_spec = pl.BlockSpec(memory_space=pltpu.SMEM)
    whole = pl.BlockSpec(memory_space=pltpu.VMEM)
    shape = jax.ShapeDtypeStruct

    def call(kernel, args, results, name, scratch=()):
        return pl.pallas_call(
            kernel,
            in_specs=[scalar_spec] + [whole] * len(args),
            out_specs=[whole] * len(results),
            out_shape=results,
            scratch_shapes=list(scratch),
            compiler_params=pltpu.CompilerParams(vmem_limit_bytes=VMEM_LIMIT),
            cost_estimate=pl.CostEstimate(flops=MODEL_FLOPS[name], bytes_accessed=1000, transcendentals=0),
            name=name,
        )(meta, *args)

    local = [qkv_weight]
    bits = range(2, pieces, 2)
    known = {}
    if pieces > 1:
        local.append(swap(qkv_weight, "fsdp", 1))
        known["core"] = local[-1]
    (partial,) = call(
        functools.partial(own_kernel, len(local)),
        [ordered("t", sequence, known), *local],
        [shape((row_count, 3 * WIDTH), F32)],
        "project_own",
    )
    known["partial"] = partial
    direct_rows, queries = [], []
    for bit in bits:
        mine_rows, other_rows = [], []
        for number, (start, rows) in enumerate(spans):
            tag = str(number)
            side = seq_index // (1 << number) % 2
            cut = lax.dynamic_slice(
                ordered("c" + tag, qkv_weight, known), (start + side * rows, WIDTH), (rows, 2 * WIDTH)
            )
            known["c" + tag] = cut
            direct = swap(cut, "fsdp", bit)
            known["x" + tag] = direct
            across = swap(ordered("f" + tag, direct, known), "fsdp", 1)
            known["f" + tag] = across
            passed = ordered("p" + tag, swap(ordered("y" + tag, direct, known), "seq", 1 << number), known)
            known["y" + tag] = passed
            mine_rows += [direct, passed]
            other_rows += [across, swap(passed, "fsdp", 1)]
            known["q" + tag] = other_rows[-1]
        known["meta"] = meta
        cut = ordered("cD", qkv_weight, known)[direct_from:, WIDTH:]
        known["cD"] = cut
        rest = swap(cut, "fsdp", bit)
        known["xD"] = rest
        rest = ordered("pD", rest, known)
        known["fD"] = swap(rest, "fsdp", 1)
        direct_rows.append(mine_rows + [rest] + other_rows + [known["fD"]])
        cut = ordered("cQ", qkv_weight, known)[:, :WIDTH]
        known["cQ"] = cut
        queries.append(swap(cut, "fsdp", bit))
    assert len(bits) <= 1
    if bits:
        layout = [offsets_at + i for i in range(len(direct_rows[0]))]
        *packs, joined = call(
            functools.partial(pack_kernel, layout, base_at, slots, slot_at),
            [sequence, partial, *direct_rows[0]],
            [shape((BLOCK, 2 * WIDTH), BF16)] * slots + [shape((2 * share, 2 * WIDTH), BF16)],
            "project_pack",
        )
        known["pack"] = packs[0]
        (kv,) = call(
            functools.partial(kv_kernel, base_at),
            [sequence, ordered("kv", partial, known), joined],
            [shape((row_count, 2 * WIDTH), BF16)],
            "project_kv",
        )
    else:
        kv = partial[:, WIDTH:].astype(BF16)
        blocks = kv.reshape(block_rate, BLOCK, 2, HEADS, HEAD_DIM)
        packs = []
        for offset in (near_offset, far_offset % block_rate)[:slots]:
            picked = blocks[offset, :, :, jnp.arange(HEADS)]
            packs.append(picked.transpose(1, 2, 0, 3).reshape(BLOCK, 2 * WIDTH))
    known["kv"] = kv
    received = []
    for pack, place, count, unit in zip(packs, (near_at, far_at), shifts, (1, STRIDE)):
        for step in NEAR_ORDER if count == len(NEAR_ORDER) else range(1, count + 1):
            received.append((step, lax.ppermute(pack, "seq", partners(seq_size, place, step))))
        known |= {f"n{step}": r for step, r in received}
    steps = [step for step, _ in received]
    received = [pack for _, pack in received]
    crossed_q, q_places = [], []
    for bit, direct in zip(bits, queries):
        direct = ordered("q", direct, known)
        (slots_out,) = call(
            functools.partial(slot_kernel, core_at), [direct], [shape((2,) + direct.shape, BF16)], "slot_queries"
        )
        both = lax.all_to_all(
            slots_out, "fsdp", 0, 0, axis_index_groups=[[i, i + 1] for i in range(0, pieces, 2)]
        )
        crossed_q += [direct, both]
        q_places += [bit, bit ^ 1]
    state_types = [BF16, F32, F32, F32]
    partial_out, *state = call(
        functools.partial(attend_kernel, q_places, core_at, slots, slot_at, match_at),
        [sequence, partial, *crossed_q, kv],
        [shape((row_count, WIDTH), BF16)] + [shape((BLOCK, WIDTH), kind) for kind in state_types] * slots,
        "attend_local",
        [pltpu.VMEM((row_count, WIDTH), kind) for kind in state_types],
    )
    count = 4 * slots + sum(shifts)
    merged = pl.pallas_call(
        functools.partial(merge_kernel, shifts, steps, slot_at, match_at, place_at),
        in_specs=[scalar_spec] + [whole] * count + [pl.BlockSpec(memory_space=pl.ANY)],
        out_specs=pl.BlockSpec(memory_space=pl.ANY),
        out_shape=shape((row_count, WIDTH), BF16),
        scratch_shapes=[pltpu.VMEM((slots, BLOCK, WIDTH), BF16), pltpu.SemaphoreType.DMA((HEADS,))],
        input_output_aliases={count + 1: 0},
        compiler_params=pltpu.CompilerParams(vmem_limit_bytes=VMEM_LIMIT),
        cost_estimate=pl.CostEstimate(flops=MODEL_FLOPS["merge_near"], bytes_accessed=1000, transcendentals=0),
        name="merge_near",
    )(meta, *state, *received, partial_out)
    return merged[None]


def solution(mesh):
    in_specs = (P("fsdp", "seq", None), P("fsdp", None), P(), P())
    out_specs = P("fsdp", "seq", None)
    return jax.shard_map(body, mesh=mesh, in_specs=in_specs, out_specs=out_specs, check_vma=False)
```

```python
import functools
import math

import jax
import jax.numpy as jnp
from jax import lax
from jax.experimental import pallas as pl
from jax.experimental.pallas import tpu as pltpu
from jax.sharding import PartitionSpec as P

HEADS = 4
HEAD_DIM = 128
BLOCK = 128
STRIDE = 8
WIDTH = HEADS * HEAD_DIM
PAIR = 2 * HEAD_DIM
NEG = -1e30
SCALE2 = HEAD_DIM ** (-0.5) * math.log2(math.e)
VMEM_LIMIT = 24 * 1024 * 1024

MODEL_FLOPS = {"project_first": 689999, "slot_queries": 575000, "project_pack": 689999, "project_own": 3680000, "project_mid": 1610000, "project_kv": 2990000, "attend_local": 6325000, "merge_near": 2990000}
ORDER = {
    'c1': ('c0',),
    'cD': ('c1',),
    'cQ': ('cD',),
    'p0': ('partial', 'xD'),
    'p1': ('partial',),
    'q': ('kv',),
    'kv': ('pack',),
}
NEAR_ORDER = (3, 2, 1)
F32 = jnp.float32
BF16 = jnp.bfloat16


def near_place(index, half, size):
    if index < half:
        return 0, index
    return 1 + (index - half) // size, (index - half) % size


def partners(count, place, bits):
    where = {place(i): i for i in range(count)}
    pairs = []
    for source in range(count):
        run, spot = place(source)
        if (run, spot ^ bits) in where:
            pairs.append((source, where[run, spot ^ bits]))
    return pairs


def swap(value, axis, bit):
    count = lax.axis_size(axis)
    return lax.ppermute(value, axis, [(i, i ^ bit) for i in range(count)])


def after(value, *others):
    return lax.optimization_barrier((value,) + others)[0]


def ordered(name, value, known):
    others = [known[other] for other in ORDER.get(name, ()) if other in known]
    return after(value, *others) if others else value


def rows_of(block):
    return pl.ds(pl.multiple_of(block * BLOCK, BLOCK), BLOCK)


def qk(query, key):
    return lax.dot_general(query, key, (((1,), (1,)), ((), ())), preferred_element_type=F32)


def pv(weights, value):
    return jnp.dot(weights.astype(BF16), value, preferred_element_type=F32)


def add_up(tokens, places, weights):
    total = None
    for place, weight in zip(places, weights):
        depth = weight.shape[0]
        columns = pl.ds(pl.multiple_of(place, depth), depth)
        term = jnp.dot(tokens[:, columns], weight[...], preferred_element_type=F32)
        total = term if total is None else total + term
    return total


def own_kernel(count, meta, tokens, *refs):
    weights, out = refs[:count], refs[count]
    for j in range(out.shape[1] // PAIR):
        lanes = slice(j * PAIR, (j + 1) * PAIR)
        out[:, lanes] = add_up(tokens, [meta[at] for at in range(count)], [weight.at[:, lanes] for weight in weights])


def near_rows_kernel(layout, place_at, first, slots, slot_at, meta, tokens, before, *refs):
    arrived, refs = refs[: len(layout)], refs[len(layout) :]
    sums, joined = refs[:slots], refs[slots]
    for at, array in zip(layout, arrived):
        rows = array.shape[0]
        joined[pl.ds(pl.multiple_of(meta[at], rows), rows), :] = array[...]
    depth = joined.shape[0]
    columns = pl.ds(pl.multiple_of(meta[place_at], depth), depth)
    for slot in range(slots):
        for head in range(HEADS):
            rows = rows_of(meta[slot_at + HEADS * slot + head])
            lanes = [slice(start, start + HEAD_DIM) for start in (head * HEAD_DIM, WIDTH + head * HEAD_DIM)]
            weight = jnp.concatenate([joined[:, part] for part in lanes], axis=1)
            product = jnp.dot(tokens[rows, columns], weight, preferred_element_type=F32)
            for field, part in enumerate(lanes):
                if first:
                    total = before[0][rows, WIDTH + part.start : WIDTH + part.stop]
                else:
                    total = before[slot][:, part]
                total = total + product[:, field * HEAD_DIM : (field + 1) * HEAD_DIM]
                sums[slot][:, part] = total.astype(sums[slot].dtype)


def first_rows_kernel(layout, place_at, slots, slot_at, meta, tokens, partial, *refs):
    near_rows_kernel(layout, place_at, True, slots, slot_at, meta, tokens, [partial], *refs)


def last_rows_kernel(layout, place_at, slots, slot_at, meta, tokens, *refs):
    near_rows_kernel(layout, place_at, False, slots, slot_at, meta, tokens, refs[:slots], *refs[slots:])


def slot_kernel(core_at, meta, source, out):
    out[1 - meta[core_at]] = source[...]


def kv_kernel(places_at, meta, tokens, partial, *refs):
    parts, kv = refs[:-1], refs[-1]
    places = [meta[at] for at in places_at]
    for j in range(2 * WIDTH // PAIR):
        lanes = slice(j * PAIR, (j + 1) * PAIR)
        product = add_up(tokens, places, [part.at[:, lanes] for part in parts])
        kv[:, lanes] = (partial[:, WIDTH + j * PAIR : WIDTH + (j + 1) * PAIR] + product).astype(BF16)


def with_ones(value):
    return jnp.concatenate([value, jnp.ones(value.shape, BF16)], axis=1)


def attend_kernel(bases_at, core_at, slots, slot_at, match_at, meta, tokens, partial, *refs):
    weights, refs = refs[: len(bases_at)], refs[len(bases_at) :]
    kv, out, refs = refs[0], refs[1], refs[2:]
    state, scratch = refs[: 4 * slots], refs[4 * slots :]
    query, acc_all, top_all, sum_all = scratch
    blocks = query.shape[0] // BLOCK
    GROUP = 2 if blocks % 2 == 0 else 1
    row = lax.broadcasted_iota(jnp.int32, (BLOCK, BLOCK), 0)
    column = lax.broadcasted_iota(jnp.int32, (BLOCK, BLOCK), 1)
    causal = column <= row
    places = [meta[at] for at in bases_at]
    other = 1 - meta[core_at]
    for pair in range(HEADS // 2):
        lanes = slice(pair * PAIR, (pair + 1) * PAIR)
        total = partial[:, lanes]
        if weights:
            parts = [weights[0].at[:, lanes], weights[1].at[other, :, lanes]]
            total = total + add_up(tokens, places, parts)
        query[:, lanes] = total.astype(BF16)

    def lanes_of(head):
        return slice(head * HEAD_DIM, (head + 1) * HEAD_DIM)

    def rows_at(b):
        return slice(b * BLOCK, (b + 1) * BLOCK)

    def score(head, group):
        first, last = group * GROUP, (group + 1) * GROUP
        rows = slice(first * BLOCK, last * BLOCK)
        return qk(query[rows, lanes_of(head)], kv[: last * BLOCK, lanes_of(head)])

    def weigh(head, group, scores):
        near_block = meta[slot_at + head]
        far_block = meta[slot_at + HEADS + head]
        tops, weights = [], []
        for i in range(GROUP):
            b = group * GROUP + i
            mine = scores[rows_at(i)]
            times = (
                1
                + jnp.where(near_block == b, 1, 0)
                + jnp.where(far_block == b, meta[match_at + head], 0)
            ).astype(F32)
            diagonal = jnp.where(causal, mine[:, rows_at(b)], NEG)
            top = jnp.max(diagonal, axis=1, keepdims=True)
            if b:
                top = jnp.maximum(top, jnp.max(mine[:, : b * BLOCK], axis=1, keepdims=True))
            parts = [(jnp.exp2((diagonal - top) * SCALE2) * times).astype(BF16)]
            if b:
                parts.insert(0, jnp.exp2((mine[:, : b * BLOCK] - top) * SCALE2).astype(BF16))
            if i < GROUP - 1:
                parts.append(jnp.zeros((BLOCK, (GROUP - 1 - i) * BLOCK), BF16))
            tops.append(top)
            weights.append(jnp.concatenate(parts, axis=1))
        return tops, jnp.concatenate(weights, axis=0)

    def finish(head, group, tops, weight):
        lanes = lanes_of(head)
        keys = (group + 1) * GROUP * BLOCK
        value = kv[:keys, WIDTH + head * HEAD_DIM : WIDTH + (head + 1) * HEAD_DIM]
        both = jnp.dot(weight, with_ones(value), preferred_element_type=F32)
        rows = slice(group * GROUP * BLOCK, keys)
        acc, summed = both[:, :HEAD_DIM], both[:, HEAD_DIM:]
        out[rows, lanes] = (acc / summed).astype(BF16)
        acc_all[rows, lanes] = acc
        sum_all[rows, lanes] = summed
        for i, top in enumerate(tops):
            top_all[rows_at(group * GROUP + i), lanes] = jnp.broadcast_to(top, (BLOCK, HEAD_DIM))
        if group == blocks // GROUP - 1:
            for slot in range(slots):
                rows = rows_of(meta[slot_at + slot * HEADS + head])
                for target, source in zip(state[4 * slot :], scratch):
                    target[:, lanes] = source[rows, lanes]

    tasks = [(head, group) for head in range(HEADS) for group in range(blocks // GROUP)]
    scored, weighed = {}, {}
    for step in range(len(tasks) + 2):
        if step < len(tasks):
            scored[step] = score(*tasks[step])
        if 0 <= step - 1 < len(tasks):
            weighed[step - 1] = weigh(*tasks[step - 1], scored.pop(step - 1))
        if 0 <= step - 2 < len(tasks):
            finish(*tasks[step - 2], *weighed.pop(step - 2))


def merge_kernel(shifts, steps, slot_at, match_at, place_at, meta, *refs):
    slots = len(shifts)
    state = refs[: 4 * slots]
    packs = refs[4 * slots : 4 * slots + sum(shifts)]
    out, results, sems = refs[4 * slots + sum(shifts) + 1 :]
    if slots == 1:
        pl.when(meta[place_at] > 0)(lambda: merge_slots(
            shifts, steps, slot_at, match_at, place_at, meta, state, packs, out, results, sems
        ))
    else:
        merge_slots(shifts, steps, slot_at, match_at, place_at, meta, state, packs, out, results, sems)


def merge_slots(shifts, steps, slot_at, match_at, place_at, meta, state, packs, out, results, sems):
    lanes = [slice(head * HEAD_DIM, (head + 1) * HEAD_DIM) for head in range(HEADS)]
    values = [slice(WIDTH + head * HEAD_DIM, WIDTH + (head + 1) * HEAD_DIM) for head in range(HEADS)]
    earlier = [None] * HEADS
    for slot, count in enumerate(shifts):
        fields = packs[sum(shifts[:slot]) : sum(shifts[: slot + 1])]
        query, acc_ref, top_ref, sum_ref = state[4 * slot : 4 * slot + 4]
        place = meta[place_at + slot]
        scores, weights = [], []
        for head in range(HEADS):
            keys = jnp.concatenate([field[:, lanes[head]] for field in fields], axis=0)
            score = qk(query[:, lanes[head]], keys)
            parts = []
            for number, step in enumerate(steps[sum(shifts[:slot]) : sum(shifts[: slot + 1])]):
                seen = place ^ step < place
                if slot:
                    seen = seen & (meta[match_at + head] == 1)
                part = score[:, number * BLOCK : (number + 1) * BLOCK]
                parts.append(jnp.where(seen, part, NEG))
            scores.append(jnp.concatenate(parts, axis=1))
        for head in range(HEADS):
            acc, top, summed = (ref[:, lanes[head]] for ref in (acc_ref, top_ref, sum_ref))
            if slot:
                same = meta[slot_at + head] == meta[slot_at + HEADS + head]
                acc, top, summed = (
                    jnp.where(same, new, old) for new, old in zip(earlier[head], (acc, top, summed))
                )
            best = jnp.maximum(top, jnp.max(scores[head], axis=1, keepdims=True))
            decay = jnp.exp2((top - best) * SCALE2)
            weight = jnp.exp2((scores[head] - best[:, :1]) * SCALE2).astype(BF16)
            weights.append((acc * decay, best, summed * decay, weight))
        copies = []
        for head in range(HEADS):
            acc, best, summed, weight = weights[head]
            value = jnp.concatenate([field[:, values[head]] for field in fields], axis=0)
            both = jnp.dot(weight, with_ones(value), preferred_element_type=F32)
            acc = acc + both[:, :HEAD_DIM]
            summed = summed + both[:, HEAD_DIM:]
            earlier[head] = (acc, best, summed)
            results[slot, :, lanes[head]] = (acc / summed).astype(BF16)
            rows = rows_of(meta[slot_at + slot * HEADS + head])
            copies.append(
                pltpu.make_async_copy(
                    results.at[slot, :, lanes[head]], out.at[rows, lanes[head]], sems.at[head]
                )
            )
            copies[-1].start()
        for copy in copies:
            copy.wait()


def body(tokens, qkv_weight, near_offset, far_offset):
    sequence = tokens[0]
    row_count, depth = sequence.shape
    share = qkv_weight.shape[0]
    block_rate = row_count // BLOCK
    seq_size = lax.axis_size("seq")
    seq_index = lax.axis_index("seq")
    pieces = lax.axis_size("fsdp")
    mine = lax.axis_index("fsdp")
    near_size = min(16, seq_size)
    half = near_size // 2
    far_size = max(1, min(16, seq_size // STRIDE))
    near_at = lambda i: near_place(i, half, near_size)
    far_at = lambda i: (i // (STRIDE * far_size) * STRIDE + i % STRIDE, i // STRIDE % far_size)
    reach = max(near_at(i)[1] for i in range(seq_size))
    near_shifts = (1 << reach.bit_length()) - 1
    far_shifts = (1 << (far_size - 1).bit_length()) - 1
    slots = 2 if far_shifts else 1
    shifts = (near_shifts, far_shifts)[:slots]

    near_position = jnp.where(seq_index < half, seq_index, (seq_index - half) % near_size)
    far_position = seq_index // STRIDE % far_size
    far_match = (seq_index % STRIDE == far_offset // block_rate).astype(jnp.int32)
    spans = [(0, share // 4), (share // 2, share // 8)] if seq_size % 4 == 0 else []
    direct_from = spans[-1][0] + 2 * spans[-1][1] if spans else 0
    full_places = [(mine ^ j) * share for j in range(pieces)]
    scalars = list(full_places)
    place_at = len(scalars)
    scalars += [near_position, far_position]
    base_at = len(scalars)
    scalars += [(mine ^ bit) // 2 * 2 * share for bit in range(2, pieces, 2)]
    core_at = len(scalars)
    scalars.append(mine % 2)
    slot_at = len(scalars)
    match_at = slot_at + 2 * HEADS
    offsets_at = match_at + HEADS
    offsets = []
    for number, (start, rows) in enumerate(spans):
        side = seq_index // (1 << number) % 2
        offsets += [start + side * rows, start + (1 - side) * rows]
    offsets.append(direct_from)
    as_array = lambda values: jnp.stack([jnp.asarray(value, jnp.int32) for value in values])
    meta = jnp.concatenate(
        [as_array(scalars), near_offset, far_offset % block_rate, far_match, as_array(offsets)]
    )

    scalar_spec = pl.BlockSpec(memory_space=pltpu.SMEM)
    whole = pl.BlockSpec(memory_space=pltpu.VMEM)
    shape = jax.ShapeDtypeStruct

    def call(kernel, args, results, name, scratch=()):
        return pl.pallas_call(
            kernel,
            in_specs=[scalar_spec] + [whole] * len(args),
            out_specs=[whole] * len(results),
            out_shape=results,
            scratch_shapes=list(scratch),
            compiler_params=pltpu.CompilerParams(vmem_limit_bytes=VMEM_LIMIT),
            cost_estimate=pl.CostEstimate(flops=MODEL_FLOPS[name], bytes_accessed=1000, transcendentals=0),
            name=name,
        )(meta, *args)

    local = [qkv_weight]
    bits = range(2, pieces, 2)
    known = {}
    if pieces > 1:
        local.append(swap(qkv_weight, "fsdp", 1))
        known["core"] = local[-1]
    (partial,) = call(
        functools.partial(own_kernel, len(local)),
        [ordered("t", sequence, known), *local],
        [shape((row_count, 3 * WIDTH), F32)],
        "project_own",
    )
    known["partial"] = partial
    direct_rows, queries = [], []
    for bit in bits:
        mine_rows, other_rows = [], []
        for number, (start, rows) in enumerate(spans):
            tag = str(number)
            side = seq_index // (1 << number) % 2
            cut = lax.dynamic_slice(
                ordered("c" + tag, qkv_weight, known), (start + side * rows, WIDTH), (rows, 2 * WIDTH)
            )
            known["c" + tag] = cut
            direct = swap(cut, "fsdp", bit)
            known["x" + tag] = direct
            across = swap(ordered("f" + tag, direct, known), "fsdp", 1)
            known["f" + tag] = across
            passed = ordered("p" + tag, swap(ordered("y" + tag, direct, known), "seq", 1 << number), known)
            known["y" + tag] = passed
            mine_rows += [direct, passed]
            other_rows += [across, swap(passed, "fsdp", 1)]
            known["q" + tag] = other_rows[-1]
        known["meta"] = meta
        cut = ordered("cD", qkv_weight, known)[direct_from:, WIDTH:]
        known["cD"] = cut
        rest = swap(cut, "fsdp", bit)
        known["xD"] = rest
        rest = ordered("pD", rest, known)
        known["fD"] = swap(rest, "fsdp", 1)
        direct_rows.append(mine_rows + [rest] + other_rows + [known["fD"]])
        cut = ordered("cQ", qkv_weight, known)[:, :WIDTH]
        known["cQ"] = cut
        queries.append(swap(cut, "fsdp", bit))
    assert len(bits) <= 1
    if bits:
        bit = bits[0]
        count = len(direct_rows[0]) // 2
        layout = [offsets_at + i for i in range(count)]
        *sums, joined = call(
            functools.partial(first_rows_kernel, layout, bit, slots, slot_at),
            [sequence, ordered("a", partial, known), *direct_rows[0][:count]],
            [shape((BLOCK, 2 * WIDTH), F32)] * slots + [shape((share, 2 * WIDTH), BF16)],
            "project_first",
        )
        *packs, joined_other = call(
            functools.partial(last_rows_kernel, layout, bit ^ 1, slots, slot_at),
            [sequence, *sums, *direct_rows[0][count:]],
            [shape((BLOCK, 2 * WIDTH), BF16)] * slots + [shape((share, 2 * WIDTH), BF16)],
            "project_pack",
        )
        known["pack"] = packs[0]
        (kv,) = call(
            functools.partial(kv_kernel, [bit, bit ^ 1]),
            [sequence, ordered("kv", partial, known), joined, joined_other],
            [shape((row_count, 2 * WIDTH), BF16)],
            "project_kv",
        )
    else:
        kv = partial[:, WIDTH:].astype(BF16)
        blocks = kv.reshape(block_rate, BLOCK, 2, HEADS, HEAD_DIM)
        packs = []
        for offset in (near_offset, far_offset % block_rate)[:slots]:
            picked = blocks[offset, :, :, jnp.arange(HEADS)]
            packs.append(picked.transpose(1, 2, 0, 3).reshape(BLOCK, 2 * WIDTH))
    known["kv"] = kv
    received = []
    for pack, place, count, unit in zip(packs, (near_at, far_at), shifts, (1, STRIDE)):
        for step in NEAR_ORDER if count == len(NEAR_ORDER) else range(1, count + 1):
            received.append((step, lax.ppermute(pack, "seq", partners(seq_size, place, step))))
        known |= {f"n{step}": r for step, r in received}
    steps = [step for step, _ in received]
    received = [pack for _, pack in received]
    crossed_q, q_places = [], []
    for bit, direct in zip(bits, queries):
        direct = ordered("q", direct, known)
        (slots_out,) = call(
            functools.partial(slot_kernel, core_at), [direct], [shape((2,) + direct.shape, BF16)], "slot_queries"
        )
        both = lax.all_to_all(
            slots_out, "fsdp", 0, 0, axis_index_groups=[[i, i + 1] for i in range(0, pieces, 2)]
        )
        crossed_q += [direct, both]
        q_places += [bit, bit ^ 1]
    state_types = [BF16, F32, F32, F32]
    partial_out, *state = call(
        functools.partial(attend_kernel, q_places, core_at, slots, slot_at, match_at),
        [sequence, partial, *crossed_q, kv],
        [shape((row_count, WIDTH), BF16)] + [shape((BLOCK, WIDTH), kind) for kind in state_types] * slots,
        "attend_local",
        [pltpu.VMEM((row_count, WIDTH), kind) for kind in state_types],
    )
    count = 4 * slots + sum(shifts)
    merged = pl.pallas_call(
        functools.partial(merge_kernel, shifts, steps, slot_at, match_at, place_at),
        in_specs=[scalar_spec] + [whole] * count + [pl.BlockSpec(memory_space=pl.ANY)],
        out_specs=pl.BlockSpec(memory_space=pl.ANY),
        out_shape=shape((row_count, WIDTH), BF16),
        scratch_shapes=[pltpu.VMEM((slots, BLOCK, WIDTH), BF16), pltpu.SemaphoreType.DMA((HEADS,))],
        input_output_aliases={count + 1: 0},
        compiler_params=pltpu.CompilerParams(vmem_limit_bytes=VMEM_LIMIT),
        cost_estimate=pl.CostEstimate(flops=MODEL_FLOPS["merge_near"], bytes_accessed=1000, transcendentals=0),
        name="merge_near",
    )(meta, *state, *received, partial_out)
    return merged[None]


def solution(mesh):
    in_specs = (P("fsdp", "seq", None), P("fsdp", None), P(), P())
    out_specs = P("fsdp", "seq", None)
    return jax.shard_map(body, mesh=mesh, in_specs=in_specs, out_specs=out_specs, check_vma=False)
```

```python
import functools
import math

import jax
import jax.numpy as jnp
from jax import lax
from jax.experimental import pallas as pl
from jax.experimental.pallas import tpu as pltpu
from jax.sharding import PartitionSpec as P

HEADS = 4
HEAD_DIM = 128
BLOCK = 128
STRIDE = 8
WIDTH = HEADS * HEAD_DIM
PAIR = 2 * HEAD_DIM
NEG = -1e30
SCALE2 = HEAD_DIM ** (-0.5) * math.log2(math.e)
VMEM_LIMIT = 24 * 1024 * 1024

MODEL_FLOPS = {"project_first": 689999, "slot_queries": 575000, "project_pack": 689999, "project_own": 3680000, "project_mid": 1610000, "project_kv": 2990000, "attend_local": 6325000, "merge_near": 2990000}
ORDER = {
    'c1': ('c0',),
    'cD': ('c1',),
    'cQ': ('cD',),
    'p0': ('partial', 'xD'),
    'p1': ('partial',),
    'q': ('kv',),
    'kv': ('pack',),
}
NEAR_ORDER = (3, 2, 1)
F32 = jnp.float32
BF16 = jnp.bfloat16


def near_place(index, half, size):
    if index < half:
        return 0, index
    return 1 + (index - half) // size, (index - half) % size


def partners(count, place, bits):
    where = {place(i): i for i in range(count)}
    pairs = []
    for source in range(count):
        run, spot = place(source)
        if (run, spot ^ bits) in where:
            pairs.append((source, where[run, spot ^ bits]))
    return pairs


def swap(value, axis, bit):
    count = lax.axis_size(axis)
    return lax.ppermute(value, axis, [(i, i ^ bit) for i in range(count)])


def after(value, *others):
    return lax.optimization_barrier((value,) + others)[0]


def ordered(name, value, known):
    others = [known[other] for other in ORDER.get(name, ()) if other in known]
    return after(value, *others) if others else value


def rows_of(block):
    return pl.ds(pl.multiple_of(block * BLOCK, BLOCK), BLOCK)


def qk(query, key):
    return lax.dot_general(query, key, (((1,), (1,)), ((), ())), preferred_element_type=F32)


def pv(weights, value):
    return jnp.dot(weights.astype(BF16), value, preferred_element_type=F32)


def add_up(tokens, places, weights):
    total = None
    for place, weight in zip(places, weights):
        depth = weight.shape[0]
        columns = pl.ds(pl.multiple_of(place, depth), depth)
        term = jnp.dot(tokens[:, columns], weight[...], preferred_element_type=F32)
        total = term if total is None else total + term
    return total


def own_kernel(count, meta, tokens, *refs):
    weights, out = refs[:count], refs[count]
    for j in range(out.shape[1] // PAIR):
        lanes = slice(j * PAIR, (j + 1) * PAIR)
        out[:, lanes] = add_up(tokens, [meta[at] for at in range(count)], [weight.at[:, lanes] for weight in weights])


def near_rows_kernel(layout, place_at, first, slots, slot_at, meta, tokens, before, *refs):
    arrived, refs = refs[: len(layout)], refs[len(layout) :]
    sums, joined = refs[:slots], refs[slots]
    for at, array in zip(layout, arrived):
        rows = array.shape[0]
        joined[pl.ds(pl.multiple_of(meta[at], rows), rows), :] = array[...]
    depth = joined.shape[0]
    columns = pl.ds(pl.multiple_of(meta[place_at], depth), depth)
    for slot in range(slots):
        for head in range(HEADS):
            rows = rows_of(meta[slot_at + HEADS * slot + head])
            lanes = [slice(start, start + HEAD_DIM) for start in (head * HEAD_DIM, WIDTH + head * HEAD_DIM)]
            weight = jnp.concatenate([joined[:, part] for part in lanes], axis=1)
            product = jnp.dot(tokens[rows, columns], weight, preferred_element_type=F32)
            for field, part in enumerate(lanes):
                if first:
                    total = before[0][rows, WIDTH + part.start : WIDTH + part.stop]
                else:
                    total = before[slot][:, part]
                total = total + product[:, field * HEAD_DIM : (field + 1) * HEAD_DIM]
                sums[slot][:, part] = total.astype(sums[slot].dtype)


def first_rows_kernel(layout, place_at, slots, slot_at, meta, tokens, partial, *refs):
    near_rows_kernel(layout, place_at, True, slots, slot_at, meta, tokens, [partial], *refs)


def last_rows_kernel(layout, place_at, slots, slot_at, meta, tokens, *refs):
    near_rows_kernel(layout, place_at, False, slots, slot_at, meta, tokens, refs[:slots], *refs[slots:])


def slot_kernel(core_at, meta, source, *outs):
    done = 0
    for out in outs[:-1]:
        rows = out.shape[0]
        out[...] = source[done : done + rows, :]
        done += rows
    outs[-1][1 - meta[core_at]] = source[done:, :]


def kv_kernel(places_at, meta, tokens, partial, *refs):
    parts, kv = refs[:-1], refs[-1]
    places = [meta[at] for at in places_at]
    for j in range(2 * WIDTH // PAIR):
        lanes = slice(j * PAIR, (j + 1) * PAIR)
        product = add_up(tokens, places, [part.at[:, lanes] for part in parts])
        kv[:, lanes] = (partial[:, WIDTH + j * PAIR : WIDTH + (j + 1) * PAIR] + product).astype(BF16)


def with_ones(value):
    return jnp.concatenate([value, jnp.ones(value.shape, BF16)], axis=1)


def attend_kernel(count, bases_at, core_at, slots, slot_at, match_at, meta, tokens, partial, *refs):
    weights, refs = refs[:count], refs[count:]
    kv, out, refs = refs[0], refs[1], refs[2:]
    state, scratch, joined = refs[: 4 * slots], refs[4 * slots : -1], refs[-1]
    query, acc_all, top_all, sum_all = scratch
    blocks = query.shape[0] // BLOCK
    GROUP = 2 if blocks % 2 == 0 else 1
    row = lax.broadcasted_iota(jnp.int32, (BLOCK, BLOCK), 0)
    column = lax.broadcasted_iota(jnp.int32, (BLOCK, BLOCK), 1)
    causal = column <= row
    places = [meta[at] for at in bases_at]
    if weights:
        done = 0
        for weight in weights[2:]:
            joined[done : done + weight.shape[0], :] = weight[...]
            done += weight.shape[0]
        joined[done:, :] = weights[1][1 - meta[core_at]]
    for pair in range(HEADS // 2):
        lanes = slice(pair * PAIR, (pair + 1) * PAIR)
        total = partial[:, lanes]
        if weights:
            total = total + add_up(tokens, places, [weights[0].at[:, lanes], joined.at[:, lanes]])
        query[:, lanes] = total.astype(BF16)

    def lanes_of(head):
        return slice(head * HEAD_DIM, (head + 1) * HEAD_DIM)

    def rows_at(b):
        return slice(b * BLOCK, (b + 1) * BLOCK)

    def score(head, group):
        first, last = group * GROUP, (group + 1) * GROUP
        rows = slice(first * BLOCK, last * BLOCK)
        return qk(query[rows, lanes_of(head)], kv[: last * BLOCK, lanes_of(head)])

    def weigh(head, group, scores):
        near_block = meta[slot_at + head]
        far_block = meta[slot_at + HEADS + head]
        tops, weights = [], []
        for i in range(GROUP):
            b = group * GROUP + i
            mine = scores[rows_at(i)]
            times = (
                1
                + jnp.where(near_block == b, 1, 0)
                + jnp.where(far_block == b, meta[match_at + head], 0)
            ).astype(F32)
            diagonal = jnp.where(causal, mine[:, rows_at(b)], NEG)
            top = jnp.max(diagonal, axis=1, keepdims=True)
            if b:
                top = jnp.maximum(top, jnp.max(mine[:, : b * BLOCK], axis=1, keepdims=True))
            parts = [(jnp.exp2((diagonal - top) * SCALE2) * times).astype(BF16)]
            if b:
                parts.insert(0, jnp.exp2((mine[:, : b * BLOCK] - top) * SCALE2).astype(BF16))
            if i < GROUP - 1:
                parts.append(jnp.zeros((BLOCK, (GROUP - 1 - i) * BLOCK), BF16))
            tops.append(top)
            weights.append(jnp.concatenate(parts, axis=1))
        return tops, jnp.concatenate(weights, axis=0)

    def finish(head, group, tops, weight):
        lanes = lanes_of(head)
        keys = (group + 1) * GROUP * BLOCK
        value = kv[:keys, WIDTH + head * HEAD_DIM : WIDTH + (head + 1) * HEAD_DIM]
        both = jnp.dot(weight, with_ones(value), preferred_element_type=F32)
        rows = slice(group * GROUP * BLOCK, keys)
        acc, summed = both[:, :HEAD_DIM], both[:, HEAD_DIM:]
        out[rows, lanes] = (acc / summed).astype(BF16)
        acc_all[rows, lanes] = acc
        sum_all[rows, lanes] = summed
        for i, top in enumerate(tops):
            top_all[rows_at(group * GROUP + i), lanes] = jnp.broadcast_to(top, (BLOCK, HEAD_DIM))
        if group == blocks // GROUP - 1:
            for slot in range(slots):
                rows = rows_of(meta[slot_at + slot * HEADS + head])
                for target, source in zip(state[4 * slot :], scratch):
                    target[:, lanes] = source[rows, lanes]

    tasks = [(head, group) for head in range(HEADS) for group in range(blocks // GROUP)]
    scored, weighed = {}, {}
    for step in range(len(tasks) + 2):
        if step < len(tasks):
            scored[step] = score(*tasks[step])
        if 0 <= step - 1 < len(tasks):
            weighed[step - 1] = weigh(*tasks[step - 1], scored.pop(step - 1))
        if 0 <= step - 2 < len(tasks):
            finish(*tasks[step - 2], *weighed.pop(step - 2))


def merge_kernel(shifts, steps, slot_at, match_at, place_at, meta, *refs):
    slots = len(shifts)
    state = refs[: 4 * slots]
    packs = refs[4 * slots : 4 * slots + sum(shifts)]
    out, results, sems = refs[4 * slots + sum(shifts) + 1 :]
    if slots == 1:
        pl.when(meta[place_at] > 0)(lambda: merge_slots(
            shifts, steps, slot_at, match_at, place_at, meta, state, packs, out, results, sems
        ))
    else:
        merge_slots(shifts, steps, slot_at, match_at, place_at, meta, state, packs, out, results, sems)


def merge_slots(shifts, steps, slot_at, match_at, place_at, meta, state, packs, out, results, sems):
    lanes = [slice(head * HEAD_DIM, (head + 1) * HEAD_DIM) for head in range(HEADS)]
    values = [slice(WIDTH + head * HEAD_DIM, WIDTH + (head + 1) * HEAD_DIM) for head in range(HEADS)]
    earlier = [None] * HEADS
    for slot, count in enumerate(shifts):
        fields = packs[sum(shifts[:slot]) : sum(shifts[: slot + 1])]
        query, acc_ref, top_ref, sum_ref = state[4 * slot : 4 * slot + 4]
        place = meta[place_at + slot]
        scores, weights = [], []
        for head in range(HEADS):
            keys = jnp.concatenate([field[:, lanes[head]] for field in fields], axis=0)
            score = qk(query[:, lanes[head]], keys)
            parts = []
            for number, step in enumerate(steps[sum(shifts[:slot]) : sum(shifts[: slot + 1])]):
                seen = place ^ step < place
                if slot:
                    seen = seen & (meta[match_at + head] == 1)
                part = score[:, number * BLOCK : (number + 1) * BLOCK]
                parts.append(jnp.where(seen, part, NEG))
            scores.append(jnp.concatenate(parts, axis=1))
        for head in range(HEADS):
            acc, top, summed = (ref[:, lanes[head]] for ref in (acc_ref, top_ref, sum_ref))
            if slot:
                same = meta[slot_at + head] == meta[slot_at + HEADS + head]
                acc, top, summed = (
                    jnp.where(same, new, old) for new, old in zip(earlier[head], (acc, top, summed))
                )
            best = jnp.maximum(top, jnp.max(scores[head], axis=1, keepdims=True))
            decay = jnp.exp2((top - best) * SCALE2)
            weight = jnp.exp2((scores[head] - best[:, :1]) * SCALE2).astype(BF16)
            weights.append((acc * decay, best, summed * decay, weight))
        copies = []
        for head in range(HEADS):
            acc, best, summed, weight = weights[head]
            value = jnp.concatenate([field[:, values[head]] for field in fields], axis=0)
            both = jnp.dot(weight, with_ones(value), preferred_element_type=F32)
            acc = acc + both[:, :HEAD_DIM]
            summed = summed + both[:, HEAD_DIM:]
            earlier[head] = (acc, best, summed)
            results[slot, :, lanes[head]] = (acc / summed).astype(BF16)
            rows = rows_of(meta[slot_at + slot * HEADS + head])
            copies.append(
                pltpu.make_async_copy(
                    results.at[slot, :, lanes[head]], out.at[rows, lanes[head]], sems.at[head]
                )
            )
            copies[-1].start()
        for copy in copies:
            copy.wait()


def body(tokens, qkv_weight, near_offset, far_offset):
    sequence = tokens[0]
    row_count, depth = sequence.shape
    share = qkv_weight.shape[0]
    block_rate = row_count // BLOCK
    seq_size = lax.axis_size("seq")
    seq_index = lax.axis_index("seq")
    pieces = lax.axis_size("fsdp")
    mine = lax.axis_index("fsdp")
    near_size = min(16, seq_size)
    half = near_size // 2
    far_size = max(1, min(16, seq_size // STRIDE))
    near_at = lambda i: near_place(i, half, near_size)
    far_at = lambda i: (i // (STRIDE * far_size) * STRIDE + i % STRIDE, i // STRIDE % far_size)
    reach = max(near_at(i)[1] for i in range(seq_size))
    near_shifts = (1 << reach.bit_length()) - 1
    far_shifts = (1 << (far_size - 1).bit_length()) - 1
    slots = 2 if far_shifts else 1
    shifts = (near_shifts, far_shifts)[:slots]

    near_position = jnp.where(seq_index < half, seq_index, (seq_index - half) % near_size)
    far_position = seq_index // STRIDE % far_size
    far_match = (seq_index % STRIDE == far_offset // block_rate).astype(jnp.int32)
    spans = [(0, share // 4), (share // 2, share // 8)] if seq_size % 4 == 0 else []
    direct_from = spans[-1][0] + 2 * spans[-1][1] if spans else 0
    full_places = [(mine ^ j) * share for j in range(pieces)]
    scalars = list(full_places)
    place_at = len(scalars)
    scalars += [near_position, far_position]
    base_at = len(scalars)
    scalars += [(mine ^ bit) // 2 * 2 * share for bit in range(2, pieces, 2)]
    core_at = len(scalars)
    scalars.append(mine % 2)
    slot_at = len(scalars)
    match_at = slot_at + 2 * HEADS
    offsets_at = match_at + HEADS
    offsets = []
    for number, (start, rows) in enumerate(spans):
        side = seq_index // (1 << number) % 2
        offsets += [start + side * rows, start + (1 - side) * rows]
    offsets.append(direct_from)
    as_array = lambda values: jnp.stack([jnp.asarray(value, jnp.int32) for value in values])
    meta = jnp.concatenate(
        [as_array(scalars), near_offset, far_offset % block_rate, far_match, as_array(offsets)]
    )

    scalar_spec = pl.BlockSpec(memory_space=pltpu.SMEM)
    whole = pl.BlockSpec(memory_space=pltpu.VMEM)
    shape = jax.ShapeDtypeStruct

    def call(kernel, args, results, name, scratch=()):
        return pl.pallas_call(
            kernel,
            in_specs=[scalar_spec] + [whole] * len(args),
            out_specs=[whole] * len(results),
            out_shape=results,
            scratch_shapes=list(scratch),
            compiler_params=pltpu.CompilerParams(vmem_limit_bytes=VMEM_LIMIT),
            cost_estimate=pl.CostEstimate(flops=MODEL_FLOPS[name], bytes_accessed=1000, transcendentals=0),
            name=name,
        )(meta, *args)

    local = [qkv_weight]
    bits = range(2, pieces, 2)
    known = {}
    if pieces > 1:
        local.append(swap(qkv_weight, "fsdp", 1))
        known["core"] = local[-1]
    (partial,) = call(
        functools.partial(own_kernel, len(local)),
        [ordered("t", sequence, known), *local],
        [shape((row_count, 3 * WIDTH), F32)],
        "project_own",
    )
    known["partial"] = partial
    direct_rows, queries = [], []
    for bit in bits:
        mine_rows, other_rows = [], []
        for number, (start, rows) in enumerate(spans):
            tag = str(number)
            side = seq_index // (1 << number) % 2
            cut = lax.dynamic_slice(
                ordered("c" + tag, qkv_weight, known), (start + side * rows, WIDTH), (rows, 2 * WIDTH)
            )
            known["c" + tag] = cut
            direct = swap(cut, "fsdp", bit)
            known["x" + tag] = direct
            across = swap(ordered("f" + tag, direct, known), "fsdp", 1)
            known["f" + tag] = across
            passed = ordered("p" + tag, swap(ordered("y" + tag, direct, known), "seq", 1 << number), known)
            known["y" + tag] = passed
            mine_rows += [direct, passed]
            other_rows += [across, swap(passed, "fsdp", 1)]
            known["q" + tag] = other_rows[-1]
        known["meta"] = meta
        cut = ordered("cD", qkv_weight, known)[direct_from:, WIDTH:]
        known["cD"] = cut
        rest = swap(cut, "fsdp", bit)
        known["xD"] = rest
        rest = ordered("pD", rest, known)
        known["fD"] = swap(rest, "fsdp", 1)
        direct_rows.append(mine_rows + [rest] + other_rows + [known["fD"]])
        cut = ordered("cQ", qkv_weight, known)[:, :WIDTH]
        known["cQ"] = cut
        queries.append(swap(cut, "fsdp", bit))
    assert len(bits) <= 1
    if bits:
        bit = bits[0]
        count = len(direct_rows[0]) // 2
        layout = [offsets_at + i for i in range(count)]
        *sums, joined = call(
            functools.partial(first_rows_kernel, layout, bit, slots, slot_at),
            [sequence, ordered("a", partial, known), *direct_rows[0][:count]],
            [shape((BLOCK, 2 * WIDTH), F32)] * slots + [shape((share, 2 * WIDTH), BF16)],
            "project_first",
        )
        *packs, joined_other = call(
            functools.partial(last_rows_kernel, layout, bit ^ 1, slots, slot_at),
            [sequence, *sums, *direct_rows[0][count:]],
            [shape((BLOCK, 2 * WIDTH), BF16)] * slots + [shape((share, 2 * WIDTH), BF16)],
            "project_pack",
        )
        known["pack"] = packs[0]
        (kv,) = call(
            functools.partial(kv_kernel, [bit, bit ^ 1]),
            [sequence, ordered("kv", partial, known), joined, joined_other],
            [shape((row_count, 2 * WIDTH), BF16)],
            "project_kv",
        )
    else:
        kv = partial[:, WIDTH:].astype(BF16)
        blocks = kv.reshape(block_rate, BLOCK, 2, HEADS, HEAD_DIM)
        packs = []
        for offset in (near_offset, far_offset % block_rate)[:slots]:
            picked = blocks[offset, :, :, jnp.arange(HEADS)]
            packs.append(picked.transpose(1, 2, 0, 3).reshape(BLOCK, 2 * WIDTH))
    known["kv"] = kv
    received = []
    for pack, place, count, unit in zip(packs, (near_at, far_at), shifts, (1, STRIDE)):
        for step in NEAR_ORDER if count == len(NEAR_ORDER) else range(1, count + 1):
            received.append((step, lax.ppermute(pack, "seq", partners(seq_size, place, step))))
        known |= {f"n{step}": r for step, r in received}
    steps = [step for step, _ in received]
    received = [pack for _, pack in received]
    crossed_q, q_places = [], []
    for bit, direct in zip(bits, queries):
        direct = ordered("q", direct, known)
        passing = [share * 15 // 32 // 16 * 16] * 2
        left = share - sum(passing)
        *parts, slots_out = call(
            functools.partial(slot_kernel, core_at),
            [direct],
            [shape((rows, WIDTH), BF16) for rows in passing] + [shape((2, left, WIDTH), BF16)],
            "slot_queries",
        )
        both = lax.all_to_all(
            slots_out, "fsdp", 0, 0, axis_index_groups=[[i, i + 1] for i in range(0, pieces, 2)]
        )
        crossed_q += [direct, both] + [swap(part, "fsdp", 1) for part in parts]
        q_places += [bit, bit ^ 1]
    state_types = [BF16, F32, F32, F32]
    partial_out, *state = call(
        functools.partial(attend_kernel, len(crossed_q), q_places, core_at, slots, slot_at, match_at),
        [sequence, partial, *crossed_q, kv],
        [shape((row_count, WIDTH), BF16)] + [shape((BLOCK, WIDTH), kind) for kind in state_types] * slots,
        "attend_local",
        [pltpu.VMEM((row_count, WIDTH), kind) for kind in state_types]
        + [pltpu.VMEM((share, WIDTH), BF16)],
    )
    count = 4 * slots + sum(shifts)
    merged = pl.pallas_call(
        functools.partial(merge_kernel, shifts, steps, slot_at, match_at, place_at),
        in_specs=[scalar_spec] + [whole] * count + [pl.BlockSpec(memory_space=pl.ANY)],
        out_specs=pl.BlockSpec(memory_space=pl.ANY),
        out_shape=shape((row_count, WIDTH), BF16),
        scratch_shapes=[pltpu.VMEM((slots, BLOCK, WIDTH), BF16), pltpu.SemaphoreType.DMA((HEADS,))],
        input_output_aliases={count + 1: 0},
        compiler_params=pltpu.CompilerParams(vmem_limit_bytes=VMEM_LIMIT),
        cost_estimate=pl.CostEstimate(flops=MODEL_FLOPS["merge_near"], bytes_accessed=1000, transcendentals=0),
        name="merge_near",
    )(meta, *state, *received, partial_out)
    return merged[None]


def solution(mesh):
    in_specs = (P("fsdp", "seq", None), P("fsdp", None), P(), P())
    out_specs = P("fsdp", "seq", None)
    return jax.shard_map(body, mesh=mesh, in_specs=in_specs, out_specs=out_specs, check_vma=False)
```

```python
import functools
import math

import jax
import jax.numpy as jnp
from jax import lax
from jax.experimental import pallas as pl
from jax.experimental.pallas import tpu as pltpu
from jax.sharding import PartitionSpec as P

HEADS = 4
HEAD_DIM = 128
BLOCK = 128
STRIDE = 8
WIDTH = HEADS * HEAD_DIM
PAIR = 2 * HEAD_DIM
NEG = -1e30
SCALE2 = HEAD_DIM ** (-0.5) * math.log2(math.e)
VMEM_LIMIT = 24 * 1024 * 1024

MODEL_FLOPS = {"project_first": 689999, "split_queries": 575000, "project_pack": 689999, "project_own": 3680000, "project_mid": 1610000, "project_kv": 2990000, "attend_local": 6325000, "merge_near": 2990000}
ORDER = {
    'c1': ('c0',),
    'cD': ('c1',),
    'cQ': ('cD',),
    'p0': ('partial', 'xD'),
    'p1': ('partial',),
    'q': ('kv',),
    'kv': ('pack',),
}
NEAR_ORDER = (3, 1, 2)
F32 = jnp.float32
BF16 = jnp.bfloat16


def near_place(index, half, size):
    if index < half:
        return 0, index
    return 1 + (index - half) // size, (index - half) % size


def partners(count, place, bits):
    where = {place(i): i for i in range(count)}
    pairs = []
    for source in range(count):
        run, spot = place(source)
        one_bit = bits & (bits - 1) == 0
        if (run, spot ^ bits) in where and (one_bit or spot ^ bits > spot):
            pairs.append((source, where[run, spot ^ bits]))
    return pairs


def swap(value, axis, bit):
    count = lax.axis_size(axis)
    return lax.ppermute(value, axis, [(i, i ^ bit) for i in range(count)])


def after(value, *others):
    return lax.optimization_barrier((value,) + others)[0]


def ordered(name, value, known):
    others = [known[other] for other in ORDER.get(name, ()) if other in known]
    return after(value, *others) if others else value


def rows_of(block):
    return pl.ds(pl.multiple_of(block * BLOCK, BLOCK), BLOCK)


def qk(query, key):
    return lax.dot_general(query, key, (((1,), (1,)), ((), ())), preferred_element_type=F32)


def pv(weights, value):
    return jnp.dot(weights.astype(BF16), value, preferred_element_type=F32)


def add_up(tokens, places, weights):
    total = None
    for place, weight in zip(places, weights):
        depth = weight.shape[0]
        columns = pl.ds(pl.multiple_of(place, depth), depth)
        term = jnp.dot(tokens[:, columns], weight[...], preferred_element_type=F32)
        total = term if total is None else total + term
    return total


def own_kernel(count, meta, tokens, *refs):
    weights, out = refs[:count], refs[count]
    for j in range(out.shape[1] // PAIR):
        lanes = slice(j * PAIR, (j + 1) * PAIR)
        out[:, lanes] = add_up(tokens, [meta[at] for at in range(count)], [weight.at[:, lanes] for weight in weights])


def near_rows_kernel(layout, place_at, first, slots, slot_at, meta, tokens, before, *refs):
    arrived, refs = refs[: len(layout)], refs[len(layout) :]
    sums, joined = refs[:slots], refs[slots]
    for at, array in zip(layout, arrived):
        rows = array.shape[0]
        joined[pl.ds(pl.multiple_of(meta[at], rows), rows), :] = array[...]
    depth = joined.shape[0]
    columns = pl.ds(pl.multiple_of(meta[place_at], depth), depth)
    for slot in range(slots):
        for head in range(HEADS):
            rows = rows_of(meta[slot_at + HEADS * slot + head])
            lanes = [slice(start, start + HEAD_DIM) for start in (head * HEAD_DIM, WIDTH + head * HEAD_DIM)]
            weight = jnp.concatenate([joined[:, part] for part in lanes], axis=1)
            product = jnp.dot(tokens[rows, columns], weight, preferred_element_type=F32)
            for field, part in enumerate(lanes):
                if first:
                    total = before[0][rows, WIDTH + part.start : WIDTH + part.stop]
                else:
                    total = before[slot][:, part]
                total = total + product[:, field * HEAD_DIM : (field + 1) * HEAD_DIM]
                sums[slot][:, part] = total.astype(sums[slot].dtype)


def first_rows_kernel(layout, place_at, slots, slot_at, meta, tokens, partial, *refs):
    near_rows_kernel(layout, place_at, True, slots, slot_at, meta, tokens, [partial], *refs)


def last_rows_kernel(layout, place_at, slots, slot_at, meta, tokens, *refs):
    near_rows_kernel(layout, place_at, False, slots, slot_at, meta, tokens, refs[:slots], *refs[slots:])


def split_kernel(meta, source, *outs):
    done = 0
    for out in outs:
        rows = out.shape[0]
        out[...] = source[done : done + rows, :]
        done += rows


def kv_kernel(places_at, meta, tokens, partial, *refs):
    parts, kv = refs[:-1], refs[-1]
    places = [meta[at] for at in places_at]
    for j in range(2 * WIDTH // PAIR):
        lanes = slice(j * PAIR, (j + 1) * PAIR)
        product = add_up(tokens, places, [part.at[:, lanes] for part in parts])
        kv[:, lanes] = (partial[:, WIDTH + j * PAIR : WIDTH + (j + 1) * PAIR] + product).astype(BF16)


def with_ones(value):
    return jnp.concatenate([value, jnp.ones(value.shape, BF16)], axis=1)


def attend_kernel(count, bases_at, slots, slot_at, match_at, meta, tokens, partial, *refs):
    weights, refs = refs[:count], refs[count:]
    kv, out, refs = refs[0], refs[1], refs[2:]
    state, scratch, joined = refs[: 4 * slots], refs[4 * slots : -1], refs[-1]
    query, acc_all, top_all, sum_all = scratch
    blocks = query.shape[0] // BLOCK
    GROUP = 2 if blocks % 2 == 0 else 1
    row = lax.broadcasted_iota(jnp.int32, (BLOCK, BLOCK), 0)
    column = lax.broadcasted_iota(jnp.int32, (BLOCK, BLOCK), 1)
    causal = column <= row
    places = [meta[at] for at in bases_at]
    if weights:
        done = 0
        for weight in weights[1:]:
            joined[done : done + weight.shape[0], :] = weight[...]
            done += weight.shape[0]
        if done < joined.shape[0]:
            joined[done:, :] = weights[0][joined.shape[0] :, :]
    for pair in range(HEADS // 2):
        lanes = slice(pair * PAIR, (pair + 1) * PAIR)
        total = partial[:, lanes]
        if weights:
            total = total + add_up(tokens, places, [weights[0].at[: joined.shape[0], lanes], joined.at[:, lanes]])
        query[:, lanes] = total.astype(BF16)

    def lanes_of(head):
        return slice(head * HEAD_DIM, (head + 1) * HEAD_DIM)

    def rows_at(b):
        return slice(b * BLOCK, (b + 1) * BLOCK)

    def score(head, group):
        first, last = group * GROUP, (group + 1) * GROUP
        rows = slice(first * BLOCK, last * BLOCK)
        return qk(query[rows, lanes_of(head)], kv[: last * BLOCK, lanes_of(head)])

    def weigh(head, group, scores):
        near_block = meta[slot_at + head]
        far_block = meta[slot_at + HEADS + head]
        tops, weights = [], []
        for i in range(GROUP):
            b = group * GROUP + i
            mine = scores[rows_at(i)]
            times = (
                1
                + jnp.where(near_block == b, 1, 0)
                + jnp.where(far_block == b, meta[match_at + head], 0)
            ).astype(F32)
            diagonal = jnp.where(causal, mine[:, rows_at(b)], NEG)
            top = jnp.max(diagonal, axis=1, keepdims=True)
            if b:
                top = jnp.maximum(top, jnp.max(mine[:, : b * BLOCK], axis=1, keepdims=True))
            parts = [(jnp.exp2((diagonal - top) * SCALE2) * times).astype(BF16)]
            if b:
                parts.insert(0, jnp.exp2((mine[:, : b * BLOCK] - top) * SCALE2).astype(BF16))
            if i < GROUP - 1:
                parts.append(jnp.zeros((BLOCK, (GROUP - 1 - i) * BLOCK), BF16))
            tops.append(top)
            weights.append(jnp.concatenate(parts, axis=1))
        return tops, jnp.concatenate(weights, axis=0)

    def finish(head, group, tops, weight):
        lanes = lanes_of(head)
        keys = (group + 1) * GROUP * BLOCK
        value = kv[:keys, WIDTH + head * HEAD_DIM : WIDTH + (head + 1) * HEAD_DIM]
        both = jnp.dot(weight, with_ones(value), preferred_element_type=F32)
        rows = slice(group * GROUP * BLOCK, keys)
        acc, summed = both[:, :HEAD_DIM], both[:, HEAD_DIM:]
        out[rows, lanes] = (acc / summed).astype(BF16)
        acc_all[rows, lanes] = acc
        sum_all[rows, lanes] = summed
        for i, top in enumerate(tops):
            top_all[rows_at(group * GROUP + i), lanes] = jnp.broadcast_to(top, (BLOCK, HEAD_DIM))
        if group == blocks // GROUP - 1:
            for slot in range(slots):
                rows = rows_of(meta[slot_at + slot * HEADS + head])
                for target, source in zip(state[4 * slot :], scratch):
                    target[:, lanes] = source[rows, lanes]

    tasks = [(head, group) for head in range(HEADS) for group in range(blocks // GROUP)]
    scored, weighed = {}, {}
    for step in range(len(tasks) + 2):
        if step < len(tasks):
            scored[step] = score(*tasks[step])
        if 0 <= step - 1 < len(tasks):
            weighed[step - 1] = weigh(*tasks[step - 1], scored.pop(step - 1))
        if 0 <= step - 2 < len(tasks):
            finish(*tasks[step - 2], *weighed.pop(step - 2))


def merge_kernel(shifts, steps, slot_at, match_at, place_at, meta, *refs):
    slots = len(shifts)
    state = refs[: 4 * slots]
    packs = refs[4 * slots : 4 * slots + sum(shifts)]
    out, results, sems = refs[4 * slots + sum(shifts) + 1 :]
    if slots == 1:
        pl.when(meta[place_at] > 0)(lambda: merge_slots(
            shifts, steps, slot_at, match_at, place_at, meta, state, packs, out, results, sems
        ))
    else:
        merge_slots(shifts, steps, slot_at, match_at, place_at, meta, state, packs, out, results, sems)


def merge_slots(shifts, steps, slot_at, match_at, place_at, meta, state, packs, out, results, sems):
    lanes = [slice(head * HEAD_DIM, (head + 1) * HEAD_DIM) for head in range(HEADS)]
    values = [slice(WIDTH + head * HEAD_DIM, WIDTH + (head + 1) * HEAD_DIM) for head in range(HEADS)]
    earlier = [None] * HEADS
    for slot, count in enumerate(shifts):
        fields = packs[sum(shifts[:slot]) : sum(shifts[: slot + 1])]
        query, acc_ref, top_ref, sum_ref = state[4 * slot : 4 * slot + 4]
        place = meta[place_at + slot]
        scores, weights = [], []
        for head in range(HEADS):
            keys = jnp.concatenate([field[:, lanes[head]] for field in fields], axis=0)
            score = qk(query[:, lanes[head]], keys)
            parts = []
            for number, step in enumerate(steps[sum(shifts[:slot]) : sum(shifts[: slot + 1])]):
                seen = place ^ step < place
                if slot:
                    seen = seen & (meta[match_at + head] == 1)
                part = score[:, number * BLOCK : (number + 1) * BLOCK]
                parts.append(jnp.where(seen, part, NEG))
            scores.append(jnp.concatenate(parts, axis=1))
        for head in range(HEADS):
            acc, top, summed = (ref[:, lanes[head]] for ref in (acc_ref, top_ref, sum_ref))
            if slot:
                same = meta[slot_at + head] == meta[slot_at + HEADS + head]
                acc, top, summed = (
                    jnp.where(same, new, old) for new, old in zip(earlier[head], (acc, top, summed))
                )
            best = jnp.maximum(top, jnp.max(scores[head], axis=1, keepdims=True))
            decay = jnp.exp2((top - best) * SCALE2)
            weight = jnp.exp2((scores[head] - best[:, :1]) * SCALE2).astype(BF16)
            weights.append((acc * decay, best, summed * decay, weight))
        copies = []
        for head in range(HEADS):
            acc, best, summed, weight = weights[head]
            value = jnp.concatenate([field[:, values[head]] for field in fields], axis=0)
            both = jnp.dot(weight, with_ones(value), preferred_element_type=F32)
            acc = acc + both[:, :HEAD_DIM]
            summed = summed + both[:, HEAD_DIM:]
            earlier[head] = (acc, best, summed)
            results[slot, :, lanes[head]] = (acc / summed).astype(BF16)
            rows = rows_of(meta[slot_at + slot * HEADS + head])
            copies.append(
                pltpu.make_async_copy(
                    results.at[slot, :, lanes[head]], out.at[rows, lanes[head]], sems.at[head]
                )
            )
            copies[-1].start()
        for copy in copies:
            copy.wait()


def body(tokens, qkv_weight, near_offset, far_offset):
    sequence = tokens[0]
    row_count, depth = sequence.shape
    share = qkv_weight.shape[0]
    block_rate = row_count // BLOCK
    seq_size = lax.axis_size("seq")
    seq_index = lax.axis_index("seq")
    pieces = lax.axis_size("fsdp")
    mine = lax.axis_index("fsdp")
    near_size = min(16, seq_size)
    half = near_size // 2
    far_size = max(1, min(16, seq_size // STRIDE))
    near_at = lambda i: near_place(i, half, near_size)
    far_at = lambda i: (i // (STRIDE * far_size) * STRIDE + i % STRIDE, i // STRIDE % far_size)
    reach = max(near_at(i)[1] for i in range(seq_size))
    near_shifts = (1 << reach.bit_length()) - 1
    far_shifts = (1 << (far_size - 1).bit_length()) - 1
    slots = 2 if far_shifts else 1
    shifts = (near_shifts, far_shifts)[:slots]

    near_position = jnp.where(seq_index < half, seq_index, (seq_index - half) % near_size)
    far_position = seq_index // STRIDE % far_size
    far_match = (seq_index % STRIDE == far_offset // block_rate).astype(jnp.int32)
    spans = [(0, share // 4), (share // 2, share // 8)] if seq_size % 4 == 0 else []
    direct_from = spans[-1][0] + 2 * spans[-1][1] if spans else 0
    full_places = [(mine ^ j) * share for j in range(pieces)]
    scalars = list(full_places)
    place_at = len(scalars)
    scalars += [near_position, far_position]
    base_at = len(scalars)
    scalars += [(mine ^ bit) // 2 * 2 * share for bit in range(2, pieces, 2)]
    core_at = len(scalars)
    scalars.append(mine % 2)
    slot_at = len(scalars)
    match_at = slot_at + 2 * HEADS
    offsets_at = match_at + HEADS
    offsets = []
    for number, (start, rows) in enumerate(spans):
        side = seq_index // (1 << number) % 2
        offsets += [start + side * rows, start + (1 - side) * rows]
    offsets.append(direct_from)
    as_array = lambda values: jnp.stack([jnp.asarray(value, jnp.int32) for value in values])
    meta = jnp.concatenate(
        [as_array(scalars), near_offset, far_offset % block_rate, far_match, as_array(offsets)]
    )

    scalar_spec = pl.BlockSpec(memory_space=pltpu.SMEM)
    whole = pl.BlockSpec(memory_space=pltpu.VMEM)
    shape = jax.ShapeDtypeStruct

    def call(kernel, args, results, name, scratch=()):
        return pl.pallas_call(
            kernel,
            in_specs=[scalar_spec] + [whole] * len(args),
            out_specs=[whole] * len(results),
            out_shape=results,
            scratch_shapes=list(scratch),
            compiler_params=pltpu.CompilerParams(vmem_limit_bytes=VMEM_LIMIT),
            cost_estimate=pl.CostEstimate(flops=MODEL_FLOPS[name], bytes_accessed=1000, transcendentals=0),
            name=name,
        )(meta, *args)

    passing = [share * 15 // 32 // 16 * 16] * 2
    local = [qkv_weight]
    bits = range(2, pieces, 2)
    known = {}
    if pieces > 1:
        local.append(swap(qkv_weight, "fsdp", 1))
        known["core"] = local[-1]
    (partial,) = call(
        functools.partial(own_kernel, len(local)),
        [ordered("t", sequence, known), *local],
        [shape((row_count, 3 * WIDTH), F32)],
        "project_own",
    )
    known["partial"] = partial
    direct_rows, queries = [], []
    for bit in bits:
        mine_rows, other_rows = [], []
        for number, (start, rows) in enumerate(spans):
            tag = str(number)
            side = seq_index // (1 << number) % 2
            cut = lax.dynamic_slice(
                ordered("c" + tag, qkv_weight, known), (start + side * rows, WIDTH), (rows, 2 * WIDTH)
            )
            known["c" + tag] = cut
            direct = swap(cut, "fsdp", bit)
            known["x" + tag] = direct
            across = swap(ordered("f" + tag, direct, known), "fsdp", 1)
            known["f" + tag] = across
            passed = ordered("p" + tag, swap(ordered("y" + tag, direct, known), "seq", 1 << number), known)
            known["y" + tag] = passed
            mine_rows += [direct, passed]
            other_rows += [across, swap(passed, "fsdp", 1)]
            known["q" + tag] = other_rows[-1]
        known["meta"] = meta
        cut = ordered("cD", qkv_weight, known)[direct_from:, WIDTH:]
        known["cD"] = cut
        rest = swap(cut, "fsdp", bit)
        known["xD"] = rest
        rest = ordered("pD", rest, known)
        known["fD"] = swap(rest, "fsdp", 1)
        direct_rows.append(mine_rows + [rest] + other_rows + [known["fD"]])
        cut = ordered("cQ", qkv_weight, known)[:, :WIDTH]
        left = share - sum(passing)
        if left:
            cut = jnp.concatenate([cut, known["core"][share - left :, :WIDTH]], axis=0)
        known["cQ"] = cut
        queries.append(swap(cut, "fsdp", bit))
    assert len(bits) <= 1
    if bits:
        bit = bits[0]
        count = len(direct_rows[0]) // 2
        layout = [offsets_at + i for i in range(count)]
        *sums, joined = call(
            functools.partial(first_rows_kernel, layout, bit, slots, slot_at),
            [sequence, ordered("a", partial, known), *direct_rows[0][:count]],
            [shape((BLOCK, 2 * WIDTH), F32)] * slots + [shape((share, 2 * WIDTH), BF16)],
            "project_first",
        )
        *packs, joined_other = call(
            functools.partial(last_rows_kernel, layout, bit ^ 1, slots, slot_at),
            [sequence, *sums, *direct_rows[0][count:]],
            [shape((BLOCK, 2 * WIDTH), BF16)] * slots + [shape((share, 2 * WIDTH), BF16)],
            "project_pack",
        )
        known["pack"] = packs[0]
        (kv,) = call(
            functools.partial(kv_kernel, [bit, bit ^ 1]),
            [sequence, ordered("kv", partial, known), joined, joined_other],
            [shape((row_count, 2 * WIDTH), BF16)],
            "project_kv",
        )
    else:
        kv = partial[:, WIDTH:].astype(BF16)
        blocks = kv.reshape(block_rate, BLOCK, 2, HEADS, HEAD_DIM)
        packs = []
        for offset in (near_offset, far_offset % block_rate)[:slots]:
            picked = blocks[offset, :, :, jnp.arange(HEADS)]
            packs.append(picked.transpose(1, 2, 0, 3).reshape(BLOCK, 2 * WIDTH))
    known["kv"] = kv
    received = []
    for pack, place, count, unit in zip(packs, (near_at, far_at), shifts, (1, STRIDE)):
        for step in NEAR_ORDER if count == len(NEAR_ORDER) else range(1, count + 1):
            received.append((step, lax.ppermute(pack, "seq", partners(seq_size, place, step))))
        known |= {f"n{step}": r for step, r in received}
    steps = [step for step, _ in received]
    received = [pack for _, pack in received]
    crossed_q, q_places = [], []
    for bit, direct in zip(bits, queries):
        direct = ordered("q", direct, known)
        parts = call(
            split_kernel,
            [direct],
            [shape((rows, WIDTH), BF16) for rows in passing],
            "split_queries",
        )
        crossed_q += [direct] + [swap(part, "fsdp", 1) for part in parts]
        q_places += [bit, bit ^ 1]
    state_types = [BF16, F32, F32, F32]
    partial_out, *state = call(
        functools.partial(attend_kernel, len(crossed_q), q_places, slots, slot_at, match_at),
        [sequence, partial, *crossed_q, kv],
        [shape((row_count, WIDTH), BF16)] + [shape((BLOCK, WIDTH), kind) for kind in state_types] * slots,
        "attend_local",
        [pltpu.VMEM((row_count, WIDTH), kind) for kind in state_types]
        + [pltpu.VMEM((share, WIDTH), BF16)],
    )
    count = 4 * slots + sum(shifts)
    merged = pl.pallas_call(
        functools.partial(merge_kernel, shifts, steps, slot_at, match_at, place_at),
        in_specs=[scalar_spec] + [whole] * count + [pl.BlockSpec(memory_space=pl.ANY)],
        out_specs=pl.BlockSpec(memory_space=pl.ANY),
        out_shape=shape((row_count, WIDTH), BF16),
        scratch_shapes=[pltpu.VMEM((slots, BLOCK, WIDTH), BF16), pltpu.SemaphoreType.DMA((HEADS,))],
        input_output_aliases={count + 1: 0},
        compiler_params=pltpu.CompilerParams(vmem_limit_bytes=VMEM_LIMIT),
        cost_estimate=pl.CostEstimate(flops=MODEL_FLOPS["merge_near"], bytes_accessed=1000, transcendentals=0),
        name="merge_near",
    )(meta, *state, *received, partial_out)
    return merged[None]


def solution(mesh):
    in_specs = (P("fsdp", "seq", None), P("fsdp", None), P(), P())
    out_specs = P("fsdp", "seq", None)
    return jax.shard_map(body, mesh=mesh, in_specs=in_specs, out_specs=out_specs, check_vma=False)
```

```python
import functools
import math

import jax
import jax.numpy as jnp
from jax import lax
from jax.experimental import pallas as pl
from jax.experimental.pallas import tpu as pltpu
from jax.sharding import PartitionSpec as P

HEADS = 4
HEAD_DIM = 128
BLOCK = 128
STRIDE = 8
WIDTH = HEADS * HEAD_DIM
PAIR = 2 * HEAD_DIM
NEG = -1e30
SCALE2 = HEAD_DIM ** (-0.5) * math.log2(math.e)
VMEM_LIMIT = 24 * 1024 * 1024

MODEL_FLOPS = {"project_first": 689999, "split_queries": 575000, "project_pack": 689999, "project_own": 3680000, "project_mid": 1610000, "project_kv": 2990000, "attend_local": 6325000, "merge_near": 2990000}
ORDER = {
    'p0': ('partial', 'xD'),
    'p1': ('partial',),
    'q': ('kv',),
    'kv': ('pack',),
}
NEAR_ORDER = (3, 1, 2)
F32 = jnp.float32
BF16 = jnp.bfloat16


def near_place(index, half, size):
    if index < half:
        return 0, index
    return 1 + (index - half) // size, (index - half) % size


def partners(count, place, bits):
    where = {place(i): i for i in range(count)}
    pairs = []
    for source in range(count):
        run, spot = place(source)
        one_bit = bits & (bits - 1) == 0
        if (run, spot ^ bits) in where and (one_bit or spot ^ bits > spot):
            pairs.append((source, where[run, spot ^ bits]))
    return pairs


def swap(value, axis, bit):
    count = lax.axis_size(axis)
    return lax.ppermute(value, axis, [(i, i ^ bit) for i in range(count)])


def after(value, *others):
    return lax.optimization_barrier((value,) + others)[0]


def ordered(name, value, known):
    others = [known[other] for other in ORDER.get(name, ()) if other in known]
    return after(value, *others) if others else value


def rows_of(block):
    return pl.ds(pl.multiple_of(block * BLOCK, BLOCK), BLOCK)


def qk(query, key):
    return lax.dot_general(query, key, (((1,), (1,)), ((), ())), preferred_element_type=F32)


def pv(weights, value):
    return jnp.dot(weights.astype(BF16), value, preferred_element_type=F32)


def add_up(tokens, places, weights):
    total = None
    for place, weight in zip(places, weights):
        depth = weight.shape[0]
        columns = pl.ds(pl.multiple_of(place, depth), depth)
        term = jnp.dot(tokens[:, columns], weight[...], preferred_element_type=F32)
        total = term if total is None else total + term
    return total


def own_kernel(count, meta, tokens, *refs):
    weights, out = refs[:count], refs[count]
    for j in range(out.shape[1] // PAIR):
        lanes = slice(j * PAIR, (j + 1) * PAIR)
        out[:, lanes] = add_up(tokens, [meta[at] for at in range(count)], [weight.at[:, lanes] for weight in weights])


def near_rows_kernel(layout, place_at, first, slots, slot_at, meta, tokens, before, *refs):
    arrived, refs = refs[: len(layout)], refs[len(layout) :]
    sums, joined = refs[:slots], refs[slots]
    for at, array in zip(layout, arrived):
        rows = array.shape[0]
        joined[pl.ds(pl.multiple_of(meta[at], rows), rows), :] = array[...]
    depth = joined.shape[0]
    columns = pl.ds(pl.multiple_of(meta[place_at], depth), depth)
    for slot in range(slots):
        for head in range(HEADS):
            rows = rows_of(meta[slot_at + HEADS * slot + head])
            lanes = [slice(start, start + HEAD_DIM) for start in (head * HEAD_DIM, WIDTH + head * HEAD_DIM)]
            weight = jnp.concatenate([joined[:, part] for part in lanes], axis=1)
            product = jnp.dot(tokens[rows, columns], weight, preferred_element_type=F32)
            for field, part in enumerate(lanes):
                if first:
                    total = before[0][rows, WIDTH + part.start : WIDTH + part.stop]
                else:
                    total = before[slot][:, part]
                total = total + product[:, field * HEAD_DIM : (field + 1) * HEAD_DIM]
                sums[slot][:, part] = total.astype(sums[slot].dtype)


def first_rows_kernel(layout, place_at, slots, slot_at, meta, tokens, partial, *refs):
    near_rows_kernel(layout, place_at, True, slots, slot_at, meta, tokens, [partial], *refs)


def last_rows_kernel(layout, place_at, slots, slot_at, meta, tokens, *refs):
    near_rows_kernel(layout, place_at, False, slots, slot_at, meta, tokens, refs[:slots], *refs[slots:])


def split_kernel(meta, source, *outs):
    done = 0
    for out in outs:
        rows = out.shape[0]
        out[...] = source[done : done + rows, :]
        done += rows


def kv_kernel(places_at, meta, tokens, partial, *refs):
    parts, kv = refs[:-1], refs[-1]
    places = [meta[at] for at in places_at]
    for j in range(2 * WIDTH // PAIR):
        lanes = slice(j * PAIR, (j + 1) * PAIR)
        product = add_up(tokens, places, [part.at[:, lanes] for part in parts])
        kv[:, lanes] = (partial[:, WIDTH + j * PAIR : WIDTH + (j + 1) * PAIR] + product).astype(BF16)


def with_ones(value):
    return jnp.concatenate([value, jnp.ones(value.shape, BF16)], axis=1)


def attend_kernel(count, bases_at, slots, slot_at, match_at, meta, tokens, partial, *refs):
    weights, refs = refs[:count], refs[count:]
    kv, out, refs = refs[0], refs[1], refs[2:]
    state, scratch, joined = refs[: 4 * slots], refs[4 * slots : -1], refs[-1]
    query, acc_all, top_all, sum_all = scratch
    blocks = query.shape[0] // BLOCK
    GROUP = 2 if blocks % 2 == 0 else 1
    row = lax.broadcasted_iota(jnp.int32, (BLOCK, BLOCK), 0)
    column = lax.broadcasted_iota(jnp.int32, (BLOCK, BLOCK), 1)
    causal = column <= row
    places = [meta[at] for at in bases_at]
    if weights:
        done = 0
        for weight in weights[1:]:
            joined[done : done + weight.shape[0], :] = weight[...]
            done += weight.shape[0]
        if done < joined.shape[0]:
            joined[done:, :] = weights[0][joined.shape[0] :, :]
    for pair in range(HEADS // 2):
        lanes = slice(pair * PAIR, (pair + 1) * PAIR)
        total = partial[:, lanes]
        if weights:
            total = total + add_up(tokens, places, [weights[0].at[: joined.shape[0], lanes], joined.at[:, lanes]])
        query[:, lanes] = total.astype(BF16)

    def lanes_of(head):
        return slice(head * HEAD_DIM, (head + 1) * HEAD_DIM)

    def rows_at(b):
        return slice(b * BLOCK, (b + 1) * BLOCK)

    def score(head, group):
        first, last = group * GROUP, (group + 1) * GROUP
        rows = slice(first * BLOCK, last * BLOCK)
        return qk(query[rows, lanes_of(head)], kv[: last * BLOCK, lanes_of(head)])

    def weigh(head, group, scores):
        near_block = meta[slot_at + head]
        far_block = meta[slot_at + HEADS + head]
        tops, weights = [], []
        for i in range(GROUP):
            b = group * GROUP + i
            mine = scores[rows_at(i)]
            times = (
                1
                + jnp.where(near_block == b, 1, 0)
                + jnp.where(far_block == b, meta[match_at + head], 0)
            ).astype(F32)
            diagonal = jnp.where(causal, mine[:, rows_at(b)], NEG)
            top = jnp.max(diagonal, axis=1, keepdims=True)
            if b:
                top = jnp.maximum(top, jnp.max(mine[:, : b * BLOCK], axis=1, keepdims=True))
            parts = [(jnp.exp2((diagonal - top) * SCALE2) * times).astype(BF16)]
            if b:
                parts.insert(0, jnp.exp2((mine[:, : b * BLOCK] - top) * SCALE2).astype(BF16))
            if i < GROUP - 1:
                parts.append(jnp.zeros((BLOCK, (GROUP - 1 - i) * BLOCK), BF16))
            tops.append(top)
            weights.append(jnp.concatenate(parts, axis=1))
        return tops, jnp.concatenate(weights, axis=0)

    def finish(head, group, tops, weight):
        lanes = lanes_of(head)
        keys = (group + 1) * GROUP * BLOCK
        value = kv[:keys, WIDTH + head * HEAD_DIM : WIDTH + (head + 1) * HEAD_DIM]
        both = jnp.dot(weight, with_ones(value), preferred_element_type=F32)
        rows = slice(group * GROUP * BLOCK, keys)
        acc, summed = both[:, :HEAD_DIM], both[:, HEAD_DIM:]
        out[rows, lanes] = (acc / summed).astype(BF16)
        acc_all[rows, lanes] = acc
        sum_all[rows, lanes] = summed
        for i, top in enumerate(tops):
            top_all[rows_at(group * GROUP + i), lanes] = jnp.broadcast_to(top, (BLOCK, HEAD_DIM))
        if group == blocks // GROUP - 1:
            for slot in range(slots):
                rows = rows_of(meta[slot_at + slot * HEADS + head])
                for target, source in zip(state[4 * slot :], scratch):
                    target[:, lanes] = source[rows, lanes]

    tasks = [(head, group) for head in range(HEADS) for group in range(blocks // GROUP)]
    scored, weighed = {}, {}
    for step in range(len(tasks) + 2):
        if step < len(tasks):
            scored[step] = score(*tasks[step])
        if 0 <= step - 1 < len(tasks):
            weighed[step - 1] = weigh(*tasks[step - 1], scored.pop(step - 1))
        if 0 <= step - 2 < len(tasks):
            finish(*tasks[step - 2], *weighed.pop(step - 2))


def merge_kernel(shifts, steps, slot_at, match_at, place_at, meta, *refs):
    slots = len(shifts)
    state = refs[: 4 * slots]
    packs = refs[4 * slots : 4 * slots + sum(shifts)]
    out, results, sems = refs[4 * slots + sum(shifts) + 1 :]
    if slots == 1:
        pl.when(meta[place_at] > 0)(lambda: merge_slots(
            shifts, steps, slot_at, match_at, place_at, meta, state, packs, out, results, sems
        ))
    else:
        merge_slots(shifts, steps, slot_at, match_at, place_at, meta, state, packs, out, results, sems)


def merge_slots(shifts, steps, slot_at, match_at, place_at, meta, state, packs, out, results, sems):
    lanes = [slice(head * HEAD_DIM, (head + 1) * HEAD_DIM) for head in range(HEADS)]
    values = [slice(WIDTH + head * HEAD_DIM, WIDTH + (head + 1) * HEAD_DIM) for head in range(HEADS)]
    earlier = [None] * HEADS
    for slot, count in enumerate(shifts):
        fields = packs[sum(shifts[:slot]) : sum(shifts[: slot + 1])]
        query, acc_ref, top_ref, sum_ref = state[4 * slot : 4 * slot + 4]
        place = meta[place_at + slot]
        scores, weights = [], []
        for head in range(HEADS):
            keys = jnp.concatenate([field[:, lanes[head]] for field in fields], axis=0)
            score = qk(query[:, lanes[head]], keys)
            parts = []
            for number, step in enumerate(steps[sum(shifts[:slot]) : sum(shifts[: slot + 1])]):
                seen = place ^ step < place
                if slot:
                    seen = seen & (meta[match_at + head] == 1)
                part = score[:, number * BLOCK : (number + 1) * BLOCK]
                parts.append(jnp.where(seen, part, NEG))
            scores.append(jnp.concatenate(parts, axis=1))
        for head in range(HEADS):
            acc, top, summed = (ref[:, lanes[head]] for ref in (acc_ref, top_ref, sum_ref))
            if slot:
                same = meta[slot_at + head] == meta[slot_at + HEADS + head]
                acc, top, summed = (
                    jnp.where(same, new, old) for new, old in zip(earlier[head], (acc, top, summed))
                )
            best = jnp.maximum(top, jnp.max(scores[head], axis=1, keepdims=True))
            decay = jnp.exp2((top - best) * SCALE2)
            weight = jnp.exp2((scores[head] - best[:, :1]) * SCALE2).astype(BF16)
            weights.append((acc * decay, best, summed * decay, weight))
        copies = []
        for head in range(HEADS):
            acc, best, summed, weight = weights[head]
            value = jnp.concatenate([field[:, values[head]] for field in fields], axis=0)
            both = jnp.dot(weight, with_ones(value), preferred_element_type=F32)
            acc = acc + both[:, :HEAD_DIM]
            summed = summed + both[:, HEAD_DIM:]
            earlier[head] = (acc, best, summed)
            results[slot, :, lanes[head]] = (acc / summed).astype(BF16)
            rows = rows_of(meta[slot_at + slot * HEADS + head])
            copies.append(
                pltpu.make_async_copy(
                    results.at[slot, :, lanes[head]], out.at[rows, lanes[head]], sems.at[head]
                )
            )
            copies[-1].start()
        for copy in copies:
            copy.wait()


def body(tokens, qkv_weight, near_offset, far_offset):
    sequence = tokens[0]
    row_count, depth = sequence.shape
    share = qkv_weight.shape[0]
    block_rate = row_count // BLOCK
    seq_size = lax.axis_size("seq")
    seq_index = lax.axis_index("seq")
    pieces = lax.axis_size("fsdp")
    mine = lax.axis_index("fsdp")
    near_size = min(16, seq_size)
    half = near_size // 2
    far_size = max(1, min(16, seq_size // STRIDE))
    near_at = lambda i: near_place(i, half, near_size)
    far_at = lambda i: (i // (STRIDE * far_size) * STRIDE + i % STRIDE, i // STRIDE % far_size)
    reach = max(near_at(i)[1] for i in range(seq_size))
    near_shifts = (1 << reach.bit_length()) - 1
    far_shifts = (1 << (far_size - 1).bit_length()) - 1
    slots = 2 if far_shifts else 1
    shifts = (near_shifts, far_shifts)[:slots]

    near_position = jnp.where(seq_index < half, seq_index, (seq_index - half) % near_size)
    far_position = seq_index // STRIDE % far_size
    far_match = (seq_index % STRIDE == far_offset // block_rate).astype(jnp.int32)
    spans = [(0, share // 4), (share // 2, share // 8)] if seq_size % 4 == 0 else []
    direct_from = spans[-1][0] + 2 * spans[-1][1] if spans else 0
    full_places = [(mine ^ j) * share for j in range(pieces)]
    scalars = list(full_places)
    place_at = len(scalars)
    scalars += [near_position, far_position]
    base_at = len(scalars)
    scalars += [(mine ^ bit) // 2 * 2 * share for bit in range(2, pieces, 2)]
    core_at = len(scalars)
    scalars.append(mine % 2)
    slot_at = len(scalars)
    match_at = slot_at + 2 * HEADS
    offsets_at = match_at + HEADS
    offsets = []
    for number, (start, rows) in enumerate(spans):
        side = seq_index // (1 << number) % 2
        offsets += [start + side * rows, start + (1 - side) * rows]
    offsets.append(direct_from)
    as_array = lambda values: jnp.stack([jnp.asarray(value, jnp.int32) for value in values])
    meta = jnp.concatenate(
        [as_array(scalars), near_offset, far_offset % block_rate, far_match, as_array(offsets)]
    )

    scalar_spec = pl.BlockSpec(memory_space=pltpu.SMEM)
    whole = pl.BlockSpec(memory_space=pltpu.VMEM)
    shape = jax.ShapeDtypeStruct

    def call(kernel, args, results, name, scratch=()):
        return pl.pallas_call(
            kernel,
            in_specs=[scalar_spec] + [whole] * len(args),
            out_specs=[whole] * len(results),
            out_shape=results,
            scratch_shapes=list(scratch),
            compiler_params=pltpu.CompilerParams(vmem_limit_bytes=VMEM_LIMIT),
            cost_estimate=pl.CostEstimate(flops=MODEL_FLOPS[name], bytes_accessed=1000, transcendentals=0),
            name=name,
        )(meta, *args)

    passing = [share * 15 // 32 // 16 * 16] * 2
    local = [qkv_weight]
    bits = range(2, pieces, 2)
    known = {}
    if pieces > 1:
        local.append(swap(qkv_weight, "fsdp", 1))
        known["core"] = local[-1]
    (partial,) = call(
        functools.partial(own_kernel, len(local)),
        [ordered("t", sequence, known), *local],
        [shape((row_count, 3 * WIDTH), F32)],
        "project_own",
    )
    known["partial"] = partial
    direct_rows, queries = [], []
    for bit in bits:
        mine_rows, other_rows = [], []
        for number, (start, rows) in enumerate(spans):
            tag = str(number)
            side = seq_index // (1 << number) % 2
            cut = lax.dynamic_slice(
                ordered("c" + tag, qkv_weight, known), (start + side * rows, WIDTH), (rows, 2 * WIDTH)
            )
            known["c" + tag] = cut
            direct = swap(cut, "fsdp", bit)
            known["x" + tag] = direct
            across = swap(ordered("f" + tag, direct, known), "fsdp", 1)
            known["f" + tag] = across
            passed = ordered("p" + tag, swap(ordered("y" + tag, direct, known), "seq", 1 << number), known)
            known["y" + tag] = passed
            mine_rows += [direct, passed]
            other_rows += [across, swap(passed, "fsdp", 1)]
            known["q" + tag] = other_rows[-1]
        known["meta"] = meta
        cut = ordered("cD", qkv_weight, known)[direct_from:, WIDTH:]
        known["cD"] = cut
        rest = swap(cut, "fsdp", bit)
        known["xD"] = rest
        rest = ordered("pD", rest, known)
        known["fD"] = swap(rest, "fsdp", 1)
        direct_rows.append(mine_rows + [rest] + other_rows + [known["fD"]])
        cut = ordered("cQ", qkv_weight, known)[:, :WIDTH]
        left = share - sum(passing)
        if left:
            cut = jnp.concatenate([cut, known["core"][share - left :, :WIDTH]], axis=0)
        known["cQ"] = cut
        queries.append(swap(cut, "fsdp", bit))
    assert len(bits) <= 1
    if bits:
        bit = bits[0]
        count = len(direct_rows[0]) // 2
        layout = [offsets_at + i for i in range(count)]
        *sums, joined = call(
            functools.partial(first_rows_kernel, layout, bit, slots, slot_at),
            [sequence, ordered("a", partial, known), *direct_rows[0][:count]],
            [shape((BLOCK, 2 * WIDTH), F32)] * slots + [shape((share, 2 * WIDTH), BF16)],
            "project_first",
        )
        *packs, joined_other = call(
            functools.partial(last_rows_kernel, layout, bit ^ 1, slots, slot_at),
            [sequence, *sums, *direct_rows[0][count:]],
            [shape((BLOCK, 2 * WIDTH), BF16)] * slots + [shape((share, 2 * WIDTH), BF16)],
            "project_pack",
        )
        known["pack"] = packs[0]
        (kv,) = call(
            functools.partial(kv_kernel, [bit, bit ^ 1]),
            [sequence, ordered("kv", partial, known), joined, joined_other],
            [shape((row_count, 2 * WIDTH), BF16)],
            "project_kv",
        )
    else:
        kv = partial[:, WIDTH:].astype(BF16)
        blocks = kv.reshape(block_rate, BLOCK, 2, HEADS, HEAD_DIM)
        packs = []
        for offset in (near_offset, far_offset % block_rate)[:slots]:
            picked = blocks[offset, :, :, jnp.arange(HEADS)]
            packs.append(picked.transpose(1, 2, 0, 3).reshape(BLOCK, 2 * WIDTH))
    known["kv"] = kv
    received = []
    for pack, place, count, unit in zip(packs, (near_at, far_at), shifts, (1, STRIDE)):
        for step in NEAR_ORDER if count == len(NEAR_ORDER) else range(1, count + 1):
            received.append((step, lax.ppermute(pack, "seq", partners(seq_size, place, step))))
        known |= {f"n{step}": r for step, r in received}
    steps = [step for step, _ in received]
    received = [pack for _, pack in received]
    crossed_q, q_places = [], []
    for bit, direct in zip(bits, queries):
        direct = ordered("q", direct, known)
        parts = call(
            split_kernel,
            [direct],
            [shape((rows, WIDTH), BF16) for rows in passing],
            "split_queries",
        )
        crossed_q += [direct] + [swap(part, "fsdp", 1) for part in parts]
        q_places += [bit, bit ^ 1]
    state_types = [BF16, F32, F32, F32]
    partial_out, *state = call(
        functools.partial(attend_kernel, len(crossed_q), q_places, slots, slot_at, match_at),
        [sequence, partial, *crossed_q, kv],
        [shape((row_count, WIDTH), BF16)] + [shape((BLOCK, WIDTH), kind) for kind in state_types] * slots,
        "attend_local",
        [pltpu.VMEM((row_count, WIDTH), kind) for kind in state_types]
        + [pltpu.VMEM((share, WIDTH), BF16)],
    )
    count = 4 * slots + sum(shifts)
    merged = pl.pallas_call(
        functools.partial(merge_kernel, shifts, steps, slot_at, match_at, place_at),
        in_specs=[scalar_spec] + [whole] * count + [pl.BlockSpec(memory_space=pl.ANY)],
        out_specs=pl.BlockSpec(memory_space=pl.ANY),
        out_shape=shape((row_count, WIDTH), BF16),
        scratch_shapes=[pltpu.VMEM((slots, BLOCK, WIDTH), BF16), pltpu.SemaphoreType.DMA((HEADS,))],
        input_output_aliases={count + 1: 0},
        compiler_params=pltpu.CompilerParams(vmem_limit_bytes=VMEM_LIMIT),
        cost_estimate=pl.CostEstimate(flops=MODEL_FLOPS["merge_near"], bytes_accessed=1000, transcendentals=0),
        name="merge_near",
    )(meta, *state, *received, partial_out)
    return merged[None]


def solution(mesh):
    in_specs = (P("fsdp", "seq", None), P("fsdp", None), P(), P())
    out_specs = P("fsdp", "seq", None)
    return jax.shard_map(body, mesh=mesh, in_specs=in_specs, out_specs=out_specs, check_vma=False)
```

```python
import functools
import math

import jax
import jax.numpy as jnp
from jax import lax
from jax.experimental import pallas as pl
from jax.experimental.pallas import tpu as pltpu
from jax.sharding import PartitionSpec as P

HEADS = 4
HEAD_DIM = 128
BLOCK = 128
STRIDE = 8
WIDTH = HEADS * HEAD_DIM
PAIR = 2 * HEAD_DIM
NEG = -1e30
SCALE2 = HEAD_DIM ** (-0.5) * math.log2(math.e)
VMEM_LIMIT = 12 * 1024 * 1024

MODEL_FLOPS = {"slot_queries": 575000, "project_first": 689999, "project_pack": 689999, "project_own": 3680000, "project_mid": 1610000, "project_kv": 2990000, "attend_local": 6325000, "merge_near": 2990000}
ORDER = {
    'c1': ('c0',),
    'cD': ('c1',),
    'cQ': ('cD',),
    'p0': ('partial', 'xD'),
    'p1': ('partial',),
    'q': ('kv',),
    'kv': ('pack',),
}
NEAR_ORDER = (3, 2, 1)
F32 = jnp.float32
BF16 = jnp.bfloat16


def near_place(index, half, size):
    if index < half:
        return 0, index
    return 1 + (index - half) // size, (index - half) % size


def partners(count, place, bits):
    where = {place(i): i for i in range(count)}
    pairs = []
    for source in range(count):
        run, spot = place(source)
        if (run, spot ^ bits) in where:
            pairs.append((source, where[run, spot ^ bits]))
    return pairs


def swap(value, axis, bit):
    count = lax.axis_size(axis)
    return lax.ppermute(value, axis, [(i, i ^ bit) for i in range(count)])


def after(value, *others):
    return lax.optimization_barrier((value,) + others)[0]


def ordered(name, value, known):
    others = [known[other] for other in ORDER.get(name, ()) if other in known]
    return after(value, *others) if others else value


def rows_of(block):
    return pl.ds(pl.multiple_of(block * BLOCK, BLOCK), BLOCK)


def qk(query, key):
    return lax.dot_general(query, key, (((1,), (1,)), ((), ())), preferred_element_type=F32)


def pv(weights, value):
    return jnp.dot(weights.astype(BF16), value, preferred_element_type=F32)


def add_up(tokens, places, weights):
    total = None
    for place, weight in zip(places, weights):
        depth = weight.shape[0]
        columns = pl.ds(pl.multiple_of(place, depth), depth)
        term = jnp.dot(tokens[:, columns], weight[...], preferred_element_type=F32)
        total = term if total is None else total + term
    return total


def own_kernel(count, meta, tokens, *refs):
    weights, out = refs[:count], refs[count]
    for j in range(out.shape[1] // PAIR):
        lanes = slice(j * PAIR, (j + 1) * PAIR)
        out[:, lanes] = add_up(tokens, [meta[at] for at in range(count)], [weight.at[:, lanes] for weight in weights])


def near_rows_kernel(layout, place_at, first, slots, slot_at, meta, tokens, before, *refs):
    arrived, refs = refs[: len(layout)], refs[len(layout) :]
    sums, joined = refs[:slots], refs[slots]
    for at, array in zip(layout, arrived):
        rows = array.shape[0]
        joined[pl.ds(pl.multiple_of(meta[at], rows), rows), :] = array[...]
    depth = joined.shape[0]
    columns = pl.ds(pl.multiple_of(meta[place_at], depth), depth)
    for slot in range(slots):
        for head in range(HEADS):
            rows = rows_of(meta[slot_at + HEADS * slot + head])
            lanes = [slice(start, start + HEAD_DIM) for start in (head * HEAD_DIM, WIDTH + head * HEAD_DIM)]
            weight = jnp.concatenate([joined[:, part] for part in lanes], axis=1)
            product = jnp.dot(tokens[rows, columns], weight, preferred_element_type=F32)
            for field, part in enumerate(lanes):
                if first:
                    total = before[0][rows, WIDTH + part.start : WIDTH + part.stop]
                else:
                    total = before[slot][:, part]
                total = total + product[:, field * HEAD_DIM : (field + 1) * HEAD_DIM]
                sums[slot][:, part] = total.astype(sums[slot].dtype)


def first_rows_kernel(layout, place_at, slots, slot_at, meta, tokens, partial, *refs):
    near_rows_kernel(layout, place_at, True, slots, slot_at, meta, tokens, [partial], *refs)


def last_rows_kernel(layout, place_at, slots, slot_at, meta, tokens, *refs):
    near_rows_kernel(layout, place_at, False, slots, slot_at, meta, tokens, refs[:slots], *refs[slots:])


def slot_kernel(core_at, meta, source, out):
    out[1 - meta[core_at]] = source[...]


def kv_kernel(places_at, meta, tokens, partial, *refs):
    parts, kv = refs[:-1], refs[-1]
    places = [meta[at] for at in places_at]
    for j in range(2 * WIDTH // PAIR):
        lanes = slice(j * PAIR, (j + 1) * PAIR)
        product = add_up(tokens, places, [part.at[:, lanes] for part in parts])
        kv[:, lanes] = (partial[:, WIDTH + j * PAIR : WIDTH + (j + 1) * PAIR] + product).astype(BF16)


def with_ones(value):
    return jnp.concatenate([value, jnp.ones(value.shape, BF16)], axis=1)


def attend_kernel(bases_at, core_at, slots, slot_at, match_at, meta, tokens, partial, *refs):
    weights, refs = refs[: len(bases_at)], refs[len(bases_at) :]
    kv, out, refs = refs[0], refs[1], refs[2:]
    state, scratch = refs[: 4 * slots], refs[4 * slots :]
    query, acc_all, top_all, sum_all = scratch
    blocks = query.shape[0] // BLOCK
    GROUP = 2 if blocks % 2 == 0 else 1
    row = lax.broadcasted_iota(jnp.int32, (BLOCK, BLOCK), 0)
    column = lax.broadcasted_iota(jnp.int32, (BLOCK, BLOCK), 1)
    causal = column <= row
    places = [meta[at] for at in bases_at]
    other = 1 - meta[core_at]
    for pair in range(HEADS // 2):
        lanes = slice(pair * PAIR, (pair + 1) * PAIR)
        total = partial[:, lanes]
        if weights:
            parts = [weights[0].at[:, lanes], weights[1].at[other, :, lanes]]
            total = total + add_up(tokens, places, parts)
        query[:, lanes] = total.astype(BF16)

    def lanes_of(head):
        return slice(head * HEAD_DIM, (head + 1) * HEAD_DIM)

    def rows_at(b):
        return slice(b * BLOCK, (b + 1) * BLOCK)

    def score(head, group):
        first, last = group * GROUP, (group + 1) * GROUP
        rows = slice(first * BLOCK, last * BLOCK)
        return qk(query[rows, lanes_of(head)], kv[: last * BLOCK, lanes_of(head)])

    def weigh(head, group, scores):
        near_block = meta[slot_at + head]
        far_block = meta[slot_at + HEADS + head]
        tops, weights = [], []
        for i in range(GROUP):
            b = group * GROUP + i
            mine = scores[rows_at(i)]
            times = (
                1
                + jnp.where(near_block == b, 1, 0)
                + jnp.where(far_block == b, meta[match_at + head], 0)
            ).astype(F32)
            diagonal = jnp.where(causal, mine[:, rows_at(b)], NEG)
            top = jnp.max(diagonal, axis=1, keepdims=True)
            if b:
                top = jnp.maximum(top, jnp.max(mine[:, : b * BLOCK], axis=1, keepdims=True))
            parts = [(jnp.exp2((diagonal - top) * SCALE2) * times).astype(BF16)]
            if b:
                parts.insert(0, jnp.exp2((mine[:, : b * BLOCK] - top) * SCALE2).astype(BF16))
            if i < GROUP - 1:
                parts.append(jnp.zeros((BLOCK, (GROUP - 1 - i) * BLOCK), BF16))
            tops.append(top)
            weights.append(jnp.concatenate(parts, axis=1))
        return tops, jnp.concatenate(weights, axis=0)

    def finish(head, group, tops, weight):
        lanes = lanes_of(head)
        keys = (group + 1) * GROUP * BLOCK
        value = kv[:keys, WIDTH + head * HEAD_DIM : WIDTH + (head + 1) * HEAD_DIM]
        both = jnp.dot(weight, with_ones(value), preferred_element_type=F32)
        rows = slice(group * GROUP * BLOCK, keys)
        acc, summed = both[:, :HEAD_DIM], both[:, HEAD_DIM:]
        out[rows, lanes] = (acc / summed).astype(BF16)
        acc_all[rows, lanes] = acc
        sum_all[rows, lanes] = summed
        for i, top in enumerate(tops):
            top_all[rows_at(group * GROUP + i), lanes] = jnp.broadcast_to(top, (BLOCK, HEAD_DIM))
        if group == blocks // GROUP - 1:
            for slot in range(slots):
                rows = rows_of(meta[slot_at + slot * HEADS + head])
                for target, source in zip(state[4 * slot :], scratch):
                    target[:, lanes] = source[rows, lanes]

    tasks = [(head, group) for head in range(HEADS) for group in range(blocks // GROUP)]
    scored, weighed = {}, {}
    for step in range(len(tasks) + 2):
        if step < len(tasks):
            scored[step] = score(*tasks[step])
        if 0 <= step - 1 < len(tasks):
            weighed[step - 1] = weigh(*tasks[step - 1], scored.pop(step - 1))
        if 0 <= step - 2 < len(tasks):
            finish(*tasks[step - 2], *weighed.pop(step - 2))


def merge_kernel(shifts, steps, slot_at, match_at, place_at, meta, *refs):
    slots = len(shifts)
    state = refs[: 4 * slots]
    packs = refs[4 * slots : 4 * slots + sum(shifts)]
    out, results, sems = refs[4 * slots + sum(shifts) + 1 :]
    if slots == 1:
        pl.when(meta[place_at] > 0)(lambda: merge_slots(
            shifts, steps, slot_at, match_at, place_at, meta, state, packs, out, results, sems
        ))
    else:
        merge_slots(shifts, steps, slot_at, match_at, place_at, meta, state, packs, out, results, sems)


def merge_slots(shifts, steps, slot_at, match_at, place_at, meta, state, packs, out, results, sems):
    lanes = [slice(head * HEAD_DIM, (head + 1) * HEAD_DIM) for head in range(HEADS)]
    values = [slice(WIDTH + head * HEAD_DIM, WIDTH + (head + 1) * HEAD_DIM) for head in range(HEADS)]
    earlier = [None] * HEADS
    for slot, count in enumerate(shifts):
        fields = packs[sum(shifts[:slot]) : sum(shifts[: slot + 1])]
        query, acc_ref, top_ref, sum_ref = state[4 * slot : 4 * slot + 4]
        place = meta[place_at + slot]
        scores, weights = [], []
        for head in range(HEADS):
            keys = jnp.concatenate([field[:, lanes[head]] for field in fields], axis=0)
            score = qk(query[:, lanes[head]], keys)
            parts = []
            for number, step in enumerate(steps[sum(shifts[:slot]) : sum(shifts[: slot + 1])]):
                seen = place ^ step < place
                if slot:
                    seen = seen & (meta[match_at + head] == 1)
                part = score[:, number * BLOCK : (number + 1) * BLOCK]
                parts.append(jnp.where(seen, part, NEG))
            scores.append(jnp.concatenate(parts, axis=1))
        for head in range(HEADS):
            acc, top, summed = (ref[:, lanes[head]] for ref in (acc_ref, top_ref, sum_ref))
            if slot:
                same = meta[slot_at + head] == meta[slot_at + HEADS + head]
                acc, top, summed = (
                    jnp.where(same, new, old) for new, old in zip(earlier[head], (acc, top, summed))
                )
            best = jnp.maximum(top, jnp.max(scores[head], axis=1, keepdims=True))
            decay = jnp.exp2((top - best) * SCALE2)
            weight = jnp.exp2((scores[head] - best[:, :1]) * SCALE2).astype(BF16)
            weights.append((acc * decay, best, summed * decay, weight))
        copies = []
        for head in range(HEADS):
            acc, best, summed, weight = weights[head]
            value = jnp.concatenate([field[:, values[head]] for field in fields], axis=0)
            both = jnp.dot(weight, with_ones(value), preferred_element_type=F32)
            acc = acc + both[:, :HEAD_DIM]
            summed = summed + both[:, HEAD_DIM:]
            earlier[head] = (acc, best, summed)
            results[slot, :, lanes[head]] = (acc / summed).astype(BF16)
            rows = rows_of(meta[slot_at + slot * HEADS + head])
            copies.append(
                pltpu.make_async_copy(
                    results.at[slot, :, lanes[head]], out.at[rows, lanes[head]], sems.at[head]
                )
            )
            copies[-1].start()
        for copy in copies:
            copy.wait()


def body(tokens, qkv_weight, near_offset, far_offset):
    sequence = tokens[0]
    row_count, depth = sequence.shape
    share = qkv_weight.shape[0]
    block_rate = row_count // BLOCK
    seq_size = lax.axis_size("seq")
    seq_index = lax.axis_index("seq")
    pieces = lax.axis_size("fsdp")
    mine = lax.axis_index("fsdp")
    near_size = min(16, seq_size)
    half = near_size // 2
    far_size = max(1, min(16, seq_size // STRIDE))
    near_at = lambda i: near_place(i, half, near_size)
    far_at = lambda i: (i // (STRIDE * far_size) * STRIDE + i % STRIDE, i // STRIDE % far_size)
    reach = max(near_at(i)[1] for i in range(seq_size))
    near_shifts = (1 << reach.bit_length()) - 1
    far_shifts = (1 << (far_size - 1).bit_length()) - 1
    slots = 2 if far_shifts else 1
    shifts = (near_shifts, far_shifts)[:slots]

    near_position = jnp.where(seq_index < half, seq_index, (seq_index - half) % near_size)
    far_position = seq_index // STRIDE % far_size
    far_match = (seq_index % STRIDE == far_offset // block_rate).astype(jnp.int32)
    spans = [(0, share // 4), (share // 2, share // 8)] if seq_size % 4 == 0 else []
    direct_from = spans[-1][0] + 2 * spans[-1][1] if spans else 0
    full_places = [(mine ^ j) * share for j in range(pieces)]
    scalars = list(full_places)
    place_at = len(scalars)
    scalars += [near_position, far_position]
    base_at = len(scalars)
    scalars += [(mine ^ bit) // 2 * 2 * share for bit in range(2, pieces, 2)]
    core_at = len(scalars)
    scalars.append(mine % 2)
    slot_at = len(scalars)
    match_at = slot_at + 2 * HEADS
    offsets_at = match_at + HEADS
    offsets = []
    for number, (start, rows) in enumerate(spans):
        side = seq_index // (1 << number) % 2
        offsets += [start + side * rows, start + (1 - side) * rows]
    offsets.append(direct_from)
    as_array = lambda values: jnp.stack([jnp.asarray(value, jnp.int32) for value in values])
    meta = jnp.concatenate(
        [as_array(scalars), near_offset, far_offset % block_rate, far_match, as_array(offsets)]
    )

    scalar_spec = pl.BlockSpec(memory_space=pltpu.SMEM)
    whole = pl.BlockSpec(memory_space=pltpu.VMEM)
    shape = jax.ShapeDtypeStruct

    def call(kernel, args, results, name, scratch=()):
        return pl.pallas_call(
            kernel,
            in_specs=[scalar_spec] + [whole] * len(args),
            out_specs=[whole] * len(results),
            out_shape=results,
            scratch_shapes=list(scratch),
            compiler_params=pltpu.CompilerParams(vmem_limit_bytes=VMEM_LIMIT),
            cost_estimate=pl.CostEstimate(flops=MODEL_FLOPS[name], bytes_accessed=1000, transcendentals=0),
            name=name,
        )(meta, *args)

    local = [qkv_weight]
    bits = range(2, pieces, 2)
    known = {}
    if pieces > 1:
        local.append(swap(qkv_weight, "fsdp", 1))
        known["core"] = local[-1]
    (partial,) = call(
        functools.partial(own_kernel, len(local)),
        [ordered("t", sequence, known), *local],
        [shape((row_count, 3 * WIDTH), F32)],
        "project_own",
    )
    known["partial"] = partial
    direct_rows, queries = [], []
    for bit in bits:
        mine_rows, other_rows = [], []
        for number, (start, rows) in enumerate(spans):
            tag = str(number)
            side = seq_index // (1 << number) % 2
            cut = lax.dynamic_slice(
                ordered("c" + tag, qkv_weight, known), (start + side * rows, WIDTH), (rows, 2 * WIDTH)
            )
            known["c" + tag] = cut
            direct = swap(cut, "fsdp", bit)
            known["x" + tag] = direct
            across = swap(ordered("f" + tag, direct, known), "fsdp", 1)
            known["f" + tag] = across
            passed = ordered("p" + tag, swap(ordered("y" + tag, direct, known), "seq", 1 << number), known)
            known["y" + tag] = passed
            mine_rows += [direct, passed]
            other_rows += [across, swap(passed, "fsdp", 1)]
            known["q" + tag] = other_rows[-1]
        known["meta"] = meta
        cut = ordered("cD", qkv_weight, known)[direct_from:, WIDTH:]
        known["cD"] = cut
        rest = swap(cut, "fsdp", bit)
        known["xD"] = rest
        rest = ordered("pD", rest, known)
        known["fD"] = swap(rest, "fsdp", 1)
        direct_rows.append(mine_rows + [rest] + other_rows + [known["fD"]])
        cut = ordered("cQ", qkv_weight, known)[:, :WIDTH]
        known["cQ"] = cut
        queries.append(swap(cut, "fsdp", bit))
    assert len(bits) <= 1
    if bits:
        bit = bits[0]
        count = len(direct_rows[0]) // 2
        layout = [offsets_at + i for i in range(count)]
        *sums, joined = call(
            functools.partial(first_rows_kernel, layout, bit, slots, slot_at),
            [sequence, ordered("a", partial, known), *direct_rows[0][:count]],
            [shape((BLOCK, 2 * WIDTH), F32)] * slots + [shape((share, 2 * WIDTH), BF16)],
            "project_first",
        )
        *packs, joined_other = call(
            functools.partial(last_rows_kernel, layout, bit ^ 1, slots, slot_at),
            [sequence, *sums, *direct_rows[0][count:]],
            [shape((BLOCK, 2 * WIDTH), BF16)] * slots + [shape((share, 2 * WIDTH), BF16)],
            "project_pack",
        )
        known["pack"] = packs[0]
        (kv,) = call(
            functools.partial(kv_kernel, [bit, bit ^ 1]),
            [sequence, ordered("kv", partial, known), joined, joined_other],
            [shape((row_count, 2 * WIDTH), BF16)],
            "project_kv",
        )
    else:
        kv = partial[:, WIDTH:].astype(BF16)
        blocks = kv.reshape(block_rate, BLOCK, 2, HEADS, HEAD_DIM)
        packs = []
        for offset in (near_offset, far_offset % block_rate)[:slots]:
            picked = blocks[offset, :, :, jnp.arange(HEADS)]
            packs.append(picked.transpose(1, 2, 0, 3).reshape(BLOCK, 2 * WIDTH))
    known["kv"] = kv
    received = []
    for pack, place, count, unit in zip(packs, (near_at, far_at), shifts, (1, STRIDE)):
        for step in NEAR_ORDER if count == len(NEAR_ORDER) else range(1, count + 1):
            received.append((step, lax.ppermute(pack, "seq", partners(seq_size, place, step))))
        known |= {f"n{step}": r for step, r in received}
    steps = [step for step, _ in received]
    received = [pack for _, pack in received]
    crossed_q, q_places = [], []
    for bit, direct in zip(bits, queries):
        direct = ordered("q", direct, known)
        (slots_out,) = call(
            functools.partial(slot_kernel, core_at), [direct], [shape((2,) + direct.shape, BF16)], "slot_queries"
        )
        both = lax.all_to_all(
            slots_out, "fsdp", 0, 0, axis_index_groups=[[i, i + 1] for i in range(0, pieces, 2)]
        )
        crossed_q += [direct, both]
        q_places += [bit, bit ^ 1]
    state_types = [BF16, F32, F32, F32]
    partial_out, *state = call(
        functools.partial(attend_kernel, q_places, core_at, slots, slot_at, match_at),
        [sequence, partial, *crossed_q, kv],
        [shape((row_count, WIDTH), BF16)] + [shape((BLOCK, WIDTH), kind) for kind in state_types] * slots,
        "attend_local",
        [pltpu.VMEM((row_count, WIDTH), kind) for kind in state_types],
    )
    count = 4 * slots + sum(shifts)
    merged = pl.pallas_call(
        functools.partial(merge_kernel, shifts, steps, slot_at, match_at, place_at),
        in_specs=[scalar_spec] + [whole] * count + [pl.BlockSpec(memory_space=pl.ANY)],
        out_specs=pl.BlockSpec(memory_space=pl.ANY),
        out_shape=shape((row_count, WIDTH), BF16),
        scratch_shapes=[pltpu.VMEM((slots, BLOCK, WIDTH), BF16), pltpu.SemaphoreType.DMA((HEADS,))],
        input_output_aliases={count + 1: 0},
        compiler_params=pltpu.CompilerParams(vmem_limit_bytes=VMEM_LIMIT),
        cost_estimate=pl.CostEstimate(flops=MODEL_FLOPS["merge_near"], bytes_accessed=1000, transcendentals=0),
        name="merge_near",
    )(meta, *state, *received, partial_out)
    return merged[None]


def solution(mesh):
    in_specs = (P("fsdp", "seq", None), P("fsdp", None), P(), P())
    out_specs = P("fsdp", "seq", None)
    return jax.shard_map(body, mesh=mesh, in_specs=in_specs, out_specs=out_specs, check_vma=False)
```

```python
import functools
import math

import jax
import jax.numpy as jnp
from jax import lax
from jax.experimental import pallas as pl
from jax.experimental.pallas import tpu as pltpu
from jax.sharding import PartitionSpec as P

HEADS = 4
HEAD_DIM = 128
BLOCK = 128
STRIDE = 8
WIDTH = HEADS * HEAD_DIM
PAIR = 2 * HEAD_DIM
NEG = -1e30
SCALE2 = HEAD_DIM ** (-0.5) * math.log2(math.e)
VMEM_LIMIT = 24 * 1024 * 1024

MODEL_FLOPS = {"project_first": 689999, "split_queries": 575000, "sides": 11500000000, "cut_rest": 1150000, "project_pack": 689999, "project_own": 3680000, "project_mid": 1610000, "project_kv": 2990000, "attend_local": 6325000, "merge_near": 2990000}
ORDER = {
    'cut': ('c0',),
    'p0': ('partial', 'xD'),
    'p1': ('partial',),
    'q': ('kv',),
    'kv': ('pack',),
}
NEAR_ORDER = (1, 2, 3)
F32 = jnp.float32
BF16 = jnp.bfloat16


def near_place(index, half, size):
    if index < half:
        return 0, index
    return 1 + (index - half) // size, (index - half) % size


def partners(count, place, bits):
    where = {place(i): i for i in range(count)}
    pairs = []
    for source in range(count):
        run, spot = place(source)
        if (run, spot ^ bits) in where:
            pairs.append((source, where[run, spot ^ bits]))
    return pairs


def swap(value, axis, bit):
    count = lax.axis_size(axis)
    return lax.ppermute(value, axis, [(i, i ^ bit) for i in range(count)])


def after(value, *others):
    return lax.optimization_barrier((value,) + others)[0]


def ordered(name, value, known):
    others = [known[other] for other in ORDER.get(name, ()) if other in known]
    return after(value, *others) if others else value


def rows_of(block):
    return pl.ds(pl.multiple_of(block * BLOCK, BLOCK), BLOCK)


def qk(query, key):
    return lax.dot_general(query, key, (((1,), (1,)), ((), ())), preferred_element_type=F32)


def pv(weights, value):
    return jnp.dot(weights.astype(BF16), value, preferred_element_type=F32)


def add_up(tokens, places, weights):
    total = None
    for place, weight in zip(places, weights):
        depth = weight.shape[0]
        columns = pl.ds(pl.multiple_of(place, depth), depth)
        term = jnp.dot(tokens[:, columns], weight[...], preferred_element_type=F32)
        total = term if total is None else total + term
    return total


def own_kernel(count, meta, tokens, *refs):
    weights, out = refs[:count], refs[count]
    for j in range(out.shape[1] // PAIR):
        lanes = slice(j * PAIR, (j + 1) * PAIR)
        out[:, lanes] = add_up(tokens, [meta[at] for at in range(count)], [weight.at[:, lanes] for weight in weights])


def cut_kernel(spans, direct_from, sides, weight, *outs):
    for (number, start, rows), out in zip(spans, outs):
        first = pl.multiple_of(start + sides[number] * rows, rows)
        out[...] = weight[pl.ds(first, rows), WIDTH:]
    outs[-2][...] = weight[direct_from:, WIDTH:]
    outs[-1][: weight.shape[0], :] = weight[:, :WIDTH]


def near_rows_kernel(layout, place_at, first, slots, slot_at, meta, tokens, before, *refs):
    arrived, refs = refs[: len(layout)], refs[len(layout) :]
    sums, joined = refs[:slots], refs[slots]
    for at, array in zip(layout, arrived):
        rows = array.shape[0]
        joined[pl.ds(pl.multiple_of(meta[at], rows), rows), :] = array[...]
    depth = joined.shape[0]
    columns = pl.ds(pl.multiple_of(meta[place_at], depth), depth)
    for slot in range(slots):
        for head in range(HEADS):
            rows = rows_of(meta[slot_at + HEADS * slot + head])
            lanes = [slice(start, start + HEAD_DIM) for start in (head * HEAD_DIM, WIDTH + head * HEAD_DIM)]
            weight = jnp.concatenate([joined[:, part] for part in lanes], axis=1)
            product = jnp.dot(tokens[rows, columns], weight, preferred_element_type=F32)
            for field, part in enumerate(lanes):
                if first:
                    total = before[0][rows, WIDTH + part.start : WIDTH + part.stop]
                else:
                    total = before[slot][:, part]
                total = total + product[:, field * HEAD_DIM : (field + 1) * HEAD_DIM]
                sums[slot][:, part] = total.astype(sums[slot].dtype)


def first_rows_kernel(layout, place_at, slots, slot_at, meta, tokens, partial, *refs):
    near_rows_kernel(layout, place_at, True, slots, slot_at, meta, tokens, [partial], *refs)


def last_rows_kernel(layout, place_at, slots, slot_at, meta, tokens, *refs):
    near_rows_kernel(layout, place_at, False, slots, slot_at, meta, tokens, refs[:slots], *refs[slots:])


def split_kernel(meta, source, *outs):
    done = 0
    for out in outs:
        rows = out.shape[0]
        out[...] = source[done : done + rows, :]
        done += rows


def kv_kernel(places_at, meta, tokens, partial, *refs):
    parts, kv = refs[:-1], refs[-1]
    places = [meta[at] for at in places_at]
    for j in range(2 * WIDTH // PAIR):
        lanes = slice(j * PAIR, (j + 1) * PAIR)
        product = add_up(tokens, places, [part.at[:, lanes] for part in parts])
        kv[:, lanes] = (partial[:, WIDTH + j * PAIR : WIDTH + (j + 1) * PAIR] + product).astype(BF16)


def with_ones(value):
    return jnp.concatenate([value, jnp.ones(value.shape, BF16)], axis=1)


def attend_kernel(count, bases_at, slots, slot_at, match_at, meta, tokens, partial, *refs):
    weights, refs = refs[:count], refs[count:]
    kv, out, refs = refs[0], refs[1], refs[2:]
    state, scratch, joined = refs[: 4 * slots], refs[4 * slots : -1], refs[-1]
    query, acc_all, top_all, sum_all = scratch
    blocks = query.shape[0] // BLOCK
    GROUP = 2 if blocks % 2 == 0 else 1
    row = lax.broadcasted_iota(jnp.int32, (BLOCK, BLOCK), 0)
    column = lax.broadcasted_iota(jnp.int32, (BLOCK, BLOCK), 1)
    causal = column <= row
    places = [meta[at] for at in bases_at]
    if weights:
        done = 0
        for weight in weights[1:]:
            joined[done : done + weight.shape[0], :] = weight[...]
            done += weight.shape[0]
        if done < joined.shape[0]:
            joined[done:, :] = weights[0][joined.shape[0] :, :]
    for pair in range(HEADS // 2):
        lanes = slice(pair * PAIR, (pair + 1) * PAIR)
        total = partial[:, lanes]
        if weights:
            total = total + add_up(tokens, places, [weights[0].at[: joined.shape[0], lanes], joined.at[:, lanes]])
        query[:, lanes] = total.astype(BF16)

    def lanes_of(head):
        return slice(head * HEAD_DIM, (head + 1) * HEAD_DIM)

    def rows_at(b):
        return slice(b * BLOCK, (b + 1) * BLOCK)

    def score(head, group):
        first, last = group * GROUP, (group + 1) * GROUP
        rows = slice(first * BLOCK, last * BLOCK)
        return qk(query[rows, lanes_of(head)], kv[: last * BLOCK, lanes_of(head)])

    def weigh(head, group, scores):
        near_block = meta[slot_at + head]
        far_block = meta[slot_at + HEADS + head]
        tops, weights = [], []
        for i in range(GROUP):
            b = group * GROUP + i
            mine = scores[rows_at(i)]
            times = (
                1
                + jnp.where(near_block == b, 1, 0)
                + jnp.where(far_block == b, meta[match_at + head], 0)
            ).astype(F32)
            diagonal = jnp.where(causal, mine[:, rows_at(b)], NEG)
            top = jnp.max(diagonal, axis=1, keepdims=True)
            if b:
                top = jnp.maximum(top, jnp.max(mine[:, : b * BLOCK], axis=1, keepdims=True))
            parts = [(jnp.exp2((diagonal - top) * SCALE2) * times).astype(BF16)]
            if b:
                parts.insert(0, jnp.exp2((mine[:, : b * BLOCK] - top) * SCALE2).astype(BF16))
            if i < GROUP - 1:
                parts.append(jnp.zeros((BLOCK, (GROUP - 1 - i) * BLOCK), BF16))
            tops.append(top)
            weights.append(jnp.concatenate(parts, axis=1))
        return tops, jnp.concatenate(weights, axis=0)

    def finish(head, group, tops, weight):
        lanes = lanes_of(head)
        keys = (group + 1) * GROUP * BLOCK
        value = kv[:keys, WIDTH + head * HEAD_DIM : WIDTH + (head + 1) * HEAD_DIM]
        both = jnp.dot(weight, with_ones(value), preferred_element_type=F32)
        rows = slice(group * GROUP * BLOCK, keys)
        acc, summed = both[:, :HEAD_DIM], both[:, HEAD_DIM:]
        out[rows, lanes] = (acc / summed).astype(BF16)
        acc_all[rows, lanes] = acc
        sum_all[rows, lanes] = summed
        for i, top in enumerate(tops):
            top_all[rows_at(group * GROUP + i), lanes] = jnp.broadcast_to(top, (BLOCK, HEAD_DIM))
        if group == blocks // GROUP - 1:
            for slot in range(slots):
                rows = rows_of(meta[slot_at + slot * HEADS + head])
                for target, source in zip(state[4 * slot :], scratch):
                    target[:, lanes] = source[rows, lanes]

    tasks = [(head, group) for head in range(HEADS) for group in range(blocks // GROUP)]
    scored, weighed = {}, {}
    for step in range(len(tasks) + 2):
        if step < len(tasks):
            scored[step] = score(*tasks[step])
        if 0 <= step - 1 < len(tasks):
            weighed[step - 1] = weigh(*tasks[step - 1], scored.pop(step - 1))
        if 0 <= step - 2 < len(tasks):
            finish(*tasks[step - 2], *weighed.pop(step - 2))


def merge_kernel(shifts, steps, slot_at, match_at, place_at, meta, *refs):
    slots = len(shifts)
    state = refs[: 4 * slots]
    packs = refs[4 * slots : 4 * slots + sum(shifts)]
    out, results, sems = refs[4 * slots + sum(shifts) + 1 :]
    if slots == 1:
        pl.when(meta[place_at] > 0)(lambda: merge_slots(
            shifts, steps, slot_at, match_at, place_at, meta, state, packs, out, results, sems
        ))
    else:
        merge_slots(shifts, steps, slot_at, match_at, place_at, meta, state, packs, out, results, sems)


def merge_slots(shifts, steps, slot_at, match_at, place_at, meta, state, packs, out, results, sems):
    lanes = [slice(head * HEAD_DIM, (head + 1) * HEAD_DIM) for head in range(HEADS)]
    values = [slice(WIDTH + head * HEAD_DIM, WIDTH + (head + 1) * HEAD_DIM) for head in range(HEADS)]
    earlier = [None] * HEADS
    for slot, count in enumerate(shifts):
        fields = packs[sum(shifts[:slot]) : sum(shifts[: slot + 1])]
        query, acc_ref, top_ref, sum_ref = state[4 * slot : 4 * slot + 4]
        place = meta[place_at + slot]
        scores, weights = [], []
        for head in range(HEADS):
            keys = jnp.concatenate([field[:, lanes[head]] for field in fields], axis=0)
            score = qk(query[:, lanes[head]], keys)
            parts = []
            for number, step in enumerate(steps[sum(shifts[:slot]) : sum(shifts[: slot + 1])]):
                seen = place ^ step < place
                if slot:
                    seen = seen & (meta[match_at + head] == 1)
                part = score[:, number * BLOCK : (number + 1) * BLOCK]
                parts.append(jnp.where(seen, part, NEG))
            scores.append(jnp.concatenate(parts, axis=1))
        for head in range(HEADS):
            acc, top, summed = (ref[:, lanes[head]] for ref in (acc_ref, top_ref, sum_ref))
            if slot:
                same = meta[slot_at + head] == meta[slot_at + HEADS + head]
                acc, top, summed = (
                    jnp.where(same, new, old) for new, old in zip(earlier[head], (acc, top, summed))
                )
            best = jnp.maximum(top, jnp.max(scores[head], axis=1, keepdims=True))
            decay = jnp.exp2((top - best) * SCALE2)
            weight = jnp.exp2((scores[head] - best[:, :1]) * SCALE2).astype(BF16)
            weights.append((acc * decay, best, summed * decay, weight))
        copies = []
        for head in range(HEADS):
            acc, best, summed, weight = weights[head]
            value = jnp.concatenate([field[:, values[head]] for field in fields], axis=0)
            both = jnp.dot(weight, with_ones(value), preferred_element_type=F32)
            acc = acc + both[:, :HEAD_DIM]
            summed = summed + both[:, HEAD_DIM:]
            earlier[head] = (acc, best, summed)
            results[slot, :, lanes[head]] = (acc / summed).astype(BF16)
            rows = rows_of(meta[slot_at + slot * HEADS + head])
            copies.append(
                pltpu.make_async_copy(
                    results.at[slot, :, lanes[head]], out.at[rows, lanes[head]], sems.at[head]
                )
            )
            copies[-1].start()
        for copy in copies:
            copy.wait()


def body(tokens, qkv_weight, near_offset, far_offset):
    sequence = tokens[0]
    row_count, depth = sequence.shape
    share = qkv_weight.shape[0]
    block_rate = row_count // BLOCK
    seq_size = lax.axis_size("seq")
    seq_index = lax.axis_index("seq")
    pieces = lax.axis_size("fsdp")
    mine = lax.axis_index("fsdp")
    near_size = min(16, seq_size)
    half = near_size // 2
    far_size = max(1, min(16, seq_size // STRIDE))
    near_at = lambda i: near_place(i, half, near_size)
    far_at = lambda i: (i // (STRIDE * far_size) * STRIDE + i % STRIDE, i // STRIDE % far_size)
    reach = max(near_at(i)[1] for i in range(seq_size))
    near_shifts = (1 << reach.bit_length()) - 1
    far_shifts = (1 << (far_size - 1).bit_length()) - 1
    slots = 2 if far_shifts else 1
    shifts = (near_shifts, far_shifts)[:slots]

    near_position = jnp.where(seq_index < half, seq_index, (seq_index - half) % near_size)
    far_position = seq_index // STRIDE % far_size
    far_match = (seq_index % STRIDE == far_offset // block_rate).astype(jnp.int32)
    spans = [(0, share // 4), (share // 2, share // 8)] if seq_size % 4 == 0 else []
    direct_from = spans[-1][0] + 2 * spans[-1][1] if spans else 0
    full_places = [(mine ^ j) * share for j in range(pieces)]
    scalars = list(full_places)
    place_at = len(scalars)
    scalars += [near_position, far_position]
    base_at = len(scalars)
    scalars += [(mine ^ bit) // 2 * 2 * share for bit in range(2, pieces, 2)]
    core_at = len(scalars)
    scalars.append(mine % 2)
    slot_at = len(scalars)
    match_at = slot_at + 2 * HEADS
    offsets_at = match_at + HEADS
    offsets = []
    for number, (start, rows) in enumerate(spans):
        side = seq_index // (1 << number) % 2
        offsets += [start + side * rows, start + (1 - side) * rows]
    offsets.append(direct_from)
    as_array = lambda values: jnp.stack([jnp.asarray(value, jnp.int32) for value in values])
    meta = jnp.concatenate(
        [as_array(scalars), near_offset, far_offset % block_rate, far_match, as_array(offsets)]
    )

    scalar_spec = pl.BlockSpec(memory_space=pltpu.SMEM)
    whole = pl.BlockSpec(memory_space=pltpu.VMEM)
    shape = jax.ShapeDtypeStruct

    def call(kernel, args, results, name, scratch=(), scalars=None):
        return pl.pallas_call(
            kernel,
            in_specs=[scalar_spec] + [whole] * len(args),
            out_specs=[whole] * len(results),
            out_shape=results,
            scratch_shapes=list(scratch),
            compiler_params=pltpu.CompilerParams(vmem_limit_bytes=VMEM_LIMIT),
            cost_estimate=pl.CostEstimate(flops=MODEL_FLOPS[name], bytes_accessed=1000, transcendentals=0),
            name=name,
        )(meta if scalars is None else scalars, *args)

    passing = [share * 15 // 32 // 16 * 16] * 2
    local = [qkv_weight]
    bits = range(2, pieces, 2)
    known = {}
    if pieces > 1:
        local.append(swap(qkv_weight, "fsdp", 1))
        known["core"] = local[-1]
    (partial,) = call(
        functools.partial(own_kernel, len(local)),
        [ordered("t", sequence, known), *local],
        [shape((row_count, 3 * WIDTH), F32)],
        "project_own",
    )
    known["partial"] = partial
    direct_rows, queries = [], []
    for bit in bits:
        mine_rows, other_rows = [], []
        first_cut = [
            lax.dynamic_slice(qkv_weight, (start + seq_index % 2 * rows, WIDTH), (rows, 2 * WIDTH))
            for start, rows in spans[:1]
        ]
        known |= {"c0": value for value in first_cut}
        rest_spans = [(number, *span) for number, span in enumerate(spans)][1:]
        left = share - sum(passing)
        *rest_cuts, direct_cut, query_cut = call(
            functools.partial(cut_kernel, rest_spans, direct_from),
            [ordered("cut", qkv_weight, known)],
            [shape((rows, 2 * WIDTH), BF16) for _, _, rows in rest_spans]
            + [shape((share - direct_from, 2 * WIDTH), BF16), shape((share + left, WIDTH), BF16)],
            "cut_rest",
            scalars=as_array([seq_index % 2, seq_index // 2 % 2]),
        )
        span_cuts = first_cut + rest_cuts
        for number, (start, rows) in enumerate(spans):
            tag = str(number)
            cut = span_cuts[number]
            known["c" + tag] = cut
            direct = swap(cut, "fsdp", bit)
            known["x" + tag] = direct
            across = swap(ordered("f" + tag, direct, known), "fsdp", 1)
            known["f" + tag] = across
            passed = ordered("p" + tag, swap(ordered("y" + tag, direct, known), "seq", 1 << number), known)
            known["y" + tag] = passed
            mine_rows += [direct, passed]
            other_rows += [across, swap(passed, "fsdp", 1)]
            known["q" + tag] = other_rows[-1]
        cut = direct_cut
        known["cD"] = cut
        rest = swap(cut, "fsdp", bit)
        known["xD"] = rest
        rest = ordered("pD", rest, known)
        known["fD"] = swap(rest, "fsdp", 1)
        direct_rows.append(mine_rows + [rest] + other_rows + [known["fD"]])
        cut = query_cut
        if left:
            cut = lax.dynamic_update_slice(cut, known["core"][share - left :, :WIDTH], (share, 0))
        known["cQ"] = cut
        queries.append(swap(cut, "fsdp", bit))
    assert len(bits) <= 1
    if bits:
        bit = bits[0]
        count = len(direct_rows[0]) // 2
        layout = [offsets_at + i for i in range(count)]
        *sums, joined = call(
            functools.partial(first_rows_kernel, layout, bit, slots, slot_at),
            [sequence, ordered("a", partial, known), *direct_rows[0][:count]],
            [shape((BLOCK, 2 * WIDTH), F32)] * slots + [shape((share, 2 * WIDTH), BF16)],
            "project_first",
        )
        *packs, joined_other = call(
            functools.partial(last_rows_kernel, layout, bit ^ 1, slots, slot_at),
            [sequence, *sums, *direct_rows[0][count:]],
            [shape((BLOCK, 2 * WIDTH), BF16)] * slots + [shape((share, 2 * WIDTH), BF16)],
            "project_pack",
        )
        known["pack"] = packs[0]
        (kv,) = call(
            functools.partial(kv_kernel, [bit, bit ^ 1]),
            [sequence, ordered("kv", partial, known), joined, joined_other],
            [shape((row_count, 2 * WIDTH), BF16)],
            "project_kv",
        )
    else:
        kv = partial[:, WIDTH:].astype(BF16)
        blocks = kv.reshape(block_rate, BLOCK, 2, HEADS, HEAD_DIM)
        packs = []
        for offset in (near_offset, far_offset % block_rate)[:slots]:
            picked = blocks[offset, :, :, jnp.arange(HEADS)]
            packs.append(picked.transpose(1, 2, 0, 3).reshape(BLOCK, 2 * WIDTH))
    known["kv"] = kv
    received = []
    for pack, place, count, unit in zip(packs, (near_at, far_at), shifts, (1, STRIDE)):
        for step in NEAR_ORDER if count == len(NEAR_ORDER) else range(1, count + 1):
            received.append((step, lax.ppermute(pack, "seq", partners(seq_size, place, step))))
        known |= {f"n{step}": r for step, r in received}
    steps = [step for step, _ in received]
    received = [pack for _, pack in received]
    crossed_q, q_places = [], []
    for bit, direct in zip(bits, queries):
        direct = ordered("q", direct, known)
        parts = call(
            split_kernel,
            [direct],
            [shape((rows, WIDTH), BF16) for rows in passing],
            "split_queries",
        )
        crossed_q += [direct] + [swap(part, "fsdp", 1) for part in parts]
        q_places += [bit, bit ^ 1]
    state_types = [BF16, F32, F32, F32]
    partial_out, *state = call(
        functools.partial(attend_kernel, len(crossed_q), q_places, slots, slot_at, match_at),
        [sequence, partial, *crossed_q, kv],
        [shape((row_count, WIDTH), BF16)] + [shape((BLOCK, WIDTH), kind) for kind in state_types] * slots,
        "attend_local",
        [pltpu.VMEM((row_count, WIDTH), kind) for kind in state_types]
        + [pltpu.VMEM((share, WIDTH), BF16)],
    )
    count = 4 * slots + sum(shifts)
    merged = pl.pallas_call(
        functools.partial(merge_kernel, shifts, steps, slot_at, match_at, place_at),
        in_specs=[scalar_spec] + [whole] * count + [pl.BlockSpec(memory_space=pl.ANY)],
        out_specs=pl.BlockSpec(memory_space=pl.ANY),
        out_shape=shape((row_count, WIDTH), BF16),
        scratch_shapes=[pltpu.VMEM((slots, BLOCK, WIDTH), BF16), pltpu.SemaphoreType.DMA((HEADS,))],
        input_output_aliases={count + 1: 0},
        compiler_params=pltpu.CompilerParams(vmem_limit_bytes=VMEM_LIMIT),
        cost_estimate=pl.CostEstimate(flops=MODEL_FLOPS["merge_near"], bytes_accessed=1000, transcendentals=0),
        name="merge_near",
    )(meta, *state, *received, partial_out)
    return merged[None]


def solution(mesh):
    in_specs = (P("fsdp", "seq", None), P("fsdp", None), P(), P())
    out_specs = P("fsdp", "seq", None)
    return jax.shard_map(body, mesh=mesh, in_specs=in_specs, out_specs=out_specs, check_vma=False)
```

```python
import functools
import math

import jax
import jax.numpy as jnp
from jax import lax
from jax.experimental import pallas as pl
from jax.experimental.pallas import tpu as pltpu
from jax.sharding import PartitionSpec as P

HEADS = 4
HEAD_DIM = 128
BLOCK = 128
STRIDE = 8
WIDTH = HEADS * HEAD_DIM
PAIR = 2 * HEAD_DIM
NEG = -1e30
SCALE2 = HEAD_DIM ** (-0.5) * math.log2(math.e)
VMEM_LIMIT = 24 * 1024 * 1024

MODEL_FLOPS = {"slot_queries": 575000, "project_first": 689999, "project_pack": 689999, "project_own": 3680000, "project_mid": 1610000, "project_kv": 2990000, "attend_local": 6325000, "merge_near": 2990000}
ORDER = {
    'core': ('c0',),
    'c1': ('c0',),
    'cD': ('c1',),
    'cQ': ('cD',),
    'p0': ('partial', 'xD'),
    'p1': ('partial',),
    'q': ('kv',),
    'kv': ('pack',),
}
NEAR_ORDER = (3, 2, 1)
F32 = jnp.float32
BF16 = jnp.bfloat16


def near_place(index, half, size):
    if index < half:
        return 0, index
    return 1 + (index - half) // size, (index - half) % size


def partners(count, place, bits):
    where = {place(i): i for i in range(count)}
    pairs = []
    for source in range(count):
        run, spot = place(source)
        if (run, spot ^ bits) in where:
            pairs.append((source, where[run, spot ^ bits]))
    return pairs


def swap(value, axis, bit):
    count = lax.axis_size(axis)
    return lax.ppermute(value, axis, [(i, i ^ bit) for i in range(count)])


def after(value, *others):
    return lax.optimization_barrier((value,) + others)[0]


def ordered(name, value, known):
    others = [known[other] for other in ORDER.get(name, ()) if other in known]
    return after(value, *others) if others else value


def rows_of(block):
    return pl.ds(pl.multiple_of(block * BLOCK, BLOCK), BLOCK)


def qk(query, key):
    return lax.dot_general(query, key, (((1,), (1,)), ((), ())), preferred_element_type=F32)


def pv(weights, value):
    return jnp.dot(weights.astype(BF16), value, preferred_element_type=F32)


def add_up(tokens, places, weights):
    total = None
    for place, weight in zip(places, weights):
        depth = weight.shape[0]
        columns = pl.ds(pl.multiple_of(place, depth), depth)
        term = jnp.dot(tokens[:, columns], weight[...], preferred_element_type=F32)
        total = term if total is None else total + term
    return total


def own_kernel(count, meta, tokens, *refs):
    weights, out = refs[:count], refs[count]
    for j in range(out.shape[1] // PAIR):
        lanes = slice(j * PAIR, (j + 1) * PAIR)
        out[:, lanes] = add_up(tokens, [meta[at] for at in range(count)], [weight.at[:, lanes] for weight in weights])


def near_rows_kernel(layout, place_at, first, slots, slot_at, meta, tokens, before, *refs):
    arrived, refs = refs[: len(layout)], refs[len(layout) :]
    sums, joined = refs[:slots], refs[slots]
    for at, array in zip(layout, arrived):
        rows = array.shape[0]
        joined[pl.ds(pl.multiple_of(meta[at], rows), rows), :] = array[...]
    depth = joined.shape[0]
    columns = pl.ds(pl.multiple_of(meta[place_at], depth), depth)
    for slot in range(slots):
        for head in range(HEADS):
            rows = rows_of(meta[slot_at + HEADS * slot + head])
            lanes = [slice(start, start + HEAD_DIM) for start in (head * HEAD_DIM, WIDTH + head * HEAD_DIM)]
            weight = jnp.concatenate([joined[:, part] for part in lanes], axis=1)
            product = jnp.dot(tokens[rows, columns], weight, preferred_element_type=F32)
            for field, part in enumerate(lanes):
                if first:
                    total = before[0][rows, WIDTH + part.start : WIDTH + part.stop]
                else:
                    total = before[slot][:, part]
                total = total + product[:, field * HEAD_DIM : (field + 1) * HEAD_DIM]
                sums[slot][:, part] = total.astype(sums[slot].dtype)


def first_rows_kernel(layout, place_at, slots, slot_at, meta, tokens, partial, *refs):
    near_rows_kernel(layout, place_at, True, slots, slot_at, meta, tokens, [partial], *refs)


def last_rows_kernel(layout, place_at, slots, slot_at, meta, tokens, *refs):
    near_rows_kernel(layout, place_at, False, slots, slot_at, meta, tokens, refs[:slots], *refs[slots:])


def slot_kernel(core_at, meta, source, out):
    out[1 - meta[core_at]] = source[...]


def kv_kernel(places_at, meta, tokens, partial, *refs):
    parts, kv = refs[:-1], refs[-1]
    places = [meta[at] for at in places_at]
    for j in range(2 * WIDTH // PAIR):
        lanes = slice(j * PAIR, (j + 1) * PAIR)
        product = add_up(tokens, places, [part.at[:, lanes] for part in parts])
        kv[:, lanes] = (partial[:, WIDTH + j * PAIR : WIDTH + (j + 1) * PAIR] + product).astype(BF16)


def with_ones(value):
    return jnp.concatenate([value, jnp.ones(value.shape, BF16)], axis=1)


def attend_kernel(bases_at, core_at, slots, slot_at, match_at, meta, tokens, partial, *refs):
    weights, refs = refs[: len(bases_at)], refs[len(bases_at) :]
    kv, out, refs = refs[0], refs[1], refs[2:]
    state, scratch = refs[: 4 * slots], refs[4 * slots :]
    query, acc_all, top_all, sum_all = scratch
    blocks = query.shape[0] // BLOCK
    GROUP = 2 if blocks % 2 == 0 else 1
    row = lax.broadcasted_iota(jnp.int32, (BLOCK, BLOCK), 0)
    column = lax.broadcasted_iota(jnp.int32, (BLOCK, BLOCK), 1)
    causal = column <= row
    places = [meta[at] for at in bases_at]
    other = 1 - meta[core_at]
    for pair in range(HEADS // 2):
        lanes = slice(pair * PAIR, (pair + 1) * PAIR)
        total = partial[:, lanes]
        if weights:
            parts = [weights[0].at[:, lanes], weights[1].at[other, :, lanes]]
            total = total + add_up(tokens, places, parts)
        query[:, lanes] = total.astype(BF16)

    def lanes_of(head):
        return slice(head * HEAD_DIM, (head + 1) * HEAD_DIM)

    def rows_at(b):
        return slice(b * BLOCK, (b + 1) * BLOCK)

    def score(head, group):
        first, last = group * GROUP, (group + 1) * GROUP
        rows = slice(first * BLOCK, last * BLOCK)
        return qk(query[rows, lanes_of(head)], kv[: last * BLOCK, lanes_of(head)])

    def weigh(head, group, scores):
        near_block = meta[slot_at + head]
        far_block = meta[slot_at + HEADS + head]
        tops, weights = [], []
        for i in range(GROUP):
            b = group * GROUP + i
            mine = scores[rows_at(i)]
            times = (
                1
                + jnp.where(near_block == b, 1, 0)
                + jnp.where(far_block == b, meta[match_at + head], 0)
            ).astype(F32)
            diagonal = jnp.where(causal, mine[:, rows_at(b)], NEG)
            top = jnp.max(diagonal, axis=1, keepdims=True)
            if b:
                top = jnp.maximum(top, jnp.max(mine[:, : b * BLOCK], axis=1, keepdims=True))
            parts = [(jnp.exp2((diagonal - top) * SCALE2) * times).astype(BF16)]
            if b:
                parts.insert(0, jnp.exp2((mine[:, : b * BLOCK] - top) * SCALE2).astype(BF16))
            if i < GROUP - 1:
                parts.append(jnp.zeros((BLOCK, (GROUP - 1 - i) * BLOCK), BF16))
            tops.append(top)
            weights.append(jnp.concatenate(parts, axis=1))
        return tops, jnp.concatenate(weights, axis=0)

    def finish(head, group, tops, weight):
        lanes = lanes_of(head)
        keys = (group + 1) * GROUP * BLOCK
        value = kv[:keys, WIDTH + head * HEAD_DIM : WIDTH + (head + 1) * HEAD_DIM]
        both = jnp.dot(weight, with_ones(value), preferred_element_type=F32)
        rows = slice(group * GROUP * BLOCK, keys)
        acc, summed = both[:, :HEAD_DIM], both[:, HEAD_DIM:]
        out[rows, lanes] = (acc / summed).astype(BF16)
        acc_all[rows, lanes] = acc
        sum_all[rows, lanes] = summed
        for i, top in enumerate(tops):
            top_all[rows_at(group * GROUP + i), lanes] = jnp.broadcast_to(top, (BLOCK, HEAD_DIM))
        if group == blocks // GROUP - 1:
            for slot in range(slots):
                rows = rows_of(meta[slot_at + slot * HEADS + head])
                for target, source in zip(state[4 * slot :], scratch):
                    target[:, lanes] = source[rows, lanes]

    tasks = [(head, group) for head in range(HEADS) for group in range(blocks // GROUP)]
    scored, weighed = {}, {}
    for step in range(len(tasks) + 2):
        if step < len(tasks):
            scored[step] = score(*tasks[step])
        if 0 <= step - 1 < len(tasks):
            weighed[step - 1] = weigh(*tasks[step - 1], scored.pop(step - 1))
        if 0 <= step - 2 < len(tasks):
            finish(*tasks[step - 2], *weighed.pop(step - 2))


def merge_kernel(shifts, steps, slot_at, match_at, place_at, meta, *refs):
    slots = len(shifts)
    state = refs[: 4 * slots]
    packs = refs[4 * slots : 4 * slots + sum(shifts)]
    out, results, sems = refs[4 * slots + sum(shifts) + 1 :]
    if slots == 1:
        pl.when(meta[place_at] > 0)(lambda: merge_slots(
            shifts, steps, slot_at, match_at, place_at, meta, state, packs, out, results, sems
        ))
    else:
        merge_slots(shifts, steps, slot_at, match_at, place_at, meta, state, packs, out, results, sems)


def merge_slots(shifts, steps, slot_at, match_at, place_at, meta, state, packs, out, results, sems):
    lanes = [slice(head * HEAD_DIM, (head + 1) * HEAD_DIM) for head in range(HEADS)]
    values = [slice(WIDTH + head * HEAD_DIM, WIDTH + (head + 1) * HEAD_DIM) for head in range(HEADS)]
    earlier = [None] * HEADS
    for slot, count in enumerate(shifts):
        fields = packs[sum(shifts[:slot]) : sum(shifts[: slot + 1])]
        query, acc_ref, top_ref, sum_ref = state[4 * slot : 4 * slot + 4]
        place = meta[place_at + slot]
        scores, weights = [], []
        for head in range(HEADS):
            keys = jnp.concatenate([field[:, lanes[head]] for field in fields], axis=0)
            score = qk(query[:, lanes[head]], keys)
            parts = []
            for number, step in enumerate(steps[sum(shifts[:slot]) : sum(shifts[: slot + 1])]):
                seen = place ^ step < place
                if slot:
                    seen = seen & (meta[match_at + head] == 1)
                part = score[:, number * BLOCK : (number + 1) * BLOCK]
                parts.append(jnp.where(seen, part, NEG))
            scores.append(jnp.concatenate(parts, axis=1))
        for head in range(HEADS):
            acc, top, summed = (ref[:, lanes[head]] for ref in (acc_ref, top_ref, sum_ref))
            if slot:
                same = meta[slot_at + head] == meta[slot_at + HEADS + head]
                acc, top, summed = (
                    jnp.where(same, new, old) for new, old in zip(earlier[head], (acc, top, summed))
                )
            best = jnp.maximum(top, jnp.max(scores[head], axis=1, keepdims=True))
            decay = jnp.exp2((top - best) * SCALE2)
            weight = jnp.exp2((scores[head] - best[:, :1]) * SCALE2).astype(BF16)
            weights.append((acc * decay, best, summed * decay, weight))
        copies = []
        for head in range(HEADS):
            acc, best, summed, weight = weights[head]
            value = jnp.concatenate([field[:, values[head]] for field in fields], axis=0)
            both = jnp.dot(weight, with_ones(value), preferred_element_type=F32)
            acc = acc + both[:, :HEAD_DIM]
            summed = summed + both[:, HEAD_DIM:]
            earlier[head] = (acc, best, summed)
            results[slot, :, lanes[head]] = (acc / summed).astype(BF16)
            rows = rows_of(meta[slot_at + slot * HEADS + head])
            copies.append(
                pltpu.make_async_copy(
                    results.at[slot, :, lanes[head]], out.at[rows, lanes[head]], sems.at[head]
                )
            )
            copies[-1].start()
        for copy in copies:
            copy.wait()


def body(tokens, qkv_weight, near_offset, far_offset):
    sequence = tokens[0]
    row_count, depth = sequence.shape
    share = qkv_weight.shape[0]
    block_rate = row_count // BLOCK
    seq_size = lax.axis_size("seq")
    seq_index = lax.axis_index("seq")
    pieces = lax.axis_size("fsdp")
    mine = lax.axis_index("fsdp")
    near_size = min(16, seq_size)
    half = near_size // 2
    far_size = max(1, min(16, seq_size // STRIDE))
    near_at = lambda i: near_place(i, half, near_size)
    far_at = lambda i: (i // (STRIDE * far_size) * STRIDE + i % STRIDE, i // STRIDE % far_size)
    reach = max(near_at(i)[1] for i in range(seq_size))
    near_shifts = (1 << reach.bit_length()) - 1
    far_shifts = (1 << (far_size - 1).bit_length()) - 1
    slots = 2 if far_shifts else 1
    shifts = (near_shifts, far_shifts)[:slots]

    near_position = jnp.where(seq_index < half, seq_index, (seq_index - half) % near_size)
    far_position = seq_index // STRIDE % far_size
    far_match = (seq_index % STRIDE == far_offset // block_rate).astype(jnp.int32)
    spans = [(0, share // 4), (share // 2, share // 8)] if seq_size % 4 == 0 else []
    direct_from = spans[-1][0] + 2 * spans[-1][1] if spans else 0
    full_places = [(mine ^ j) * share for j in range(pieces)]
    scalars = list(full_places)
    place_at = len(scalars)
    scalars += [near_position, far_position]
    base_at = len(scalars)
    scalars += [(mine ^ bit) // 2 * 2 * share for bit in range(2, pieces, 2)]
    core_at = len(scalars)
    scalars.append(mine % 2)
    slot_at = len(scalars)
    match_at = slot_at + 2 * HEADS
    offsets_at = match_at + HEADS
    offsets = []
    for number, (start, rows) in enumerate(spans):
        side = seq_index // (1 << number) % 2
        offsets += [start + side * rows, start + (1 - side) * rows]
    offsets.append(direct_from)
    as_array = lambda values: jnp.stack([jnp.asarray(value, jnp.int32) for value in values])
    meta = jnp.concatenate(
        [as_array(scalars), near_offset, far_offset % block_rate, far_match, as_array(offsets)]
    )

    scalar_spec = pl.BlockSpec(memory_space=pltpu.SMEM)
    whole = pl.BlockSpec(memory_space=pltpu.VMEM)
    shape = jax.ShapeDtypeStruct

    def call(kernel, args, results, name, scratch=()):
        return pl.pallas_call(
            kernel,
            in_specs=[scalar_spec] + [whole] * len(args),
            out_specs=[whole] * len(results),
            out_shape=results,
            scratch_shapes=list(scratch),
            compiler_params=pltpu.CompilerParams(vmem_limit_bytes=VMEM_LIMIT),
            cost_estimate=pl.CostEstimate(flops=MODEL_FLOPS[name], bytes_accessed=1000, transcendentals=0),
            name=name,
        )(meta, *args)

    local = [qkv_weight]
    bits = range(2, pieces, 2)
    known = {}
    if pieces > 2 and spans:
        start, rows = spans[0]
        known["c0"] = lax.dynamic_slice(qkv_weight, (start + seq_index % 2 * rows, WIDTH), (rows, 2 * WIDTH))
    if pieces > 1:
        local.append(swap(ordered("core", qkv_weight, known), "fsdp", 1))
        known["core"] = local[-1]
    (partial,) = call(
        functools.partial(own_kernel, len(local)),
        [ordered("t", sequence, known), *local],
        [shape((row_count, 3 * WIDTH), F32)],
        "project_own",
    )
    known["partial"] = partial
    direct_rows, queries = [], []
    for bit in bits:
        mine_rows, other_rows = [], []
        for number, (start, rows) in enumerate(spans):
            tag = str(number)
            side = seq_index // (1 << number) % 2
            if number:
                known["c" + tag] = lax.dynamic_slice(
                    ordered("c" + tag, qkv_weight, known), (start + side * rows, WIDTH), (rows, 2 * WIDTH)
                )
            cut = known["c" + tag]
            direct = swap(cut, "fsdp", bit)
            known["x" + tag] = direct
            across = swap(ordered("f" + tag, direct, known), "fsdp", 1)
            known["f" + tag] = across
            passed = ordered("p" + tag, swap(ordered("y" + tag, direct, known), "seq", 1 << number), known)
            known["y" + tag] = passed
            mine_rows += [direct, passed]
            other_rows += [across, swap(passed, "fsdp", 1)]
            known["q" + tag] = other_rows[-1]
        known["meta"] = meta
        cut = ordered("cD", qkv_weight, known)[direct_from:, WIDTH:]
        known["cD"] = cut
        rest = swap(cut, "fsdp", bit)
        known["xD"] = rest
        rest = ordered("pD", rest, known)
        known["fD"] = swap(rest, "fsdp", 1)
        direct_rows.append(mine_rows + [rest] + other_rows + [known["fD"]])
        cut = ordered("cQ", qkv_weight, known)[:, :WIDTH]
        known["cQ"] = cut
        queries.append(swap(cut, "fsdp", bit))
    assert len(bits) <= 1
    if bits:
        bit = bits[0]
        count = len(direct_rows[0]) // 2
        layout = [offsets_at + i for i in range(count)]
        *sums, joined = call(
            functools.partial(first_rows_kernel, layout, bit, slots, slot_at),
            [sequence, ordered("a", partial, known), *direct_rows[0][:count]],
            [shape((BLOCK, 2 * WIDTH), F32)] * slots + [shape((share, 2 * WIDTH), BF16)],
            "project_first",
        )
        *packs, joined_other = call(
            functools.partial(last_rows_kernel, layout, bit ^ 1, slots, slot_at),
            [sequence, *sums, *direct_rows[0][count:]],
            [shape((BLOCK, 2 * WIDTH), BF16)] * slots + [shape((share, 2 * WIDTH), BF16)],
            "project_pack",
        )
        known["pack"] = packs[0]
        (kv,) = call(
            functools.partial(kv_kernel, [bit, bit ^ 1]),
            [sequence, ordered("kv", partial, known), joined, joined_other],
            [shape((row_count, 2 * WIDTH), BF16)],
            "project_kv",
        )
    else:
        kv = partial[:, WIDTH:].astype(BF16)
        blocks = kv.reshape(block_rate, BLOCK, 2, HEADS, HEAD_DIM)
        packs = []
        for offset in (near_offset, far_offset % block_rate)[:slots]:
            picked = blocks[offset, :, :, jnp.arange(HEADS)]
            packs.append(picked.transpose(1, 2, 0, 3).reshape(BLOCK, 2 * WIDTH))
    known["kv"] = kv
    received = []
    for pack, place, count, unit in zip(packs, (near_at, far_at), shifts, (1, STRIDE)):
        for step in NEAR_ORDER if count == len(NEAR_ORDER) else range(1, count + 1):
            received.append((step, lax.ppermute(pack, "seq", partners(seq_size, place, step))))
        known |= {f"n{step}": r for step, r in received}
    steps = [step for step, _ in received]
    received = [pack for _, pack in received]
    crossed_q, q_places = [], []
    for bit, direct in zip(bits, queries):
        direct = ordered("q", direct, known)
        (slots_out,) = call(
            functools.partial(slot_kernel, core_at), [direct], [shape((2,) + direct.shape, BF16)], "slot_queries"
        )
        both = lax.all_to_all(
            slots_out, "fsdp", 0, 0, axis_index_groups=[[i, i + 1] for i in range(0, pieces, 2)]
        )
        crossed_q += [direct, both]
        q_places += [bit, bit ^ 1]
    state_types = [BF16, F32, F32, F32]
    partial_out, *state = call(
        functools.partial(attend_kernel, q_places, core_at, slots, slot_at, match_at),
        [sequence, partial, *crossed_q, kv],
        [shape((row_count, WIDTH), BF16)] + [shape((BLOCK, WIDTH), kind) for kind in state_types] * slots,
        "attend_local",
        [pltpu.VMEM((row_count, WIDTH), kind) for kind in state_types],
    )
    count = 4 * slots + sum(shifts)
    merged = pl.pallas_call(
        functools.partial(merge_kernel, shifts, steps, slot_at, match_at, place_at),
        in_specs=[scalar_spec] + [whole] * count + [pl.BlockSpec(memory_space=pl.ANY)],
        out_specs=pl.BlockSpec(memory_space=pl.ANY),
        out_shape=shape((row_count, WIDTH), BF16),
        scratch_shapes=[pltpu.VMEM((slots, BLOCK, WIDTH), BF16), pltpu.SemaphoreType.DMA((HEADS,))],
        input_output_aliases={count + 1: 0},
        compiler_params=pltpu.CompilerParams(vmem_limit_bytes=VMEM_LIMIT),
        cost_estimate=pl.CostEstimate(flops=MODEL_FLOPS["merge_near"], bytes_accessed=1000, transcendentals=0),
        name="merge_near",
    )(meta, *state, *received, partial_out)
    return merged[None]


def solution(mesh):
    in_specs = (P("fsdp", "seq", None), P("fsdp", None), P(), P())
    out_specs = P("fsdp", "seq", None)
    return jax.shard_map(body, mesh=mesh, in_specs=in_specs, out_specs=out_specs, check_vma=False)
```

```python
import functools
import math

import jax
import jax.numpy as jnp
from jax import lax
from jax.experimental import pallas as pl
from jax.experimental.pallas import tpu as pltpu
from jax.sharding import PartitionSpec as P

HEADS = 4
HEAD_DIM = 128
BLOCK = 128
STRIDE = 8
WIDTH = HEADS * HEAD_DIM
PAIR = 2 * HEAD_DIM
NEG = -1e30
SCALE2 = HEAD_DIM ** (-0.5) * math.log2(math.e)
VMEM_LIMIT = 24 * 1024 * 1024

MODEL_FLOPS = {
    "slot_queries": 575000,
    "project_first": 689999,
    "project_pack": 689999,
    "project_own": 3680000,
    "project_kv": 2990000,
    "attend_local": 6325000,
    "merge_near": 2990000,
}
ORDER = {
    "c1": ("c0",),
    "cD": ("c1",),
    "cQ": ("cD",),
    "p0": ("partial", "xD"),
    "p1": ("partial",),
    "q": ("kv",),
    "kv": ("pack",),
}
NEAR_ORDER = (2, 3, 1)
F32 = jnp.float32
BF16 = jnp.bfloat16


def near_place(index, half, size):
    if index < half:
        return 0, index
    return 1 + (index - half) // size, (index - half) % size


def partners(count, place, bits):
    where = {place(i): i for i in range(count)}
    pairs = []
    for source in range(count):
        run, spot = place(source)
        if (run, spot ^ bits) in where:
            pairs.append((source, where[run, spot ^ bits]))
    return pairs


def swap(value, axis, bit):
    count = lax.axis_size(axis)
    return lax.ppermute(value, axis, [(i, i ^ bit) for i in range(count)])


def after(value, *others):
    return lax.optimization_barrier((value,) + others)[0]


def ordered(name, value, known):
    others = [known[other] for other in ORDER.get(name, ()) if other in known]
    return after(value, *others) if others else value


def rows_of(block):
    return pl.ds(pl.multiple_of(block * BLOCK, BLOCK), BLOCK)


def qk(query, key):
    return lax.dot_general(query, key, (((1,), (1,)), ((), ())), preferred_element_type=F32)


def add_up(tokens, places, weights):
    total = None
    for place, weight in zip(places, weights):
        depth = weight.shape[0]
        columns = pl.ds(pl.multiple_of(place, depth), depth)
        term = jnp.dot(tokens[:, columns], weight[...], preferred_element_type=F32)
        total = term if total is None else total + term
    return total


def own_kernel(count, meta, tokens, *refs):
    weights, out = refs[:count], refs[count]
    for j in range(out.shape[1] // PAIR):
        lanes = slice(j * PAIR, (j + 1) * PAIR)
        out[:, lanes] = add_up(tokens, [meta[at] for at in range(count)], [weight.at[:, lanes] for weight in weights])


def near_rows_kernel(layout, place_at, first, slots, slot_at, meta, tokens, before, *refs):
    arrived, refs = refs[: len(layout)], refs[len(layout) :]
    sums, joined = refs[:slots], refs[slots]
    for at, array in zip(layout, arrived):
        rows = array.shape[0]
        joined[pl.ds(pl.multiple_of(meta[at], rows), rows), :] = array[...]
    depth = joined.shape[0]
    columns = pl.ds(pl.multiple_of(meta[place_at], depth), depth)
    for slot in range(slots):
        for head in range(HEADS):
            rows = rows_of(meta[slot_at + HEADS * slot + head])
            lanes = [slice(start, start + HEAD_DIM) for start in (head * HEAD_DIM, WIDTH + head * HEAD_DIM)]
            weight = jnp.concatenate([joined[:, part] for part in lanes], axis=1)
            product = jnp.dot(tokens[rows, columns], weight, preferred_element_type=F32)
            for field, part in enumerate(lanes):
                if first:
                    total = before[0][rows, WIDTH + part.start : WIDTH + part.stop]
                else:
                    total = before[slot][:, part]
                total = total + product[:, field * HEAD_DIM : (field + 1) * HEAD_DIM]
                sums[slot][:, part] = total.astype(sums[slot].dtype)


def first_rows_kernel(layout, place_at, slots, slot_at, meta, tokens, partial, *refs):
    near_rows_kernel(layout, place_at, True, slots, slot_at, meta, tokens, [partial], *refs)


def last_rows_kernel(layout, place_at, slots, slot_at, meta, tokens, *refs):
    near_rows_kernel(layout, place_at, False, slots, slot_at, meta, tokens, refs[:slots], *refs[slots:])


def slot_kernel(core_at, meta, source, out):
    out[1 - meta[core_at]] = source[...]


def kv_kernel(places_at, meta, tokens, partial, *refs):
    parts, kv = refs[:-1], refs[-1]
    places = [meta[at] for at in places_at]
    for j in range(2 * WIDTH // PAIR):
        lanes = slice(j * PAIR, (j + 1) * PAIR)
        product = add_up(tokens, places, [part.at[:, lanes] for part in parts])
        kv[:, lanes] = (partial[:, WIDTH + j * PAIR : WIDTH + (j + 1) * PAIR] + product).astype(BF16)


def with_ones(value):
    return jnp.concatenate([value, jnp.ones(value.shape, BF16)], axis=1)


def attend_kernel(bases_at, core_at, slots, slot_at, match_at, meta, tokens, partial, *refs):
    weights, refs = refs[: len(bases_at)], refs[len(bases_at) :]
    kv, out, refs = refs[0], refs[1], refs[2:]
    state, scratch = refs[: 4 * slots], refs[4 * slots :]
    query, acc_all, top_all, sum_all = scratch
    blocks = query.shape[0] // BLOCK
    GROUP = 2 if blocks % 2 == 0 else 1
    row = lax.broadcasted_iota(jnp.int32, (BLOCK, BLOCK), 0)
    column = lax.broadcasted_iota(jnp.int32, (BLOCK, BLOCK), 1)
    causal = column <= row
    places = [meta[at] for at in bases_at]
    other = 1 - meta[core_at]
    for pair in range(HEADS // 2):
        lanes = slice(pair * PAIR, (pair + 1) * PAIR)
        total = partial[:, lanes]
        if weights:
            parts = [weights[0].at[:, lanes], weights[1].at[other, :, lanes]]
            total = total + add_up(tokens, places, parts)
        query[:, lanes] = total.astype(BF16)

    def lanes_of(head):
        return slice(head * HEAD_DIM, (head + 1) * HEAD_DIM)

    def rows_at(b):
        return slice(b * BLOCK, (b + 1) * BLOCK)

    def score(head, group):
        first, last = group * GROUP, (group + 1) * GROUP
        rows = slice(first * BLOCK, last * BLOCK)
        return qk(query[rows, lanes_of(head)], kv[: last * BLOCK, lanes_of(head)])

    def weigh(head, group, scores):
        near_block = meta[slot_at + head]
        far_block = meta[slot_at + HEADS + head]
        tops, weights = [], []
        for i in range(GROUP):
            b = group * GROUP + i
            mine = scores[rows_at(i)]
            times = (
                1
                + jnp.where(near_block == b, 1, 0)
                + jnp.where(far_block == b, meta[match_at + head], 0)
            ).astype(F32)
            diagonal = jnp.where(causal, mine[:, rows_at(b)], NEG)
            top = jnp.max(diagonal, axis=1, keepdims=True)
            if b:
                top = jnp.maximum(top, jnp.max(mine[:, : b * BLOCK], axis=1, keepdims=True))
            parts = [(jnp.exp2((diagonal - top) * SCALE2) * times).astype(BF16)]
            if b:
                parts.insert(0, jnp.exp2((mine[:, : b * BLOCK] - top) * SCALE2).astype(BF16))
            if i < GROUP - 1:
                parts.append(jnp.zeros((BLOCK, (GROUP - 1 - i) * BLOCK), BF16))
            tops.append(top)
            weights.append(jnp.concatenate(parts, axis=1))
        return tops, jnp.concatenate(weights, axis=0)

    def finish(head, group, tops, weight):
        lanes = lanes_of(head)
        keys = (group + 1) * GROUP * BLOCK
        value = kv[:keys, WIDTH + head * HEAD_DIM : WIDTH + (head + 1) * HEAD_DIM]
        both = jnp.dot(weight, with_ones(value), preferred_element_type=F32)
        rows = slice(group * GROUP * BLOCK, keys)
        acc, summed = both[:, :HEAD_DIM], both[:, HEAD_DIM:]
        out[rows, lanes] = (acc / summed).astype(BF16)
        acc_all[rows, lanes] = acc
        sum_all[rows, lanes] = summed
        for i, top in enumerate(tops):
            top_all[rows_at(group * GROUP + i), lanes] = jnp.broadcast_to(top, (BLOCK, HEAD_DIM))
        if group == blocks // GROUP - 1:
            for slot in range(slots):
                rows = rows_of(meta[slot_at + slot * HEADS + head])
                for target, source in zip(state[4 * slot :], scratch):
                    target[:, lanes] = source[rows, lanes]

    tasks = [(head, group) for head in range(HEADS) for group in range(blocks // GROUP)]
    scored, weighed = {}, {}
    for step in range(len(tasks) + 2):
        if step < len(tasks):
            scored[step] = score(*tasks[step])
        if 0 <= step - 1 < len(tasks):
            weighed[step - 1] = weigh(*tasks[step - 1], scored.pop(step - 1))
        if 0 <= step - 2 < len(tasks):
            finish(*tasks[step - 2], *weighed.pop(step - 2))


def merge_kernel(shifts, steps, slot_at, match_at, place_at, meta, *refs):
    slots = len(shifts)
    state = refs[: 4 * slots]
    packs = refs[4 * slots : 4 * slots + sum(shifts)]
    out, results, sems = refs[4 * slots + sum(shifts) + 1 :]
    if slots == 1:
        pl.when(meta[place_at] > 0)(lambda: merge_slots(
            shifts, steps, slot_at, match_at, place_at, meta, state, packs, out, results, sems
        ))
    else:
        merge_slots(shifts, steps, slot_at, match_at, place_at, meta, state, packs, out, results, sems)


def merge_slots(shifts, steps, slot_at, match_at, place_at, meta, state, packs, out, results, sems):
    lanes = [slice(head * HEAD_DIM, (head + 1) * HEAD_DIM) for head in range(HEADS)]
    values = [slice(WIDTH + head * HEAD_DIM, WIDTH + (head + 1) * HEAD_DIM) for head in range(HEADS)]
    earlier = [None] * HEADS
    for slot, count in enumerate(shifts):
        fields = packs[sum(shifts[:slot]) : sum(shifts[: slot + 1])]
        query, acc_ref, top_ref, sum_ref = state[4 * slot : 4 * slot + 4]
        place = meta[place_at + slot]
        scores, weights = [], []
        for head in range(HEADS):
            keys = jnp.concatenate([field[:, lanes[head]] for field in fields], axis=0)
            score = qk(query[:, lanes[head]], keys)
            parts = []
            for number, step in enumerate(steps[sum(shifts[:slot]) : sum(shifts[: slot + 1])]):
                seen = place ^ step < place
                if slot:
                    seen = seen & (meta[match_at + head] == 1)
                part = score[:, number * BLOCK : (number + 1) * BLOCK]
                parts.append(jnp.where(seen, part, NEG))
            scores.append(jnp.concatenate(parts, axis=1))
        for head in range(HEADS):
            acc, top, summed = (ref[:, lanes[head]] for ref in (acc_ref, top_ref, sum_ref))
            if slot:
                same = meta[slot_at + head] == meta[slot_at + HEADS + head]
                acc, top, summed = (
                    jnp.where(same, new, old) for new, old in zip(earlier[head], (acc, top, summed))
                )
            best = jnp.maximum(top, jnp.max(scores[head], axis=1, keepdims=True))
            decay = jnp.exp2((top - best) * SCALE2)
            weight = jnp.exp2((scores[head] - best[:, :1]) * SCALE2).astype(BF16)
            weights.append((acc * decay, best, summed * decay, weight))
        copies = []
        for head in range(HEADS):
            acc, best, summed, weight = weights[head]
            value = jnp.concatenate([field[:, values[head]] for field in fields], axis=0)
            both = jnp.dot(weight, with_ones(value), preferred_element_type=F32)
            acc = acc + both[:, :HEAD_DIM]
            summed = summed + both[:, HEAD_DIM:]
            earlier[head] = (acc, best, summed)
            results[slot, :, lanes[head]] = (acc / summed).astype(BF16)
            rows = rows_of(meta[slot_at + slot * HEADS + head])
            copies.append(
                pltpu.make_async_copy(
                    results.at[slot, :, lanes[head]], out.at[rows, lanes[head]], sems.at[head]
                )
            )
            copies[-1].start()
        for copy in copies:
            copy.wait()


def body(tokens, qkv_weight, near_offset, far_offset):
    sequence = tokens[0]
    row_count, depth = sequence.shape
    share = qkv_weight.shape[0]
    block_rate = row_count // BLOCK
    seq_size = lax.axis_size("seq")
    seq_index = lax.axis_index("seq")
    pieces = lax.axis_size("fsdp")
    mine = lax.axis_index("fsdp")
    near_size = min(16, seq_size)
    half = near_size // 2
    far_size = max(1, min(16, seq_size // STRIDE))
    near_at = lambda i: near_place(i, half, near_size)
    far_at = lambda i: (i // (STRIDE * far_size) * STRIDE + i % STRIDE, i // STRIDE % far_size)
    reach = max(near_at(i)[1] for i in range(seq_size))
    near_shifts = (1 << reach.bit_length()) - 1
    far_shifts = (1 << (far_size - 1).bit_length()) - 1
    slots = 2 if far_shifts else 1
    shifts = (near_shifts, far_shifts)[:slots]

    near_position = jnp.where(seq_index < half, seq_index, (seq_index - half) % near_size)
    far_position = seq_index // STRIDE % far_size
    far_match = (seq_index % STRIDE == far_offset // block_rate).astype(jnp.int32)
    spans = [(0, share // 4), (share // 2, share // 8)] if seq_size % 4 == 0 else []
    direct_from = spans[-1][0] + 2 * spans[-1][1] if spans else 0
    full_places = [(mine ^ j) * share for j in range(pieces)]
    scalars = list(full_places)
    place_at = len(scalars)
    scalars += [near_position, far_position]
    core_at = len(scalars)
    scalars.append(mine % 2)
    slot_at = len(scalars)
    match_at = slot_at + 2 * HEADS
    offsets_at = match_at + HEADS
    offsets = []
    for number, (start, rows) in enumerate(spans):
        side = seq_index // (1 << number) % 2
        offsets += [start + side * rows, start + (1 - side) * rows]
    offsets.append(direct_from)
    as_array = lambda values: jnp.stack([jnp.asarray(value, jnp.int32) for value in values])
    meta = jnp.concatenate(
        [as_array(scalars), near_offset, far_offset % block_rate, far_match, as_array(offsets)]
    )

    scalar_spec = pl.BlockSpec(memory_space=pltpu.SMEM)
    whole = pl.BlockSpec(memory_space=pltpu.VMEM)
    shape = jax.ShapeDtypeStruct

    def call(kernel, args, results, name, scratch=()):
        return pl.pallas_call(
            kernel,
            in_specs=[scalar_spec] + [whole] * len(args),
            out_specs=[whole] * len(results),
            out_shape=results,
            scratch_shapes=list(scratch),
            compiler_params=pltpu.CompilerParams(vmem_limit_bytes=VMEM_LIMIT),
            cost_estimate=pl.CostEstimate(flops=MODEL_FLOPS[name], bytes_accessed=1000, transcendentals=0),
            name=name,
        )(meta, *args)

    local = [qkv_weight]
    bits = range(2, pieces, 2)
    known = {}
    if pieces > 1:
        local.append(swap(qkv_weight, "fsdp", 1))
        known["core"] = local[-1]
    (partial,) = call(
        functools.partial(own_kernel, len(local)),
        [ordered("t", sequence, known), *local],
        [shape((row_count, 3 * WIDTH), F32)],
        "project_own",
    )
    known["partial"] = partial
    direct_rows, queries = [], []
    for bit in bits:
        mine_rows, other_rows = [], []
        for number, (start, rows) in enumerate(spans):
            tag = str(number)
            side = seq_index // (1 << number) % 2
            cut = lax.dynamic_slice(
                ordered("c" + tag, qkv_weight, known), (start + side * rows, WIDTH), (rows, 2 * WIDTH)
            )
            known["c" + tag] = cut
            direct = swap(cut, "fsdp", bit)
            known["x" + tag] = direct
            across = swap(ordered("f" + tag, direct, known), "fsdp", 1)
            known["f" + tag] = across
            passed = ordered("p" + tag, swap(ordered("y" + tag, direct, known), "seq", 1 << number), known)
            known["y" + tag] = passed
            mine_rows += [direct, passed]
            other_rows += [across, swap(passed, "fsdp", 1)]
            known["q" + tag] = other_rows[-1]
        cut = ordered("cD", qkv_weight, known)[direct_from:, WIDTH:]
        known["cD"] = cut
        rest = swap(cut, "fsdp", bit)
        known["xD"] = rest
        rest = ordered("pD", rest, known)
        known["fD"] = swap(rest, "fsdp", 1)
        direct_rows.append(mine_rows + [rest] + other_rows + [known["fD"]])
        cut = ordered("cQ", qkv_weight, known)[:, :WIDTH]
        known["cQ"] = cut
        queries.append(swap(cut, "fsdp", bit))
    assert len(bits) <= 1
    if bits:
        bit = bits[0]
        count = len(direct_rows[0]) // 2
        layout = [offsets_at + i for i in range(count)]
        *sums, joined = call(
            functools.partial(first_rows_kernel, layout, bit, slots, slot_at),
            [sequence, ordered("a", partial, known), *direct_rows[0][:count]],
            [shape((BLOCK, 2 * WIDTH), F32)] * slots + [shape((share, 2 * WIDTH), BF16)],
            "project_first",
        )
        *packs, joined_other = call(
            functools.partial(last_rows_kernel, layout, bit ^ 1, slots, slot_at),
            [sequence, *sums, *direct_rows[0][count:]],
            [shape((BLOCK, 2 * WIDTH), BF16)] * slots + [shape((share, 2 * WIDTH), BF16)],
            "project_pack",
        )
        known["pack"] = packs[0]
        (kv,) = call(
            functools.partial(kv_kernel, [bit, bit ^ 1]),
            [sequence, ordered("kv", partial, known), joined, joined_other],
            [shape((row_count, 2 * WIDTH), BF16)],
            "project_kv",
        )
    else:
        kv = partial[:, WIDTH:].astype(BF16)
        blocks = kv.reshape(block_rate, BLOCK, 2, HEADS, HEAD_DIM)
        packs = []
        for offset in (near_offset, far_offset % block_rate)[:slots]:
            picked = blocks[offset, :, :, jnp.arange(HEADS)]
            packs.append(picked.transpose(1, 2, 0, 3).reshape(BLOCK, 2 * WIDTH))
    known["kv"] = kv
    received = []
    for pack, place, count, unit in zip(packs, (near_at, far_at), shifts, (1, STRIDE)):
        for step in NEAR_ORDER if count == len(NEAR_ORDER) else range(1, count + 1):
            received.append((step, lax.ppermute(pack, "seq", partners(seq_size, place, step))))
        known |= {f"n{step}": r for step, r in received}
    steps = [step for step, _ in received]
    received = [pack for _, pack in received]
    crossed_q, q_places = [], []
    for bit, direct in zip(bits, queries):
        direct = ordered("q", direct, known)
        (slots_out,) = call(
            functools.partial(slot_kernel, core_at), [direct], [shape((2,) + direct.shape, BF16)], "slot_queries"
        )
        both = lax.all_to_all(
            slots_out, "fsdp", 0, 0, axis_index_groups=[[i, i + 1] for i in range(0, pieces, 2)]
        )
        crossed_q += [direct, both]
        q_places += [bit, bit ^ 1]
    state_types = [BF16, F32, F32, F32]
    partial_out, *state = call(
        functools.partial(attend_kernel, q_places, core_at, slots, slot_at, match_at),
        [sequence, partial, *crossed_q, kv],
        [shape((row_count, WIDTH), BF16)] + [shape((BLOCK, WIDTH), kind) for kind in state_types] * slots,
        "attend_local",
        [pltpu.VMEM((row_count, WIDTH), kind) for kind in state_types],
    )
    count = 4 * slots + sum(shifts)
    merged = pl.pallas_call(
        functools.partial(merge_kernel, shifts, steps, slot_at, match_at, place_at),
        in_specs=[scalar_spec] + [whole] * count + [pl.BlockSpec(memory_space=pl.ANY)],
        out_specs=pl.BlockSpec(memory_space=pl.ANY),
        out_shape=shape((row_count, WIDTH), BF16),
        scratch_shapes=[pltpu.VMEM((slots, BLOCK, WIDTH), BF16), pltpu.SemaphoreType.DMA((HEADS,))],
        input_output_aliases={count + 1: 0},
        compiler_params=pltpu.CompilerParams(vmem_limit_bytes=VMEM_LIMIT),
        cost_estimate=pl.CostEstimate(flops=MODEL_FLOPS["merge_near"], bytes_accessed=1000, transcendentals=0),
        name="merge_near",
    )(meta, *state, *received, partial_out)
    return merged[None]


def solution(mesh):
    in_specs = (P("fsdp", "seq", None), P("fsdp", None), P(), P())
    out_specs = P("fsdp", "seq", None)
    return jax.shard_map(body, mesh=mesh, in_specs=in_specs, out_specs=out_specs, check_vma=False)
```

```python
import functools
import math

import jax
import jax.numpy as jnp
from jax import lax
from jax.experimental import pallas as pl
from jax.experimental.pallas import tpu as pltpu
from jax.sharding import PartitionSpec as P

HEADS = 4
HEAD_DIM = 128
BLOCK = 128
STRIDE = 8
WIDTH = HEADS * HEAD_DIM
PAIR = 2 * HEAD_DIM
NEG = -1e30
SCALE2 = HEAD_DIM ** (-0.5) * math.log2(math.e)
VMEM_LIMIT = 24 * 1024 * 1024

MODEL_FLOPS = {
    "slot_queries": 575000,
    "project_first": 689999,
    "project_pack": 689999,
    "project_own": 3680000,
    "project_kv": 2990000,
    "attend_local": 6325000,
    "merge_near": 2990000,
}
ORDER = {
    "c1": ("c0",),
    "cD": ("c1",),
    "cQ": ("cD",),
    "p0": ("partial", "xD"),
    "p1": ("partial",),
    "q": ("kv",),
    "kv": ("pack",),
}
NEAR_ORDER = (3, 2, 1)
F32 = jnp.float32
BF16 = jnp.bfloat16


def near_place(index, half, size):
    if index < half:
        return 0, index
    return 1 + (index - half) // size, (index - half) % size


def partners(count, place, bits):
    where = {place(i): i for i in range(count)}
    pairs = []
    for source in range(count):
        run, spot = place(source)
        if (run, spot ^ bits) in where:
            pairs.append((source, where[run, spot ^ bits]))
    return pairs


def swap(value, axis, bit):
    count = lax.axis_size(axis)
    return lax.ppermute(value, axis, [(i, i ^ bit) for i in range(count)])


def after(value, *others):
    return lax.optimization_barrier((value,) + others)[0]


def ordered(name, value, known):
    others = [known[other] for other in ORDER.get(name, ()) if other in known]
    return after(value, *others) if others else value


def rows_of(block):
    return pl.ds(pl.multiple_of(block * BLOCK, BLOCK), BLOCK)


def qk(query, key):
    return lax.dot_general(query, key, (((1,), (1,)), ((), ())), preferred_element_type=F32)


def add_up(tokens, places, weights):
    total = None
    for place, weight in zip(places, weights):
        depth = weight.shape[0]
        columns = pl.ds(pl.multiple_of(place, depth), depth)
        term = jnp.dot(tokens[:, columns], weight[...], preferred_element_type=F32)
        total = term if total is None else total + term
    return total


def own_kernel(count, meta, tokens, *refs):
    weights, out = refs[:count], refs[count]
    for j in range(out.shape[1] // PAIR):
        lanes = slice(j * PAIR, (j + 1) * PAIR)
        out[:, lanes] = add_up(tokens, [meta[at] for at in range(count)], [weight.at[:, lanes] for weight in weights])


def near_rows_kernel(layout, place_at, first, slots, slot_at, meta, tokens, before, *refs):
    arrived, refs = refs[: len(layout)], refs[len(layout) :]
    sums, joined = refs[:slots], refs[slots]
    for at, array in zip(layout, arrived):
        rows = array.shape[0]
        joined[pl.ds(pl.multiple_of(meta[at], rows), rows), :] = array[...]
    depth = joined.shape[0]
    columns = pl.ds(pl.multiple_of(meta[place_at], depth), depth)
    for slot in range(slots):
        for head in range(HEADS):
            rows = rows_of(meta[slot_at + HEADS * slot + head])
            lanes = [slice(start, start + HEAD_DIM) for start in (head * HEAD_DIM, WIDTH + head * HEAD_DIM)]
            weight = jnp.concatenate([joined[:, part] for part in lanes], axis=1)
            product = jnp.dot(tokens[rows, columns], weight, preferred_element_type=F32)
            for field, part in enumerate(lanes):
                if first:
                    total = before[0][rows, WIDTH + part.start : WIDTH + part.stop]
                else:
                    total = before[slot][:, part]
                total = total + product[:, field * HEAD_DIM : (field + 1) * HEAD_DIM]
                sums[slot][:, part] = total.astype(sums[slot].dtype)


def first_rows_kernel(layout, place_at, slots, slot_at, meta, tokens, partial, *refs):
    near_rows_kernel(layout, place_at, True, slots, slot_at, meta, tokens, [partial], *refs)


def last_rows_kernel(layout, place_at, slots, slot_at, meta, tokens, *refs):
    near_rows_kernel(layout, place_at, False, slots, slot_at, meta, tokens, refs[:slots], *refs[slots:])


def slot_kernel(core_at, meta, source, out):
    out[1 - meta[core_at]] = source[...]


def kv_kernel(places_at, meta, tokens, partial, *refs):
    parts, kv = refs[:-1], refs[-1]
    places = [meta[at] for at in places_at]
    for j in range(2 * WIDTH // PAIR):
        lanes = slice(j * PAIR, (j + 1) * PAIR)
        product = add_up(tokens, places, [part.at[:, lanes] for part in parts])
        kv[:, lanes] = (partial[:, WIDTH + j * PAIR : WIDTH + (j + 1) * PAIR] + product).astype(BF16)


def with_ones(value):
    return jnp.concatenate([value, jnp.ones(value.shape, BF16)], axis=1)


def attend_kernel(bases_at, core_at, slots, slot_at, match_at, meta, tokens, partial, *refs):
    weights, refs = refs[: len(bases_at)], refs[len(bases_at) :]
    kv, out, refs = refs[0], refs[1], refs[2:]
    state, scratch = refs[: 4 * slots], refs[4 * slots :]
    query, acc_all, top_all, sum_all = scratch
    blocks = query.shape[0] // BLOCK
    GROUP = 2 if blocks % 2 == 0 else 1
    row = lax.broadcasted_iota(jnp.int32, (BLOCK, BLOCK), 0)
    column = lax.broadcasted_iota(jnp.int32, (BLOCK, BLOCK), 1)
    causal = column <= row
    places = [meta[at] for at in bases_at]
    other = 1 - meta[core_at]
    for pair in range(HEADS // 2):
        lanes = slice(pair * PAIR, (pair + 1) * PAIR)
        total = partial[:, lanes]
        if weights:
            parts = [weights[0].at[:, lanes], weights[1].at[other, :, lanes]]
            total = total + add_up(tokens, places, parts)
        query[:, lanes] = total.astype(BF16)

    def lanes_of(head):
        return slice(head * HEAD_DIM, (head + 1) * HEAD_DIM)

    def rows_at(b):
        return slice(b * BLOCK, (b + 1) * BLOCK)

    def score(head, group):
        first, last = group * GROUP, (group + 1) * GROUP
        rows = slice(first * BLOCK, last * BLOCK)
        return qk(query[rows, lanes_of(head)], kv[: last * BLOCK, lanes_of(head)])

    def weigh(head, group, scores):
        near_block = meta[slot_at + head]
        far_block = meta[slot_at + HEADS + head]
        tops, weights = [], []
        for i in range(GROUP):
            b = group * GROUP + i
            mine = scores[rows_at(i)]
            times = (
                1
                + jnp.where(near_block == b, 1, 0)
                + jnp.where(far_block == b, meta[match_at + head], 0)
            ).astype(F32)
            diagonal = jnp.where(causal, mine[:, rows_at(b)], NEG)
            top = jnp.max(diagonal, axis=1, keepdims=True)
            if b:
                top = jnp.maximum(top, jnp.max(mine[:, : b * BLOCK], axis=1, keepdims=True))
            parts = [(jnp.exp2((diagonal - top) * SCALE2) * times).astype(BF16)]
            if b:
                parts.insert(0, jnp.exp2((mine[:, : b * BLOCK] - top) * SCALE2).astype(BF16))
            if i < GROUP - 1:
                parts.append(jnp.zeros((BLOCK, (GROUP - 1 - i) * BLOCK), BF16))
            tops.append(top)
            weights.append(jnp.concatenate(parts, axis=1))
        return tops, jnp.concatenate(weights, axis=0)

    def finish(head, group, tops, weight):
        lanes = lanes_of(head)
        keys = (group + 1) * GROUP * BLOCK
        value = kv[:keys, WIDTH + head * HEAD_DIM : WIDTH + (head + 1) * HEAD_DIM]
        both = jnp.dot(weight, with_ones(value), preferred_element_type=F32)
        rows = slice(group * GROUP * BLOCK, keys)
        acc, summed = both[:, :HEAD_DIM], both[:, HEAD_DIM:]
        out[rows, lanes] = (acc / summed).astype(BF16)
        acc_all[rows, lanes] = acc
        sum_all[rows, lanes] = summed
        for i, top in enumerate(tops):
            top_all[rows_at(group * GROUP + i), lanes] = jnp.broadcast_to(top, (BLOCK, HEAD_DIM))
        if group == blocks // GROUP - 1:
            for slot in range(slots):
                rows = rows_of(meta[slot_at + slot * HEADS + head])
                for target, source in zip(state[4 * slot :], scratch):
                    target[:, lanes] = source[rows, lanes]

    tasks = [(head, group) for head in range(HEADS) for group in range(blocks // GROUP)]
    scored, weighed = {}, {}
    for step in range(len(tasks) + 2):
        if step < len(tasks):
            scored[step] = score(*tasks[step])
        if 0 <= step - 1 < len(tasks):
            weighed[step - 1] = weigh(*tasks[step - 1], scored.pop(step - 1))
        if 0 <= step - 2 < len(tasks):
            finish(*tasks[step - 2], *weighed.pop(step - 2))


def merge_kernel(shifts, steps, slot_at, match_at, place_at, meta, *refs):
    slots = len(shifts)
    state = refs[: 4 * slots]
    packs = refs[4 * slots : 4 * slots + sum(shifts)]
    out, results, sems = refs[4 * slots + sum(shifts) + 1 :]
    if slots == 1:
        pl.when(meta[place_at] > 0)(lambda: merge_slots(
            shifts, steps, slot_at, match_at, place_at, meta, state, packs, out, results, sems
        ))
    else:
        merge_slots(shifts, steps, slot_at, match_at, place_at, meta, state, packs, out, results, sems)


def merge_slots(shifts, steps, slot_at, match_at, place_at, meta, state, packs, out, results, sems):
    lanes = [slice(head * HEAD_DIM, (head + 1) * HEAD_DIM) for head in range(HEADS)]
    values = [slice(WIDTH + head * HEAD_DIM, WIDTH + (head + 1) * HEAD_DIM) for head in range(HEADS)]
    earlier = [None] * HEADS
    for slot, count in enumerate(shifts):
        fields = packs[sum(shifts[:slot]) : sum(shifts[: slot + 1])]
        query, acc_ref, top_ref, sum_ref = state[4 * slot : 4 * slot + 4]
        place = meta[place_at + slot]
        scores, weights = [], []
        for head in range(HEADS):
            keys = jnp.concatenate([field[:, lanes[head]] for field in fields], axis=0)
            score = qk(query[:, lanes[head]], keys)
            parts = []
            for number, step in enumerate(steps[sum(shifts[:slot]) : sum(shifts[: slot + 1])]):
                seen = place ^ step < place
                if slot:
                    seen = seen & (meta[match_at + head] == 1)
                part = score[:, number * BLOCK : (number + 1) * BLOCK]
                parts.append(jnp.where(seen, part, NEG))
            scores.append(jnp.concatenate(parts, axis=1))
        for head in range(HEADS):
            acc, top, summed = (ref[:, lanes[head]] for ref in (acc_ref, top_ref, sum_ref))
            if slot:
                same = meta[slot_at + head] == meta[slot_at + HEADS + head]
                acc, top, summed = (
                    jnp.where(same, new, old) for new, old in zip(earlier[head], (acc, top, summed))
                )
            best = jnp.maximum(top, jnp.max(scores[head], axis=1, keepdims=True))
            decay = jnp.exp2((top - best) * SCALE2)
            weight = jnp.exp2((scores[head] - best[:, :1]) * SCALE2).astype(BF16)
            weights.append((acc * decay, best, summed * decay, weight))
        copies = []
        for head in range(HEADS):
            acc, best, summed, weight = weights[head]
            value = jnp.concatenate([field[:, values[head]] for field in fields], axis=0)
            both = jnp.dot(weight, with_ones(value), preferred_element_type=F32)
            acc = acc + both[:, :HEAD_DIM]
            summed = summed + both[:, HEAD_DIM:]
            earlier[head] = (acc, best, summed)
            results[slot, :, lanes[head]] = (acc / summed).astype(BF16)
            rows = rows_of(meta[slot_at + slot * HEADS + head])
            copies.append(
                pltpu.make_async_copy(
                    results.at[slot, :, lanes[head]], out.at[rows, lanes[head]], sems.at[head]
                )
            )
            copies[-1].start()
        for copy in copies:
            copy.wait()


def body(tokens, qkv_weight, near_offset, far_offset):
    sequence = tokens[0]
    row_count, depth = sequence.shape
    share = qkv_weight.shape[0]
    block_rate = row_count // BLOCK
    seq_size = lax.axis_size("seq")
    seq_index = lax.axis_index("seq")
    pieces = lax.axis_size("fsdp")
    mine = lax.axis_index("fsdp")
    near_size = min(16, seq_size)
    half = near_size // 2
    far_size = max(1, min(16, seq_size // STRIDE))
    near_at = lambda i: near_place(i, half, near_size)
    far_at = lambda i: (i // (STRIDE * far_size) * STRIDE + i % STRIDE, i // STRIDE % far_size)
    reach = max(near_at(i)[1] for i in range(seq_size))
    near_shifts = (1 << reach.bit_length()) - 1
    far_shifts = (1 << (far_size - 1).bit_length()) - 1
    slots = 2 if far_shifts else 1
    shifts = (near_shifts, far_shifts)[:slots]

    near_position = jnp.where(seq_index < half, seq_index, (seq_index - half) % near_size)
    far_position = seq_index // STRIDE % far_size
    far_match = (seq_index % STRIDE == far_offset // block_rate).astype(jnp.int32)
    spans = [(0, share // 4), (share // 2, share // 8)] if seq_size % 4 == 0 else []
    direct_from = spans[-1][0] + 2 * spans[-1][1] if spans else 0
    full_places = [(mine ^ j) * share for j in range(pieces)]
    scalars = list(full_places)
    place_at = len(scalars)
    scalars += [near_position, far_position]
    core_at = len(scalars)
    scalars.append(mine % 2)
    slot_at = len(scalars)
    match_at = slot_at + 2 * HEADS
    offsets_at = match_at + HEADS
    offsets = []
    for number, (start, rows) in enumerate(spans):
        side = seq_index // (1 << number) % 2
        offsets += [start + side * rows, start + (1 - side) * rows]
    offsets.append(direct_from)
    as_array = lambda values: jnp.stack([jnp.asarray(value, jnp.int32) for value in values])
    meta = jnp.concatenate(
        [as_array(scalars), near_offset, far_offset % block_rate, far_match, as_array(offsets)]
    )

    scalar_spec = pl.BlockSpec(memory_space=pltpu.SMEM)
    whole = pl.BlockSpec(memory_space=pltpu.VMEM)
    shape = jax.ShapeDtypeStruct

    def call(kernel, args, results, name, scratch=()):
        return pl.pallas_call(
            kernel,
            in_specs=[scalar_spec] + [whole] * len(args),
            out_specs=[whole] * len(results),
            out_shape=results,
            scratch_shapes=list(scratch),
            compiler_params=pltpu.CompilerParams(vmem_limit_bytes=VMEM_LIMIT),
            cost_estimate=pl.CostEstimate(flops=MODEL_FLOPS[name], bytes_accessed=1000, transcendentals=0),
            name=name,
        )(meta, *args)

    local = [qkv_weight]
    bits = range(2, pieces, 2)
    known = {}
    if pieces > 1:
        local.append(swap(qkv_weight, "fsdp", 1))
        known["core"] = local[-1]
    (partial,) = call(
        functools.partial(own_kernel, len(local)),
        [ordered("t", sequence, known), *local],
        [shape((row_count, 3 * WIDTH), F32)],
        "project_own",
    )
    known["partial"] = partial
    direct_rows, queries = [], []
    for bit in bits:
        mine_rows, other_rows = [], []
        for number, (start, rows) in enumerate(spans):
            tag = str(number)
            side = seq_index // (1 << number) % 2
            cut = lax.dynamic_slice(
                ordered("c" + tag, qkv_weight, known), (start + side * rows, WIDTH), (rows, 2 * WIDTH)
            )
            known["c" + tag] = cut
            direct = swap(cut, "fsdp", bit)
            known["x" + tag] = direct
            across = swap(ordered("f" + tag, direct, known), "fsdp", 1)
            known["f" + tag] = across
            passed = ordered("p" + tag, swap(ordered("y" + tag, direct, known), "seq", 1 << number), known)
            known["y" + tag] = passed
            mine_rows += [direct, passed]
            other_rows += [across, swap(passed, "fsdp", 1)]
            known["q" + tag] = other_rows[-1]
        cut = ordered("cD", qkv_weight, known)[direct_from:, WIDTH:]
        known["cD"] = cut
        rest = swap(cut, "fsdp", bit)
        known["xD"] = rest
        rest = ordered("pD", rest, known)
        known["fD"] = swap(rest, "fsdp", 1)
        direct_rows.append(mine_rows + [rest] + other_rows + [known["fD"]])
        cut = ordered("cQ", qkv_weight, known)[:, :WIDTH]
        known["cQ"] = cut
        queries.append(swap(cut, "fsdp", bit))
    assert len(bits) <= 1
    if bits:
        bit = bits[0]
        count = len(direct_rows[0]) // 2
        layout = [offsets_at + i for i in range(count)]
        *sums, joined = call(
            functools.partial(first_rows_kernel, layout, bit, slots, slot_at),
            [sequence, ordered("a", partial, known), *direct_rows[0][:count]],
            [shape((BLOCK, 2 * WIDTH), F32)] * slots + [shape((share, 2 * WIDTH), BF16)],
            "project_first",
        )
        *packs, joined_other = call(
            functools.partial(last_rows_kernel, layout, bit ^ 1, slots, slot_at),
            [sequence, *sums, *direct_rows[0][count:]],
            [shape((BLOCK, 2 * WIDTH), BF16)] * slots + [shape((share, 2 * WIDTH), BF16)],
            "project_pack",
        )
        known["pack"] = packs[0]
        (kv,) = call(
            functools.partial(kv_kernel, [bit, bit ^ 1]),
            [sequence, ordered("kv", partial, known), joined, joined_other],
            [shape((row_count, 2 * WIDTH), BF16)],
            "project_kv",
        )
    else:
        kv = partial[:, WIDTH:].astype(BF16)
        blocks = kv.reshape(block_rate, BLOCK, 2, HEADS, HEAD_DIM)
        packs = []
        for offset in (near_offset, far_offset % block_rate)[:slots]:
            picked = blocks[offset, :, :, jnp.arange(HEADS)]
            packs.append(picked.transpose(1, 2, 0, 3).reshape(BLOCK, 2 * WIDTH))
    known["kv"] = kv
    received = []
    for pack, place, count, unit in zip(packs, (near_at, far_at), shifts, (1, STRIDE)):
        for step in NEAR_ORDER if count == len(NEAR_ORDER) else range(1, count + 1):
            received.append((step, lax.ppermute(pack, "seq", partners(seq_size, place, step))))
        known |= {f"n{step}": r for step, r in received}
    steps = [step for step, _ in received]
    received = [pack for _, pack in received]
    crossed_q, q_places = [], []
    for bit, direct in zip(bits, queries):
        direct = ordered("q", direct, known)
        (slots_out,) = call(
            functools.partial(slot_kernel, core_at), [direct], [shape((2,) + direct.shape, BF16)], "slot_queries"
        )
        both = lax.all_to_all(
            slots_out, "fsdp", 0, 0, axis_index_groups=[[i, i + 1] for i in range(0, pieces, 2)]
        )
        crossed_q += [direct, both]
        q_places += [bit, bit ^ 1]
    state_types = [BF16, F32, F32, F32]
    partial_out, *state = call(
        functools.partial(attend_kernel, q_places, core_at, slots, slot_at, match_at),
        [sequence, partial, *crossed_q, kv],
        [shape((row_count, WIDTH), BF16)] + [shape((BLOCK, WIDTH), kind) for kind in state_types] * slots,
        "attend_local",
        [pltpu.VMEM((row_count, WIDTH), kind) for kind in state_types],
    )
    count = 4 * slots + sum(shifts)
    merged = pl.pallas_call(
        functools.partial(merge_kernel, shifts, steps, slot_at, match_at, place_at),
        in_specs=[scalar_spec] + [whole] * count + [pl.BlockSpec(memory_space=pl.ANY)],
        out_specs=pl.BlockSpec(memory_space=pl.ANY),
        out_shape=shape((row_count, WIDTH), BF16),
        scratch_shapes=[pltpu.VMEM((slots, BLOCK, WIDTH), BF16), pltpu.SemaphoreType.DMA((HEADS,))],
        input_output_aliases={count + 1: 0},
        compiler_params=pltpu.CompilerParams(vmem_limit_bytes=VMEM_LIMIT),
        cost_estimate=pl.CostEstimate(flops=MODEL_FLOPS["merge_near"], bytes_accessed=1000, transcendentals=0),
        name="merge_near",
    )(meta, *state, *received, partial_out)
    return merged[None]


def solution(mesh):
    in_specs = (P("fsdp", "seq", None), P("fsdp", None), P(), P())
    out_specs = P("fsdp", "seq", None)
    return jax.shard_map(body, mesh=mesh, in_specs=in_specs, out_specs=out_specs, check_vma=False)
```

```python
import functools
import math

import jax
import jax.numpy as jnp
from jax import lax
from jax.experimental import pallas as pl
from jax.experimental.pallas import tpu as pltpu
from jax.sharding import PartitionSpec as P

HEADS = 4
HEAD_DIM = 128
BLOCK = 128
STRIDE = 8
WIDTH = HEADS * HEAD_DIM
PAIR = 2 * HEAD_DIM
NEG = -1e30
SCALE2 = HEAD_DIM ** (-0.5) * math.log2(math.e)
VMEM_LIMIT = 24 * 1024 * 1024

MODEL_FLOPS = {"project_first": 689999, "slot_queries": 575000, "project_pack": 689999, "project_own": 3680000, "project_mid": 1610000, "project_kv": 2990000, "attend_local": 6325000, "merge_near": 2990000}
ORDER = {
    'c1': ('c0',),
    'cD': ('c1',),
    'cQ': ('cD',),
    'p0': ('partial', 'xD'),
    'p1': ('partial',),
    'q': ('kv',),
    'kv': ('pack',),
}
NEAR_ORDER = (3, 2, 1)
F32 = jnp.float32
BF16 = jnp.bfloat16


def near_place(index, half, size):
    if index < half:
        return 0, index
    return 1 + (index - half) // size, (index - half) % size


def partners(count, place, bits):
    where = {place(i): i for i in range(count)}
    pairs = []
    for source in range(count):
        run, spot = place(source)
        if (run, spot ^ bits) in where:
            pairs.append((source, where[run, spot ^ bits]))
    return pairs


def swap(value, axis, bit):
    count = lax.axis_size(axis)
    return lax.ppermute(value, axis, [(i, i ^ bit) for i in range(count)])


def after(value, *others):
    return lax.optimization_barrier((value,) + others)[0]


def ordered(name, value, known):
    others = [known[other] for other in ORDER.get(name, ()) if other in known]
    return after(value, *others) if others else value


def rows_of(block):
    return pl.ds(pl.multiple_of(block * BLOCK, BLOCK), BLOCK)


def qk(query, key):
    return lax.dot_general(query, key, (((1,), (1,)), ((), ())), preferred_element_type=F32)


def pv(weights, value):
    return jnp.dot(weights.astype(BF16), value, preferred_element_type=F32)


def add_up(tokens, places, weights):
    total = None
    for place, weight in zip(places, weights):
        depth = weight.shape[0]
        columns = pl.ds(pl.multiple_of(place, depth), depth)
        term = jnp.dot(tokens[:, columns], weight[...], preferred_element_type=F32)
        total = term if total is None else total + term
    return total


def own_kernel(count, meta, tokens, *refs):
    weights, out = refs[:count], refs[count]
    for j in range(out.shape[1] // PAIR):
        lanes = slice(j * PAIR, (j + 1) * PAIR)
        out[:, lanes] = add_up(tokens, [meta[at] for at in range(count)], [weight.at[:, lanes] for weight in weights])


def near_rows_kernel(layout, place_at, first, slots, slot_at, meta, tokens, before, *refs):
    arrived, refs = refs[: len(layout)], refs[len(layout) :]
    sums, joined = refs[:slots], refs[slots]
    for at, array in zip(layout, arrived):
        rows = array.shape[0]
        joined[pl.ds(pl.multiple_of(meta[at], 16), rows), :] = array[...]
    depth = joined.shape[0]
    columns = pl.ds(pl.multiple_of(meta[place_at], depth), depth)
    for slot in range(slots):
        for head in range(HEADS):
            rows = rows_of(meta[slot_at + HEADS * slot + head])
            lanes = [slice(start, start + HEAD_DIM) for start in (head * HEAD_DIM, WIDTH + head * HEAD_DIM)]
            weight = jnp.concatenate([joined[:, part] for part in lanes], axis=1)
            product = jnp.dot(tokens[rows, columns], weight, preferred_element_type=F32)
            for field, part in enumerate(lanes):
                if first:
                    total = before[0][rows, WIDTH + part.start : WIDTH + part.stop]
                else:
                    total = before[slot][:, part]
                total = total + product[:, field * HEAD_DIM : (field + 1) * HEAD_DIM]
                sums[slot][:, part] = total.astype(sums[slot].dtype)


def first_rows_kernel(layout, place_at, slots, slot_at, meta, tokens, partial, *refs):
    near_rows_kernel(layout, place_at, True, slots, slot_at, meta, tokens, [partial], *refs)


def last_rows_kernel(layout, place_at, slots, slot_at, meta, tokens, *refs):
    near_rows_kernel(layout, place_at, False, slots, slot_at, meta, tokens, refs[:slots], *refs[slots:])


def slot_kernel(core_at, meta, source, out):
    out[1 - meta[core_at]] = source[...]


def kv_kernel(places_at, meta, tokens, partial, *refs):
    parts, kv = refs[:-1], refs[-1]
    places = [meta[at] for at in places_at]
    for j in range(2 * WIDTH // PAIR):
        lanes = slice(j * PAIR, (j + 1) * PAIR)
        product = add_up(tokens, places, [part.at[:, lanes] for part in parts])
        kv[:, lanes] = (partial[:, WIDTH + j * PAIR : WIDTH + (j + 1) * PAIR] + product).astype(BF16)


def with_ones(value):
    return jnp.concatenate([value, jnp.ones(value.shape, BF16)], axis=1)


def attend_kernel(bases_at, core_at, slots, slot_at, match_at, meta, tokens, partial, *refs):
    weights, refs = refs[: len(bases_at)], refs[len(bases_at) :]
    kv, out, refs = refs[0], refs[1], refs[2:]
    state, scratch = refs[: 4 * slots], refs[4 * slots :]
    query, acc_all, top_all, sum_all = scratch
    blocks = query.shape[0] // BLOCK
    GROUP = 2 if blocks % 2 == 0 else 1
    row = lax.broadcasted_iota(jnp.int32, (BLOCK, BLOCK), 0)
    column = lax.broadcasted_iota(jnp.int32, (BLOCK, BLOCK), 1)
    causal = column <= row
    places = [meta[at] for at in bases_at]
    other = 1 - meta[core_at]
    for pair in range(HEADS // 2):
        lanes = slice(pair * PAIR, (pair + 1) * PAIR)
        total = partial[:, lanes]
        if weights:
            parts = [weights[0].at[:, lanes], weights[1].at[other, :, lanes]]
            total = total + add_up(tokens, places, parts)
        query[:, lanes] = total.astype(BF16)

    def lanes_of(head):
        return slice(head * HEAD_DIM, (head + 1) * HEAD_DIM)

    def rows_at(b):
        return slice(b * BLOCK, (b + 1) * BLOCK)

    def score(head, group):
        first, last = group * GROUP, (group + 1) * GROUP
        rows = slice(first * BLOCK, last * BLOCK)
        return qk(query[rows, lanes_of(head)], kv[: last * BLOCK, lanes_of(head)])

    def weigh(head, group, scores):
        near_block = meta[slot_at + head]
        far_block = meta[slot_at + HEADS + head]
        tops, weights = [], []
        for i in range(GROUP):
            b = group * GROUP + i
            mine = scores[rows_at(i)]
            times = (
                1
                + jnp.where(near_block == b, 1, 0)
                + jnp.where(far_block == b, meta[match_at + head], 0)
            ).astype(F32)
            diagonal = jnp.where(causal, mine[:, rows_at(b)], NEG)
            top = jnp.max(diagonal, axis=1, keepdims=True)
            if b:
                top = jnp.maximum(top, jnp.max(mine[:, : b * BLOCK], axis=1, keepdims=True))
            parts = [(jnp.exp2((diagonal - top) * SCALE2) * times).astype(BF16)]
            if b:
                parts.insert(0, jnp.exp2((mine[:, : b * BLOCK] - top) * SCALE2).astype(BF16))
            if i < GROUP - 1:
                parts.append(jnp.zeros((BLOCK, (GROUP - 1 - i) * BLOCK), BF16))
            tops.append(top)
            weights.append(jnp.concatenate(parts, axis=1))
        return tops, jnp.concatenate(weights, axis=0)

    def finish(head, group, tops, weight):
        lanes = lanes_of(head)
        keys = (group + 1) * GROUP * BLOCK
        value = kv[:keys, WIDTH + head * HEAD_DIM : WIDTH + (head + 1) * HEAD_DIM]
        both = jnp.dot(weight, with_ones(value), preferred_element_type=F32)
        rows = slice(group * GROUP * BLOCK, keys)
        acc, summed = both[:, :HEAD_DIM], both[:, HEAD_DIM:]
        out[rows, lanes] = (acc / summed).astype(BF16)
        acc_all[rows, lanes] = acc
        sum_all[rows, lanes] = summed
        for i, top in enumerate(tops):
            top_all[rows_at(group * GROUP + i), lanes] = jnp.broadcast_to(top, (BLOCK, HEAD_DIM))
        if group == blocks // GROUP - 1:
            for slot in range(slots):
                rows = rows_of(meta[slot_at + slot * HEADS + head])
                for target, source in zip(state[4 * slot :], scratch):
                    target[:, lanes] = source[rows, lanes]

    tasks = [(head, group) for head in range(HEADS) for group in range(blocks // GROUP)]
    scored, weighed = {}, {}
    for step in range(len(tasks) + 2):
        if step < len(tasks):
            scored[step] = score(*tasks[step])
        if 0 <= step - 1 < len(tasks):
            weighed[step - 1] = weigh(*tasks[step - 1], scored.pop(step - 1))
        if 0 <= step - 2 < len(tasks):
            finish(*tasks[step - 2], *weighed.pop(step - 2))


def merge_kernel(shifts, steps, slot_at, match_at, place_at, meta, *refs):
    slots = len(shifts)
    state = refs[: 4 * slots]
    packs = refs[4 * slots : 4 * slots + sum(shifts)]
    out, results, sems = refs[4 * slots + sum(shifts) + 1 :]
    if slots == 1:
        pl.when(meta[place_at] > 0)(lambda: merge_slots(
            shifts, steps, slot_at, match_at, place_at, meta, state, packs, out, results, sems
        ))
    else:
        merge_slots(shifts, steps, slot_at, match_at, place_at, meta, state, packs, out, results, sems)


def merge_slots(shifts, steps, slot_at, match_at, place_at, meta, state, packs, out, results, sems):
    lanes = [slice(head * HEAD_DIM, (head + 1) * HEAD_DIM) for head in range(HEADS)]
    values = [slice(WIDTH + head * HEAD_DIM, WIDTH + (head + 1) * HEAD_DIM) for head in range(HEADS)]
    earlier = [None] * HEADS
    for slot, count in enumerate(shifts):
        fields = packs[sum(shifts[:slot]) : sum(shifts[: slot + 1])]
        query, acc_ref, top_ref, sum_ref = state[4 * slot : 4 * slot + 4]
        place = meta[place_at + slot]
        scores, weights = [], []
        for head in range(HEADS):
            keys = jnp.concatenate([field[:, lanes[head]] for field in fields], axis=0)
            score = qk(query[:, lanes[head]], keys)
            parts = []
            for number, step in enumerate(steps[sum(shifts[:slot]) : sum(shifts[: slot + 1])]):
                seen = place ^ step < place
                if slot:
                    seen = seen & (meta[match_at + head] == 1)
                part = score[:, number * BLOCK : (number + 1) * BLOCK]
                parts.append(jnp.where(seen, part, NEG))
            scores.append(jnp.concatenate(parts, axis=1))
        for head in range(HEADS):
            acc, top, summed = (ref[:, lanes[head]] for ref in (acc_ref, top_ref, sum_ref))
            if slot:
                same = meta[slot_at + head] == meta[slot_at + HEADS + head]
                acc, top, summed = (
                    jnp.where(same, new, old) for new, old in zip(earlier[head], (acc, top, summed))
                )
            best = jnp.maximum(top, jnp.max(scores[head], axis=1, keepdims=True))
            decay = jnp.exp2((top - best) * SCALE2)
            weight = jnp.exp2((scores[head] - best[:, :1]) * SCALE2).astype(BF16)
            weights.append((acc * decay, best, summed * decay, weight))
        copies = []
        for head in range(HEADS):
            acc, best, summed, weight = weights[head]
            value = jnp.concatenate([field[:, values[head]] for field in fields], axis=0)
            both = jnp.dot(weight, with_ones(value), preferred_element_type=F32)
            acc = acc + both[:, :HEAD_DIM]
            summed = summed + both[:, HEAD_DIM:]
            earlier[head] = (acc, best, summed)
            results[slot, :, lanes[head]] = (acc / summed).astype(BF16)
            rows = rows_of(meta[slot_at + slot * HEADS + head])
            copies.append(
                pltpu.make_async_copy(
                    results.at[slot, :, lanes[head]], out.at[rows, lanes[head]], sems.at[head]
                )
            )
            copies[-1].start()
        for copy in copies:
            copy.wait()


def body(tokens, qkv_weight, near_offset, far_offset):
    sequence = tokens[0]
    row_count, depth = sequence.shape
    share = qkv_weight.shape[0]
    block_rate = row_count // BLOCK
    seq_size = lax.axis_size("seq")
    seq_index = lax.axis_index("seq")
    pieces = lax.axis_size("fsdp")
    mine = lax.axis_index("fsdp")
    near_size = min(16, seq_size)
    half = near_size // 2
    far_size = max(1, min(16, seq_size // STRIDE))
    near_at = lambda i: near_place(i, half, near_size)
    far_at = lambda i: (i // (STRIDE * far_size) * STRIDE + i % STRIDE, i // STRIDE % far_size)
    reach = max(near_at(i)[1] for i in range(seq_size))
    near_shifts = (1 << reach.bit_length()) - 1
    far_shifts = (1 << (far_size - 1).bit_length()) - 1
    slots = 2 if far_shifts else 1
    shifts = (near_shifts, far_shifts)[:slots]

    near_position = jnp.where(seq_index < half, seq_index, (seq_index - half) % near_size)
    far_position = seq_index // STRIDE % far_size
    far_match = (seq_index % STRIDE == far_offset // block_rate).astype(jnp.int32)
    spans = [(0, share // 4), (share // 2, share * 5 // 512 * 16)] if seq_size % 4 == 0 else []
    direct_from = spans[-1][0] + 2 * spans[-1][1] if spans else 0
    full_places = [(mine ^ j) * share for j in range(pieces)]
    scalars = list(full_places)
    place_at = len(scalars)
    scalars += [near_position, far_position]
    base_at = len(scalars)
    scalars += [(mine ^ bit) // 2 * 2 * share for bit in range(2, pieces, 2)]
    core_at = len(scalars)
    scalars.append(mine % 2)
    slot_at = len(scalars)
    match_at = slot_at + 2 * HEADS
    offsets_at = match_at + HEADS
    offsets = []
    for number, (start, rows) in enumerate(spans):
        side = seq_index // (1 << number) % 2
        offsets += [start + side * rows, start + (1 - side) * rows]
    offsets.append(direct_from)
    as_array = lambda values: jnp.stack([jnp.asarray(value, jnp.int32) for value in values])
    meta = jnp.concatenate(
        [as_array(scalars), near_offset, far_offset % block_rate, far_match, as_array(offsets)]
    )

    scalar_spec = pl.BlockSpec(memory_space=pltpu.SMEM)
    whole = pl.BlockSpec(memory_space=pltpu.VMEM)
    shape = jax.ShapeDtypeStruct

    def call(kernel, args, results, name, scratch=()):
        return pl.pallas_call(
            kernel,
            in_specs=[scalar_spec] + [whole] * len(args),
            out_specs=[whole] * len(results),
            out_shape=results,
            scratch_shapes=list(scratch),
            compiler_params=pltpu.CompilerParams(vmem_limit_bytes=VMEM_LIMIT),
            cost_estimate=pl.CostEstimate(flops=MODEL_FLOPS[name], bytes_accessed=1000, transcendentals=0),
            name=name,
        )(meta, *args)

    local = [qkv_weight]
    bits = range(2, pieces, 2)
    known = {}
    if pieces > 1:
        local.append(swap(qkv_weight, "fsdp", 1))
        known["core"] = local[-1]
    (partial,) = call(
        functools.partial(own_kernel, len(local)),
        [ordered("t", sequence, known), *local],
        [shape((row_count, 3 * WIDTH), F32)],
        "project_own",
    )
    known["partial"] = partial
    direct_rows, queries = [], []
    for bit in bits:
        mine_rows, other_rows = [], []
        for number, (start, rows) in enumerate(spans):
            tag = str(number)
            side = seq_index // (1 << number) % 2
            cut = lax.dynamic_slice(
                ordered("c" + tag, qkv_weight, known), (start + side * rows, WIDTH), (rows, 2 * WIDTH)
            )
            known["c" + tag] = cut
            direct = swap(cut, "fsdp", bit)
            known["x" + tag] = direct
            across = swap(ordered("f" + tag, direct, known), "fsdp", 1)
            known["f" + tag] = across
            passed = ordered("p" + tag, swap(ordered("y" + tag, direct, known), "seq", 1 << number), known)
            known["y" + tag] = passed
            mine_rows += [direct, passed]
            other_rows += [across, swap(passed, "fsdp", 1)]
            known["q" + tag] = other_rows[-1]
        known["meta"] = meta
        cut = ordered("cD", qkv_weight, known)[direct_from:, WIDTH:]
        known["cD"] = cut
        rest = swap(cut, "fsdp", bit)
        known["xD"] = rest
        rest = ordered("pD", rest, known)
        known["fD"] = swap(rest, "fsdp", 1)
        direct_rows.append(mine_rows + [rest] + other_rows + [known["fD"]])
        cut = ordered("cQ", qkv_weight, known)[:, :WIDTH]
        known["cQ"] = cut
        queries.append(swap(cut, "fsdp", bit))
    assert len(bits) <= 1
    if bits:
        bit = bits[0]
        count = len(direct_rows[0]) // 2
        layout = [offsets_at + i for i in range(count)]
        *sums, joined = call(
            functools.partial(first_rows_kernel, layout, bit, slots, slot_at),
            [sequence, ordered("a", partial, known), *direct_rows[0][:count]],
            [shape((BLOCK, 2 * WIDTH), F32)] * slots + [shape((share, 2 * WIDTH), BF16)],
            "project_first",
        )
        *packs, joined_other = call(
            functools.partial(last_rows_kernel, layout, bit ^ 1, slots, slot_at),
            [sequence, *sums, *direct_rows[0][count:]],
            [shape((BLOCK, 2 * WIDTH), BF16)] * slots + [shape((share, 2 * WIDTH), BF16)],
            "project_pack",
        )
        known["pack"] = packs[0]
        (kv,) = call(
            functools.partial(kv_kernel, [bit, bit ^ 1]),
            [sequence, ordered("kv", partial, known), joined, joined_other],
            [shape((row_count, 2 * WIDTH), BF16)],
            "project_kv",
        )
    else:
        kv = partial[:, WIDTH:].astype(BF16)
        blocks = kv.reshape(block_rate, BLOCK, 2, HEADS, HEAD_DIM)
        packs = []
        for offset in (near_offset, far_offset % block_rate)[:slots]:
            picked = blocks[offset, :, :, jnp.arange(HEADS)]
            packs.append(picked.transpose(1, 2, 0, 3).reshape(BLOCK, 2 * WIDTH))
    known["kv"] = kv
    received = []
    for pack, place, count, unit in zip(packs, (near_at, far_at), shifts, (1, STRIDE)):
        for step in NEAR_ORDER if count == len(NEAR_ORDER) else range(1, count + 1):
            received.append((step, lax.ppermute(pack, "seq", partners(seq_size, place, step))))
        known |= {f"n{step}": r for step, r in received}
    steps = [step for step, _ in received]
    received = [pack for _, pack in received]
    crossed_q, q_places = [], []
    for bit, direct in zip(bits, queries):
        direct = ordered("q", direct, known)
        (slots_out,) = call(
            functools.partial(slot_kernel, core_at), [direct], [shape((2,) + direct.shape, BF16)], "slot_queries"
        )
        both = lax.all_to_all(
            slots_out, "fsdp", 0, 0, axis_index_groups=[[i, i + 1] for i in range(0, pieces, 2)]
        )
        crossed_q += [direct, both]
        q_places += [bit, bit ^ 1]
    state_types = [BF16, F32, F32, F32]
    partial_out, *state = call(
        functools.partial(attend_kernel, q_places, core_at, slots, slot_at, match_at),
        [sequence, partial, *crossed_q, kv],
        [shape((row_count, WIDTH), BF16)] + [shape((BLOCK, WIDTH), kind) for kind in state_types] * slots,
        "attend_local",
        [pltpu.VMEM((row_count, WIDTH), kind) for kind in state_types],
    )
    count = 4 * slots + sum(shifts)
    merged = pl.pallas_call(
        functools.partial(merge_kernel, shifts, steps, slot_at, match_at, place_at),
        in_specs=[scalar_spec] + [whole] * count + [pl.BlockSpec(memory_space=pl.ANY)],
        out_specs=pl.BlockSpec(memory_space=pl.ANY),
        out_shape=shape((row_count, WIDTH), BF16),
        scratch_shapes=[pltpu.VMEM((slots, BLOCK, WIDTH), BF16), pltpu.SemaphoreType.DMA((HEADS,))],
        input_output_aliases={count + 1: 0},
        compiler_params=pltpu.CompilerParams(vmem_limit_bytes=VMEM_LIMIT),
        cost_estimate=pl.CostEstimate(flops=MODEL_FLOPS["merge_near"], bytes_accessed=1000, transcendentals=0),
        name="merge_near",
    )(meta, *state, *received, partial_out)
    return merged[None]


def solution(mesh):
    in_specs = (P("fsdp", "seq", None), P("fsdp", None), P(), P())
    out_specs = P("fsdp", "seq", None)
    return jax.shard_map(body, mesh=mesh, in_specs=in_specs, out_specs=out_specs, check_vma=False)
```

```python
import functools
import math

import jax
import jax.numpy as jnp
from jax import lax
from jax.experimental import pallas as pl
from jax.experimental.pallas import tpu as pltpu
from jax.sharding import PartitionSpec as P

HEADS = 4
HEAD_DIM = 128
BLOCK = 128
STRIDE = 8
WIDTH = HEADS * HEAD_DIM
PAIR = 2 * HEAD_DIM
NEG = -1e30
SCALE2 = HEAD_DIM ** (-0.5) * math.log2(math.e)
VMEM_LIMIT = 24 * 1024 * 1024

MODEL_FLOPS = {"project_first": 689999, "slot_queries": 575000, "project_pack": 689999, "project_own": 3680000, "project_mid": 1610000, "project_kv": 2990000, "attend_local": 6325000, "merge_near": 2990000}
ORDER = {
    'c1': ('c0',),
    'cD': ('c1',),
    'cQ': ('cD',),
    'p0': ('partial', 'xD'),
    'p1': ('partial',),
    'q': ('kv',),
    'kv': ('pack',),
}
NEAR_ORDER = (3, 2, 1)
F32 = jnp.float32
BF16 = jnp.bfloat16


def near_place(index, half, size):
    if index < half:
        return 0, index
    return 1 + (index - half) // size, (index - half) % size


def partners(count, place, bits):
    where = {place(i): i for i in range(count)}
    pairs = []
    for source in range(count):
        run, spot = place(source)
        if (run, spot ^ bits) in where:
            pairs.append((source, where[run, spot ^ bits]))
    return pairs


def swap(value, axis, bit):
    count = lax.axis_size(axis)
    return lax.ppermute(value, axis, [(i, i ^ bit) for i in range(count)])


def after(value, *others):
    return lax.optimization_barrier((value,) + others)[0]


def ordered(name, value, known):
    others = [known[other] for other in ORDER.get(name, ()) if other in known]
    return after(value, *others) if others else value


def rows_of(block):
    return pl.ds(pl.multiple_of(block * BLOCK, BLOCK), BLOCK)


def qk(query, key):
    return lax.dot_general(query, key, (((1,), (1,)), ((), ())), preferred_element_type=F32)


def pv(weights, value):
    return jnp.dot(weights.astype(BF16), value, preferred_element_type=F32)


def add_up(tokens, places, weights):
    total = None
    for place, weight in zip(places, weights):
        depth = weight.shape[0]
        columns = pl.ds(pl.multiple_of(place, depth), depth)
        term = jnp.dot(tokens[:, columns], weight[...], preferred_element_type=F32)
        total = term if total is None else total + term
    return total


def own_kernel(count, meta, tokens, *refs):
    weights, out = refs[:count], refs[count]
    for j in range(out.shape[1] // WIDTH):
        lanes = slice(j * WIDTH, (j + 1) * WIDTH)
        out[:, lanes] = add_up(tokens, [meta[at] for at in range(count)], [weight.at[:, lanes] for weight in weights])


def near_rows_kernel(layout, place_at, first, slots, slot_at, meta, tokens, before, *refs):
    arrived, refs = refs[: len(layout)], refs[len(layout) :]
    sums, joined = refs[:slots], refs[slots]
    for at, array in zip(layout, arrived):
        rows = array.shape[0]
        joined[pl.ds(pl.multiple_of(meta[at], rows), rows), :] = array[...]
    depth = joined.shape[0]
    columns = pl.ds(pl.multiple_of(meta[place_at], depth), depth)
    for slot in range(slots):
        for head in range(HEADS):
            rows = rows_of(meta[slot_at + HEADS * slot + head])
            lanes = [slice(start, start + HEAD_DIM) for start in (head * HEAD_DIM, WIDTH + head * HEAD_DIM)]
            weight = jnp.concatenate([joined[:, part] for part in lanes], axis=1)
            product = jnp.dot(tokens[rows, columns], weight, preferred_element_type=F32)
            for field, part in enumerate(lanes):
                if first:
                    total = before[0][rows, WIDTH + part.start : WIDTH + part.stop]
                else:
                    total = before[slot][:, part]
                total = total + product[:, field * HEAD_DIM : (field + 1) * HEAD_DIM]
                sums[slot][:, part] = total.astype(sums[slot].dtype)


def first_rows_kernel(layout, place_at, slots, slot_at, meta, tokens, partial, *refs):
    near_rows_kernel(layout, place_at, True, slots, slot_at, meta, tokens, [partial], *refs)


def last_rows_kernel(layout, place_at, slots, slot_at, meta, tokens, *refs):
    near_rows_kernel(layout, place_at, False, slots, slot_at, meta, tokens, refs[:slots], *refs[slots:])


def slot_kernel(core_at, meta, source, out):
    out[1 - meta[core_at]] = source[...]


def kv_kernel(places_at, meta, tokens, partial, *refs):
    parts, kv = refs[:-1], refs[-1]
    places = [meta[at] for at in places_at]
    for j in range(2):
        lanes = slice(j * WIDTH, (j + 1) * WIDTH)
        product = add_up(tokens, places, [part.at[:, lanes] for part in parts])
        kv[:, lanes] = (partial[:, (j + 1) * WIDTH : (j + 2) * WIDTH] + product).astype(BF16)


def with_ones(value):
    return jnp.concatenate([value, jnp.ones(value.shape, BF16)], axis=1)


def attend_kernel(bases_at, core_at, slots, slot_at, match_at, meta, tokens, partial, *refs):
    weights, refs = refs[: len(bases_at)], refs[len(bases_at) :]
    kv, out, refs = refs[0], refs[1], refs[2:]
    state, scratch = refs[: 4 * slots], refs[4 * slots :]
    query, acc_all, top_all, sum_all = scratch
    blocks = query.shape[0] // BLOCK
    GROUP = 2 if blocks % 2 == 0 else 1
    row = lax.broadcasted_iota(jnp.int32, (BLOCK, BLOCK), 0)
    column = lax.broadcasted_iota(jnp.int32, (BLOCK, BLOCK), 1)
    causal = column <= row
    places = [meta[at] for at in bases_at]
    other = 1 - meta[core_at]
    for pair in range(HEADS // 2):
        lanes = slice(pair * PAIR, (pair + 1) * PAIR)
        total = partial[:, lanes]
        if weights:
            parts = [weights[0].at[:, lanes], weights[1].at[other, :, lanes]]
            total = total + add_up(tokens, places, parts)
        query[:, lanes] = total.astype(BF16)

    def lanes_of(head):
        return slice(head * HEAD_DIM, (head + 1) * HEAD_DIM)

    def rows_at(b):
        return slice(b * BLOCK, (b + 1) * BLOCK)

    def score(head, group):
        first, last = group * GROUP, (group + 1) * GROUP
        rows = slice(first * BLOCK, last * BLOCK)
        return qk(query[rows, lanes_of(head)], kv[: last * BLOCK, lanes_of(head)])

    def weigh(head, group, scores):
        near_block = meta[slot_at + head]
        far_block = meta[slot_at + HEADS + head]
        tops, weights = [], []
        for i in range(GROUP):
            b = group * GROUP + i
            mine = scores[rows_at(i)]
            times = (
                1
                + jnp.where(near_block == b, 1, 0)
                + jnp.where(far_block == b, meta[match_at + head], 0)
            ).astype(F32)
            diagonal = jnp.where(causal, mine[:, rows_at(b)], NEG)
            top = jnp.max(diagonal, axis=1, keepdims=True)
            if b:
                top = jnp.maximum(top, jnp.max(mine[:, : b * BLOCK], axis=1, keepdims=True))
            parts = [(jnp.exp2((diagonal - top) * SCALE2) * times).astype(BF16)]
            if b:
                parts.insert(0, jnp.exp2((mine[:, : b * BLOCK] - top) * SCALE2).astype(BF16))
            if i < GROUP - 1:
                parts.append(jnp.zeros((BLOCK, (GROUP - 1 - i) * BLOCK), BF16))
            tops.append(top)
            weights.append(jnp.concatenate(parts, axis=1))
        return tops, jnp.concatenate(weights, axis=0)

    def finish(head, group, tops, weight):
        lanes = lanes_of(head)
        keys = (group + 1) * GROUP * BLOCK
        value = kv[:keys, WIDTH + head * HEAD_DIM : WIDTH + (head + 1) * HEAD_DIM]
        both = jnp.dot(weight, with_ones(value), preferred_element_type=F32)
        rows = slice(group * GROUP * BLOCK, keys)
        acc, summed = both[:, :HEAD_DIM], both[:, HEAD_DIM:]
        out[rows, lanes] = (acc / summed).astype(BF16)
        acc_all[rows, lanes] = acc
        sum_all[rows, lanes] = summed
        for i, top in enumerate(tops):
            top_all[rows_at(group * GROUP + i), lanes] = jnp.broadcast_to(top, (BLOCK, HEAD_DIM))
        if group == blocks // GROUP - 1:
            for slot in range(slots):
                rows = rows_of(meta[slot_at + slot * HEADS + head])
                for target, source in zip(state[4 * slot :], scratch):
                    target[:, lanes] = source[rows, lanes]

    tasks = [(head, group) for head in range(HEADS) for group in range(blocks // GROUP)]
    scored, weighed = {}, {}
    for step in range(len(tasks) + 2):
        if step < len(tasks):
            scored[step] = score(*tasks[step])
        if 0 <= step - 1 < len(tasks):
            weighed[step - 1] = weigh(*tasks[step - 1], scored.pop(step - 1))
        if 0 <= step - 2 < len(tasks):
            finish(*tasks[step - 2], *weighed.pop(step - 2))


def merge_kernel(shifts, steps, slot_at, match_at, place_at, meta, *refs):
    slots = len(shifts)
    state = refs[: 4 * slots]
    packs = refs[4 * slots : 4 * slots + sum(shifts)]
    out, results, sems = refs[4 * slots + sum(shifts) + 1 :]
    if slots == 1:
        pl.when(meta[place_at] > 0)(lambda: merge_slots(
            shifts, steps, slot_at, match_at, place_at, meta, state, packs, out, results, sems
        ))
    else:
        merge_slots(shifts, steps, slot_at, match_at, place_at, meta, state, packs, out, results, sems)


def merge_slots(shifts, steps, slot_at, match_at, place_at, meta, state, packs, out, results, sems):
    lanes = [slice(head * HEAD_DIM, (head + 1) * HEAD_DIM) for head in range(HEADS)]
    values = [slice(WIDTH + head * HEAD_DIM, WIDTH + (head + 1) * HEAD_DIM) for head in range(HEADS)]
    earlier = [None] * HEADS
    for slot, count in enumerate(shifts):
        fields = packs[sum(shifts[:slot]) : sum(shifts[: slot + 1])]
        query, acc_ref, top_ref, sum_ref = state[4 * slot : 4 * slot + 4]
        place = meta[place_at + slot]
        scores, weights = [], []
        for head in range(HEADS):
            keys = jnp.concatenate([field[:, lanes[head]] for field in fields], axis=0)
            score = qk(query[:, lanes[head]], keys)
            parts = []
            for number, step in enumerate(steps[sum(shifts[:slot]) : sum(shifts[: slot + 1])]):
                seen = place ^ step < place
                if slot:
                    seen = seen & (meta[match_at + head] == 1)
                part = score[:, number * BLOCK : (number + 1) * BLOCK]
                parts.append(jnp.where(seen, part, NEG))
            scores.append(jnp.concatenate(parts, axis=1))
        for head in range(HEADS):
            acc, top, summed = (ref[:, lanes[head]] for ref in (acc_ref, top_ref, sum_ref))
            if slot:
                same = meta[slot_at + head] == meta[slot_at + HEADS + head]
                acc, top, summed = (
                    jnp.where(same, new, old) for new, old in zip(earlier[head], (acc, top, summed))
                )
            best = jnp.maximum(top, jnp.max(scores[head], axis=1, keepdims=True))
            decay = jnp.exp2((top - best) * SCALE2)
            weight = jnp.exp2((scores[head] - best[:, :1]) * SCALE2).astype(BF16)
            weights.append((acc * decay, best, summed * decay, weight))
        copies = []
        for head in range(HEADS):
            acc, best, summed, weight = weights[head]
            value = jnp.concatenate([field[:, values[head]] for field in fields], axis=0)
            both = jnp.dot(weight, with_ones(value), preferred_element_type=F32)
            acc = acc + both[:, :HEAD_DIM]
            summed = summed + both[:, HEAD_DIM:]
            earlier[head] = (acc, best, summed)
            results[slot, :, lanes[head]] = (acc / summed).astype(BF16)
            rows = rows_of(meta[slot_at + slot * HEADS + head])
            copies.append(
                pltpu.make_async_copy(
                    results.at[slot, :, lanes[head]], out.at[rows, lanes[head]], sems.at[head]
                )
            )
            copies[-1].start()
        for copy in copies:
            copy.wait()


def body(tokens, qkv_weight, near_offset, far_offset):
    sequence = tokens[0]
    row_count, depth = sequence.shape
    share = qkv_weight.shape[0]
    block_rate = row_count // BLOCK
    seq_size = lax.axis_size("seq")
    seq_index = lax.axis_index("seq")
    pieces = lax.axis_size("fsdp")
    mine = lax.axis_index("fsdp")
    near_size = min(16, seq_size)
    half = near_size // 2
    far_size = max(1, min(16, seq_size // STRIDE))
    near_at = lambda i: near_place(i, half, near_size)
    far_at = lambda i: (i // (STRIDE * far_size) * STRIDE + i % STRIDE, i // STRIDE % far_size)
    reach = max(near_at(i)[1] for i in range(seq_size))
    near_shifts = (1 << reach.bit_length()) - 1
    far_shifts = (1 << (far_size - 1).bit_length()) - 1
    slots = 2 if far_shifts else 1
    shifts = (near_shifts, far_shifts)[:slots]

    near_position = jnp.where(seq_index < half, seq_index, (seq_index - half) % near_size)
    far_position = seq_index // STRIDE % far_size
    far_match = (seq_index % STRIDE == far_offset // block_rate).astype(jnp.int32)
    spans = [(0, share // 4), (share // 2, share // 8)] if seq_size % 4 == 0 else []
    direct_from = spans[-1][0] + 2 * spans[-1][1] if spans else 0
    full_places = [(mine ^ j) * share for j in range(pieces)]
    scalars = list(full_places)
    place_at = len(scalars)
    scalars += [near_position, far_position]
    base_at = len(scalars)
    scalars += [(mine ^ bit) // 2 * 2 * share for bit in range(2, pieces, 2)]
    core_at = len(scalars)
    scalars.append(mine % 2)
    slot_at = len(scalars)
    match_at = slot_at + 2 * HEADS
    offsets_at = match_at + HEADS
    offsets = []
    for number, (start, rows) in enumerate(spans):
        side = seq_index // (1 << number) % 2
        offsets += [start + side * rows, start + (1 - side) * rows]
    offsets.append(direct_from)
    as_array = lambda values: jnp.stack([jnp.asarray(value, jnp.int32) for value in values])
    meta = jnp.concatenate(
        [as_array(scalars), near_offset, far_offset % block_rate, far_match, as_array(offsets)]
    )

    scalar_spec = pl.BlockSpec(memory_space=pltpu.SMEM)
    whole = pl.BlockSpec(memory_space=pltpu.VMEM)
    shape = jax.ShapeDtypeStruct

    def call(kernel, args, results, name, scratch=()):
        return pl.pallas_call(
            kernel,
            in_specs=[scalar_spec] + [whole] * len(args),
            out_specs=[whole] * len(results),
            out_shape=results,
            scratch_shapes=list(scratch),
            compiler_params=pltpu.CompilerParams(vmem_limit_bytes=VMEM_LIMIT),
            cost_estimate=pl.CostEstimate(flops=MODEL_FLOPS[name], bytes_accessed=1000, transcendentals=0),
            name=name,
        )(meta, *args)

    local = [qkv_weight]
    bits = range(2, pieces, 2)
    known = {}
    if pieces > 1:
        local.append(swap(qkv_weight, "fsdp", 1))
        known["core"] = local[-1]
    (partial,) = call(
        functools.partial(own_kernel, len(local)),
        [ordered("t", sequence, known), *local],
        [shape((row_count, 3 * WIDTH), F32)],
        "project_own",
    )
    known["partial"] = partial
    direct_rows, queries = [], []
    for bit in bits:
        mine_rows, other_rows = [], []
        for number, (start, rows) in enumerate(spans):
            tag = str(number)
            side = seq_index // (1 << number) % 2
            cut = lax.dynamic_slice(
                ordered("c" + tag, qkv_weight, known), (start + side * rows, WIDTH), (rows, 2 * WIDTH)
            )
            known["c" + tag] = cut
            direct = swap(cut, "fsdp", bit)
            known["x" + tag] = direct
            across = swap(ordered("f" + tag, direct, known), "fsdp", 1)
            known["f" + tag] = across
            passed = ordered("p" + tag, swap(ordered("y" + tag, direct, known), "seq", 1 << number), known)
            known["y" + tag] = passed
            mine_rows += [direct, passed]
            other_rows += [across, swap(passed, "fsdp", 1)]
            known["q" + tag] = other_rows[-1]
        known["meta"] = meta
        cut = ordered("cD", qkv_weight, known)[direct_from:, WIDTH:]
        known["cD"] = cut
        rest = swap(cut, "fsdp", bit)
        known["xD"] = rest
        rest = ordered("pD", rest, known)
        known["fD"] = swap(rest, "fsdp", 1)
        direct_rows.append(mine_rows + [rest] + other_rows + [known["fD"]])
        cut = ordered("cQ", qkv_weight, known)[:, :WIDTH]
        known["cQ"] = cut
        queries.append(swap(cut, "fsdp", bit))
    assert len(bits) <= 1
    if bits:
        bit = bits[0]
        count = len(direct_rows[0]) // 2
        layout = [offsets_at + i for i in range(count)]
        *sums, joined = call(
            functools.partial(first_rows_kernel, layout, bit, slots, slot_at),
            [sequence, ordered("a", partial, known), *direct_rows[0][:count]],
            [shape((BLOCK, 2 * WIDTH), F32)] * slots + [shape((share, 2 * WIDTH), BF16)],
            "project_first",
        )
        *packs, joined_other = call(
            functools.partial(last_rows_kernel, layout, bit ^ 1, slots, slot_at),
            [sequence, *sums, *direct_rows[0][count:]],
            [shape((BLOCK, 2 * WIDTH), BF16)] * slots + [shape((share, 2 * WIDTH), BF16)],
            "project_pack",
        )
        known["pack"] = packs[0]
        (kv,) = call(
            functools.partial(kv_kernel, [bit, bit ^ 1]),
            [sequence, ordered("kv", partial, known), joined, joined_other],
            [shape((row_count, 2 * WIDTH), BF16)],
            "project_kv",
        )
    else:
        kv = partial[:, WIDTH:].astype(BF16)
        blocks = kv.reshape(block_rate, BLOCK, 2, HEADS, HEAD_DIM)
        packs = []
        for offset in (near_offset, far_offset % block_rate)[:slots]:
            picked = blocks[offset, :, :, jnp.arange(HEADS)]
            packs.append(picked.transpose(1, 2, 0, 3).reshape(BLOCK, 2 * WIDTH))
    known["kv"] = kv
    received = []
    for pack, place, count, unit in zip(packs, (near_at, far_at), shifts, (1, STRIDE)):
        for step in NEAR_ORDER if count == len(NEAR_ORDER) else range(1, count + 1):
            received.append((step, lax.ppermute(pack, "seq", partners(seq_size, place, step))))
        known |= {f"n{step}": r for step, r in received}
    steps = [step for step, _ in received]
    received = [pack for _, pack in received]
    crossed_q, q_places = [], []
    for bit, direct in zip(bits, queries):
        direct = ordered("q", direct, known)
        (slots_out,) = call(
            functools.partial(slot_kernel, core_at), [direct], [shape((2,) + direct.shape, BF16)], "slot_queries"
        )
        both = lax.all_to_all(
            slots_out, "fsdp", 0, 0, axis_index_groups=[[i, i + 1] for i in range(0, pieces, 2)]
        )
        crossed_q += [direct, both]
        q_places += [bit, bit ^ 1]
    state_types = [BF16, F32, F32, F32]
    partial_out, *state = call(
        functools.partial(attend_kernel, q_places, core_at, slots, slot_at, match_at),
        [sequence, partial, *crossed_q, kv],
        [shape((row_count, WIDTH), BF16)] + [shape((BLOCK, WIDTH), kind) for kind in state_types] * slots,
        "attend_local",
        [pltpu.VMEM((row_count, WIDTH), kind) for kind in state_types],
    )
    count = 4 * slots + sum(shifts)
    merged = pl.pallas_call(
        functools.partial(merge_kernel, shifts, steps, slot_at, match_at, place_at),
        in_specs=[scalar_spec] + [whole] * count + [pl.BlockSpec(memory_space=pl.ANY)],
        out_specs=pl.BlockSpec(memory_space=pl.ANY),
        out_shape=shape((row_count, WIDTH), BF16),
        scratch_shapes=[pltpu.VMEM((slots, BLOCK, WIDTH), BF16), pltpu.SemaphoreType.DMA((HEADS,))],
        input_output_aliases={count + 1: 0},
        compiler_params=pltpu.CompilerParams(vmem_limit_bytes=VMEM_LIMIT),
        cost_estimate=pl.CostEstimate(flops=MODEL_FLOPS["merge_near"], bytes_accessed=1000, transcendentals=0),
        name="merge_near",
    )(meta, *state, *received, partial_out)
    return merged[None]


def solution(mesh):
    in_specs = (P("fsdp", "seq", None), P("fsdp", None), P(), P())
    out_specs = P("fsdp", "seq", None)
    return jax.shard_map(body, mesh=mesh, in_specs=in_specs, out_specs=out_specs, check_vma=False)
```

```python
import functools
import math

import jax
import jax.numpy as jnp
from jax import lax
from jax.experimental import pallas as pl
from jax.experimental.pallas import tpu as pltpu
from jax.sharding import PartitionSpec as P

HEADS = 4
HEAD_DIM = 128
BLOCK = 128
STRIDE = 8
WIDTH = HEADS * HEAD_DIM
PAIR = 2 * HEAD_DIM
NEG = -1e30
SCALE2 = HEAD_DIM ** (-0.5) * math.log2(math.e)
VMEM_LIMIT = 24 * 1024 * 1024

MODEL_FLOPS = {"project_first": 689999, "slot_queries": 575000, "project_pack": 689999, "project_own": 3680000, "project_mid": 1610000, "project_kv": 2990000, "attend_local": 6325000, "merge_near": 2990000}
ORDER = {
    'c1': ('c0',),
    'cD': ('c1',),
    'cQ': ('cD',),
    'p0': ('partial', 'xD'),
    'p1': ('partial',),
    'q': ('kv',),
    'kv': ('pack',),
}
NEAR_ORDER = (3, 2, 1)
F32 = jnp.float32
BF16 = jnp.bfloat16


def near_place(index, half, size):
    if index < half:
        return 0, index
    return 1 + (index - half) // size, (index - half) % size


def partners(count, place, bits):
    where = {place(i): i for i in range(count)}
    pairs = []
    for source in range(count):
        run, spot = place(source)
        if (run, spot ^ bits) in where:
            pairs.append((source, where[run, spot ^ bits]))
    return pairs


def swap(value, axis, bit):
    count = lax.axis_size(axis)
    return lax.ppermute(value, axis, [(i, i ^ bit) for i in range(count)])


def after(value, *others):
    return lax.optimization_barrier((value,) + others)[0]


def ordered(name, value, known):
    others = [known[other] for other in ORDER.get(name, ()) if other in known]
    return after(value, *others) if others else value


def rows_of(block):
    return pl.ds(pl.multiple_of(block * BLOCK, BLOCK), BLOCK)


def qk(query, key):
    return lax.dot_general(query, key, (((1,), (1,)), ((), ())), preferred_element_type=F32)


def pv(weights, value):
    return jnp.dot(weights.astype(BF16), value, preferred_element_type=F32)


def add_up(tokens, places, weights):
    total = None
    for place, weight in zip(places, weights):
        depth = weight.shape[0]
        columns = pl.ds(pl.multiple_of(place, depth), depth)
        term = jnp.dot(tokens[:, columns], weight[...], preferred_element_type=F32)
        total = term if total is None else total + term
    return total


def own_kernel(count, meta, tokens, *refs):
    weights, out = refs[:count], refs[count]
    for j in range(out.shape[1] // WIDTH):
        lanes = slice(j * WIDTH, (j + 1) * WIDTH)
        out[:, lanes] = add_up(tokens, [meta[at] for at in range(count)], [weight.at[:, lanes] for weight in weights])


def near_rows_kernel(layout, place_at, first, slots, slot_at, meta, tokens, before, *refs):
    arrived, refs = refs[: len(layout)], refs[len(layout) :]
    sums, joined = refs[:slots], refs[slots]
    for at, array in zip(layout, arrived):
        rows = array.shape[0]
        joined[pl.ds(pl.multiple_of(meta[at], rows), rows), :] = array[...]
    depth = joined.shape[0]
    columns = pl.ds(pl.multiple_of(meta[place_at], depth), depth)
    for slot in range(slots):
        for head in range(HEADS):
            rows = rows_of(meta[slot_at + HEADS * slot + head])
            lanes = [slice(start, start + HEAD_DIM) for start in (head * HEAD_DIM, WIDTH + head * HEAD_DIM)]
            weight = jnp.concatenate([joined[:, part] for part in lanes], axis=1)
            product = jnp.dot(tokens[rows, columns], weight, preferred_element_type=F32)
            for field, part in enumerate(lanes):
                if first:
                    total = before[0][rows, WIDTH + part.start : WIDTH + part.stop]
                else:
                    total = before[slot][:, part]
                total = total + product[:, field * HEAD_DIM : (field + 1) * HEAD_DIM]
                sums[slot][:, part] = total.astype(sums[slot].dtype)


def first_rows_kernel(layout, place_at, slots, slot_at, meta, tokens, partial, *refs):
    near_rows_kernel(layout, place_at, True, slots, slot_at, meta, tokens, [partial], *refs)


def last_rows_kernel(layout, place_at, slots, slot_at, meta, tokens, *refs):
    near_rows_kernel(layout, place_at, False, slots, slot_at, meta, tokens, refs[:slots], *refs[slots:])


def slot_kernel(core_at, meta, source, out):
    out[1 - meta[core_at]] = source[...]


def kv_kernel(places_at, meta, tokens, partial, *refs):
    parts, kv = refs[:-1], refs[-1]
    places = [meta[at] for at in places_at]
    for j in range(2):
        lanes = slice(j * WIDTH, (j + 1) * WIDTH)
        product = add_up(tokens, places, [part.at[:, lanes] for part in parts])
        kv[:, lanes] = (partial[:, (j + 1) * WIDTH : (j + 2) * WIDTH] + product).astype(BF16)


def with_ones(value):
    return jnp.concatenate([value, jnp.ones(value.shape, BF16)], axis=1)


def attend_kernel(bases_at, core_at, slots, slot_at, match_at, meta, tokens, partial, *refs):
    weights, refs = refs[: len(bases_at)], refs[len(bases_at) :]
    kv, out, refs = refs[0], refs[1], refs[2:]
    state, scratch = refs[: 4 * slots], refs[4 * slots :]
    query, acc_all, top_all, sum_all = scratch
    blocks = query.shape[0] // BLOCK
    GROUP = 2 if blocks % 2 == 0 else 1
    row = lax.broadcasted_iota(jnp.int32, (BLOCK, BLOCK), 0)
    column = lax.broadcasted_iota(jnp.int32, (BLOCK, BLOCK), 1)
    causal = column <= row
    places = [meta[at] for at in bases_at]
    other = 1 - meta[core_at]
    for lanes in (slice(0, WIDTH),):
        total = partial[:, lanes]
        if weights:
            parts = [weights[0].at[:, lanes], weights[1].at[other, :, lanes]]
            total = total + add_up(tokens, places, parts)
        query[:, lanes] = total.astype(BF16)

    def lanes_of(head):
        return slice(head * HEAD_DIM, (head + 1) * HEAD_DIM)

    def rows_at(b):
        return slice(b * BLOCK, (b + 1) * BLOCK)

    def score(head, group):
        first, last = group * GROUP, (group + 1) * GROUP
        rows = slice(first * BLOCK, last * BLOCK)
        return qk(query[rows, lanes_of(head)], kv[: last * BLOCK, lanes_of(head)])

    def weigh(head, group, scores):
        near_block = meta[slot_at + head]
        far_block = meta[slot_at + HEADS + head]
        tops, weights = [], []
        for i in range(GROUP):
            b = group * GROUP + i
            mine = scores[rows_at(i)]
            times = (
                1
                + jnp.where(near_block == b, 1, 0)
                + jnp.where(far_block == b, meta[match_at + head], 0)
            ).astype(F32)
            diagonal = jnp.where(causal, mine[:, rows_at(b)], NEG)
            top = jnp.max(diagonal, axis=1, keepdims=True)
            if b:
                top = jnp.maximum(top, jnp.max(mine[:, : b * BLOCK], axis=1, keepdims=True))
            parts = [(jnp.exp2((diagonal - top) * SCALE2) * times).astype(BF16)]
            if b:
                parts.insert(0, jnp.exp2((mine[:, : b * BLOCK] - top) * SCALE2).astype(BF16))
            if i < GROUP - 1:
                parts.append(jnp.zeros((BLOCK, (GROUP - 1 - i) * BLOCK), BF16))
            tops.append(top)
            weights.append(jnp.concatenate(parts, axis=1))
        return tops, jnp.concatenate(weights, axis=0)

    def finish(head, group, tops, weight):
        lanes = lanes_of(head)
        keys = (group + 1) * GROUP * BLOCK
        value = kv[:keys, WIDTH + head * HEAD_DIM : WIDTH + (head + 1) * HEAD_DIM]
        both = jnp.dot(weight, with_ones(value), preferred_element_type=F32)
        rows = slice(group * GROUP * BLOCK, keys)
        acc, summed = both[:, :HEAD_DIM], both[:, HEAD_DIM:]
        out[rows, lanes] = (acc / summed).astype(BF16)
        acc_all[rows, lanes] = acc
        sum_all[rows, lanes] = summed
        for i, top in enumerate(tops):
            top_all[rows_at(group * GROUP + i), lanes] = jnp.broadcast_to(top, (BLOCK, HEAD_DIM))
        if group == blocks // GROUP - 1:
            for slot in range(slots):
                rows = rows_of(meta[slot_at + slot * HEADS + head])
                for target, source in zip(state[4 * slot :], scratch):
                    target[:, lanes] = source[rows, lanes]

    tasks = [(head, group) for head in range(HEADS) for group in range(blocks // GROUP)]
    scored, weighed = {}, {}
    for step in range(len(tasks) + 2):
        if step < len(tasks):
            scored[step] = score(*tasks[step])
        if 0 <= step - 1 < len(tasks):
            weighed[step - 1] = weigh(*tasks[step - 1], scored.pop(step - 1))
        if 0 <= step - 2 < len(tasks):
            finish(*tasks[step - 2], *weighed.pop(step - 2))


def merge_kernel(shifts, steps, slot_at, match_at, place_at, meta, *refs):
    slots = len(shifts)
    state = refs[: 4 * slots]
    packs = refs[4 * slots : 4 * slots + sum(shifts)]
    out, results, sems = refs[4 * slots + sum(shifts) + 1 :]
    if slots == 1:
        pl.when(meta[place_at] > 0)(lambda: merge_slots(
            shifts, steps, slot_at, match_at, place_at, meta, state, packs, out, results, sems
        ))
    else:
        merge_slots(shifts, steps, slot_at, match_at, place_at, meta, state, packs, out, results, sems)


def merge_slots(shifts, steps, slot_at, match_at, place_at, meta, state, packs, out, results, sems):
    lanes = [slice(head * HEAD_DIM, (head + 1) * HEAD_DIM) for head in range(HEADS)]
    values = [slice(WIDTH + head * HEAD_DIM, WIDTH + (head + 1) * HEAD_DIM) for head in range(HEADS)]
    earlier = [None] * HEADS
    for slot, count in enumerate(shifts):
        fields = packs[sum(shifts[:slot]) : sum(shifts[: slot + 1])]
        query, acc_ref, top_ref, sum_ref = state[4 * slot : 4 * slot + 4]
        place = meta[place_at + slot]
        scores, weights = [], []
        for head in range(HEADS):
            keys = jnp.concatenate([field[:, lanes[head]] for field in fields], axis=0)
            score = qk(query[:, lanes[head]], keys)
            parts = []
            for number, step in enumerate(steps[sum(shifts[:slot]) : sum(shifts[: slot + 1])]):
                seen = place ^ step < place
                if slot:
                    seen = seen & (meta[match_at + head] == 1)
                part = score[:, number * BLOCK : (number + 1) * BLOCK]
                parts.append(jnp.where(seen, part, NEG))
            scores.append(jnp.concatenate(parts, axis=1))
        for head in range(HEADS):
            acc, top, summed = (ref[:, lanes[head]] for ref in (acc_ref, top_ref, sum_ref))
            if slot:
                same = meta[slot_at + head] == meta[slot_at + HEADS + head]
                acc, top, summed = (
                    jnp.where(same, new, old) for new, old in zip(earlier[head], (acc, top, summed))
                )
            best = jnp.maximum(top, jnp.max(scores[head], axis=1, keepdims=True))
            decay = jnp.exp2((top - best) * SCALE2)
            weight = jnp.exp2((scores[head] - best[:, :1]) * SCALE2).astype(BF16)
            weights.append((acc * decay, best, summed * decay, weight))
        copies = []
        for head in range(HEADS):
            acc, best, summed, weight = weights[head]
            value = jnp.concatenate([field[:, values[head]] for field in fields], axis=0)
            both = jnp.dot(weight, with_ones(value), preferred_element_type=F32)
            acc = acc + both[:, :HEAD_DIM]
            summed = summed + both[:, HEAD_DIM:]
            earlier[head] = (acc, best, summed)
            results[slot, :, lanes[head]] = (acc / summed).astype(BF16)
            rows = rows_of(meta[slot_at + slot * HEADS + head])
            copies.append(
                pltpu.make_async_copy(
                    results.at[slot, :, lanes[head]], out.at[rows, lanes[head]], sems.at[head]
                )
            )
            copies[-1].start()
        for copy in copies:
            copy.wait()


def body(tokens, qkv_weight, near_offset, far_offset):
    sequence = tokens[0]
    row_count, depth = sequence.shape
    share = qkv_weight.shape[0]
    block_rate = row_count // BLOCK
    seq_size = lax.axis_size("seq")
    seq_index = lax.axis_index("seq")
    pieces = lax.axis_size("fsdp")
    mine = lax.axis_index("fsdp")
    near_size = min(16, seq_size)
    half = near_size // 2
    far_size = max(1, min(16, seq_size // STRIDE))
    near_at = lambda i: near_place(i, half, near_size)
    far_at = lambda i: (i // (STRIDE * far_size) * STRIDE + i % STRIDE, i // STRIDE % far_size)
    reach = max(near_at(i)[1] for i in range(seq_size))
    near_shifts = (1 << reach.bit_length()) - 1
    far_shifts = (1 << (far_size - 1).bit_length()) - 1
    slots = 2 if far_shifts else 1
    shifts = (near_shifts, far_shifts)[:slots]

    near_position = jnp.where(seq_index < half, seq_index, (seq_index - half) % near_size)
    far_position = seq_index // STRIDE % far_size
    far_match = (seq_index % STRIDE == far_offset // block_rate).astype(jnp.int32)
    spans = [(0, share // 4), (share // 2, share // 8)] if seq_size % 4 == 0 else []
    direct_from = spans[-1][0] + 2 * spans[-1][1] if spans else 0
    full_places = [(mine ^ j) * share for j in range(pieces)]
    scalars = list(full_places)
    place_at = len(scalars)
    scalars += [near_position, far_position]
    base_at = len(scalars)
    scalars += [(mine ^ bit) // 2 * 2 * share for bit in range(2, pieces, 2)]
    core_at = len(scalars)
    scalars.append(mine % 2)
    slot_at = len(scalars)
    match_at = slot_at + 2 * HEADS
    offsets_at = match_at + HEADS
    offsets = []
    for number, (start, rows) in enumerate(spans):
        side = seq_index // (1 << number) % 2
        offsets += [start + side * rows, start + (1 - side) * rows]
    offsets.append(direct_from)
    as_array = lambda values: jnp.stack([jnp.asarray(value, jnp.int32) for value in values])
    meta = jnp.concatenate(
        [as_array(scalars), near_offset, far_offset % block_rate, far_match, as_array(offsets)]
    )

    scalar_spec = pl.BlockSpec(memory_space=pltpu.SMEM)
    whole = pl.BlockSpec(memory_space=pltpu.VMEM)
    shape = jax.ShapeDtypeStruct

    def call(kernel, args, results, name, scratch=()):
        return pl.pallas_call(
            kernel,
            in_specs=[scalar_spec] + [whole] * len(args),
            out_specs=[whole] * len(results),
            out_shape=results,
            scratch_shapes=list(scratch),
            compiler_params=pltpu.CompilerParams(vmem_limit_bytes=VMEM_LIMIT),
            cost_estimate=pl.CostEstimate(flops=MODEL_FLOPS[name], bytes_accessed=1000, transcendentals=0),
            name=name,
        )(meta, *args)

    local = [qkv_weight]
    bits = range(2, pieces, 2)
    known = {}
    if pieces > 1:
        local.append(swap(qkv_weight, "fsdp", 1))
        known["core"] = local[-1]
    (partial,) = call(
        functools.partial(own_kernel, len(local)),
        [ordered("t", sequence, known), *local],
        [shape((row_count, 3 * WIDTH), F32)],
        "project_own",
    )
    known["partial"] = partial
    direct_rows, queries = [], []
    for bit in bits:
        mine_rows, other_rows = [], []
        for number, (start, rows) in enumerate(spans):
            tag = str(number)
            side = seq_index // (1 << number) % 2
            cut = lax.dynamic_slice(
                ordered("c" + tag, qkv_weight, known), (start + side * rows, WIDTH), (rows, 2 * WIDTH)
            )
            known["c" + tag] = cut
            direct = swap(cut, "fsdp", bit)
            known["x" + tag] = direct
            across = swap(ordered("f" + tag, direct, known), "fsdp", 1)
            known["f" + tag] = across
            passed = ordered("p" + tag, swap(ordered("y" + tag, direct, known), "seq", 1 << number), known)
            known["y" + tag] = passed
            mine_rows += [direct, passed]
            other_rows += [across, swap(passed, "fsdp", 1)]
            known["q" + tag] = other_rows[-1]
        known["meta"] = meta
        cut = ordered("cD", qkv_weight, known)[direct_from:, WIDTH:]
        known["cD"] = cut
        rest = swap(cut, "fsdp", bit)
        known["xD"] = rest
        rest = ordered("pD", rest, known)
        known["fD"] = swap(rest, "fsdp", 1)
        direct_rows.append(mine_rows + [rest] + other_rows + [known["fD"]])
        cut = ordered("cQ", qkv_weight, known)[:, :WIDTH]
        known["cQ"] = cut
        queries.append(swap(cut, "fsdp", bit))
    assert len(bits) <= 1
    if bits:
        bit = bits[0]
        count = len(direct_rows[0]) // 2
        layout = [offsets_at + i for i in range(count)]
        *sums, joined = call(
            functools.partial(first_rows_kernel, layout, bit, slots, slot_at),
            [sequence, ordered("a", partial, known), *direct_rows[0][:count]],
            [shape((BLOCK, 2 * WIDTH), F32)] * slots + [shape((share, 2 * WIDTH), BF16)],
            "project_first",
        )
        *packs, joined_other = call(
            functools.partial(last_rows_kernel, layout, bit ^ 1, slots, slot_at),
            [sequence, *sums, *direct_rows[0][count:]],
            [shape((BLOCK, 2 * WIDTH), BF16)] * slots + [shape((share, 2 * WIDTH), BF16)],
            "project_pack",
        )
        known["pack"] = packs[0]
        (kv,) = call(
            functools.partial(kv_kernel, [bit, bit ^ 1]),
            [sequence, ordered("kv", partial, known), joined, joined_other],
            [shape((row_count, 2 * WIDTH), BF16)],
            "project_kv",
        )
    else:
        kv = partial[:, WIDTH:].astype(BF16)
        blocks = kv.reshape(block_rate, BLOCK, 2, HEADS, HEAD_DIM)
        packs = []
        for offset in (near_offset, far_offset % block_rate)[:slots]:
            picked = blocks[offset, :, :, jnp.arange(HEADS)]
            packs.append(picked.transpose(1, 2, 0, 3).reshape(BLOCK, 2 * WIDTH))
    known["kv"] = kv
    received = []
    for pack, place, count, unit in zip(packs, (near_at, far_at), shifts, (1, STRIDE)):
        for step in NEAR_ORDER if count == len(NEAR_ORDER) else range(1, count + 1):
            received.append((step, lax.ppermute(pack, "seq", partners(seq_size, place, step))))
        known |= {f"n{step}": r for step, r in received}
    steps = [step for step, _ in received]
    received = [pack for _, pack in received]
    crossed_q, q_places = [], []
    for bit, direct in zip(bits, queries):
        direct = ordered("q", direct, known)
        (slots_out,) = call(
            functools.partial(slot_kernel, core_at), [direct], [shape((2,) + direct.shape, BF16)], "slot_queries"
        )
        both = lax.all_to_all(
            slots_out, "fsdp", 0, 0, axis_index_groups=[[i, i + 1] for i in range(0, pieces, 2)]
        )
        crossed_q += [direct, both]
        q_places += [bit, bit ^ 1]
    state_types = [BF16, F32, F32, F32]
    partial_out, *state = call(
        functools.partial(attend_kernel, q_places, core_at, slots, slot_at, match_at),
        [sequence, partial, *crossed_q, kv],
        [shape((row_count, WIDTH), BF16)] + [shape((BLOCK, WIDTH), kind) for kind in state_types] * slots,
        "attend_local",
        [pltpu.VMEM((row_count, WIDTH), kind) for kind in state_types],
    )
    count = 4 * slots + sum(shifts)
    merged = pl.pallas_call(
        functools.partial(merge_kernel, shifts, steps, slot_at, match_at, place_at),
        in_specs=[scalar_spec] + [whole] * count + [pl.BlockSpec(memory_space=pl.ANY)],
        out_specs=pl.BlockSpec(memory_space=pl.ANY),
        out_shape=shape((row_count, WIDTH), BF16),
        scratch_shapes=[pltpu.VMEM((slots, BLOCK, WIDTH), BF16), pltpu.SemaphoreType.DMA((HEADS,))],
        input_output_aliases={count + 1: 0},
        compiler_params=pltpu.CompilerParams(vmem_limit_bytes=VMEM_LIMIT),
        cost_estimate=pl.CostEstimate(flops=MODEL_FLOPS["merge_near"], bytes_accessed=1000, transcendentals=0),
        name="merge_near",
    )(meta, *state, *received, partial_out)
    return merged[None]


def solution(mesh):
    in_specs = (P("fsdp", "seq", None), P("fsdp", None), P(), P())
    out_specs = P("fsdp", "seq", None)
    return jax.shard_map(body, mesh=mesh, in_specs=in_specs, out_specs=out_specs, check_vma=False)
```
